32 devices in a mesh: dp: 8 (over y, x, core), tensor: 4 (over z).
Axes of the slice: x: 2, y: 2, z: 4, core: 2. Of those that a mesh axis runs over, the one named last changes fastest.
Arguments:
- latent: bfloat16 [8192, 1408], P(('dp', 'tensor')), may hold values from -6 to 6
- skip_in: bfloat16 [8192, 1408], P(('dp', 'tensor')), may hold values from -6 to 6
- text_tokens: bfloat16 [2560, 1408], P(('dp', 'tensor')), may hold values from -6 to 6
- time_embed: float32 [8, 1408], P('dp'), may hold values from -6 to 6
- t_index: int32 [8], P('dp'), may hold values from 0 to 999
- grid_pos: int32 [2, 8192], P(None, 'dp'), may hold values from 0 to 127, as said below
- skip_weight: bfloat16 [2816, 1408], P('dp'), may hold values from -0.109375 to 0.109375
- mod_weight: bfloat16 [1408, 1408], P('dp'), may hold values from -0.15625 to 0.15625
- vectors: bfloat16 [25, 1408], P(None, 'dp'), may hold values from -0.75 to 1.5
- up_bias: bfloat16 [6144], P('dp'), may hold values from -2 to 2
- qkv_weight: bfloat16 [1408, 3, 1408], P('dp', None, 'tensor'), may hold values from -0.15625 to 0.15625
- proj_weight: bfloat16 [1408, 1408], P('tensor', 'dp'), may hold values from -0.625 to 0.625
- query_weight: bfloat16 [1408, 1408], P('dp', 'tensor'), may hold values from -0.15625 to 0.15625
- text_weight: bfloat16 [1408, 2, 1408], P('dp', None, 'tensor'), may hold values from -0.15625 to 0.15625
- cross_weight: bfloat16 [1408, 1408], P('tensor', 'dp'), may hold values from -0.4375 to 0.4375
- up_weight: bfloat16 [1408, 6144], P('dp', 'tensor'), may hold values from -0.15625 to 0.15625
- down_weight: bfloat16 [6144, 1408], P('tensor', 'dp'), may hold values from -0.3125 to 0.3125
- out_grad: bfloat16 [8192, 1408], P(('dp', 'tensor')), may hold values from -6 to 6
Outputs:
- block_out: bfloat16 [8192, 1408], P(('dp', 'tensor'))
- latent_grad: float32 [8192, 1408], P(('dp', 'tensor'))
- skip_grad: float32 [8192, 1408], P(('dp', 'tensor'))
- text_grad: float32 [2560, 1408], P(('dp', 'tensor'))
- time_grad: float32 [8, 1408], P('dp', 'tensor')
- skip_weight_grad: float32 [2816, 1408], P('dp')
- mod_weight_grad: float32 [1408, 1408], P('dp')
- vectors_grad: float32 [25, 1408], P(None, 'dp')
- up_bias_grad: float32 [6144], P('dp')
- qkv_weight_grad: float32 [1408, 3, 1408], P('dp', None, 'tensor')
- proj_weight_grad: float32 [1408, 1408], P('tensor', 'dp')
- query_weight_grad: float32 [1408, 1408], P('dp', 'tensor')
- text_weight_grad: float32 [1408, 2, 1408], P('dp', None, 'tensor')
- cross_weight_grad: float32 [1408, 1408], P('tensor', 'dp')
- up_weight_grad: float32 [1408, 6144], P('dp', 'tensor')
- down_weight_grad: float32 [6144, 1408], P('tensor', 'dp')
The draws below stay inside these ranges and needn't reach their ends.
Inputs may be any that keep to these rules, and one draw needn't show every extreme that they name: `grid_pos`: token i of an image lies at row i // w and column i % w of a grid whose width w is a power of two from 8 to 64, chosen for each image; some image has w = 8 and another w = 64.
All inputs are finite; a program needn't handle non-finite values.
Results may differ from the reference program's by a relative error of at most 0.029.
Values may be sent and summed in bfloat16 or wider, within the bound.
A program may use at most 384 MiB of HBM per device.

```python
import math
import jax
import jax.numpy as jnp
import numpy as np
from jax import lax

HEADS = 16
HD = 88
D = 1408
FF = 6144
SEQ = 1024
TEXT = 320
NV = 25
IMAGES = 8
TOKENS = 8192
TEXT_ROWS = 2560


GAIN_ROWS = np.array([1 if index in (0, 1, 6, 12, 13, 14, 20, 21, 22) else 0 for index in range(25)], dtype=np.int32)


def draw_grid_pos(key, part):
    key_one, key_two, key_three = jax.random.split(key, 3)
    powers = jax.random.randint(key_one, (IMAGES,), 3, 7)
    first_pick = jax.random.randint(key_two, (), 0, IMAGES)
    second_pick = (first_pick + 1 + jax.random.randint(key_three, (), 0, IMAGES - 1)) % IMAGES
    image_ids = jnp.arange(IMAGES)
    powers = jnp.where(image_ids == first_pick, 3, powers)
    powers = jnp.where(image_ids == second_pick, 6, powers)
    widths = jnp.left_shift(jnp.ones((IMAGES,), jnp.int32), powers.astype(jnp.int32))
    places = jnp.arange(SEQ, dtype=jnp.int32)
    grid_rows = places[None, :] // widths[:, None]
    grid_cols = places[None, :] % widths[:, None]
    return jnp.stack([grid_rows.reshape(-1), grid_cols.reshape(-1)]).astype(jnp.int32)


def draw_vectors(key, part):
    base = jnp.clip(jax.random.normal(key, (NV, D), jnp.float32), -4.0, 4.0)
    gain_mask = jnp.asarray(GAIN_ROWS)[:NV] > 0
    return jnp.where(gain_mask[:, None], 1.0 + 0.125 * base, 0.1875 * base).astype(jnp.bfloat16)


def with_ends(values, rng, least, high):
    index_at = [jax.random.randint(jax.random.fold_in(rng, axis), (), 0, length) for axis, length in enumerate(values.shape)]
    longest = values.shape.index(max(values.shape))
    neighbour = index_at[:longest] + [(index_at[longest] + 1) % values.shape[longest]] + index_at[longest + 1:]
    return values.at[tuple(index_at)].set(least).at[tuple(neighbour)].set(high)


def shard_levels(own_key, shape, cuts, smallest, largest):
    gain = 1.0
    for axis_at, blocks in cuts:
        steps = jax.random.uniform(jax.random.fold_in(jax.random.fold_in(own_key, 6), axis_at), (blocks,), jnp.float32, smallest / len(cuts), largest / len(cuts))
        gain = gain * jnp.repeat(jnp.exp(steps), shape[axis_at] // blocks).reshape((-1,) + (1,) * (len(shape) - 1 - axis_at))
    return gain


def gaussian(own_key, shape, spread, bound, shards=(), kind=jnp.bfloat16):
    factor_of = shard_levels(own_key, shape, shards, -0.22, 0.18) if shards else 1.0
    drawn = jax.random.normal(own_key, shape, jnp.float32) * spread * factor_of
    return jnp.minimum(jnp.maximum(drawn, -bound), bound).astype(kind)


def setup_inputs(seed: int = 0) -> dict:
    key_of = jax.random.split(jax.random.key(seed), 19)
    latent = gaussian(key_of[0], (TOKENS, D), 1.0, 6.0, ((0, 32),))
    skip_in = gaussian(key_of[1], (TOKENS, D), 1.0, 6.0, ((0, 32),))
    text_tokens = gaussian(key_of[2], (TEXT_ROWS, D), 1.0, 6.0, ((0, 32),))
    time_embed = gaussian(key_of[3], (IMAGES, D), 1.0, 6.0, ((0, 8),), jnp.float32)
    t_index = with_ends(jax.random.randint(key_of[4], (IMAGES,), 0, 1000), jax.random.fold_in(key_of[4], 1), 0, 999).astype(jnp.int32)
    grid_pos = draw_grid_pos(jax.random.fold_in(key_of[18], 71), 0)
    skip_weight = gaussian(key_of[6], (2 * D, D), (2 * D) ** -0.5, 0.109375, ((0, 8),))
    mod_weight = gaussian(key_of[7], (D, D), D ** -0.5, 0.15625, ((0, 8),))
    vectors = draw_vectors(jax.random.fold_in(key_of[18], 71), 0)
    up_bias = gaussian(key_of[9], (FF,), 0.3, 2.0, ((0, 8),))
    qkv_weight = gaussian(key_of[10], (D, 3, D), D ** -0.5, 0.15625, ((0, 8), (2, 4)))
    proj_weight = gaussian(key_of[11], (D, D), (D // 16) ** -0.5, 0.625, ((0, 4), (1, 8)))
    query_weight = gaussian(key_of[12], (D, D), D ** -0.5, 0.15625, ((0, 8), (1, 4)))
    text_weight = gaussian(key_of[13], (D, 2, D), D ** -0.5, 0.15625, ((0, 8), (2, 4)))
    cross_weight = gaussian(key_of[14], (D, D), (D // 8) ** -0.5, 0.4375, ((0, 4), (1, 8)))
    up_weight = gaussian(key_of[15], (D, FF), D ** -0.5, 0.15625, ((0, 8), (1, 4)))
    down_weight = gaussian(key_of[16], (FF, D), (FF // 16) ** -0.5, 0.3125, ((0, 4), (1, 8)))
    out_grad = gaussian(key_of[17], (TOKENS, D), 1.0, 6.0, ((0, 32),))
    return {"latent": latent, "skip_in": skip_in, "text_tokens": text_tokens, "time_embed": time_embed, "t_index": t_index, "grid_pos": grid_pos, "skip_weight": skip_weight, "mod_weight": mod_weight, "vectors": vectors, "up_bias": up_bias, "qkv_weight": qkv_weight, "proj_weight": proj_weight, "query_weight": query_weight, "text_weight": text_weight, "cross_weight": cross_weight, "up_weight": up_weight, "down_weight": down_weight, "out_grad": out_grad}


EPSILON = 1e-06
HIGHEST = lax.Precision.HIGHEST

@jax.custom_vjp
def low(v):
    return lax.optimization_barrier(v.astype(jnp.bfloat16)).astype(jnp.float32)

@jax.custom_vjp
def low_back(v):
    return v

def low_keep(v):
    return (low(v), None)

def low_pass(kept, grad):
    return (grad,)

def back_keep(v):
    return (v, None)

def back_low(kept, grad):
    return (low(grad),)
low.defvjp(low_keep, low_pass)
low_back.defvjp(back_keep, back_low)

def matmul(left, right):
    return jnp.dot(left, right, precision=HIGHEST)

def layer_norm(values, norm_gain, norm_bias):
    centred = values - lax.optimization_barrier(jnp.mean(values, axis=-1, keepdims=True))
    variance = lax.optimization_barrier(jnp.mean(centred * centred, axis=-1, keepdims=True))
    return centred * lax.rsqrt(variance + EPSILON) * norm_gain + norm_bias

def head_norm(values, norm_gain):
    centred = values - lax.optimization_barrier(jnp.mean(values, axis=-1, keepdims=True))
    variance = lax.optimization_barrier(jnp.mean(centred * centred, axis=-1, keepdims=True))
    return centred * lax.rsqrt(variance + EPSILON) * norm_gain

def rotate(values, grid_rows, grid_cols):
    half_dim = values.shape[-1] // 2
    quarter = half_dim // 2
    inverse = 10000.0 ** (-jnp.arange(quarter, dtype=jnp.float32) / quarter)
    pieces = []
    for position, offset in ((grid_rows, 0), (grid_cols, half_dim)):
        angles = position.astype(jnp.float32)[:, None] * inverse[None, :]
        cosine = jnp.cos(angles)[:, None, :]
        sine_part = jnp.sin(angles)[:, None, :]
        front_part = values[..., offset:offset + quarter]
        back_part = values[..., offset + quarter:offset + half_dim]
        pieces.append(front_part * cosine - back_part * sine_part)
        pieces.append(back_part * cosine + front_part * sine_part)
    return jnp.concatenate(pieces, axis=-1)

def silu(values):
    return values / (1.0 + jnp.exp(-values))

def gelu(values):
    inner = math.sqrt(2.0 / math.pi) * (values + 0.044715 * values * values * values)
    return 0.5 * values * (1.0 + jnp.tanh(inner))

def attend(queries, keys, values_in, scale):
    length, heads, depth = queries.shape
    rows_block = min(512, length)

    def one_block(query_block):
        scores = low_back(jnp.einsum('qhd,khd->hqk', query_block, keys, precision=HIGHEST) * scale)
        row_peak = lax.optimization_barrier(jnp.max(scores, axis=-1, keepdims=True))
        powers = jnp.exp(scores - row_peak)
        weights = powers / lax.optimization_barrier(jnp.sum(powers, axis=-1, keepdims=True))
        return jnp.einsum('hqk,khd->qhd', low(weights), values_in, precision=HIGHEST)
    blocks = queries.reshape(length // rows_block, rows_block, heads, depth)
    return lax.map(jax.checkpoint(one_block), blocks).reshape(length, heads, depth)

def forward(params, latent, skip_in, text_tokens, condition, grid_rows, grid_cols):
    w_skip, w_mod, vectors, up_bias, w_qkv, w_proj, w_query, w_text, w_cross, w_up, w_down = params
    length = latent.shape[0]
    width = latent.shape[1]
    scale = 1.0 / math.sqrt(HD)

    def head_view(values):
        return values.reshape(values.shape[0], HEADS, HD)

    def gains_view(index):
        return vectors[index].reshape(HEADS, HD)
    shift = matmul(low(silu(condition)), w_mod) + vectors[5]
    joined = jnp.concatenate([latent, skip_in], axis=-1)
    normed = layer_norm(joined, jnp.concatenate([vectors[0], vectors[1]]), jnp.concatenate([vectors[2], vectors[3]]))
    stream_one = low_back(matmul(low(normed), w_skip)) + vectors[4]
    attn_in = low(layer_norm(stream_one, vectors[6], vectors[7]) + shift)
    projected = low_back(jnp.einsum('sd,dkh->skh', attn_in, w_qkv, precision=HIGHEST) + vectors[8:11])
    queries = low(rotate(head_norm(head_view(projected[:, 0]), gains_view(12)), grid_rows, grid_cols))
    keys = low(rotate(head_norm(head_view(projected[:, 1]), gains_view(13)), grid_rows, grid_cols))
    values_self = low(head_view(projected[:, 2]))
    mixed = low(low_back(attend(queries, keys, values_self, scale)).reshape(length, width))
    stream_two = stream_one + low_back(matmul(mixed, w_proj)) + vectors[11]
    cross_in = low(layer_norm(stream_two, vectors[14], vectors[15]))
    cross_raw = low_back(matmul(cross_in, w_query) + vectors[16])
    text_raw = low_back(jnp.einsum('md,dkh->mkh', text_tokens, w_text, precision=HIGHEST) + vectors[17:19])
    cross_queries = low(head_norm(head_view(cross_raw), gains_view(20)))
    text_keys = low(head_norm(head_view(text_raw[:, 0]), gains_view(21)))
    text_values = low(head_view(text_raw[:, 1]))
    cross_mixed = low(low_back(attend(cross_queries, text_keys, text_values, scale)).reshape(length, width))
    stream_three = stream_two + low_back(matmul(cross_mixed, w_cross)) + vectors[19]
    mlp_in = low(layer_norm(stream_three, vectors[22], vectors[23]))
    hidden_pre = low_back(matmul(mlp_in, w_up) + up_bias)
    hidden = low(gelu(hidden_pre))
    return stream_three + low_back(matmul(hidden, w_down)) + vectors[24]

def reference(latent, skip_in, text_tokens, time_embed, t_index, grid_pos, skip_weight, mod_weight, vectors, up_bias, qkv_weight, proj_weight, query_weight, text_weight, cross_weight, up_weight, down_weight, out_grad):
    params = tuple((item.astype(jnp.float32) for item in (skip_weight, mod_weight, vectors, up_bias, qkv_weight, proj_weight, query_weight, text_weight, cross_weight, up_weight, down_weight)))
    half_dim = D // 2
    frequencies = jnp.exp(-math.log(10000.0) * jnp.arange(half_dim, dtype=jnp.float32) / half_dim)
    angles = t_index.astype(jnp.float32)[:, None] * frequencies[None, :]
    condition = time_embed + jnp.concatenate([jnp.cos(angles), jnp.sin(angles)], axis=-1)
    stacked = (latent.astype(jnp.float32).reshape(IMAGES, SEQ, D), skip_in.astype(jnp.float32).reshape(IMAGES, SEQ, D), text_tokens.astype(jnp.float32).reshape(IMAGES, TEXT, D), condition, jnp.transpose(grid_pos.reshape(2, IMAGES, SEQ), (1, 0, 2)), out_grad.astype(jnp.float32).reshape(IMAGES, SEQ, D))

    def one_image(totals, item):
        lat_part, skip_part, text_part, cond_part, grid_part, cot_part = item

        def run(weights, lat_in, skip_one, text_one, cond_one):
            return forward(weights, lat_in, skip_one, text_one, cond_one, grid_part[0], grid_part[1])
        result, pull = jax.vjp(run, params, lat_part, skip_part, text_part, cond_part)
        grads = pull(cot_part)
        totals = jax.tree.map(lambda running, added: running + added, totals, grads[0])
        return (totals, (result.astype(jnp.bfloat16), grads[1], grads[2], grads[3], grads[4]))
    zeros = jax.tree.map(jnp.zeros_like, params)
    totals, (outputs, lat_grads, skip_grads, text_grads, cond_grads) = lax.scan(one_image, zeros, stacked)
    return (outputs.reshape(TOKENS, D), lat_grads.reshape(TOKENS, D), skip_grads.reshape(TOKENS, D), text_grads.reshape(TEXT_ROWS, D), cond_grads, totals[0], totals[1], totals[2], totals[3], totals[4], totals[5], totals[6], totals[7], totals[8], totals[9], totals[10])
```

```python
import functools
import math

import jax
import jax.numpy as jnp
import numpy as np
from jax import lax
from jax.experimental import pallas as pl
from jax.experimental.pallas import tpu as pltpu
from jax.sharding import PartitionSpec as P

HEADS = 16
HD = 88
LANES = 128
EPSILON = 1e-06
HIGHEST = lax.Precision.HIGHEST
FLOAT = jnp.float32
BFLOAT = jnp.bfloat16
LOG2E = 1.4426950408889634
SCALE = 1.0 / math.sqrt(HD)


def layer_norm(values, norm_gain, norm_bias):
    centred = values - jnp.mean(values, axis=-1, keepdims=True)
    variance = jnp.mean(centred * centred, axis=-1, keepdims=True)
    return centred * lax.rsqrt(variance + EPSILON) * norm_gain + norm_bias


def head_norm(values, norm_gain):
    centred = values - jnp.mean(values, axis=-1, keepdims=True)
    variance = jnp.mean(centred * centred, axis=-1, keepdims=True)
    return centred * lax.rsqrt(variance + EPSILON) * norm_gain


def silu(values):
    return values / (1.0 + jnp.exp(-values))


def gelu(values):
    inner = math.sqrt(2.0 / math.pi) * (values + 0.044715 * values * values * values)
    return 0.5 * values * (1.0 + jnp.tanh(inner))


def dot(left, right, contract=((1,), (0,))):
    return lax.dot_general(left, right, (contract, ((), ())), preferred_element_type=FLOAT)


NT = ((1,), (1,))
TN = ((0,), (0,))


def rot(values, step):
    count = lax.axis_size("tensor")
    return lax.ppermute(values, "tensor", [(i, (i + step) % count) for i in range(count)])


def ring_gather(own):
    blocks = [own]
    for _ in range(lax.axis_size("tensor") - 1):
        blocks.append(rot(blocks[-1], 1))
    return blocks


def ring_scatter(parts):
    running = parts[1].astype(BFLOAT)
    for part in parts[2:]:
        running = (rot(running, 1).astype(FLOAT) + part.astype(FLOAT)).astype(BFLOAT)
    return rot(running, 1).astype(FLOAT) + parts[0].astype(FLOAT)


def exchange(parts):
    count = len(parts)
    return [parts[0]] + [rot(parts[count - r], r) for r in range(1, count)]


def after(values, *earlier):
    return lax.optimization_barrier((values, *earlier))[0]


def small_gather(own):
    have = own[None]
    me = lax.axis_index("dp")
    count = lax.axis_size("dp")
    step = 1
    while step < count:
        other = lax.ppermute(have, "dp", [(i, i ^ step) for i in range(count)])
        upper = (me // step) % 2 == 1
        have = jnp.where(upper, jnp.concatenate([other, have]), jnp.concatenate([have, other]))
        step *= 2
    return have


def tensor_sum(values):
    total = values
    for step in range(1, lax.axis_size("tensor")):
        total = total + rot(values, step)
    return total


def grad_kernel(*refs):
    left_ref, right_ref, out_ref, turned_ref = refs[0], refs[1], refs[-2], refs[-1]

    @pl.when(pl.program_id(0) == 0)
    def _():
        turned_ref[...] = left_ref[...].T

    out_ref[...] = dot(turned_ref[...], right_ref[...]).astype(BFLOAT)


def pack_grad(packed, left, right, lanes, start, tile):
    rows, height = left.shape
    wide = right.shape[1]
    first = start // tile
    in_specs = [
        pl.BlockSpec((rows, height), lambda i: (0, 0)),
        pl.BlockSpec((rows, tile), lambda i: (0, i)),
    ]
    operands = [left, right]
    if packed is not None:
        in_specs.append(pl.BlockSpec(memory_space=pl.ANY))
        operands.append(packed)
    return pl.pallas_call(
        grad_kernel,
        grid=(pl.cdiv(wide, tile),),
        in_specs=in_specs,
        out_specs=pl.BlockSpec((height, tile), lambda i: (0, first + i)),
        out_shape=jax.ShapeDtypeStruct((height, lanes), BFLOAT),
        scratch_shapes=[pltpu.VMEM((height, rows), BFLOAT)],
        input_output_aliases={} if packed is None else {2: 0},
        compiler_params=pltpu.CompilerParams(vmem_limit_bytes=40 * 2**20),
        cost_estimate=pl.CostEstimate(
            flops=2 * rows * height * wide, bytes_accessed=2 * (rows * height + rows * wide + height * wide), transcendentals=0
        ),
    )(*operands)


def padded(values):
    return jnp.concatenate([values, jnp.zeros((values.shape[0], LANES - HD), values.dtype)], axis=1)


def lane_mask(rows):
    lanes = lax.broadcasted_iota(jnp.int32, (rows, LANES), 1)
    return (lanes < HD).astype(FLOAT)


def norm_parts(values, mask):
    mean = jnp.sum(values, axis=-1, keepdims=True) * (1.0 / HD)
    centred = (values - mean) * mask
    variance = jnp.sum(centred * centred, axis=-1, keepdims=True) * (1.0 / HD)
    inverse = lax.rsqrt(variance + EPSILON)
    return centred * inverse, inverse


CHUNK = 128


def attend_forward_kernel(
    heads, block, raw_ref, cos_ref, sin_a_ref, sin_b_ref, gain_ref, o_ref, opad_ref, q_ref, k_ref, v_ref, lse_ref
):
    length = raw_ref.shape[0]
    span = heads * HD
    mask = lane_mask(CHUNK)

    def prepare(index, carry):
        rows = pl.ds(pl.multiple_of(index * CHUNK, CHUNK), CHUNK)
        cosine, sine_a, sine_b = cos_ref[rows, :], sin_a_ref[rows, :], sin_b_ref[rows, :]
        for head in range(heads):
            for part, out_ref in ((0, q_ref), (1, k_ref)):
                start = part * span + head * HD
                values = padded(raw_ref[rows, start : start + HD])
                normed, _ = norm_parts(values, mask)
                turned = normed * gain_ref[part * heads + head, :][None, :]
                turned = (
                    turned * cosine
                    + pltpu.roll(turned, LANES - HD // 4, 1) * sine_a
                    + pltpu.roll(turned, HD // 4, 1) * sine_b
                )
                out_ref[head, rows, :] = turned.astype(BFLOAT)
            start = 2 * span + head * HD
            v_ref[head, rows, :] = padded(raw_ref[rows, start : start + HD]).astype(BFLOAT)
        return carry

    lax.fori_loop(0, length // CHUNK, prepare, 0)
    count = length // block

    def attend(index, carry):
        head = lax.div(index, count)
        rows = pl.ds(pl.multiple_of(lax.rem(index, count) * block, block), block)
        scores = dot(k_ref[head], q_ref[head, rows, :], NT)
        peak = jnp.max(scores, axis=0, keepdims=True)
        powers = jnp.exp2((scores - peak) * (SCALE * LOG2E))
        total = jnp.sum(powers, axis=0, keepdims=True)
        mixed = dot(v_ref[head], powers.astype(BFLOAT), TN) / total
        opad_ref[head, rows, :] = jnp.transpose(mixed).astype(BFLOAT)
        lse_ref[index] = peak * (SCALE * LOG2E) + jnp.log2(total)
        return carry

    lax.fori_loop(0, heads * count, attend, 0)

    def finish(index, carry):
        rows = pl.ds(pl.multiple_of(index * CHUNK, CHUNK), CHUNK)
        o_ref[rows, :] = jnp.concatenate(
            [opad_ref[head, rows, :].astype(FLOAT)[:, :HD] for head in range(heads)], axis=1
        ).astype(BFLOAT)
        return carry

    lax.fori_loop(0, length // CHUNK, finish, 0)


def attend_forward(raw, tables, gains, heads, block):
    length = raw.shape[0]
    head_shape = jax.ShapeDtypeStruct((heads, length, LANES), BFLOAT)
    return pl.pallas_call(
        functools.partial(attend_forward_kernel, heads, block),
        out_shape=(
            jax.ShapeDtypeStruct((length, heads * HD), BFLOAT),
            head_shape,
            head_shape,
            head_shape,
            head_shape,
            jax.ShapeDtypeStruct((heads * (length // block), 1, block), FLOAT),
        ),
        compiler_params=pltpu.CompilerParams(vmem_limit_bytes=56 * 2**20),
        cost_estimate=pl.CostEstimate(flops=4_000_000_000, bytes_accessed=12_000_000, transcendentals=4_200_000),
    )(raw, *tables, gains)


def attend_backward_kernel(
    heads, block, raw_ref, cos_ref, sin_a_ref, sin_b_ref, gain_ref, opad_ref, q_ref, k_ref, v_ref, lse_ref, do_ref,
    graw_ref, gain_out_ref, sums_ref, dpad_ref, dq_ref, dk_ref, dv_ref,
):
    length = raw_ref.shape[0]
    span = heads * HD
    mask = lane_mask(CHUNK)
    count = length // block

    def prepare(index, carry):
        rows = pl.ds(pl.multiple_of(index * CHUNK, CHUNK), CHUNK)
        values = do_ref[rows, :].astype(FLOAT)
        for head in range(heads):
            dpad_ref[head, rows, :] = padded(values[:, head * HD : (head + 1) * HD]).astype(BFLOAT)
        return carry

    lax.fori_loop(0, length // CHUNK, prepare, 0)

    def attend(index, carry):
        head = lax.div(index, count)
        rows = pl.ds(pl.multiple_of(lax.rem(index, count) * block, block), block)
        queries = q_ref[head, rows, :]
        grad = dpad_ref[head, rows, :]
        scores = dot(k_ref[head], queries, NT)
        probs = jnp.exp2(scores * (SCALE * LOG2E) - lse_ref[index])
        grad_probs = dot(v_ref[head], grad, NT)
        inner = jnp.transpose(grad.astype(FLOAT) * opad_ref[head, rows, :].astype(FLOAT))
        inner = jnp.sum(inner, axis=0, keepdims=True)
        grad_scores = (probs * (grad_probs - inner)).astype(BFLOAT)
        add_v = dot(probs.astype(BFLOAT), grad)
        add_k = dot(grad_scores, queries)
        dq_ref[head, rows, :] = jnp.transpose(dot(k_ref[head], grad_scores, TN))

        @pl.when(lax.rem(index, count) == 0)
        def _():
            dv_ref[head] = add_v
            dk_ref[head] = add_k

        @pl.when(lax.rem(index, count) != 0)
        def _():
            dv_ref[head] += add_v
            dk_ref[head] += add_k

        return carry

    lax.fori_loop(0, heads * count, attend, 0)
    gain_out_ref[...] = jnp.zeros_like(gain_out_ref)
    sums_ref[...] = jnp.zeros_like(sums_ref)

    def finish(index, carry):
        rows = pl.ds(pl.multiple_of(index * CHUNK, CHUNK), CHUNK)
        cosine, sine_a, sine_b = cos_ref[rows, :], sin_a_ref[rows, :], sin_b_ref[rows, :]
        for part, grad_ref in ((0, dq_ref), (1, dk_ref)):
            pieces = []
            for head in range(heads):
                start = part * span + head * HD
                normed, inverse = norm_parts(padded(raw_ref[rows, start : start + HD]), mask)
                grad = grad_ref[head, rows, :] * SCALE
                grad = (
                    grad * cosine
                    + pltpu.roll(grad * sine_a, HD // 4, 1)
                    + pltpu.roll(grad * sine_b, LANES - HD // 4, 1)
                )
                slot = part * heads + head
                gain_out_ref[slot : slot + 1, :] += jnp.sum(grad * normed, axis=0, keepdims=True)
                grad = grad * gain_ref[slot, :][None, :]
                mean = jnp.sum(grad, axis=-1, keepdims=True) * (1.0 / HD)
                slope = jnp.sum(grad * normed, axis=-1, keepdims=True) * (1.0 / HD)
                pieces.append((inverse * (grad - mean - normed * slope))[:, :HD])
            low = jnp.concatenate(pieces, axis=1).astype(BFLOAT)
            graw_ref[rows, part * span : (part + 1) * span] = low
            sums_ref[part : part + 1, :] += jnp.sum(low.astype(FLOAT), axis=0, keepdims=True)
        low = jnp.concatenate([dv_ref[head, rows, :][:, :HD] for head in range(heads)], axis=1).astype(BFLOAT)
        graw_ref[rows, 2 * span :] = low
        sums_ref[2:3, :] += jnp.sum(low.astype(FLOAT), axis=0, keepdims=True)
        return carry

    lax.fori_loop(0, length // CHUNK, finish, 0)


def attend_backward(raw, tables, gains, kept, grad_out, heads, block):
    length = raw.shape[0]
    return pl.pallas_call(
        functools.partial(attend_backward_kernel, heads, block),
        out_shape=(
            jax.ShapeDtypeStruct((length, 3 * heads * HD), BFLOAT),
            jax.ShapeDtypeStruct((2 * heads, LANES), FLOAT),
            jax.ShapeDtypeStruct((8, heads * HD), FLOAT),
        ),
        scratch_shapes=[
            pltpu.VMEM((heads, length, LANES), BFLOAT),
            pltpu.VMEM((heads, length, LANES), FLOAT),
            pltpu.VMEM((heads, length, LANES), FLOAT),
            pltpu.VMEM((heads, length, LANES), FLOAT),
        ],
        compiler_params=pltpu.CompilerParams(vmem_limit_bytes=56 * 2**20),
        cost_estimate=pl.CostEstimate(flops=10_000_000_000, bytes_accessed=16_000_000, transcendentals=4_200_000),
    )(raw, *tables, gains, *kept, grad_out)


def cross_forward(queries, keys, values_in):
    scores = jnp.einsum("qhd,khd->hqk", queries, keys, preferred_element_type=FLOAT) * SCALE
    peak = jnp.max(scores, axis=-1, keepdims=True)
    powers = jnp.exp(scores - peak)
    totals = jnp.sum(powers, axis=-1, keepdims=True)
    weights = (powers / totals).astype(BFLOAT)
    mixed = jnp.einsum("hqk,khd->qhd", weights, values_in, preferred_element_type=FLOAT)
    return mixed.astype(BFLOAT), peak + jnp.log(totals)


def cross_backward(queries, keys, values_in, log_sums, grad):
    scores = jnp.einsum("qhd,khd->hqk", queries, keys, preferred_element_type=FLOAT) * SCALE
    probs = jnp.exp(scores - log_sums)
    grad_probs = jnp.einsum("qhd,khd->hqk", grad, values_in, preferred_element_type=FLOAT)
    inner = jnp.sum(probs * grad_probs, axis=-1, keepdims=True)
    grad_scores = (probs * (grad_probs - inner)).astype(BFLOAT)
    grad_q = jnp.einsum("hqk,khd->qhd", grad_scores, keys, preferred_element_type=FLOAT) * SCALE
    grad_k = jnp.einsum("hqk,qhd->khd", grad_scores, queries, preferred_element_type=FLOAT) * SCALE
    grad_v = jnp.einsum("hqk,qhd->khd", probs.astype(BFLOAT), grad, preferred_element_type=FLOAT)
    return grad_q, grad_k, grad_v


def on_device(
    latent, skip_in, text_tokens, time_embed, t_index, grid_pos, skip_weight, mod_weight, vectors, up_bias,
    qkv_weight, proj_weight, query_weight, text_weight, cross_weight, up_weight, down_weight, out_grad,
):
    split = lax.axis_size("tensor")
    shards = lax.axis_size("dp")
    place = lax.axis_index("tensor")
    me = lax.axis_index("dp")
    own_rows, width = latent.shape
    own_text = text_tokens.shape[0]
    part = mod_weight.shape[0]
    heads = HEADS // split
    span = heads * HD
    hidden = up_weight.shape[1]
    rows_ahead = vectors.shape[0]

    def others(r):
        return lax.rem(place - r + split, split)

    condition = time_embed
    half = width // 2
    frequencies = jnp.exp(-math.log(10000.0) * jnp.arange(half, dtype=FLOAT) / half)
    angles = t_index.astype(FLOAT)[:, None] * frequencies[None, :]
    condition = time_embed + jnp.concatenate([jnp.cos(angles), jnp.sin(angles)], axis=-1)
    silu_low = silu(condition).astype(BFLOAT)
    small = jnp.concatenate([vectors.reshape(-1), up_bias, silu_low.reshape(-1)])
    small_all = small_gather(small)
    cut_one, cut_two = rows_ahead * part, rows_ahead * part + up_bias.shape[0]
    table = (
        small_all[:, :cut_one].reshape(shards, rows_ahead, part).transpose(1, 0, 2).reshape(rows_ahead, width)
    ).astype(FLOAT)
    bias_all = small_all[:, cut_one:cut_two].reshape(-1).astype(FLOAT)
    silu_all = small_all[:, cut_two:]

    packed_one = jnp.concatenate(
        [
            skip_weight[:part],
            skip_weight[part:],
            qkv_weight.reshape(part, 3 * span),
            text_weight.reshape(part, 2 * span),
        ],
        axis=1,
    )
    all_one = lax.all_gather(packed_one, "dp", axis=0, tiled=True)
    w_skip = all_one[:, : 2 * width]
    w_qkv = all_one[:, 2 * width : 2 * width + 3 * span]
    w_text = all_one[:, 2 * width + 3 * span :]

    own_full = jnp.stack([proj_weight.T, query_weight, cross_weight.T])
    full_blocks = ring_gather(own_full)
    packed_two = jnp.concatenate(
        [full_blocks[r][index] for index in range(3) for r in range(split)], axis=1
    )
    all_two = lax.all_gather(packed_two, "dp", axis=0, tiled=True)
    w_proj_t, w_query, w_cross_t = (all_two[:, i * width : (i + 1) * width] for i in range(3))

    packed_three = jnp.concatenate([up_weight, down_weight.T], axis=1)
    all_three = lax.all_gather(packed_three, "dp", axis=0, tiled=True)
    w_up, w_down_t = all_three[:, :hidden], all_three[:, hidden:]

    text_blocks = ring_gather(text_tokens)
    cot_blocks = ring_gather(out_grad)
    text_full = jnp.concatenate(text_blocks, axis=0)
    cot_full = jnp.concatenate(cot_blocks, axis=0)

    def head_slice(index):
        return lax.dynamic_slice_in_dim(table[index], place * span, span, 0)

    def relative(index):
        return jnp.concatenate(
            [lax.dynamic_slice_in_dim(table[index], others(r) * span, span, 0) for r in range(split)]
        )

    def spread(values):
        return lax.dynamic_update_slice_in_dim(jnp.zeros((width,), FLOAT), values.reshape(-1), place * span, 0)

    def absolute(values):
        result = jnp.zeros((width,), FLOAT)
        for r in range(split):
            result = lax.dynamic_update_slice_in_dim(
                result, values.reshape(-1)[r * span : (r + 1) * span], others(r) * span, 0
            )
        return result

    def padded_gains(index):
        return jnp.pad(head_slice(index).reshape(heads, HD), ((0, 0), (0, LANES - HD)))

    quarter = HD // 4
    lane = np.arange(LANES)
    rate = np.where(lane < HD, 10000.0 ** (-(lane % quarter).astype(np.float64) / quarter), 0.0).astype(np.float32)
    by_row = (lane < HD // 2)[None, :]
    first = ((lane % (HD // 2)) < quarter) & (lane < HD)
    second = ((lane % (HD // 2)) >= quarter) & (lane < HD)
    grid_rel = jnp.concatenate(
        [lax.dynamic_slice_in_dim(grid_pos, others(r) * own_rows, own_rows, 1) for r in range(split)], axis=1
    ).astype(FLOAT)
    turn = jnp.where(by_row, grid_rel[0][:, None], grid_rel[1][:, None]) * rate[None, :]
    cosine, sine = jnp.cos(turn), jnp.sin(turn)
    tables = (
        cosine * (lane < HD).astype(np.float32)[None, :],
        -sine * first.astype(np.float32)[None, :],
        sine * second.astype(np.float32)[None, :],
    )

    silu_mine = lax.dynamic_slice_in_dim(silu_all, me * part, part, 1)
    shift_terms = dot(silu_mine, mod_weight)
    shift = jnp.sum(lax.all_to_all(shift_terms, "dp", 0, 0, tiled=True), axis=0, keepdims=True) + table[5]

    joined = jnp.concatenate([latent.astype(FLOAT), skip_in.astype(FLOAT)], axis=-1)
    joined_gain = jnp.concatenate([table[0], table[1]])
    joined_bias = jnp.concatenate([table[2], table[3]])
    normed_low = layer_norm(joined, joined_gain, joined_bias).astype(BFLOAT)
    normed_perm = normed_low.reshape(own_rows, shards, 2, part).transpose(0, 2, 1, 3).reshape(own_rows, 2 * width)
    stream_one = (
        dot(normed_perm[:, :width], w_skip[:, :width]) + dot(normed_perm[:, width:], w_skip[:, width:]) + table[4]
    )
    attn_low = (layer_norm(stream_one, table[6], table[7]) + shift).astype(BFLOAT)
    attn_low = after(attn_low, text_blocks[-1], cot_blocks[-1], full_blocks[-1])
    attn_blocks = ring_gather(attn_low)
    qkv_bias = jnp.concatenate([head_slice(8), head_slice(9), head_slice(10)])
    raw = jnp.concatenate([dot(block, w_qkv) + qkv_bias for block in attn_blocks], axis=0)
    gains = jnp.concatenate([padded_gains(12), padded_gains(13)], axis=0)
    length = raw.shape[0]
    block = min(512, length)
    mixed, *kept = attend_forward(raw, tables, gains, heads, block)

    def blocks_of(values, rows):
        return [values[r * rows : (r + 1) * rows] for r in range(split)]

    mixed_own = jnp.concatenate(exchange(blocks_of(mixed, own_rows)), axis=1)

    text_raw = dot(text_full, w_text) + jnp.concatenate([head_slice(17), head_slice(18)])
    text_length = text_raw.shape[0]
    gain_21 = head_slice(21).reshape(heads, HD)
    raw_key = text_raw[:, :span].reshape(text_length, heads, HD)
    text_low = jnp.concatenate(
        [head_norm(raw_key, gain_21).reshape(text_length, span), text_raw[:, span:]], axis=1
    ).astype(BFLOAT)
    text_rel = ring_gather(after(text_low, attn_blocks[-1]))
    text_keys = jnp.concatenate([item[:, :span] for item in text_rel], axis=1).reshape(text_length, HEADS, HD)
    text_values = jnp.concatenate([item[:, span:] for item in text_rel], axis=1).reshape(text_length, HEADS, HD)

    stream_two = stream_one + dot(mixed_own, w_proj_t, NT) + table[11]
    cross_low = layer_norm(stream_two, table[14], table[15]).astype(BFLOAT)
    cross_raw = (dot(cross_low, w_query) + relative(16)).reshape(own_rows, HEADS, HD)
    gain_20 = relative(20).reshape(HEADS, HD)
    cross_queries = head_norm(cross_raw, gain_20).astype(BFLOAT)
    cross_mixed, cross_logs = cross_forward(cross_queries, text_keys, text_values)
    cross_mixed = cross_mixed.reshape(own_rows, width)
    stream_three = stream_two + dot(cross_mixed, w_cross_t, NT) + table[19]
    mlp_low = layer_norm(stream_three, table[22], table[23]).astype(BFLOAT)
    mlp_blocks = ring_gather(mlp_low)
    hidden_bias = lax.dynamic_slice_in_dim(bias_all, place * hidden, hidden, 0)

    hidden_lows, pre_lows, out_parts, back_parts = [], [], [], []
    for r in range(split):
        hidden_pre = dot(mlp_blocks[r], w_up) + hidden_bias
        activated, pull = jax.vjp(gelu, hidden_pre)
        hidden_lows.append(activated.astype(BFLOAT))
        pre_lows.append(pull(dot(cot_blocks[r], w_down_t))[0].astype(BFLOAT))
        back_parts.append(dot(pre_lows[r], w_up, NT))
        out_parts.append(dot(hidden_lows[r], w_down_t, NT))
    grad_mlp_in = ring_scatter(back_parts)

    rows_grad = {}
    mlp_full = jnp.concatenate(mlp_blocks, axis=0)
    pre_full = jnp.concatenate(pre_lows, axis=0)
    hidden_full = jnp.concatenate(hidden_lows, axis=0)
    grad_bias = jnp.sum(pre_full, axis=0, dtype=FLOAT)
    grads_one = pack_grad(None, mlp_full, pre_full, 2 * hidden, 0, 512)
    grads_one = pack_grad(grads_one, cot_full, hidden_full, 2 * hidden, hidden, 512)
    summed_one = lax.psum_scatter(grads_one, "dp", scatter_dimension=0, tiled=True).astype(FLOAT)

    cot_here = out_grad.astype(FLOAT)
    rows_grad[24] = jnp.sum(cot_here, axis=0)
    into_three, rows_grad[22], rows_grad[23] = jax.vjp(layer_norm, stream_three, table[22], table[23])[1](grad_mlp_in)
    grad_three = cot_here + into_three
    three_low = grad_three.astype(BFLOAT)
    rows_grad[19] = jnp.sum(grad_three, axis=0)
    grad_cross_mixed = dot(three_low, w_cross_t).astype(BFLOAT).reshape(own_rows, HEADS, HD)
    grad_cq, grad_ck, grad_cv = cross_backward(cross_queries, text_keys, text_values, cross_logs, grad_cross_mixed)
    into_cq, gain_cq = jax.vjp(head_norm, cross_raw, gain_20)[1](grad_cq)
    rows_grad[20] = absolute(gain_cq)
    cq_low = into_cq.reshape(own_rows, width).astype(BFLOAT)
    rows_grad[16] = absolute(jnp.sum(cq_low, axis=0, dtype=FLOAT))
    grad_cross_in = dot(cq_low, w_query, NT)
    into_two, rows_grad[14], rows_grad[15] = jax.vjp(layer_norm, stream_two, table[14], table[15])[1](grad_cross_in)
    grad_two = grad_three + into_two
    two_low = grad_two.astype(BFLOAT)
    rows_grad[11] = jnp.sum(grad_two, axis=0)
    grad_mixed = dot(two_low, w_proj_t).astype(BFLOAT)
    grad_mixed_blocks = exchange([grad_mixed[:, r * span : (r + 1) * span] for r in range(split)])
    out_parts[1] = after(out_parts[1].astype(BFLOAT), grad_mixed_blocks[-1])
    block_out = (stream_three + ring_scatter(out_parts) + table[24]).astype(BFLOAT)

    grad_ck = grad_ck.reshape(text_length, width)
    grad_cv = grad_cv.reshape(text_length, width)
    text_terms = [
        jnp.concatenate([grad_ck[:, r * span : (r + 1) * span], grad_cv[:, r * span : (r + 1) * span]], axis=1)
        for r in range(split)
    ]
    text_terms[1] = after(text_terms[1].astype(BFLOAT), grad_mixed_blocks[-1])
    text_sum = ring_scatter(text_terms)
    into_ck, gain_ck = jax.vjp(head_norm, raw_key, gain_21)[1](text_sum[:, :span].reshape(text_length, heads, HD))
    rows_grad[21] = spread(gain_ck)
    ckv_low = jnp.concatenate([into_ck.reshape(text_length, span), text_sum[:, span:]], axis=1).astype(BFLOAT)
    ckv_sums = jnp.sum(ckv_low, axis=0, dtype=FLOAT)
    rows_grad[17], rows_grad[18] = spread(ckv_sums[:span]), spread(ckv_sums[span:])
    text_grad = ring_scatter(blocks_of(dot(ckv_low, w_text, NT), own_text))

    lanes_two = 3 * width + pl.cdiv(2 * span, LANES) * LANES
    grads_two = pack_grad(None, two_low, mixed_own, lanes_two, 0, width)
    grads_two = pack_grad(grads_two, cross_low, cq_low, lanes_two, width, width)
    grads_two = pack_grad(grads_two, three_low, cross_mixed, lanes_two, 2 * width, width)
    grads_two = pack_grad(grads_two, text_full, ckv_low, lanes_two, 3 * width, LANES)
    summed_two = lax.psum_scatter(grads_two, "dp", scatter_dimension=0, tiled=True)
    full_sum = ring_scatter(
        [
            jnp.concatenate(
                [summed_two[:, i * width + r * span : i * width + (r + 1) * span] for i in range(3)], axis=1
            )
            for r in range(split)
        ]
    )

    grad_raw, gain_grads, raw_sums = attend_backward(
        raw, tables, gains, kept, jnp.concatenate(grad_mixed_blocks, axis=0), heads, block
    )
    rows_grad[12] = spread(gain_grads[:heads, :HD])
    rows_grad[13] = spread(gain_grads[heads:, :HD])
    rows_grad[8], rows_grad[9], rows_grad[10] = spread(raw_sums[0]), spread(raw_sums[1]), spread(raw_sums[2])
    raw_blocks = blocks_of(grad_raw, own_rows)
    attn_parts = [dot(item, w_qkv, NT) for item in raw_blocks]
    shift_part = sum(jnp.sum(item, axis=0) for item in attn_parts)
    rows_grad[5] = shift_part
    grad_attn_in = ring_scatter(attn_parts)
    shift_grads = small_gather(tensor_sum(shift_part))
    mod_grad = lax.dot_general(
        silu_mine.astype(FLOAT), shift_grads, ((TN), ((), ())), precision=HIGHEST, preferred_element_type=FLOAT
    )
    into_silu = lax.dot_general(
        shift_grads, mod_weight.astype(FLOAT), ((NT), ((), ())), precision=HIGHEST, preferred_element_type=FLOAT
    )
    into_silu = lax.all_to_all(into_silu, "dp", 0, 0, tiled=True).reshape(1, width)
    time_full = jax.vjp(silu, condition)[1](into_silu)[0]
    time_grad = lax.dynamic_slice_in_dim(time_full, place * (width // split), width // split, 1)

    into_one, rows_grad[6], rows_grad[7] = jax.vjp(layer_norm, stream_one, table[6], table[7])[1](grad_attn_in)
    grad_one = grad_two + into_one
    rows_grad[4] = jnp.sum(grad_one, axis=0)
    one_low = grad_one.astype(BFLOAT)
    grad_joined = jnp.concatenate([dot(one_low, w_skip[:, :width], NT), dot(one_low, w_skip[:, width:], NT)], axis=1)
    grad_joined = grad_joined.reshape(own_rows, 2, shards, part).transpose(0, 2, 1, 3).reshape(own_rows, 2 * width)
    into_joined, gain_joined, bias_joined = jax.vjp(layer_norm, joined, joined_gain, joined_bias)[1](grad_joined)
    rows_grad[0], rows_grad[1] = gain_joined[:width], gain_joined[width:]
    rows_grad[2], rows_grad[3] = bias_joined[:width], bias_joined[width:]

    bias_spread = lax.dynamic_update_slice_in_dim(jnp.zeros(bias_all.shape, FLOAT), grad_bias, place * hidden, 0)
    bias_part = up_bias.shape[0]
    bias_cols = pl.cdiv(bias_part, part)
    table_grad = jnp.stack([rows_grad[index] for index in range(rows_ahead)], axis=1)
    bias_grad = jnp.pad(bias_spread.reshape(shards, bias_part), ((0, 0), (0, bias_cols * part - bias_part)))
    bias_grad = bias_grad.reshape(shards, bias_cols, part).transpose(0, 2, 1).reshape(width, bias_cols)
    small_grads = jnp.concatenate([table_grad, bias_grad], axis=1).astype(BFLOAT)
    small_grads = jnp.pad(small_grads, ((0, 0), (0, LANES - small_grads.shape[1])))

    qkv_lanes = pl.cdiv(3 * span, LANES) * LANES
    lanes_three = 2 * width + LANES + qkv_lanes
    grads_three = pack_grad(None, jnp.concatenate(attn_blocks, axis=0), grad_raw, lanes_three, 2 * width + LANES, LANES)
    grads_three = pack_grad(grads_three, normed_perm[:, :width], one_low, lanes_three, 0, width)
    grads_three = pack_grad(grads_three, normed_perm[:, width:], one_low, lanes_three, width, width)
    grads_three = lax.dynamic_update_slice(grads_three, small_grads, (0, 2 * width))
    summed_three = lax.psum_scatter(grads_three, "dp", scatter_dimension=0, tiled=True)
    shared = 2 * width + LANES
    chunk = shared // split
    shared_terms = [lax.dynamic_slice_in_dim(summed_three, others(r) * chunk, chunk, 1) for r in range(split)]
    shared_blocks = ring_gather(ring_scatter(shared_terms).astype(BFLOAT))
    shared_sum = jnp.zeros((part, shared), FLOAT)
    for r in range(split):
        shared_sum = lax.dynamic_update_slice_in_dim(shared_sum, shared_blocks[r].astype(FLOAT), others(r) * chunk, 1)
    skip_weight_grad = jnp.concatenate([shared_sum[:, :width], shared_sum[:, width : 2 * width]], axis=0)
    vectors_grad = shared_sum[:, 2 * width : 2 * width + rows_ahead].T
    bias_grad = shared_sum[:, 2 * width + rows_ahead : 2 * width + rows_ahead + bias_cols].T.reshape(-1)[:bias_part]
    qkv_sum = summed_three[:, shared : shared + 3 * span].astype(FLOAT).reshape(part, 3, span)

    text_sum_grad = summed_two[:, 3 * width : 3 * width + 2 * span].astype(FLOAT).reshape(part, 2, span)
    return (
        block_out,
        into_joined[:, :width],
        into_joined[:, width:],
        text_grad,
        time_grad,
        skip_weight_grad,
        mod_grad,
        vectors_grad,
        bias_grad,
        qkv_sum,
        full_sum[:, :span].T,
        full_sum[:, span : 2 * span],
        text_sum_grad,
        full_sum[:, 2 * span :].T,
        summed_one[:, :hidden],
        summed_one[:, hidden:].T,
    )


def solution(mesh):
    tokens = P(("dp", "tensor"), None)
    placed = (
        tokens,
        tokens,
        tokens,
        P("dp", None),
        P("dp"),
        P(None, "dp"),
        P("dp", None),
        P("dp", None),
        P(None, "dp"),
        P("dp"),
        P("dp", None, "tensor"),
        P("tensor", "dp"),
        P("dp", "tensor"),
        P("dp", None, "tensor"),
        P("tensor", "dp"),
        P("dp", "tensor"),
        P("tensor", "dp"),
        tokens,
    )
    return jax.shard_map(
        on_device,
        mesh=mesh,
        in_specs=placed,
        out_specs=(
            tokens,
            tokens,
            tokens,
            tokens,
            P("dp", "tensor"),
            P("dp", None),
            P("dp", None),
            P(None, "dp"),
            P("dp"),
            P("dp", None, "tensor"),
            P("tensor", "dp"),
            P("dp", "tensor"),
            P("dp", None, "tensor"),
            P("tensor", "dp"),
            P("dp", "tensor"),
            P("tensor", "dp"),
        ),
        check_vma=False,
    )
```

```python
import functools
import math

import jax
import jax.numpy as jnp
import numpy as np
from jax import lax
from jax.experimental import pallas as pl
from jax.experimental.pallas import tpu as pltpu
from jax.sharding import PartitionSpec as P

HEADS = 16
HD = 88
LANES = 128
EPSILON = 1e-06
HIGHEST = lax.Precision.HIGHEST
FLOAT = jnp.float32
BFLOAT = jnp.bfloat16
LOG2E = 1.4426950408889634
SCALE = 1.0 / math.sqrt(HD)


def layer_norm(values, norm_gain, norm_bias):
    centred = values - jnp.mean(values, axis=-1, keepdims=True)
    variance = jnp.mean(centred * centred, axis=-1, keepdims=True)
    return centred * lax.rsqrt(variance + EPSILON) * norm_gain + norm_bias


def head_norm(values, norm_gain):
    centred = values - jnp.mean(values, axis=-1, keepdims=True)
    variance = jnp.mean(centred * centred, axis=-1, keepdims=True)
    return centred * lax.rsqrt(variance + EPSILON) * norm_gain


def silu(values):
    return values / (1.0 + jnp.exp(-values))


def gelu(values):
    inner = math.sqrt(2.0 / math.pi) * (values + 0.044715 * values * values * values)
    return 0.5 * values * (1.0 + jnp.tanh(inner))


def dot(left, right, contract=((1,), (0,))):
    return lax.dot_general(left, right, (contract, ((), ())), preferred_element_type=FLOAT)


NT = ((1,), (1,))
TN = ((0,), (0,))


def rot(values, step):
    count = lax.axis_size("tensor")
    return lax.ppermute(values, "tensor", [(i, (i + step) % count) for i in range(count)])


def ring_gather(own):
    blocks = [own]
    for _ in range(lax.axis_size("tensor") - 1):
        blocks.append(rot(blocks[-1], 1))
    return blocks


def ring_scatter(parts):
    running = parts[1].astype(BFLOAT)
    for part in parts[2:]:
        running = (rot(running, 1).astype(FLOAT) + part.astype(FLOAT)).astype(BFLOAT)
    return rot(running, 1).astype(FLOAT) + parts[0].astype(FLOAT)


def direct_gather(own):
    return [own] + [rot(own, r) for r in range(1, lax.axis_size("tensor"))]


def direct_scatter(parts):
    count = len(parts)
    total = parts[0].astype(FLOAT)
    for r in range(1, count):
        total = total + rot(parts[r], count - r).astype(FLOAT)
    return total


def exchange(parts):
    count = len(parts)
    return [parts[0]] + [rot(parts[count - r], r) for r in range(1, count)]


def after(values, *earlier):
    return lax.optimization_barrier((values, *earlier))[0]


def small_gather(own):
    have = own[None]
    me = lax.axis_index("dp")
    count = lax.axis_size("dp")
    step = 1
    while step < count:
        other = lax.ppermute(have, "dp", [(i, i ^ step) for i in range(count)])
        upper = (me // step) % 2 == 1
        have = jnp.where(upper, jnp.concatenate([other, have]), jnp.concatenate([have, other]))
        step *= 2
    return have


def tensor_sum(values):
    total = values
    for step in range(1, lax.axis_size("tensor")):
        total = total + rot(values, step)
    return total


def grad_kernel(*refs):
    left_ref, right_ref, out_ref, turned_ref = refs[0], refs[1], refs[-2], refs[-1]

    @pl.when(pl.program_id(0) == 0)
    def _():
        turned_ref[...] = left_ref[...].T

    out_ref[...] = dot(turned_ref[...], right_ref[...]).astype(BFLOAT)


def pack_grad(packed, left, right, lanes, start, tile):
    rows, height = left.shape
    wide = right.shape[1]
    first = start // tile
    in_specs = [
        pl.BlockSpec((rows, height), lambda i: (0, 0)),
        pl.BlockSpec((rows, tile), lambda i: (0, i)),
    ]
    operands = [left, right]
    if packed is not None:
        in_specs.append(pl.BlockSpec(memory_space=pl.ANY))
        operands.append(packed)
    return pl.pallas_call(
        grad_kernel,
        grid=(pl.cdiv(wide, tile),),
        in_specs=in_specs,
        out_specs=pl.BlockSpec((height, tile), lambda i: (0, first + i)),
        out_shape=jax.ShapeDtypeStruct((height, lanes), BFLOAT),
        scratch_shapes=[pltpu.VMEM((height, rows), BFLOAT)],
        input_output_aliases={} if packed is None else {2: 0},
        compiler_params=pltpu.CompilerParams(vmem_limit_bytes=40 * 2**20),
        cost_estimate=pl.CostEstimate(
            flops=2 * rows * height * wide, bytes_accessed=2 * (rows * height + rows * wide + height * wide), transcendentals=0
        ),
    )(*operands)


def padded(values):
    return jnp.concatenate([values, jnp.zeros((values.shape[0], LANES - HD), values.dtype)], axis=1)


def lane_mask(rows):
    lanes = lax.broadcasted_iota(jnp.int32, (rows, LANES), 1)
    return (lanes < HD).astype(FLOAT)


def norm_parts(values, mask):
    mean = jnp.sum(values, axis=-1, keepdims=True) * (1.0 / HD)
    centred = (values - mean) * mask
    variance = jnp.sum(centred * centred, axis=-1, keepdims=True) * (1.0 / HD)
    inverse = lax.rsqrt(variance + EPSILON)
    return centred * inverse, inverse


CHUNK = 128


def attend_forward_kernel(
    heads, block, raw_ref, cos_ref, sin_a_ref, sin_b_ref, gain_ref, o_ref, opad_ref, q_ref, k_ref, v_ref, lse_ref
):
    length = raw_ref.shape[0]
    span = heads * HD
    mask = lane_mask(CHUNK)

    def prepare(index, carry):
        rows = pl.ds(pl.multiple_of(index * CHUNK, CHUNK), CHUNK)
        cosine, sine_a, sine_b = cos_ref[rows, :], sin_a_ref[rows, :], sin_b_ref[rows, :]
        for head in range(heads):
            for part, out_ref in ((0, q_ref), (1, k_ref)):
                start = part * span + head * HD
                values = padded(raw_ref[rows, start : start + HD])
                normed, _ = norm_parts(values, mask)
                turned = normed * gain_ref[part * heads + head, :][None, :]
                turned = (
                    turned * cosine
                    + pltpu.roll(turned, LANES - HD // 4, 1) * sine_a
                    + pltpu.roll(turned, HD // 4, 1) * sine_b
                )
                out_ref[head, rows, :] = turned.astype(BFLOAT)
            start = 2 * span + head * HD
            v_ref[head, rows, :] = padded(raw_ref[rows, start : start + HD]).astype(BFLOAT)
        return carry

    lax.fori_loop(0, length // CHUNK, prepare, 0)
    count = length // block

    def attend(index, carry):
        head = lax.div(index, count)
        rows = pl.ds(pl.multiple_of(lax.rem(index, count) * block, block), block)
        scores = dot(k_ref[head], q_ref[head, rows, :], NT)
        peak = jnp.max(scores, axis=0, keepdims=True)
        powers = jnp.exp2((scores - peak) * (SCALE * LOG2E))
        total = jnp.sum(powers, axis=0, keepdims=True)
        mixed = dot(v_ref[head], powers.astype(BFLOAT), TN) / total
        opad_ref[head, rows, :] = jnp.transpose(mixed).astype(BFLOAT)
        lse_ref[index] = peak * (SCALE * LOG2E) + jnp.log2(total)
        return carry

    lax.fori_loop(0, heads * count, attend, 0)

    def finish(index, carry):
        rows = pl.ds(pl.multiple_of(index * CHUNK, CHUNK), CHUNK)
        o_ref[rows, :] = jnp.concatenate(
            [opad_ref[head, rows, :].astype(FLOAT)[:, :HD] for head in range(heads)], axis=1
        ).astype(BFLOAT)
        return carry

    lax.fori_loop(0, length // CHUNK, finish, 0)


def attend_forward(raw, tables, gains, heads, block):
    length = raw.shape[0]
    head_shape = jax.ShapeDtypeStruct((heads, length, LANES), BFLOAT)
    return pl.pallas_call(
        functools.partial(attend_forward_kernel, heads, block),
        out_shape=(
            jax.ShapeDtypeStruct((length, heads * HD), BFLOAT),
            head_shape,
            head_shape,
            head_shape,
            head_shape,
            jax.ShapeDtypeStruct((heads * (length // block), 1, block), FLOAT),
        ),
        compiler_params=pltpu.CompilerParams(vmem_limit_bytes=56 * 2**20),
        cost_estimate=pl.CostEstimate(flops=36_000_000_000, bytes_accessed=12_000_000, transcendentals=4_200_000),
    )(raw, *tables, gains)


def attend_backward_kernel(
    heads, block, raw_ref, cos_ref, sin_a_ref, sin_b_ref, gain_ref, opad_ref, q_ref, k_ref, v_ref, lse_ref, do_ref,
    graw_ref, gain_out_ref, sums_ref, dpad_ref, dq_ref, dk_ref, dv_ref,
):
    length = raw_ref.shape[0]
    span = heads * HD
    mask = lane_mask(CHUNK)
    count = length // block

    def prepare(index, carry):
        rows = pl.ds(pl.multiple_of(index * CHUNK, CHUNK), CHUNK)
        values = do_ref[rows, :].astype(FLOAT)
        for head in range(heads):
            dpad_ref[head, rows, :] = padded(values[:, head * HD : (head + 1) * HD]).astype(BFLOAT)
        return carry

    lax.fori_loop(0, length // CHUNK, prepare, 0)

    def attend(index, carry):
        head = lax.div(index, count)
        rows = pl.ds(pl.multiple_of(lax.rem(index, count) * block, block), block)
        queries = q_ref[head, rows, :]
        grad = dpad_ref[head, rows, :]
        scores = dot(k_ref[head], queries, NT)
        probs = jnp.exp2(scores * (SCALE * LOG2E) - lse_ref[index])
        grad_probs = dot(v_ref[head], grad, NT)
        inner = jnp.transpose(grad.astype(FLOAT) * opad_ref[head, rows, :].astype(FLOAT))
        inner = jnp.sum(inner, axis=0, keepdims=True)
        grad_scores = (probs * (grad_probs - inner)).astype(BFLOAT)
        add_v = dot(probs.astype(BFLOAT), grad)
        add_k = dot(grad_scores, queries)
        dq_ref[head, rows, :] = jnp.transpose(dot(k_ref[head], grad_scores, TN))

        @pl.when(lax.rem(index, count) == 0)
        def _():
            dv_ref[head] = add_v
            dk_ref[head] = add_k

        @pl.when(lax.rem(index, count) != 0)
        def _():
            dv_ref[head] += add_v
            dk_ref[head] += add_k

        return carry

    lax.fori_loop(0, heads * count, attend, 0)
    gain_out_ref[...] = jnp.zeros_like(gain_out_ref)
    sums_ref[...] = jnp.zeros_like(sums_ref)

    def finish(index, carry):
        rows = pl.ds(pl.multiple_of(index * CHUNK, CHUNK), CHUNK)
        cosine, sine_a, sine_b = cos_ref[rows, :], sin_a_ref[rows, :], sin_b_ref[rows, :]
        for part, grad_ref in ((0, dq_ref), (1, dk_ref)):
            pieces = []
            for head in range(heads):
                start = part * span + head * HD
                normed, inverse = norm_parts(padded(raw_ref[rows, start : start + HD]), mask)
                grad = grad_ref[head, rows, :] * SCALE
                grad = (
                    grad * cosine
                    + pltpu.roll(grad * sine_a, HD // 4, 1)
                    + pltpu.roll(grad * sine_b, LANES - HD // 4, 1)
                )
                slot = part * heads + head
                gain_out_ref[slot : slot + 1, :] += jnp.sum(grad * normed, axis=0, keepdims=True)
                grad = grad * gain_ref[slot, :][None, :]
                mean = jnp.sum(grad, axis=-1, keepdims=True) * (1.0 / HD)
                slope = jnp.sum(grad * normed, axis=-1, keepdims=True) * (1.0 / HD)
                pieces.append((inverse * (grad - mean - normed * slope))[:, :HD])
            low = jnp.concatenate(pieces, axis=1).astype(BFLOAT)
            graw_ref[rows, part * span : (part + 1) * span] = low
            sums_ref[part : part + 1, :] += jnp.sum(low.astype(FLOAT), axis=0, keepdims=True)
        low = jnp.concatenate([dv_ref[head, rows, :][:, :HD] for head in range(heads)], axis=1).astype(BFLOAT)
        graw_ref[rows, 2 * span :] = low
        sums_ref[2:3, :] += jnp.sum(low.astype(FLOAT), axis=0, keepdims=True)
        return carry

    lax.fori_loop(0, length // CHUNK, finish, 0)


def attend_backward(raw, tables, gains, kept, grad_out, heads, block):
    length = raw.shape[0]
    return pl.pallas_call(
        functools.partial(attend_backward_kernel, heads, block),
        out_shape=(
            jax.ShapeDtypeStruct((length, 3 * heads * HD), BFLOAT),
            jax.ShapeDtypeStruct((2 * heads, LANES), FLOAT),
            jax.ShapeDtypeStruct((8, heads * HD), FLOAT),
        ),
        scratch_shapes=[
            pltpu.VMEM((heads, length, LANES), BFLOAT),
            pltpu.VMEM((heads, length, LANES), FLOAT),
            pltpu.VMEM((heads, length, LANES), FLOAT),
            pltpu.VMEM((heads, length, LANES), FLOAT),
        ],
        compiler_params=pltpu.CompilerParams(vmem_limit_bytes=56 * 2**20),
        cost_estimate=pl.CostEstimate(flops=46_000_000_000, bytes_accessed=16_000_000, transcendentals=4_200_000),
    )(raw, *tables, gains, *kept, grad_out)


def norm_rows(values):
    count = values.shape[-1]
    mean = jnp.sum(values, axis=-1, keepdims=True) * (1.0 / count)
    centred = values - mean
    inverse = lax.rsqrt(jnp.sum(centred * centred, axis=-1, keepdims=True) * (1.0 / count) + EPSILON)
    return centred * inverse, inverse


def norm_rows_back(values, gain, grad):
    normed, inverse = norm_rows(values)
    count = values.shape[-1]
    gain_grad = jnp.sum(grad * normed, axis=0, keepdims=True)
    bias_grad = jnp.sum(grad, axis=0, keepdims=True)
    grad = grad * gain
    mean = jnp.sum(grad, axis=-1, keepdims=True) * (1.0 / count)
    slope = jnp.sum(grad * normed, axis=-1, keepdims=True) * (1.0 / count)
    return inverse * (grad - mean - normed * slope), gain_grad, bias_grad


def head_means(values, group):
    high = values.astype(BFLOAT)
    rest = (values - high.astype(FLOAT)).astype(BFLOAT)
    return (dot(high, group) + dot(rest, group)) * (1.0 / HD)


def norm_heads(values, group):
    centred = values - head_means(values, group)
    inverse = lax.rsqrt(head_means(centred * centred, group) + EPSILON)
    return centred * inverse, inverse


def head_masks(heads, span):
    lanes = lax.broadcasted_iota(jnp.int32, (1, span), 1)
    return [((lanes >= HD * head) & (lanes < HD * (head + 1))).astype(BFLOAT) for head in range(heads)]


def load_weights(weights_ref, kept_ref, sems):
    width = kept_ref.shape[-1]
    return [
        pltpu.make_async_copy(weights_ref.at[:, i * width : (i + 1) * width], kept_ref.at[i], sems.at[i])
        for i in range(3)
    ]


def middle_forward_kernel(
    heads, mixed_ref, one_ref, table_ref, text_ref, group_ref, weights_ref,
    two_ref, raw_ref, three_ref, cross_ref, query_ref, cross_mixed_ref, mlp_ref, kept_ref, sems,
):
    span = heads * HD
    loads = load_weights(weights_ref, kept_ref, sems)
    for load in loads:
        load.start()
    row = lambda index: table_ref[index : index + 1, :]
    loads[0].wait()
    two = one_ref[...] + dot(mixed_ref[...], kept_ref[0], NT) + row(0)
    two_ref[...] = two
    cross = (norm_rows(two)[0] * row(1) + row(2)).astype(BFLOAT)
    cross_ref[...] = cross
    loads[1].wait()
    raw_ref[...] = dot(cross, kept_ref[1]) + row(3)
    group = group_ref[...]
    masks = head_masks(heads, span)
    pieces, mixes = [], []
    for r in range(text_ref.shape[0]):
        part = slice(r * span, (r + 1) * span)
        normed, _ = norm_heads(raw_ref[:, part], group)
        queries = (normed * table_ref[4:5, part]).astype(BFLOAT)
        pieces.append(queries)
        keys, values = text_ref[r, :, :span], text_ref[r, :, span:]
        mix = None
        for head in range(heads):
            scores = dot(queries * masks[head], keys, NT)
            peak = jnp.max(scores, axis=-1, keepdims=True)
            powers = jnp.exp2((scores - peak) * (SCALE * LOG2E))
            weights = (powers / jnp.sum(powers, axis=-1, keepdims=True)).astype(BFLOAT)
            term = dot(weights, values * masks[head])
            mix = term if mix is None else mix + term
        mixes.append(mix.astype(BFLOAT))
    query_ref[...] = jnp.concatenate(pieces, axis=1)
    cross_mixed_ref[...] = jnp.concatenate(mixes, axis=1)
    loads[2].wait()
    three = two_ref[...] + dot(cross_mixed_ref[...], kept_ref[2], NT) + row(5)
    three_ref[...] = three
    mlp_ref[...] = (norm_rows(three)[0] * row(6) + row(7)).astype(BFLOAT)


def middle_forward(mixed, one, table, text, group, weights, heads):
    rows, width = one.shape
    wide = jax.ShapeDtypeStruct((rows, width), FLOAT)
    low = jax.ShapeDtypeStruct((rows, width), BFLOAT)
    vmem = pl.BlockSpec(memory_space=pltpu.VMEM)
    return pl.pallas_call(
        functools.partial(middle_forward_kernel, heads),
        in_specs=[vmem] * 5 + [pl.BlockSpec(memory_space=pl.ANY)],
        out_shape=(wide, wide, wide, low, low, low, low),
        out_specs=(vmem,) * 7,
        scratch_shapes=[pltpu.VMEM((3, width, width), BFLOAT), pltpu.SemaphoreType.DMA((3,))],
        compiler_params=pltpu.CompilerParams(vmem_limit_bytes=56 * 2**20),
        cost_estimate=pl.CostEstimate(flops=26_000_000_000, bytes_accessed=24_000_000, transcendentals=1_300_000),
    )(mixed, one, table, text, group, weights)


def middle_backward_kernel(
    heads, grad_ref, cot_ref, three_ref, two_ref, raw_ref, query_ref, table_ref, text_ref, group_ref, weights_ref,
    three_low_ref, raw_low_ref, two_low_ref, grad_two_ref, mixed_ref, text_grad_ref, rows_ref, kept_ref, grad_three_ref,
    sems,
):
    span = heads * HD
    loads = load_weights(weights_ref, kept_ref, sems)
    for load in reversed(loads):
        load.start()
    row = lambda index: table_ref[index : index + 1, :]
    into, gain_grad, bias_grad = norm_rows_back(three_ref[...], row(6), grad_ref[...])
    rows_ref[0:1, :], rows_ref[1:2, :] = gain_grad, bias_grad
    grad_three = cot_ref[...].astype(FLOAT) + into
    grad_three_ref[...] = grad_three
    rows_ref[2:3, :] = jnp.sum(grad_three, axis=0, keepdims=True)
    three_low = grad_three.astype(BFLOAT)
    three_low_ref[...] = three_low
    loads[2].wait()
    mixed_ref[...] = dot(three_low, kept_ref[2]).astype(BFLOAT)
    group = group_ref[...]
    masks = head_masks(heads, span)
    pieces = []
    for r in range(text_ref.shape[0]):
        part = slice(r * span, (r + 1) * span)
        keys, values = text_ref[r, :, :span], text_ref[r, :, span:]
        queries, mixed = query_ref[:, part], mixed_ref[:, part]
        grad_q = grad_k = grad_v = None
        for head in range(heads):
            some, grad = queries * masks[head], mixed * masks[head]
            scores = dot(keys, some, NT)
            peak = jnp.max(scores, axis=0, keepdims=True)
            powers = jnp.exp2((scores - peak) * (SCALE * LOG2E))
            probs = powers / jnp.sum(powers, axis=0, keepdims=True)
            grad_probs = dot(values, grad, NT)
            inner = jnp.sum(probs * grad_probs, axis=0, keepdims=True)
            grad_scores = (probs * (grad_probs - inner)).astype(BFLOAT)
            add_q = dot(grad_scores, keys * masks[head], TN)
            add_k = dot(grad_scores, some)
            add_v = dot(probs.astype(BFLOAT), grad)
            if head == 0:
                grad_q, grad_k, grad_v = add_q, add_k, add_v
            else:
                grad_q, grad_k, grad_v = grad_q + add_q, grad_k + add_k, grad_v + add_v
        text_grad_ref[r, :, :span] = (grad_k * SCALE).astype(BFLOAT)
        text_grad_ref[r, :, span:] = grad_v.astype(BFLOAT)
        normed, inverse = norm_heads(raw_ref[:, part], group)
        grad_q = grad_q * SCALE
        rows_ref[7:8, part] = jnp.sum(grad_q * normed, axis=0, keepdims=True)
        grad_q = grad_q * table_ref[4:5, part]
        low = (
            inverse * (grad_q - head_means(grad_q, group) - normed * head_means(grad_q * normed, group))
        ).astype(BFLOAT)
        pieces.append(low)
    raw_low_ref[...] = jnp.concatenate(pieces, axis=1)
    rows_ref[6:7, :] = jnp.sum(raw_low_ref[...].astype(FLOAT), axis=0, keepdims=True)
    loads[1].wait()
    into, gain_grad, bias_grad = norm_rows_back(two_ref[...], row(1), dot(raw_low_ref[...], kept_ref[1], NT))
    rows_ref[3:4, :], rows_ref[4:5, :] = gain_grad, bias_grad
    grad_two = grad_three_ref[...] + into
    grad_two_ref[...] = grad_two
    rows_ref[5:6, :] = jnp.sum(grad_two, axis=0, keepdims=True)
    two_low = grad_two.astype(BFLOAT)
    two_low_ref[...] = two_low
    loads[0].wait()
    mixed_ref[...] = dot(two_low, kept_ref[0]).astype(BFLOAT)


def middle_backward(grad, cot, three, two, raw, queries, table, text, group, weights, heads):
    rows, width = three.shape
    low = jax.ShapeDtypeStruct((rows, width), BFLOAT)
    vmem = pl.BlockSpec(memory_space=pltpu.VMEM)
    return pl.pallas_call(
        functools.partial(middle_backward_kernel, heads),
        in_specs=[vmem] * 9 + [pl.BlockSpec(memory_space=pl.ANY)],
        out_shape=(
            low,
            low,
            low,
            jax.ShapeDtypeStruct((rows, width), FLOAT),
            low,
            jax.ShapeDtypeStruct(text.shape, BFLOAT),
            jax.ShapeDtypeStruct((8, width), FLOAT),
        ),
        out_specs=(vmem,) * 7,
        scratch_shapes=[
            pltpu.VMEM((3, width, width), BFLOAT),
            pltpu.VMEM((rows, width), FLOAT),
            pltpu.SemaphoreType.DMA((3,)),
        ],
        compiler_params=pltpu.CompilerParams(vmem_limit_bytes=56 * 2**20),
        cost_estimate=pl.CostEstimate(flops=33_000_000_000, bytes_accessed=28_000_000, transcendentals=1_300_000),
    )(grad, cot, three, two, raw, queries, table, text, group, weights)


def on_device(
    latent, skip_in, text_tokens, time_embed, t_index, grid_pos, skip_weight, mod_weight, vectors, up_bias,
    qkv_weight, proj_weight, query_weight, text_weight, cross_weight, up_weight, down_weight, out_grad,
):
    split = lax.axis_size("tensor")
    shards = lax.axis_size("dp")
    place = lax.axis_index("tensor")
    me = lax.axis_index("dp")
    own_rows, width = latent.shape
    own_text = text_tokens.shape[0]
    part = mod_weight.shape[0]
    heads = HEADS // split
    span = heads * HD
    hidden = up_weight.shape[1]
    rows_ahead = vectors.shape[0]

    def others(r):
        return lax.rem(place - r + split, split)

    condition = time_embed
    half = width // 2
    frequencies = jnp.exp(-math.log(10000.0) * jnp.arange(half, dtype=FLOAT) / half)
    angles = t_index.astype(FLOAT)[:, None] * frequencies[None, :]
    condition = time_embed + jnp.concatenate([jnp.cos(angles), jnp.sin(angles)], axis=-1)
    silu_low = silu(condition).astype(BFLOAT)
    small = jnp.concatenate([vectors.reshape(-1), up_bias, silu_low.reshape(-1)])
    small_all = small_gather(small)
    cut_one, cut_two = rows_ahead * part, rows_ahead * part + up_bias.shape[0]
    table = (
        small_all[:, :cut_one].reshape(shards, rows_ahead, part).transpose(1, 0, 2).reshape(rows_ahead, width)
    ).astype(FLOAT)
    bias_all = small_all[:, cut_one:cut_two].reshape(-1).astype(FLOAT)
    silu_all = small_all[:, cut_two:]

    packed_one = jnp.concatenate(
        [
            skip_weight[:part],
            skip_weight[part:],
            qkv_weight.reshape(part, 3 * span),
            text_weight.reshape(part, 2 * span),
        ],
        axis=1,
    )
    all_one = lax.all_gather(packed_one, "dp", axis=0, tiled=True)
    w_skip = all_one[:, : 2 * width]
    w_qkv = all_one[:, 2 * width : 2 * width + 3 * span]
    w_text = all_one[:, 2 * width + 3 * span :]

    own_full = jnp.stack([proj_weight.T, query_weight, cross_weight.T])
    full_blocks, text_blocks = [own_full], [text_tokens]
    for _ in range(split - 1):
        both = lax.optimization_barrier((full_blocks[-1], text_blocks[-1]))
        full_blocks.append(rot(both[0], 1))
        text_blocks.append(rot(both[1], 1))
    packed_two = jnp.concatenate(
        [full_blocks[r][index] for index in range(3) for r in range(split)], axis=1
    )

    cot_blocks = [out_grad, rot(after(out_grad, full_blocks[-1], text_blocks[-1]), 1)]
    cot_blocks.append(rot(cot_blocks[1], 1))
    text_full = jnp.concatenate(text_blocks, axis=0)

    def head_slice(index):
        return lax.dynamic_slice_in_dim(table[index], place * span, span, 0)

    def relative(index):
        return jnp.concatenate(
            [lax.dynamic_slice_in_dim(table[index], others(r) * span, span, 0) for r in range(split)]
        )

    def spread(values):
        return lax.dynamic_update_slice_in_dim(jnp.zeros((width,), FLOAT), values.reshape(-1), place * span, 0)

    def absolute(values):
        result = jnp.zeros((width,), FLOAT)
        for r in range(split):
            result = lax.dynamic_update_slice_in_dim(
                result, values.reshape(-1)[r * span : (r + 1) * span], others(r) * span, 0
            )
        return result

    def padded_gains(index):
        return jnp.pad(head_slice(index).reshape(heads, HD), ((0, 0), (0, LANES - HD)))

    quarter = HD // 4
    lane = np.arange(LANES)
    rate = np.where(lane < HD, 10000.0 ** (-(lane % quarter).astype(np.float64) / quarter), 0.0).astype(np.float32)
    by_row = (lane < HD // 2)[None, :]
    first = ((lane % (HD // 2)) < quarter) & (lane < HD)
    second = ((lane % (HD // 2)) >= quarter) & (lane < HD)
    grid_rel = jnp.concatenate(
        [lax.dynamic_slice_in_dim(grid_pos, others(r) * own_rows, own_rows, 1) for r in range(split)], axis=1
    ).astype(FLOAT)
    turn = jnp.where(by_row, grid_rel[0][:, None], grid_rel[1][:, None]) * rate[None, :]
    cosine, sine = jnp.cos(turn), jnp.sin(turn)
    tables = (
        cosine * (lane < HD).astype(np.float32)[None, :],
        -sine * first.astype(np.float32)[None, :],
        sine * second.astype(np.float32)[None, :],
    )

    silu_mine = lax.dynamic_slice_in_dim(silu_all, me * part, part, 1)
    shift_terms = dot(silu_mine, mod_weight)
    shift = jnp.sum(lax.all_to_all(shift_terms, "dp", 0, 0, tiled=True), axis=0, keepdims=True) + table[5]

    joined = jnp.concatenate([latent.astype(FLOAT), skip_in.astype(FLOAT)], axis=-1)
    joined_gain = jnp.concatenate([table[0], table[1]])
    joined_bias = jnp.concatenate([table[2], table[3]])
    normed_low = layer_norm(joined, joined_gain, joined_bias).astype(BFLOAT)
    normed_perm = normed_low.reshape(own_rows, shards, 2, part).transpose(0, 2, 1, 3).reshape(own_rows, 2 * width)
    packed_two = after(packed_two, normed_perm, shift, *tables, cot_blocks[1])
    all_two = lax.all_gather(packed_two, "dp", axis=0, tiled=True)
    packed_three = jnp.concatenate([up_weight, down_weight.T], axis=1)
    all_three = lax.all_gather(packed_three, "dp", axis=0, tiled=True)
    w_up, w_down_t = all_three[:, :hidden], all_three[:, hidden:]

    stream_one = (
        dot(normed_perm[:, :width], w_skip[:, :width]) + dot(normed_perm[:, width:], w_skip[:, width:]) + table[4]
    )
    attn_low = (layer_norm(stream_one, table[6], table[7]) + shift).astype(BFLOAT)
    attn_blocks = ring_gather(after(attn_low, cot_blocks[2]))
    qkv_bias = jnp.concatenate([head_slice(8), head_slice(9), head_slice(10)])
    raw = jnp.concatenate([dot(block, w_qkv) + qkv_bias for block in attn_blocks], axis=0)
    gains = jnp.concatenate([padded_gains(12), padded_gains(13)], axis=0)
    length = raw.shape[0]
    block = min(512, length)
    mixed, *kept = attend_forward(raw, tables, gains, heads, block)

    def blocks_of(values, rows):
        return [values[r * rows : (r + 1) * rows] for r in range(split)]

    text_raw = dot(text_full, w_text) + jnp.concatenate([head_slice(17), head_slice(18)])
    text_length = text_raw.shape[0]
    gain_21 = head_slice(21).reshape(heads, HD)
    raw_key = text_raw[:, :span].reshape(text_length, heads, HD)
    text_low = jnp.concatenate(
        [head_norm(raw_key, gain_21).reshape(text_length, span), text_raw[:, span:]], axis=1
    ).astype(BFLOAT)
    text_rel = jnp.stack(direct_gather(after(text_low, attn_blocks[-1])))
    mixed_own = jnp.concatenate(exchange(blocks_of(after(mixed, text_rel), own_rows)), axis=1)
    cot_blocks[-1], mixed_own = lax.optimization_barrier((cot_blocks[-1], mixed_own))
    while len(cot_blocks) < split:
        cot_blocks.append(rot(cot_blocks[-1], 1))
    cot_full = jnp.concatenate(cot_blocks, axis=0)
    lane_head = np.arange(span) // HD
    group = jnp.asarray((lane_head[:, None] == lane_head[None, :]).astype(np.float32), BFLOAT)
    middle_table = jnp.stack(
        [table[11], table[14], table[15], relative(16), relative(20), table[19], table[22], table[23]]
    )
    stream_two, cross_raw, stream_three, cross_low, cross_queries, cross_mixed, mlp_low = middle_forward(
        mixed_own, stream_one, middle_table, text_rel, group, all_two, heads
    )
    mlp_blocks = ring_gather(after(mlp_low, cot_blocks[-1]))
    hidden_bias = lax.dynamic_slice_in_dim(bias_all, place * hidden, hidden, 0)

    hidden_lows, pre_lows, out_parts, back_parts = [], [], [], []
    for r in range(split):
        hidden_pre = dot(mlp_blocks[r], w_up) + hidden_bias
        activated, pull = jax.vjp(gelu, hidden_pre)
        hidden_lows.append(activated.astype(BFLOAT))
        pre_lows.append(pull(dot(cot_blocks[r], w_down_t))[0].astype(BFLOAT))
        back_parts.append(dot(pre_lows[r], w_up, NT))
        out_parts.append(dot(hidden_lows[r], w_down_t, NT))
    grad_mlp_in = ring_scatter(back_parts)

    rows_grad = {}
    mlp_full = jnp.concatenate(mlp_blocks, axis=0)
    pre_full = jnp.concatenate(pre_lows, axis=0)
    hidden_full = jnp.concatenate(hidden_lows, axis=0)
    grad_bias = jnp.sum(pre_full, axis=0, dtype=FLOAT)
    grads_one = pack_grad(None, mlp_full, pre_full, 2 * hidden, 0, 512)
    grads_one = pack_grad(grads_one, cot_full, hidden_full, 2 * hidden, hidden, 512)
    grads_one, grad_mlp_in = lax.optimization_barrier((grads_one, grad_mlp_in))
    summed_one = lax.psum_scatter(grads_one, "dp", scatter_dimension=0, tiled=True).astype(FLOAT)

    cot_here = out_grad.astype(FLOAT)
    rows_grad[24] = jnp.sum(cot_here, axis=0)
    three_low, cq_low, two_low, grad_two, grad_mixed, text_terms, middle_rows = middle_backward(
        grad_mlp_in, out_grad, stream_three, stream_two, cross_raw, cross_queries, middle_table, text_rel, group,
        all_two, heads,
    )
    for index, number in enumerate((22, 23, 19, 14, 15, 11)):
        rows_grad[number] = middle_rows[index]
    rows_grad[16], rows_grad[20] = absolute(middle_rows[6]), absolute(middle_rows[7])
    grad_mixed_blocks = exchange([grad_mixed[:, r * span : (r + 1) * span] for r in range(split)])
    lanes_two = 3 * width
    grads_two = pack_grad(None, two_low, mixed_own, lanes_two, 0, width)
    grads_two = pack_grad(grads_two, cross_low, cq_low, lanes_two, width, width)
    grads_two = pack_grad(grads_two, three_low, cross_mixed, lanes_two, 2 * width, width)
    grads_two, *grad_mixed_blocks = lax.optimization_barrier((grads_two, *grad_mixed_blocks))
    summed_two = lax.psum_scatter(grads_two, "dp", scatter_dimension=0, tiled=True)
    text_terms = after(text_terms, grad_mixed_blocks[-1])
    text_sum = direct_scatter([text_terms[r] for r in range(split)])
    grad_raw, gain_grads, raw_sums = attend_backward(
        raw, tables, gains, kept, jnp.concatenate(grad_mixed_blocks, axis=0), heads, block
    )
    text_sum, grad_raw, summed_one = lax.optimization_barrier((text_sum, grad_raw, summed_one))
    into_ck, gain_ck = jax.vjp(head_norm, raw_key, gain_21)[1](text_sum[:, :span].reshape(text_length, heads, HD))
    rows_grad[21] = spread(gain_ck)
    ckv_low = jnp.concatenate([into_ck.reshape(text_length, span), text_sum[:, span:]], axis=1).astype(BFLOAT)
    text_back = dot(ckv_low, w_text, NT)
    ckv_sums = jnp.sum(ckv_low, axis=0, dtype=FLOAT)
    rows_grad[17], rows_grad[18] = spread(ckv_sums[:span]), spread(ckv_sums[span:])

    rows_grad[12] = spread(gain_grads[:heads, :HD])
    rows_grad[13] = spread(gain_grads[heads:, :HD])
    rows_grad[8], rows_grad[9], rows_grad[10] = spread(raw_sums[0]), spread(raw_sums[1]), spread(raw_sums[2])
    raw_blocks = blocks_of(grad_raw, own_rows)
    attn_parts = [dot(item, w_qkv, NT) for item in raw_blocks]
    shift_part = sum(jnp.sum(item, axis=0) for item in attn_parts)
    rows_grad[5] = shift_part
    qkv_lanes = pl.cdiv(3 * span, LANES) * LANES
    text_lanes = pl.cdiv(2 * span, LANES) * LANES
    grads_qkv = pack_grad(
        None, jnp.concatenate(attn_blocks, axis=0), grad_raw, qkv_lanes + text_lanes, 0, LANES
    )
    grads_qkv = pack_grad(grads_qkv, text_full, ckv_low, qkv_lanes + text_lanes, qkv_lanes, LANES)
    summed_qkv = lax.psum_scatter(grads_qkv, "dp", scatter_dimension=0, tiled=True)
    attn_parts[3 % split] = after(attn_parts[3 % split], grads_qkv)
    grad_attn_in = ring_scatter(attn_parts)
    out_parts[1] = after(out_parts[1].astype(BFLOAT), grad_attn_in)
    block_out = (stream_three + ring_scatter(out_parts) + table[24]).astype(BFLOAT)
    text_grad = ring_scatter(blocks_of(after(text_back, grad_attn_in), own_text))

    into_one, rows_grad[6], rows_grad[7] = jax.vjp(layer_norm, stream_one, table[6], table[7])[1](grad_attn_in)
    grad_one = grad_two + into_one
    rows_grad[4] = jnp.sum(grad_one, axis=0)
    one_low, summed_two = lax.optimization_barrier((grad_one.astype(BFLOAT), summed_two))
    grad_joined = jnp.concatenate([dot(one_low, w_skip[:, :width], NT), dot(one_low, w_skip[:, width:], NT)], axis=1)
    grad_joined = grad_joined.reshape(own_rows, 2, shards, part).transpose(0, 2, 1, 3).reshape(own_rows, 2 * width)
    into_joined, gain_joined, bias_joined = jax.vjp(layer_norm, joined, joined_gain, joined_bias)[1](grad_joined)
    rows_grad[0], rows_grad[1] = gain_joined[:width], gain_joined[width:]
    rows_grad[2], rows_grad[3] = bias_joined[:width], bias_joined[width:]

    bias_spread = lax.dynamic_update_slice_in_dim(jnp.zeros(bias_all.shape, FLOAT), grad_bias, place * hidden, 0)
    bias_part = up_bias.shape[0]
    bias_cols = pl.cdiv(bias_part, part)
    table_grad = jnp.stack([rows_grad[index] for index in range(rows_ahead)], axis=1)
    bias_grad = jnp.pad(bias_spread.reshape(shards, bias_part), ((0, 0), (0, bias_cols * part - bias_part)))
    bias_grad = bias_grad.reshape(shards, bias_cols, part).transpose(0, 2, 1).reshape(width, bias_cols)
    small_grads = jnp.concatenate([table_grad, bias_grad], axis=1).astype(BFLOAT)
    small_grads = jnp.pad(small_grads, ((0, 0), (0, LANES - small_grads.shape[1])))

    shared = 2 * width + LANES
    grads_three = pack_grad(None, normed_perm[:, :width], one_low, shared, 0, width)
    grads_three = pack_grad(grads_three, normed_perm[:, width:], one_low, shared, width, width)
    grads_three = lax.dynamic_update_slice(grads_three, small_grads, (0, 2 * width))
    shift_part = after(shift_part, grads_three)
    summed_three = lax.psum_scatter(grads_three, "dp", scatter_dimension=0, tiled=True)
    full_sum = ring_scatter(
        [
            jnp.concatenate(
                [summed_two[:, i * width + r * span : i * width + (r + 1) * span] for i in range(3)], axis=1
            )
            for r in range(split)
        ]
    )

    summed_three = after(summed_three, full_sum, block_out, text_grad)
    chunk = shared // split
    shared_terms = [lax.dynamic_slice_in_dim(summed_three, others(r) * chunk, chunk, 1) for r in range(split)]
    shared_blocks = direct_gather(direct_scatter(shared_terms).astype(BFLOAT))
    shared_sum = jnp.zeros((part, shared), FLOAT)
    for r in range(split):
        shared_sum = lax.dynamic_update_slice_in_dim(shared_sum, shared_blocks[r].astype(FLOAT), others(r) * chunk, 1)
    skip_weight_grad = jnp.concatenate([shared_sum[:, :width], shared_sum[:, width : 2 * width]], axis=0)
    vectors_grad = shared_sum[:, 2 * width : 2 * width + rows_ahead].T
    bias_grad = shared_sum[:, 2 * width + rows_ahead : 2 * width + rows_ahead + bias_cols].T.reshape(-1)[:bias_part]
    qkv_sum = summed_qkv[:, : 3 * span].astype(FLOAT).reshape(part, 3, span)
    text_sum_grad = summed_qkv[:, qkv_lanes : qkv_lanes + 2 * span].astype(FLOAT).reshape(part, 2, span)

    shift_grads = small_gather(tensor_sum(shift_part))
    mod_grad = lax.dot_general(
        silu_mine.astype(FLOAT), shift_grads, ((TN), ((), ())), precision=HIGHEST, preferred_element_type=FLOAT
    )
    into_silu = lax.dot_general(
        shift_grads, mod_weight.astype(FLOAT), ((NT), ((), ())), precision=HIGHEST, preferred_element_type=FLOAT
    )
    into_silu = lax.all_to_all(into_silu, "dp", 0, 0, tiled=True).reshape(1, width)
    time_full = jax.vjp(silu, condition)[1](into_silu)[0]
    time_grad = lax.dynamic_slice_in_dim(time_full, place * (width // split), width // split, 1)

    return (
        block_out,
        into_joined[:, :width],
        into_joined[:, width:],
        text_grad,
        time_grad,
        skip_weight_grad,
        mod_grad,
        vectors_grad,
        bias_grad,
        qkv_sum,
        full_sum[:, :span].T,
        full_sum[:, span : 2 * span],
        text_sum_grad,
        full_sum[:, 2 * span :].T,
        summed_one[:, :hidden],
        summed_one[:, hidden:].T,
    )


def solution(mesh):
    tokens = P(("dp", "tensor"), None)
    placed = (
        tokens,
        tokens,
        tokens,
        P("dp", None),
        P("dp"),
        P(None, "dp"),
        P("dp", None),
        P("dp", None),
        P(None, "dp"),
        P("dp"),
        P("dp", None, "tensor"),
        P("tensor", "dp"),
        P("dp", "tensor"),
        P("dp", None, "tensor"),
        P("tensor", "dp"),
        P("dp", "tensor"),
        P("tensor", "dp"),
        tokens,
    )
    return jax.shard_map(
        on_device,
        mesh=mesh,
        in_specs=placed,
        out_specs=(
            tokens,
            tokens,
            tokens,
            tokens,
            P("dp", "tensor"),
            P("dp", None),
            P("dp", None),
            P(None, "dp"),
            P("dp"),
            P("dp", None, "tensor"),
            P("tensor", "dp"),
            P("dp", "tensor"),
            P("dp", None, "tensor"),
            P("tensor", "dp"),
            P("dp", "tensor"),
            P("tensor", "dp"),
        ),
        check_vma=False,
    )
```

```python
import functools
import math

import jax
import jax.numpy as jnp
import numpy as np
from jax import lax
from jax.experimental import pallas as pl
from jax.experimental.pallas import tpu as pltpu
from jax.sharding import PartitionSpec as P

HEADS = 16
HD = 88
LANES = 128
EPSILON = 1e-06
HIGHEST = lax.Precision.HIGHEST
FLOAT = jnp.float32
BFLOAT = jnp.bfloat16
LOG2E = 1.4426950408889634
SCALE = 1.0 / math.sqrt(HD)


def layer_norm(values, norm_gain, norm_bias):
    centred = values - jnp.mean(values, axis=-1, keepdims=True)
    variance = jnp.mean(centred * centred, axis=-1, keepdims=True)
    return centred * lax.rsqrt(variance + EPSILON) * norm_gain + norm_bias


def head_norm(values, norm_gain):
    centred = values - jnp.mean(values, axis=-1, keepdims=True)
    variance = jnp.mean(centred * centred, axis=-1, keepdims=True)
    return centred * lax.rsqrt(variance + EPSILON) * norm_gain


def silu(values):
    return values / (1.0 + jnp.exp(-values))


def gelu(values):
    inner = math.sqrt(2.0 / math.pi) * (values + 0.044715 * values * values * values)
    return 0.5 * values * (1.0 + jnp.tanh(inner))


def dot(left, right, contract=((1,), (0,))):
    return lax.dot_general(left, right, (contract, ((), ())), preferred_element_type=FLOAT)


NT = ((1,), (1,))
TN = ((0,), (0,))


def rot(values, step):
    count = lax.axis_size("tensor")
    return lax.ppermute(values, "tensor", [(i, (i + step) % count) for i in range(count)])


def ring_gather(own):
    blocks = [own]
    for _ in range(lax.axis_size("tensor") - 1):
        blocks.append(rot(blocks[-1], 1))
    return blocks


def ring_scatter(parts):
    running = parts[1].astype(BFLOAT)
    for part in parts[2:]:
        running = (rot(running, 1).astype(FLOAT) + part.astype(FLOAT)).astype(BFLOAT)
    return rot(running, 1).astype(FLOAT) + parts[0].astype(FLOAT)


def direct_gather(own):
    return [own] + [rot(own, r) for r in range(1, lax.axis_size("tensor"))]


def direct_scatter(parts):
    count = len(parts)
    total = parts[0].astype(FLOAT)
    for r in range(1, count):
        total = total + rot(parts[r], count - r).astype(FLOAT)
    return total


def exchange(parts):
    count = len(parts)
    return [parts[0]] + [rot(parts[count - r], r) for r in range(1, count)]


def after(values, *earlier):
    return lax.optimization_barrier((values, *earlier))[0]


def small_gather(own):
    have = own[None]
    me = lax.axis_index("dp")
    count = lax.axis_size("dp")
    step = 1
    while step < count:
        other = lax.ppermute(have, "dp", [(i, i ^ step) for i in range(count)])
        upper = (me // step) % 2 == 1
        have = jnp.where(upper, jnp.concatenate([other, have]), jnp.concatenate([have, other]))
        step *= 2
    return have


def tensor_sum(values):
    total = values.astype(FLOAT)
    for step in range(1, lax.axis_size("tensor")):
        total = total + rot(values, step).astype(FLOAT)
    return total


def grad_kernel(lefts, rights, turned, *refs):
    left_refs, right_refs = refs[:lefts], refs[lefts : lefts + rights]
    out_ref, kept_ref = refs[-2], refs[-1]
    rows = left_refs[0].shape[0]

    @pl.when(pl.program_id(0) == 0)
    def _():
        for r in range(lefts):
            kept_ref[:, r * rows : (r + 1) * rows] = left_refs[r][...].T

    total = None
    for r in range(rights):
        span = lefts // rights * rows
        left = kept_ref[:, r * span : (r + 1) * span]
        term = dot(left, right_refs[r][...], NT if turned else ((1,), (0,)))
        total = term if total is None else total + term
    out_ref[...] = total.astype(BFLOAT)


def pack_grad(packed, lefts, rights, lanes, start, tile, turned=False):
    rows, height = lefts[0].shape
    deep = rights[0].shape[1 if turned else 0]
    wide = rights[0].shape[0 if turned else 1]
    first = start // tile
    in_specs = [pl.BlockSpec((rows, height), lambda i: (0, 0))] * len(lefts)
    if turned:
        in_specs += [pl.BlockSpec((tile, deep), lambda i: (i, 0))] * len(rights)
    else:
        in_specs += [pl.BlockSpec((deep, tile), lambda i: (0, i))] * len(rights)
    operands = [*lefts, *rights]
    if packed is not None:
        in_specs.append(pl.BlockSpec(memory_space=pl.ANY))
        operands.append(packed)
    tokens = rows * len(lefts)
    return pl.pallas_call(
        functools.partial(grad_kernel, len(lefts), len(rights), turned),
        grid=(pl.cdiv(wide, tile),),
        in_specs=in_specs,
        out_specs=pl.BlockSpec((height, tile), lambda i: (0, first + i)),
        out_shape=jax.ShapeDtypeStruct((height, lanes), BFLOAT),
        scratch_shapes=[pltpu.VMEM((height, tokens), BFLOAT)],
        input_output_aliases={} if packed is None else {len(operands) - 1: 0},
        compiler_params=pltpu.CompilerParams(vmem_limit_bytes=40 * 2**20),
        cost_estimate=pl.CostEstimate(
            flops=4 * tokens * height * wide,
            bytes_accessed=2 * (tokens * height + tokens * wide + height * wide),
            transcendentals=0,
        ),
    )(*operands)


def flipped(index, bit):
    return index + (1 - 2 * lax.rem(lax.div(index, 2**bit), 2)) * 2**bit


def to_device(source, target, send, recv, where):
    return pltpu.make_async_remote_copy(
        src_ref=source,
        dst_ref=target,
        send_sem=send,
        recv_sem=recv,
        device_id=where,
        device_id_type=pl.DeviceIdType.MESH,
    )


def neighbours(place, split):
    return lax.rem(place + 1, split), lax.rem(place + split - 1, split)


def ring_kernel(split, start, raw_ref, packed_ref, sum_out, shift_out, weights_ref, sent, got, load_sem, sems):
    load = pltpu.make_async_copy(packed_ref.at[:, start : start + weights_ref.shape[1]], weights_ref, load_sem.at[0])
    load.start()
    place = lax.axis_index("tensor")
    right, left = neighbours(place, split)
    barrier = pltpu.get_barrier_semaphore()
    for where in (left, right):
        pl.semaphore_signal(barrier, inc=1, device_id={"tensor": where}, device_id_type=pl.DeviceIdType.MESH)
    rows = sum_out.shape[0]

    def term(r):
        return dot(weights_ref[...], raw_ref[:, r * rows : (r + 1) * rows]).T

    def hop(step):
        return to_device(sent.at[step], got.at[step], sems.at[0, step], sems.at[1, step], {"tensor": right})

    load.wait()
    part = term(1)
    total = jnp.sum(part, axis=0, keepdims=True)
    sent[0] = part.astype(BFLOAT)
    pl.semaphore_wait(barrier, 2)
    hop(0).start()
    for step in range(1, split):
        part = term((step + 1) % split)
        total = total + jnp.sum(part, axis=0, keepdims=True)
        hop(step - 1).wait_recv()
        part = part + got[step - 1].astype(FLOAT)
        if step + 1 < split:
            sent[step] = part.astype(BFLOAT)
            hop(step).start()
        else:
            sum_out[...] = part
    shift_out[...] = jnp.broadcast_to(total, shift_out.shape)
    for step in range(split - 1):
        hop(step).wait_send()


def ring_sum(raw, packed, start, split):
    rows, width = raw.shape[1] // split, packed.shape[0]
    vmem = pl.BlockSpec(memory_space=pltpu.VMEM)
    return pl.pallas_call(
        functools.partial(ring_kernel, split, start),
        in_specs=[vmem, pl.BlockSpec(memory_space=pl.ANY)],
        out_specs=(vmem,) * 2,
        out_shape=(jax.ShapeDtypeStruct((rows, width), FLOAT), jax.ShapeDtypeStruct((8, width), FLOAT)),
        scratch_shapes=[
            pltpu.VMEM((width, raw.shape[0]), BFLOAT),
            pltpu.VMEM((split - 1, rows, width), BFLOAT),
            pltpu.VMEM((split - 1, rows, width), BFLOAT),
            pltpu.SemaphoreType.DMA((1,)),
            pltpu.SemaphoreType.DMA((2, split - 1)),
        ],
        compiler_params=pltpu.CompilerParams(
            vmem_limit_bytes=40 * 2**20, collective_id=1, has_side_effects=True
        ),
        cost_estimate=pl.CostEstimate(flops=60_000_000_000, bytes_accessed=10_000_000, transcendentals=0),
    )(raw, packed)


def skip_kernel(
    grad_ref, two_ref, one_ref, gain_ref, left_ref, packed_ref, out_ref, low_ref, rows_ref
):
    @pl.when(pl.program_id(0) == 0)
    def _():
        into, gain_grad, bias_grad = norm_rows_back(one_ref[...], gain_ref[...], grad_ref[...])
        grad_one = two_ref[...] + into
        low_ref[...] = grad_one.astype(BFLOAT)
        rows_ref[...] = jnp.concatenate(
            [gain_grad, bias_grad, jnp.sum(grad_one, axis=0, keepdims=True), jnp.zeros((5, grad_one.shape[1]), FLOAT)],
            axis=0,
        )

    out_ref[...] = dot(left_ref[...].T, low_ref[...]).astype(BFLOAT)


def skip_grads(packed, grad, two, one, gain, left):
    rows, width = one.shape
    fixed = pl.BlockSpec((rows, width), lambda i: (0, 0))
    return pl.pallas_call(
        skip_kernel,
        grid=(left.shape[1] // width,),
        in_specs=[fixed] * 3
        + [
            pl.BlockSpec((1, width), lambda i: (0, 0)),
            pl.BlockSpec((rows, width), lambda i: (0, i)),
            pl.BlockSpec(memory_space=pl.ANY),
        ],
        out_specs=(
            pl.BlockSpec((width, width), lambda i: (0, i)),
            pl.BlockSpec((rows, width), lambda i: (0, 0)),
            pl.BlockSpec((8, width), lambda i: (0, 0)),
        ),
        out_shape=(
            jax.ShapeDtypeStruct(packed.shape, BFLOAT),
            jax.ShapeDtypeStruct((rows, width), BFLOAT),
            jax.ShapeDtypeStruct((8, width), FLOAT),
        ),
        input_output_aliases={5: 0},
        compiler_params=pltpu.CompilerParams(vmem_limit_bytes=40 * 2**20),
        cost_estimate=pl.CostEstimate(flops=10_000_000_000, bytes_accessed=16_000_000, transcendentals=0),
    )(grad, two, one, gain, left, packed)


def side_kernel(shards, split, hops, *refs):
    low_ref, late_ref, shift_ref, table_ref, latent_ref, skip_ref, base_ref, hop_ref, summed_ref, ckv_ref = refs[:10]
    weights_ref, refs = refs[10], refs[11:]
    out_refs, refs = refs[: hops + 1], refs[hops + 1 :]
    latent_out, skip_out, table_out, full_out, text_out, block_out = refs[:6]
    weights, text_weights, full_refs, text_refs, full_got, text_got, hop_sent, hop_got, table_sent, table_got = refs[6:16]
    load_sem, side_sems, hop_sems, table_sems = refs[16:]
    me, place = lax.axis_index("dp"), lax.axis_index("tensor")
    count = shards.bit_length() - 1
    width = latent_out.shape[1]
    part = width // shards
    right, _ = neighbours(place, split)

    loads = [
        pltpu.make_async_copy(weights_ref.at[:, half * width : (half + 1) * width], weights, load_sem.at[half])
        for half in range(2)
    ]
    text_wide = text_weights.shape[1]
    text_start = weights_ref.shape[1] - text_wide
    loads.append(pltpu.make_async_copy(weights_ref.at[:, text_start:], text_weights, load_sem.at[2]))
    loads[0].start()
    loads[2].start()
    barrier = pltpu.get_barrier_semaphore()
    for bit in range(count):
        pl.semaphore_signal(barrier, inc=1, device_id={"dp": flipped(me, bit)}, device_id_type=pl.DeviceIdType.MESH)
    for step in range(1, split):
        pl.semaphore_signal(
            barrier, inc=1, device_id={"tensor": lax.rem(place + step, split)}, device_id_type=pl.DeviceIdType.MESH
        )

    def side(step, i):
        return to_device(
            (full_refs, text_refs)[i].at[step],
            (full_got, text_got)[i].at[step - 1],
            side_sems.at[i, 0, step - 1],
            side_sems.at[i, 1, step - 1],
            {"tensor": lax.rem(place + split - step, split)},
        )

    def hop(step):
        return to_device(
            hop_sent.at[step], hop_got.at[step], hop_sems.at[0, step], hop_sems.at[1, step], {"tensor": right}
        )

    hop_sent[0] = (hop_ref[...].astype(FLOAT) + out_refs[1][...]).astype(BFLOAT)
    pl.semaphore_wait(barrier, count + split - 1)
    hop(0).start()
    low = low_ref[...]
    grads = []
    for half in range(2):
        loads[half].wait()
        grads.append(dot(low, weights[...], NT))
        if half == 0:
            loads[1].start()
    ordered = [grads[half][:, shard * part : (shard + 1) * part] for shard in range(shards) for half in range(2)]
    grads = [jnp.concatenate(ordered[:shards], axis=1), jnp.concatenate(ordered[shards:], axis=1)]
    values = [latent_ref[...].astype(FLOAT), skip_ref[...].astype(FLOAT)]

    def mean_of(one, two):
        return (jnp.sum(one, axis=-1, keepdims=True) + jnp.sum(two, axis=-1, keepdims=True)) * (0.5 / width)

    mean = mean_of(*values)
    centred = [item - mean for item in values]
    inverse = lax.rsqrt(mean_of(*[item * item for item in centred]) + EPSILON)
    normed = [item * inverse for item in centred]
    gain_rows = [jnp.sum(grads[i] * normed[i], axis=0, keepdims=True) for i in range(2)]
    bias_rows = [jnp.sum(grads[i], axis=0, keepdims=True) for i in range(2)]
    scaled = [grads[i] * table_ref[i : i + 1, :] for i in range(2)]
    mean = mean_of(*scaled)
    slope = mean_of(*[scaled[i] * normed[i] for i in range(2)])
    latent_out[...] = inverse * (scaled[0] - mean - normed[0] * slope)
    skip_out[...] = inverse * (scaled[1] - mean - normed[1] * slope)

    spare = table_out.shape[0] - 8
    table_sent[0] = jnp.concatenate(
        [
            *gain_rows,
            *bias_rows,
            late_ref[2:3, :],
            late_ref[0:2, :],
            shift_ref[0:1, :],
            jnp.zeros((spare, width), FLOAT),
        ],
        axis=0,
    )
    bits = split.bit_length() - 1
    shares = table_sent.shape[0]

    def share(step):
        where = {"tensor": flipped(place, step)} if step < bits else {"dp": flipped(me, step - bits)}
        return to_device(
            table_sent.at[step], table_got.at[step], table_sems.at[0, step], table_sems.at[1, step], where
        )

    def open_hop(step):
        hop(step - 1).wait_recv()
        hop_sent[step] = (hop_got[step - 1].astype(FLOAT) + out_refs[step + 1][...]).astype(BFLOAT)
        hop(step).start()

    def pass_on(step):
        share(step).wait_recv()
        total = table_sent[step] + table_got[step]
        if step + 1 == bits:
            at = lax.broadcasted_iota(jnp.int32, (8 + spare, 1), 0)
            total = jnp.where(at == 8 + me, total[7:8, :], total)
        if step + 1 < shares:
            table_sent[step + 1] = total
            share(step + 1).start()
        else:
            table_out[...] = total
    share(0).start()
    span = full_out.shape[1] // 3
    for r in range(split):
        full_refs[r] = jnp.concatenate(
            [summed_ref[:, k * width + r * span : k * width + (r + 1) * span] for k in range(3)], axis=1
        )
    for step in range(bits):
        pass_on(step)
    for step in range(1, split):
        side(step, 0).start()
    loads[2].wait()
    back = dot(ckv_ref[...], text_weights[...], NT).astype(BFLOAT)
    own_text = text_out.shape[0]
    for r in range(split):
        text_refs[r] = back[r * own_text : (r + 1) * own_text]
    for step in range(1, split):
        side(step, 1).start()
    for step in range(1, hops):
        open_hop(step)
    for step in range(bits, shares):
        pass_on(step)
    for i, (terms, result) in enumerate(((full_refs, full_out), (text_refs, text_out))):
        if i == 1:
            hop(hops - 1).wait_recv()
            last = hop_got[hops - 1].astype(FLOAT) + out_refs[0][...]
            block_out[...] = (base_ref[...] + table_ref[2:3, :] + last).astype(BFLOAT)
        total = terms[0].astype(FLOAT)
        for step in range(1, split):
            side(step, i).wait_recv()
            total = total + (full_got, text_got)[i][step - 1].astype(FLOAT)
        result[...] = total
    for step in range(hops):
        hop(step).wait_send()
    for step in range(shares):
        share(step).wait_send()
    for step in range(1, split):
        for i in range(2):
            side(step, i).wait_send()


def side_sums(low, late, shift, table, latent, skip_in, base, hop, summed, ckv, weights, out, shards, split):
    rows, width = low.shape
    spare = pl.cdiv(shards, 8) * 8
    shares = shards.bit_length() - 1 + split.bit_length() - 1
    vmem = pl.BlockSpec(memory_space=pltpu.VMEM)
    wide = jax.ShapeDtypeStruct((rows, width), FLOAT)
    hops = len(out) - 1
    full, text = (summed.shape[0], summed.shape[1] // split), (ckv.shape[0] // split, width)
    return pl.pallas_call(
        functools.partial(side_kernel, shards, split, hops),
        in_specs=[vmem] * 10 + [pl.BlockSpec(memory_space=pl.ANY)] + [vmem] * len(out),
        out_specs=(vmem,) * 6,
        out_shape=(
            wide,
            wide,
            jax.ShapeDtypeStruct((8 + spare, width), FLOAT),
            jax.ShapeDtypeStruct(full, FLOAT),
            jax.ShapeDtypeStruct(text, FLOAT),
            jax.ShapeDtypeStruct((rows, width), BFLOAT),
        ),
        scratch_shapes=[
            pltpu.VMEM((width, width), BFLOAT),
            pltpu.VMEM((width, ckv.shape[1]), BFLOAT),
            pltpu.VMEM((split, *full), BFLOAT),
            pltpu.VMEM((split, *text), BFLOAT),
            pltpu.VMEM((split - 1, *full), BFLOAT),
            pltpu.VMEM((split - 1, *text), BFLOAT),
            pltpu.VMEM((hops, rows, width), BFLOAT),
            pltpu.VMEM((hops, rows, width), BFLOAT),
            pltpu.VMEM((shares, 8 + spare, width), FLOAT),
            pltpu.VMEM((shares, 8 + spare, width), FLOAT),
            pltpu.SemaphoreType.DMA((3,)),
            pltpu.SemaphoreType.DMA((2, 2, split - 1)),
            pltpu.SemaphoreType.DMA((2, hops)),
            pltpu.SemaphoreType.DMA((2, shares)),
        ],
        compiler_params=pltpu.CompilerParams(
            vmem_limit_bytes=56 * 2**20, collective_id=0, has_side_effects=True
        ),
        cost_estimate=pl.CostEstimate(flops=90_000_000_000, bytes_accessed=30_000_000, transcendentals=0),
    )(low, late, shift, table, latent, skip_in, base, hop, summed, ckv, weights, *out)


def spread_kernel(split, starts, in_ref, skip_out, small_out, piece_sent, piece_got, pieces, whole, sems):
    place = lax.axis_index("tensor")
    part, width = skip_out.shape[0] // 2, skip_out.shape[1]
    wide = piece_sent.shape[2]
    barrier = pltpu.get_barrier_semaphore()
    for step in range(1, split):
        pl.semaphore_signal(
            barrier, inc=1, device_id={"tensor": lax.rem(place + step, split)}, device_id_type=pl.DeviceIdType.MESH
        )
    for i in range(split):
        piece_sent[i] = in_ref[:, starts[i] : starts[i] + wide]
    pl.semaphore_wait(barrier, split - 1)

    def scatter(step):
        where = lax.rem(place + step, split)
        return to_device(
            piece_sent.at[where], piece_got.at[step - 1], sems.at[0, step - 1], sems.at[1, step - 1], {"tensor": where}
        )

    def gather(step):
        return to_device(
            pieces.at[place], pieces.at[place], sems.at[2, step - 1], sems.at[3, step - 1],
            {"tensor": lax.rem(place + step, split)},
        )

    for step in range(1, split):
        scatter(step).start()
    total = piece_sent[place].astype(FLOAT)
    for step in range(1, split):
        scatter(step).wait_recv()
        total = total + piece_got[step - 1].astype(FLOAT)
    pieces[place] = total.astype(BFLOAT)
    for step in range(1, split):
        gather(step).start()
    for step in range(1, split):
        gather(step).wait_recv()
    for i in range(split):
        stop = starts[i + 1] if i + 1 < split else whole.shape[1]
        whole[:, starts[i] : stop] = pieces[i][:, : stop - starts[i]].astype(FLOAT)
    skip_out[:part] = whole[:, :width]
    skip_out[part:] = whole[:, width : 2 * width]
    small_out[...] = whole[:, 2 * width :]
    for step in range(1, split):
        scatter(step).wait_send()
        gather(step).wait_send()


def spread_sum(values, width, split):
    part, lanes = values.shape
    wide = pl.cdiv(lanes // LANES, split) * LANES
    starts = [min(i * wide, lanes - wide) for i in range(split)]
    vmem = pl.BlockSpec(memory_space=pltpu.VMEM)
    return pl.pallas_call(
        functools.partial(spread_kernel, split, starts),
        in_specs=[vmem],
        out_specs=(vmem,) * 2,
        out_shape=(
            jax.ShapeDtypeStruct((2 * part, width), FLOAT),
            jax.ShapeDtypeStruct((part, lanes - 2 * width), FLOAT),
        ),
        scratch_shapes=[
            pltpu.VMEM((split, part, wide), BFLOAT),
            pltpu.VMEM((split - 1, part, wide), BFLOAT),
            pltpu.VMEM((split, part, wide), BFLOAT),
            pltpu.VMEM((part, lanes), FLOAT),
            pltpu.SemaphoreType.DMA((4, split - 1)),
        ],
        compiler_params=pltpu.CompilerParams(
            vmem_limit_bytes=30 * 2**20, collective_id=2, has_side_effects=True
        ),
        cost_estimate=pl.CostEstimate(flops=40_000_000_000, bytes_accessed=4_000_000, transcendentals=0),
    )(values)


def text_kernel(parts, *refs):
    term_refs, (raw_ref, gain_ref, group_ref, low_ref, rows_ref) = refs[:parts], refs[parts:]
    span = gain_ref.shape[1]
    total = term_refs[0][...].astype(FLOAT)
    for ref in term_refs[1:]:
        total = total + ref[...].astype(FLOAT)
    group = group_ref[...]
    normed, inverse = norm_heads(raw_ref[:, :span], group)
    grad = total[:, :span]
    gain_grad = jnp.sum(grad * normed, axis=0, keepdims=True)
    grad = grad * gain_ref[...]
    grad = inverse * (grad - head_means(grad, group) - normed * head_means(grad * normed, group))
    low = jnp.concatenate([grad, total[:, span:]], axis=1).astype(BFLOAT)
    low_ref[...] = low
    zeros = jnp.zeros((1, span), FLOAT)
    rows_ref[...] = jnp.concatenate(
        [
            jnp.sum(low.astype(FLOAT), axis=0, keepdims=True),
            jnp.concatenate([gain_grad, zeros], axis=1),
            jnp.zeros((6, 2 * span), FLOAT),
        ],
        axis=0,
    )


def text_norm_back(terms, raw, gain, group):
    return pl.pallas_call(
        functools.partial(text_kernel, len(terms)),
        out_shape=(
            jax.ShapeDtypeStruct(terms[0].shape, BFLOAT),
            jax.ShapeDtypeStruct((8, terms[0].shape[1]), FLOAT),
        ),
        compiler_params=pltpu.CompilerParams(vmem_limit_bytes=30 * 2**20),
        cost_estimate=pl.CostEstimate(flops=5_000_000_000, bytes_accessed=4_000_000, transcendentals=0),
    )(*terms, raw, gain, group)


QUARTER = 24
DEEP = 4 * QUARTER


def expansion(heads):
    result = np.zeros((3 * heads * HD, 3 * heads * DEEP), np.float32)
    for part in range(3):
        for head in range(heads):
            for channel in range(HD):
                quarter = HD // 4
                place = channel if part == 2 else channel // quarter * QUARTER + channel % quarter
                result[(part * heads + head) * HD + channel, (part * heads + head) * DEEP + place] = 1.0
    return result


def real_rows():
    rows = lax.broadcasted_iota(jnp.int32, (DEEP, 1), 0)
    return (lax.rem(rows, QUARTER) < HD // 4).astype(FLOAT)


def norm_deep(values, mask):
    mean = jnp.sum(values, axis=0, keepdims=True) * (1.0 / HD)
    centred = (values - mean) * mask
    inverse = lax.rsqrt(jnp.sum(centred * centred, axis=0, keepdims=True) * (1.0 / HD) + EPSILON)
    return centred * inverse, inverse


def turn_deep(values, row_cos, row_sin, col_cos, col_sin):
    one, two, three, four = (values[i * QUARTER : (i + 1) * QUARTER] for i in range(4))
    return jnp.concatenate(
        [
            one * row_cos - two * row_sin,
            two * row_cos + one * row_sin,
            three * col_cos - four * col_sin,
            four * col_cos + three * col_sin,
        ],
        axis=0,
    )


def full_tile(values):
    return jnp.concatenate([values, jnp.zeros((LANES - DEEP, values.shape[1]), values.dtype)], axis=0)


def attend_forward_kernel(heads, parts, block, *refs):
    raw_refs, refs = refs[:parts], refs[parts:]
    turn_ref, gain_ref, refs = refs[0], refs[1], refs[2:]
    o_refs, (oturn_ref, qturn_ref, kturn_ref, k_ref, v_ref, lse_ref, vturn_ref) = refs[:parts], refs[parts:]
    rows = raw_refs[0].shape[1]
    length = parts * rows
    mask = real_rows()
    for r in range(parts):
        here = slice(r * rows, (r + 1) * rows)

        def prepare(head, carry):
            tables = [turn_ref[i, :, here] for i in range(4)]
            turned = []
            for part in range(2):
                at = pl.ds((part * heads + head) * DEEP, DEEP)
                normed, _ = norm_deep(raw_refs[r][at, :], mask)
                turned.append(full_tile(turn_deep(normed * gain_ref[at, :], *tables)))
            qturn_ref[head, :, here] = turned[0].astype(BFLOAT)
            kturn_ref[head, :, here] = turned[1].astype(BFLOAT)
            k_ref[head, here, :] = turned[1].T.astype(BFLOAT)
            values = full_tile(raw_refs[r][pl.ds((2 * heads + head) * DEEP, DEEP), :])
            vturn_ref[head, :, here] = values.astype(BFLOAT)
            v_ref[head, here, :] = values.T.astype(BFLOAT)
            return carry

        lax.fori_loop(0, heads, prepare, 0)
    for head in range(heads):
        for index in range(length // block):
            here = slice(index * block, (index + 1) * block)
            scores = dot(k_ref[head], qturn_ref[head, :, here])
            peak = jnp.max(scores, axis=0, keepdims=True)
            powers = jnp.exp2((scores - peak) * (SCALE * LOG2E))
            total = jnp.sum(powers, axis=0, keepdims=True)
            mixed = dot(vturn_ref[head], powers.astype(BFLOAT)) / total
            oturn_ref[head, :, here] = mixed.astype(BFLOAT)
            lse_ref[head, :, here] = peak * (SCALE * LOG2E) + jnp.log2(total)
    for r in range(parts):
        here = slice(r * rows, (r + 1) * rows)
        o_refs[r][...] = jnp.concatenate(
            [oturn_ref[head, :, here].astype(FLOAT).T[:, :HD] for head in range(heads)], axis=1
        ).astype(BFLOAT)


def attend_forward(raws, turns, gains, heads, block):
    rows = raws[0].shape[1]
    length = rows * len(raws)
    tall = jax.ShapeDtypeStruct((heads, LANES, length), BFLOAT)
    long = jax.ShapeDtypeStruct((heads, length, LANES), BFLOAT)
    return pl.pallas_call(
        functools.partial(attend_forward_kernel, heads, len(raws), block),
        out_shape=(
            *[jax.ShapeDtypeStruct((rows, heads * HD), BFLOAT) for _ in raws],
            tall,
            tall,
            tall,
            long,
            long,
            jax.ShapeDtypeStruct((heads, 1, length), FLOAT),
        ),
        scratch_shapes=[pltpu.VMEM((heads, LANES, length), BFLOAT)],
        compiler_params=pltpu.CompilerParams(vmem_limit_bytes=56 * 2**20),
        cost_estimate=pl.CostEstimate(flops=20_000_000_000, bytes_accessed=12_000_000, transcendentals=4_200_000),
    )(*raws, turns, gains)


def attend_backward_kernel(heads, parts, block, *refs):
    raw_refs, refs = refs[:parts], refs[parts:]
    turn_ref, gain_ref, oturn_ref, qturn_ref, kturn_ref, k_ref, v_ref, lse_ref = refs[:8]
    do_refs = refs[8 : 8 + parts]
    graw_ref, gain_out_ref, sums_ref, dturn_ref, dq_ref, dk_ref, dv_ref = refs[8 + parts :]
    rows = raw_refs[0].shape[1]
    length = parts * rows
    count = length // block
    mask = real_rows()
    for r in range(parts):
        here = slice(r * rows, (r + 1) * rows)
        values = do_refs[r][...].astype(FLOAT)
        for head in range(heads):
            wide = jnp.concatenate(
                [values[:, head * HD : (head + 1) * HD], jnp.zeros((rows, LANES - HD), FLOAT)], axis=1
            )
            dturn_ref[head, :, here] = wide.T.astype(BFLOAT)

    def attend(head, carry):
        for index in range(count):
            here = slice(index * block, (index + 1) * block)
            queries, grad = qturn_ref[head, :, here], dturn_ref[head, :, here]
            probs = jnp.exp2(dot(k_ref[head], queries) * (SCALE * LOG2E) - lse_ref[head, :, here])
            inner = jnp.sum(grad.astype(FLOAT) * oturn_ref[head, :, here].astype(FLOAT), axis=0, keepdims=True)
            grad_scores = (probs * (dot(v_ref[head], grad) - inner)).astype(BFLOAT)
            add_v = dot(grad, probs.astype(BFLOAT), NT)
            add_k = dot(queries, grad_scores, NT)
            dq_ref[head, :, here] = dot(kturn_ref[head], grad_scores)
            if index == 0:
                dv_ref[head] = add_v
                dk_ref[head] = add_k
            else:
                dv_ref[head] += add_v
                dk_ref[head] += add_k
        return carry

    lax.fori_loop(0, heads, attend, 0)
    gain_out_ref[...] = jnp.zeros_like(gain_out_ref)
    sums_ref[...] = jnp.zeros_like(sums_ref)

    def narrow(values):
        return sum(values[:, i * LANES : (i + 1) * LANES] for i in range(values.shape[1] // LANES))

    for r in range(parts):
        here = slice(r * rows, (r + 1) * rows)

        def finish(head, carry):
            row_cos, row_sin, col_cos, col_sin = (turn_ref[i, :, here] for i in range(4))
            for part, grad_ref in ((0, dq_ref), (1, dk_ref)):
                at = pl.ds((part * heads + head) * DEEP, DEEP)
                normed, inverse = norm_deep(raw_refs[r][at, :], mask)
                grad = turn_deep(grad_ref[head, :DEEP, here] * SCALE, row_cos, -row_sin, col_cos, -col_sin)
                gain_out_ref[at, :] += narrow(grad * normed)
                grad = grad * gain_ref[at, :]
                mean = jnp.sum(grad, axis=0, keepdims=True) * (1.0 / HD)
                slope = jnp.sum(grad * normed, axis=0, keepdims=True) * (1.0 / HD)
                low = ((inverse * (grad - mean - normed * slope)) * mask).astype(BFLOAT)
                graw_ref[at, here] = low
                sums_ref[at, :] += narrow(low.astype(FLOAT))
            at = pl.ds((2 * heads + head) * DEEP, DEEP)
            low = dv_ref[head, :DEEP, here].astype(BFLOAT)
            graw_ref[at, here] = low
            sums_ref[at, :] += narrow(low.astype(FLOAT))
            return carry

        lax.fori_loop(0, heads, finish, 0)


def attend_backward(raws, turns, gains, kept, grad_out, heads, block):
    length = raws[0].shape[1] * len(raws)
    return pl.pallas_call(
        functools.partial(attend_backward_kernel, heads, len(raws), block),
        out_shape=(
            jax.ShapeDtypeStruct((3 * heads * DEEP, length), BFLOAT),
            jax.ShapeDtypeStruct((2 * heads * DEEP, LANES), FLOAT),
            jax.ShapeDtypeStruct((3 * heads * DEEP, LANES), FLOAT),
        ),
        scratch_shapes=[
            pltpu.VMEM((heads, LANES, length), BFLOAT),
            pltpu.VMEM((heads, LANES, length), FLOAT),
            pltpu.VMEM((heads, LANES, length), FLOAT),
            pltpu.VMEM((heads, LANES, length), FLOAT),
        ],
        compiler_params=pltpu.CompilerParams(vmem_limit_bytes=56 * 2**20),
        cost_estimate=pl.CostEstimate(flops=28_000_000_000, bytes_accessed=16_000_000, transcendentals=4_200_000),
    )(*raws, turns, gains, *kept, *grad_out)


def norm_rows(values):
    count = values.shape[-1]
    mean = jnp.sum(values, axis=-1, keepdims=True) * (1.0 / count)
    centred = values - mean
    inverse = lax.rsqrt(jnp.sum(centred * centred, axis=-1, keepdims=True) * (1.0 / count) + EPSILON)
    return centred * inverse, inverse


def norm_rows_back(values, gain, grad):
    normed, inverse = norm_rows(values)
    count = values.shape[-1]
    gain_grad = jnp.sum(grad * normed, axis=0, keepdims=True)
    bias_grad = jnp.sum(grad, axis=0, keepdims=True)
    grad = grad * gain
    mean = jnp.sum(grad, axis=-1, keepdims=True) * (1.0 / count)
    slope = jnp.sum(grad * normed, axis=-1, keepdims=True) * (1.0 / count)
    return inverse * (grad - mean - normed * slope), gain_grad, bias_grad


def head_means(values, group):
    high = values.astype(BFLOAT)
    rest = (values - high.astype(FLOAT)).astype(BFLOAT)
    return (dot(high, group) + dot(rest, group)) * (1.0 / HD)


def norm_heads(values, group):
    centred = values - head_means(values, group)
    inverse = lax.rsqrt(head_means(centred * centred, group) + EPSILON)
    return centred * inverse, inverse


def head_masks(heads, span):
    lanes = lax.broadcasted_iota(jnp.int32, (1, span), 1)
    return [((lanes >= HD * head) & (lanes < HD * (head + 1))).astype(BFLOAT) for head in range(heads)]


def load_weights(weights_ref, kept_ref, sems):
    width = kept_ref.shape[-1]
    return [
        pltpu.make_async_copy(weights_ref.at[:, i * width : (i + 1) * width], kept_ref.at[i], sems.at[i])
        for i in range(3)
    ]


def middle_forward_kernel(
    heads, parts, *refs,
):
    mixed_refs, text_refs, refs = refs[:parts], refs[parts : 2 * parts], refs[2 * parts :]
    one_ref, table_ref, group_ref, weights_ref, two_ref, raw_ref, three_ref, mixed_ref, cross_ref = refs[:9]
    query_ref, cross_mixed_ref, mlp_ref, kept_ref, sems = refs[9:]
    span = heads * HD
    mixed_ref[...] = jnp.concatenate([ref[...] for ref in mixed_refs], axis=1)
    loads = load_weights(weights_ref, kept_ref, sems)
    for load in loads:
        load.start()
    row = lambda index: table_ref[index : index + 1, :]
    loads[0].wait()
    two = one_ref[...] + dot(mixed_ref[...], kept_ref[0], NT) + row(0)
    two_ref[...] = two
    cross = (norm_rows(two)[0] * row(1) + row(2)).astype(BFLOAT)
    cross_ref[...] = cross
    loads[1].wait()
    raw_ref[...] = dot(cross, kept_ref[1]) + row(3)
    group = group_ref[...]
    masks = head_masks(heads, span)
    pieces, mixes = [], []
    for r in range(parts):
        part = slice(r * span, (r + 1) * span)
        normed, _ = norm_heads(raw_ref[:, part], group)
        queries = (normed * table_ref[4:5, part]).astype(BFLOAT)
        pieces.append(queries)
        keys, values = text_refs[r][:, :span], text_refs[r][:, span:]
        mix = None
        for head in range(heads):
            scores = dot(queries * masks[head], keys, NT)
            peak = jnp.max(scores, axis=-1, keepdims=True)
            powers = jnp.exp2((scores - peak) * (SCALE * LOG2E))
            weights = (powers / jnp.sum(powers, axis=-1, keepdims=True)).astype(BFLOAT)
            term = dot(weights, values * masks[head])
            mix = term if mix is None else mix + term
        mixes.append(mix.astype(BFLOAT))
    query_ref[...] = jnp.concatenate(pieces, axis=1)
    cross_mixed_ref[...] = jnp.concatenate(mixes, axis=1)
    loads[2].wait()
    three = two_ref[...] + dot(cross_mixed_ref[...], kept_ref[2], NT) + row(5)
    three_ref[...] = three
    mlp_ref[...] = (norm_rows(three)[0] * row(6) + row(7)).astype(BFLOAT)


def middle_forward(mixed, one, table, text, group, weights, heads):
    rows, width = one.shape
    wide = jax.ShapeDtypeStruct((rows, width), FLOAT)
    low = jax.ShapeDtypeStruct((rows, width), BFLOAT)
    vmem = pl.BlockSpec(memory_space=pltpu.VMEM)
    return pl.pallas_call(
        functools.partial(middle_forward_kernel, heads, len(mixed)),
        in_specs=[vmem] * (2 * len(mixed) + 3) + [pl.BlockSpec(memory_space=pl.ANY)],
        out_shape=(wide, wide, wide, low, low, low, low, low),
        out_specs=(vmem,) * 8,
        scratch_shapes=[pltpu.VMEM((3, width, width), BFLOAT), pltpu.SemaphoreType.DMA((3,))],
        compiler_params=pltpu.CompilerParams(vmem_limit_bytes=56 * 2**20),
        cost_estimate=pl.CostEstimate(flops=26_000_000_000, bytes_accessed=24_000_000, transcendentals=1_300_000),
    )(*mixed, *text, one, table, group, weights)


def middle_backward_kernel(
    heads, parts, *refs,
):
    text_refs, refs = refs[:parts], refs[parts:]
    grad_ref, cot_ref, three_ref, two_ref, raw_ref, query_ref, table_ref, group_ref, weights_ref = refs[:9]
    three_low_ref, raw_low_ref, two_low_ref, grad_two_ref, rows_ref, refs = *refs[9:14], refs[14:]
    mixed_refs, text_grad_refs = refs[:parts], refs[parts : 2 * parts]
    kept_ref, grad_three_ref, mixed_ref, sems = refs[2 * parts :]
    span = heads * HD
    loads = load_weights(weights_ref, kept_ref, sems)
    for load in reversed(loads):
        load.start()
    row = lambda index: table_ref[index : index + 1, :]
    into, gain_grad, bias_grad = norm_rows_back(three_ref[...], row(6), grad_ref[...])
    rows_ref[0:1, :], rows_ref[1:2, :] = gain_grad, bias_grad
    grad_three = cot_ref[...].astype(FLOAT) + into
    grad_three_ref[...] = grad_three
    rows_ref[2:3, :] = jnp.sum(grad_three, axis=0, keepdims=True)
    three_low = grad_three.astype(BFLOAT)
    three_low_ref[...] = three_low
    loads[2].wait()
    mixed_ref[...] = dot(three_low, kept_ref[2]).astype(BFLOAT)
    group = group_ref[...]
    masks = head_masks(heads, span)
    pieces = []
    for r in range(parts):
        part = slice(r * span, (r + 1) * span)
        keys, values = text_refs[r][:, :span], text_refs[r][:, span:]
        queries, mixed = query_ref[:, part], mixed_ref[:, part]
        grad_q = grad_k = grad_v = None
        for head in range(heads):
            some, grad = queries * masks[head], mixed * masks[head]
            scores = dot(keys, some, NT)
            peak = jnp.max(scores, axis=0, keepdims=True)
            powers = jnp.exp2((scores - peak) * (SCALE * LOG2E))
            probs = powers / jnp.sum(powers, axis=0, keepdims=True)
            grad_probs = dot(values, grad, NT)
            inner = jnp.sum(probs * grad_probs, axis=0, keepdims=True)
            grad_scores = (probs * (grad_probs - inner)).astype(BFLOAT)
            add_q = dot(grad_scores, keys * masks[head], TN)
            add_k = dot(grad_scores, some)
            add_v = dot(probs.astype(BFLOAT), grad)
            if head == 0:
                grad_q, grad_k, grad_v = add_q, add_k, add_v
            else:
                grad_q, grad_k, grad_v = grad_q + add_q, grad_k + add_k, grad_v + add_v
        text_grad_refs[r][:, :span] = (grad_k * SCALE).astype(BFLOAT)
        text_grad_refs[r][:, span:] = grad_v.astype(BFLOAT)
        normed, inverse = norm_heads(raw_ref[:, part], group)
        grad_q = grad_q * SCALE
        rows_ref[7:8, part] = jnp.sum(grad_q * normed, axis=0, keepdims=True)
        grad_q = grad_q * table_ref[4:5, part]
        low = (
            inverse * (grad_q - head_means(grad_q, group) - normed * head_means(grad_q * normed, group))
        ).astype(BFLOAT)
        pieces.append(low)
    raw_low_ref[...] = jnp.concatenate(pieces, axis=1)
    rows_ref[6:7, :] = jnp.sum(raw_low_ref[...].astype(FLOAT), axis=0, keepdims=True)
    loads[1].wait()
    into, gain_grad, bias_grad = norm_rows_back(two_ref[...], row(1), dot(raw_low_ref[...], kept_ref[1], NT))
    rows_ref[3:4, :], rows_ref[4:5, :] = gain_grad, bias_grad
    grad_two = grad_three_ref[...] + into
    grad_two_ref[...] = grad_two
    rows_ref[5:6, :] = jnp.sum(grad_two, axis=0, keepdims=True)
    two_low = grad_two.astype(BFLOAT)
    two_low_ref[...] = two_low
    loads[0].wait()
    mixed = dot(two_low, kept_ref[0])
    for r in range(parts):
        mixed_refs[r][...] = mixed[:, r * span : (r + 1) * span].astype(BFLOAT)


def middle_backward(grad, cot, three, two, raw, queries, table, text, group, weights, heads):
    rows, width = three.shape
    low = jax.ShapeDtypeStruct((rows, width), BFLOAT)
    vmem = pl.BlockSpec(memory_space=pltpu.VMEM)
    return pl.pallas_call(
        functools.partial(middle_backward_kernel, heads, len(text)),
        in_specs=[vmem] * (8 + len(text)) + [pl.BlockSpec(memory_space=pl.ANY)],
        out_shape=(
            low,
            low,
            low,
            jax.ShapeDtypeStruct((rows, width), FLOAT),
            jax.ShapeDtypeStruct((8, width), FLOAT),
            *[jax.ShapeDtypeStruct((rows, heads * HD), BFLOAT) for _ in text],
            *[jax.ShapeDtypeStruct(item.shape, BFLOAT) for item in text],
        ),
        out_specs=(vmem,) * (5 + 2 * len(text)),
        scratch_shapes=[
            pltpu.VMEM((3, width, width), BFLOAT),
            pltpu.VMEM((rows, width), FLOAT),
            pltpu.VMEM((rows, width), BFLOAT),
            pltpu.SemaphoreType.DMA((3,)),
        ],
        compiler_params=pltpu.CompilerParams(vmem_limit_bytes=56 * 2**20),
        cost_estimate=pl.CostEstimate(flops=33_000_000_000, bytes_accessed=28_000_000, transcendentals=1_300_000),
    )(*text, grad, cot, three, two, raw, queries, table, group, weights)


def on_device(
    latent, skip_in, text_tokens, time_embed, t_index, grid_pos, skip_weight, mod_weight, vectors, up_bias,
    qkv_weight, proj_weight, query_weight, text_weight, cross_weight, up_weight, down_weight, out_grad,
):
    split = lax.axis_size("tensor")
    shards = lax.axis_size("dp")
    place = lax.axis_index("tensor")
    me = lax.axis_index("dp")
    own_rows, width = latent.shape
    own_text = text_tokens.shape[0]
    part = mod_weight.shape[0]
    heads = HEADS // split
    span = heads * HD
    hidden = up_weight.shape[1]
    rows_ahead = vectors.shape[0]

    def others(r):
        return lax.rem(place - r + split, split)

    condition = time_embed
    half = width // 2
    frequencies = jnp.exp(-math.log(10000.0) * jnp.arange(half, dtype=FLOAT) / half)
    angles = t_index.astype(FLOAT)[:, None] * frequencies[None, :]
    condition = time_embed + jnp.concatenate([jnp.cos(angles), jnp.sin(angles)], axis=-1)
    silu_low = silu(condition).astype(BFLOAT)
    small = jnp.concatenate([vectors.reshape(-1), up_bias, silu_low.reshape(-1)])
    small_all = small_gather(small)
    cut_one, cut_two = rows_ahead * part, rows_ahead * part + up_bias.shape[0]
    table = (
        small_all[:, :cut_one].reshape(shards, rows_ahead, part).transpose(1, 0, 2).reshape(rows_ahead, width)
    ).astype(FLOAT)
    bias_all = small_all[:, cut_one:cut_two].reshape(-1).astype(FLOAT)
    silu_all = small_all[:, cut_two:]

    expand = jnp.asarray(expansion(heads), BFLOAT)
    deep = heads * DEEP
    packed_one = jnp.concatenate(
        [
            skip_weight[:part],
            skip_weight[part:],
            dot(qkv_weight.reshape(part, 3 * span), expand).astype(BFLOAT),
            text_weight.reshape(part, 2 * span),
        ],
        axis=1,
    )
    all_one = lax.all_gather(packed_one, "dp", axis=0, tiled=True)
    w_skip = all_one[:, : 2 * width]
    w_qkv = all_one[:, 2 * width : 2 * width + 3 * deep]
    w_text = all_one[:, 2 * width + 3 * deep :]

    own_full = jnp.stack([proj_weight.T, query_weight, cross_weight.T])
    full_blocks, text_blocks = [own_full], [text_tokens]
    for _ in range(split - 1):
        both = lax.optimization_barrier((full_blocks[-1], text_blocks[-1]))
        full_blocks.append(rot(both[0], 1))
        text_blocks.append(rot(both[1], 1))
    packed_two = jnp.concatenate(
        [full_blocks[r][index] for index in range(3) for r in range(split)], axis=1
    )

    cot_blocks = [out_grad, rot(after(out_grad, all_one, full_blocks[-1], text_blocks[-1]), 1)]
    text_full = jnp.concatenate(text_blocks, axis=0)

    def head_slice(index):
        return lax.dynamic_slice_in_dim(table[index], place * span, span, 0)

    def relative(index):
        return jnp.concatenate(
            [lax.dynamic_slice_in_dim(table[index], others(r) * span, span, 0) for r in range(split)]
        )

    def spread(values):
        return lax.dynamic_update_slice_in_dim(jnp.zeros((width,), FLOAT), values.reshape(-1), place * span, 0)

    def absolute(values):
        result = jnp.zeros((width,), FLOAT)
        for r in range(split):
            result = lax.dynamic_update_slice_in_dim(
                result, values.reshape(-1)[r * span : (r + 1) * span], others(r) * span, 0
            )
        return result

    def deepen(values):
        turned = jnp.pad(values[:2].reshape(2, heads, 4, HD // 4), ((0, 0), (0, 0), (0, 0), (0, QUARTER - HD // 4)))
        plain = jnp.pad(values[2].reshape(heads, HD), ((0, 0), (0, DEEP - HD)))
        return jnp.concatenate([turned.reshape(-1), plain.reshape(-1)])

    def undeepen(values):
        turned = values[: 2 * deep].reshape(2, heads, 4, QUARTER)[..., : HD // 4].reshape(2, span)
        if values.shape[0] == 2 * deep:
            return turned
        return jnp.concatenate([turned, values[2 * deep :].reshape(heads, DEEP)[:, :HD].reshape(1, span)])

    quarter = HD // 4
    rate = np.zeros((QUARTER, 1), np.float32)
    rate[:quarter, 0] = 10000.0 ** (-np.arange(quarter, dtype=np.float64) / quarter)
    grid_rel = jnp.concatenate(
        [lax.dynamic_slice_in_dim(grid_pos, others(r) * own_rows, own_rows, 1) for r in range(split)], axis=1
    ).astype(FLOAT)
    turn = grid_rel[:, None, :] * rate[None]
    turns = jnp.stack([jnp.cos(turn[0]), jnp.sin(turn[0]), jnp.cos(turn[1]), jnp.sin(turn[1])])

    silu_mine = lax.dynamic_slice_in_dim(silu_all, me * part, part, 1)
    shift_terms = dot(silu_mine, mod_weight)
    shift = jnp.sum(lax.all_to_all(shift_terms, "dp", 0, 0, tiled=True), axis=0, keepdims=True) + table[5]

    joined = jnp.concatenate([latent.astype(FLOAT), skip_in.astype(FLOAT)], axis=-1)
    joined_gain = jnp.concatenate([table[0], table[1]])
    joined_bias = jnp.concatenate([table[2], table[3]])
    normed_low = layer_norm(joined, joined_gain, joined_bias).astype(BFLOAT)
    normed_perm = normed_low.reshape(own_rows, shards, 2, part).transpose(0, 2, 1, 3).reshape(own_rows, 2 * width)
    packed_two = after(packed_two, normed_perm, shift, turns)
    all_two = lax.all_gather(packed_two, "dp", axis=0, tiled=True)
    packed_three = jnp.concatenate([up_weight, down_weight.T], axis=1)
    all_three = lax.all_gather(packed_three, "dp", axis=0, tiled=True)
    w_up, w_down_t = all_three[:, :hidden], all_three[:, hidden:]

    stream_one = (
        dot(normed_perm[:, :width], w_skip[:, :width]) + dot(normed_perm[:, width:], w_skip[:, width:]) + table[4]
    )
    attn_low = (layer_norm(stream_one, table[6], table[7]) + shift).astype(BFLOAT)
    attn_blocks = ring_gather(after(attn_low, cot_blocks[1]))
    qkv_bias = deepen(jnp.stack([head_slice(8), head_slice(9), head_slice(10)]))[:, None]
    raws = [dot(w_qkv, block, ((0,), (1,))) + qkv_bias for block in attn_blocks]
    zero_slice = jnp.zeros((span,), FLOAT)
    gains = deepen(jnp.stack([head_slice(12), head_slice(13), zero_slice]))[: 2 * deep, None]
    length = own_rows * split
    block = min(512, length)
    kept = attend_forward(raws, turns, gains, heads, block)
    mixed, kept = kept[:split], kept[split:]

    def blocks_of(values, rows):
        return [values[r * rows : (r + 1) * rows] for r in range(split)]

    text_raw = dot(text_full, w_text) + jnp.concatenate([head_slice(17), head_slice(18)])
    text_length = text_raw.shape[0]
    gain_21 = head_slice(21).reshape(heads, HD)
    raw_key = text_raw[:, :span].reshape(text_length, heads, HD)
    text_low = jnp.concatenate(
        [head_norm(raw_key, gain_21).reshape(text_length, span), text_raw[:, span:]], axis=1
    ).astype(BFLOAT)
    text_rel = direct_gather(after(text_low, attn_blocks[-1]))
    *mixed, text_rel[-1] = lax.optimization_barrier((*mixed, text_rel[-1]))
    mixed = exchange(mixed)
    cot_blocks[-1], mixed[-1] = lax.optimization_barrier((cot_blocks[-1], mixed[-1]))
    cot_blocks.append(rot(cot_blocks[-1], 1))
    lane_head = np.arange(span) // HD
    group = jnp.asarray((lane_head[:, None] == lane_head[None, :]).astype(np.float32), BFLOAT)
    middle_table = jnp.stack(
        [table[11], table[14], table[15], relative(16), relative(20), table[19], table[22], table[23]]
    )
    stream_two, cross_raw, stream_three, mixed_own, cross_low, cross_queries, cross_mixed, mlp_low = middle_forward(
        mixed, stream_one, middle_table, text_rel, group, all_two, heads
    )
    mlp_low, cot_blocks[-1] = lax.optimization_barrier((mlp_low, cot_blocks[-1]))
    while len(cot_blocks) < split:
        cot_blocks.append(rot(cot_blocks[-1], 1))
    mlp_blocks = ring_gather(mlp_low)
    hidden_bias = lax.dynamic_slice_in_dim(bias_all, place * hidden, hidden, 0)

    hidden_lows, pre_lows, out_parts, back_parts = [], [], [], []
    for r in range(split):
        hidden_pre = dot(mlp_blocks[r], w_up) + hidden_bias
        activated, pull = jax.vjp(gelu, hidden_pre)
        hidden_lows.append(activated.astype(BFLOAT))
        pre_lows.append(pull(dot(cot_blocks[r], w_down_t))[0].astype(BFLOAT))
        back_parts.append(dot(pre_lows[r], w_up, NT))
        out_parts.append(dot(hidden_lows[r], w_down_t, NT))
    grad_mlp_in = ring_scatter(back_parts)

    rows_grad = {}
    grad_bias = sum(jnp.sum(item, axis=0, dtype=FLOAT) for item in pre_lows)
    grads_one = pack_grad(None, mlp_blocks, pre_lows, 2 * hidden, 0, 512)
    grads_one = pack_grad(grads_one, cot_blocks, hidden_lows, 2 * hidden, hidden, 512)
    grads_one, grad_mlp_in, *out_parts = lax.optimization_barrier((grads_one, grad_mlp_in, *out_parts))
    out_hop = rot(out_parts[1].astype(BFLOAT), 1)
    summed_one = lax.psum_scatter(grads_one, "dp", scatter_dimension=0, tiled=True).astype(FLOAT)
    cot_here = out_grad.astype(FLOAT)
    rows_grad[24] = jnp.sum(cot_here, axis=0)
    three_low, cq_low, two_low, grad_two, middle_rows, *pieces = middle_backward(
        grad_mlp_in, out_grad, stream_three, stream_two, cross_raw, cross_queries, middle_table, text_rel, group,
        all_two, heads,
    )
    grad_mixed, text_terms = pieces[:split], pieces[split:]
    for index, number in enumerate((22, 23, 19, 14, 15, 11)):
        rows_grad[number] = middle_rows[index]
    rows_grad[16], rows_grad[20] = absolute(middle_rows[6]), absolute(middle_rows[7])
    out_hop, *grad_mixed = lax.optimization_barrier((out_hop, *grad_mixed))
    grad_mixed = exchange(grad_mixed)
    lanes_two = 3 * width
    grads_two = pack_grad(None, [two_low], [mixed_own], lanes_two, 0, width)
    grads_two = pack_grad(grads_two, [cross_low], [cq_low], lanes_two, width, width)
    grads_two = pack_grad(grads_two, [three_low], [cross_mixed], lanes_two, 2 * width, width)
    grads_two, *grad_mixed = lax.optimization_barrier((grads_two, *grad_mixed))
    summed_two = lax.psum_scatter(grads_two, "dp", scatter_dimension=0, tiled=True)
    text_terms[1:] = lax.optimization_barrier((*text_terms[1:], grad_mixed[-1]))[:-1]
    text_got = [rot(text_terms[r], split - r) for r in range(1, split)]
    grad_raw, gain_grads, raw_sums = attend_backward(
        raws, turns, gains, kept, grad_mixed, heads, block
    )
    grad_raw, summed_one = lax.optimization_barrier((grad_raw, summed_one))
    text_got[0], grad_raw = lax.optimization_barrier((text_got[0], grad_raw))
    ckv_low, text_rows = text_norm_back([text_terms[0], *text_got], text_raw, head_slice(21)[None], group)
    rows_grad[21] = spread(text_rows[1, :span])
    rows_grad[17], rows_grad[18] = spread(text_rows[0, :span]), spread(text_rows[0, span:])

    gain_grads = undeepen(jnp.sum(gain_grads, axis=1))
    raw_sums = undeepen(jnp.sum(raw_sums, axis=1))
    rows_grad[12], rows_grad[13] = spread(gain_grads[0]), spread(gain_grads[1])
    rows_grad[8], rows_grad[9], rows_grad[10] = spread(raw_sums[0]), spread(raw_sums[1]), spread(raw_sums[2])
    qkv_lanes = 3 * deep
    text_lanes = pl.cdiv(2 * span, LANES) * LANES
    shared = 2 * width + LANES
    qkv_start = pl.cdiv(shared, deep) * deep
    text_start = qkv_start + qkv_lanes
    lanes_three = text_start + text_lanes
    bias_part = up_bias.shape[0]
    bias_cols = pl.cdiv(bias_part, part)
    bias_spread = lax.dynamic_update_slice_in_dim(jnp.zeros(bias_all.shape, FLOAT), grad_bias, place * hidden, 0)
    zero_row = jnp.zeros((width,), FLOAT)
    table_grad = jnp.stack([rows_grad.get(index, zero_row) for index in range(rows_ahead)], axis=1)
    bias_grad = jnp.pad(bias_spread.reshape(shards, bias_part), ((0, 0), (0, bias_cols * part - bias_part)))
    bias_grad = bias_grad.reshape(shards, bias_cols, part).transpose(0, 2, 1).reshape(width, bias_cols)
    small_grads = jnp.concatenate([table_grad, bias_grad], axis=1).astype(BFLOAT)
    small_grads = jnp.pad(small_grads, ((0, 0), (0, qkv_start - 2 * width - small_grads.shape[1])))

    grads_three = pack_grad(None, attn_blocks, [grad_raw], lanes_three, qkv_start, deep, turned=True)
    grads_three = pack_grad(grads_three, [text_full], [ckv_low], lanes_three, text_start, LANES)
    grads_three = lax.dynamic_update_slice(grads_three, small_grads, (0, 2 * width))
    out_hop = rot(after((out_hop.astype(FLOAT) + out_parts[2]).astype(BFLOAT), ckv_low), 1)
    grad_raw, grads_three, out_hop = lax.optimization_barrier((grad_raw, grads_three, out_hop))
    grad_attn_in, shift_part = ring_sum(grad_raw, all_one, 2 * width, split)
    grads_three, one_low, late_rows = skip_grads(
        grads_three, grad_attn_in, grad_two, stream_one, table[6:7], normed_perm
    )
    grads_three, summed_two, one_low = lax.optimization_barrier((grads_three, summed_two, one_low))
    summed_three = lax.psum_scatter(grads_three, "dp", scatter_dimension=0, tiled=True)
    latent_grad, skip_grad, late, full_sum, text_grad, block_out = side_sums(
        one_low, late_rows, shift_part, jnp.concatenate([table[:2], table[24:25]]), latent, skip_in, stream_three,
        out_hop, summed_two, ckv_low, all_one, [out_parts[0], *out_parts[3:]], shards, split,
    )
    shift_grads = late[8 : 8 + shards]
    late = lax.dynamic_slice_in_dim(late[:8], me * part, part, 1)
    mod_grad = lax.dot_general(
        silu_mine.astype(FLOAT), shift_grads, ((TN), ((), ())), precision=HIGHEST, preferred_element_type=FLOAT
    )
    into_silu = lax.dot_general(
        shift_grads, mod_weight.astype(FLOAT), ((NT), ((), ())), precision=HIGHEST, preferred_element_type=FLOAT
    )
    into_silu = lax.all_to_all(into_silu, "dp", 0, 0, tiled=True).reshape(1, width)
    time_full = jax.vjp(silu, condition)[1](into_silu)[0]
    time_grad = lax.dynamic_slice_in_dim(time_full, place * (width // split), width // split, 1)

    summed_three = after(summed_three, mod_grad, time_grad, full_sum, text_grad, summed_one)
    qkv_part = summed_three[:, qkv_start:text_start]
    text_part = summed_three[:, text_start : text_start + 2 * span]
    skip_weight_grad, small_sum = spread_sum(summed_three[:, :shared], width, split)
    vectors_grad = jnp.concatenate([late[:5], late[7:8], late[5:7], small_sum[:, 8:rows_ahead].T])
    bias_grad = small_sum[:, rows_ahead : rows_ahead + bias_cols].T.reshape(-1)[:bias_part]
    qkv_sum = dot(qkv_part, expand, NT).reshape(part, 3, span)
    text_sum_grad = text_part.astype(FLOAT).reshape(part, 2, span)

    return (
        block_out,
        latent_grad,
        skip_grad,
        text_grad,
        time_grad,
        skip_weight_grad,
        mod_grad,
        vectors_grad,
        bias_grad,
        qkv_sum,
        full_sum[:, :span].T,
        full_sum[:, span : 2 * span],
        text_sum_grad,
        full_sum[:, 2 * span :].T,
        summed_one[:, :hidden],
        summed_one[:, hidden:].T,
    )


def solution(mesh):
    tokens = P(("dp", "tensor"), None)
    placed = (
        tokens,
        tokens,
        tokens,
        P("dp", None),
        P("dp"),
        P(None, "dp"),
        P("dp", None),
        P("dp", None),
        P(None, "dp"),
        P("dp"),
        P("dp", None, "tensor"),
        P("tensor", "dp"),
        P("dp", "tensor"),
        P("dp", None, "tensor"),
        P("tensor", "dp"),
        P("dp", "tensor"),
        P("tensor", "dp"),
        tokens,
    )
    return jax.shard_map(
        on_device,
        mesh=mesh,
        in_specs=placed,
        out_specs=(
            tokens,
            tokens,
            tokens,
            tokens,
            P("dp", "tensor"),
            P("dp", None),
            P("dp", None),
            P(None, "dp"),
            P("dp"),
            P("dp", None, "tensor"),
            P("tensor", "dp"),
            P("dp", "tensor"),
            P("dp", None, "tensor"),
            P("tensor", "dp"),
            P("dp", "tensor"),
            P("tensor", "dp"),
        ),
        check_vma=False,
    )
```

```python
import functools
import math

import jax
import jax.numpy as jnp
import numpy as np
from jax import lax
from jax.experimental import pallas as pl
from jax.experimental.pallas import tpu as pltpu
from jax.sharding import PartitionSpec as P

HEADS = 16
HD = 88
LANES = 128
EPSILON = 1e-06
HIGHEST = lax.Precision.HIGHEST
FLOAT = jnp.float32
BFLOAT = jnp.bfloat16
LOG2E = 1.4426950408889634
SCALE = 1.0 / math.sqrt(HD)


def layer_norm(values, norm_gain, norm_bias):
    centred = values - jnp.mean(values, axis=-1, keepdims=True)
    variance = jnp.mean(centred * centred, axis=-1, keepdims=True)
    return centred * lax.rsqrt(variance + EPSILON) * norm_gain + norm_bias


def head_norm(values, norm_gain):
    centred = values - jnp.mean(values, axis=-1, keepdims=True)
    variance = jnp.mean(centred * centred, axis=-1, keepdims=True)
    return centred * lax.rsqrt(variance + EPSILON) * norm_gain


def silu(values):
    return values / (1.0 + jnp.exp(-values))


def gelu(values):
    inner = math.sqrt(2.0 / math.pi) * (values + 0.044715 * values * values * values)
    return 0.5 * values * (1.0 + jnp.tanh(inner))


def dot(left, right, contract=((1,), (0,))):
    return lax.dot_general(left, right, (contract, ((), ())), preferred_element_type=FLOAT)


NT = ((1,), (1,))
TN = ((0,), (0,))


def rot(values, step):
    count = lax.axis_size("tensor")
    return lax.ppermute(values, "tensor", [(i, (i + step) % count) for i in range(count)])


def ring_gather(own):
    blocks = [own]
    for _ in range(lax.axis_size("tensor") - 1):
        blocks.append(rot(blocks[-1], 1))
    return blocks


def ring_scatter(parts):
    running = parts[1].astype(BFLOAT)
    for part in parts[2:]:
        running = (rot(running, 1).astype(FLOAT) + part.astype(FLOAT)).astype(BFLOAT)
    return rot(running, 1).astype(FLOAT) + parts[0].astype(FLOAT)


def direct_gather(own):
    return [own] + [rot(own, r) for r in range(1, lax.axis_size("tensor"))]


def direct_scatter(parts):
    count = len(parts)
    total = parts[0].astype(FLOAT)
    for r in range(1, count):
        total = total + rot(parts[r], count - r).astype(FLOAT)
    return total


def exchange(parts):
    count = len(parts)
    return [parts[0]] + [rot(parts[count - r], r) for r in range(1, count)]


def after(values, *earlier):
    return lax.optimization_barrier((values, *earlier))[0]


def small_gather(own):
    have = own[None]
    me = lax.axis_index("dp")
    count = lax.axis_size("dp")
    step = 1
    while step < count:
        other = lax.ppermute(have, "dp", [(i, i ^ step) for i in range(count)])
        upper = (me // step) % 2 == 1
        have = jnp.where(upper, jnp.concatenate([other, have]), jnp.concatenate([have, other]))
        step *= 2
    return have


def tensor_sum(values):
    total = values.astype(FLOAT)
    for step in range(1, lax.axis_size("tensor")):
        total = total + rot(values, step).astype(FLOAT)
    return total


def grad_kernel(lefts, rights, turned, *refs):
    left_refs, right_refs = refs[:lefts], refs[lefts : lefts + rights]
    out_ref, kept_ref = refs[-2], refs[-1]
    rows = left_refs[0].shape[0]

    @pl.when(pl.program_id(0) == 0)
    def _():
        for r in range(lefts):
            kept_ref[:, r * rows : (r + 1) * rows] = left_refs[r][...].T

    total = None
    for r in range(rights):
        span = lefts // rights * rows
        left = kept_ref[:, r * span : (r + 1) * span]
        term = dot(left, right_refs[r][...], NT if turned else ((1,), (0,)))
        total = term if total is None else total + term
    out_ref[...] = total.astype(BFLOAT)


def pack_grad(packed, lefts, rights, lanes, start, tile, turned=False):
    rows, height = lefts[0].shape
    deep = rights[0].shape[1 if turned else 0]
    wide = rights[0].shape[0 if turned else 1]
    first = start // tile
    in_specs = [pl.BlockSpec((rows, height), lambda i: (0, 0))] * len(lefts)
    if turned:
        in_specs += [pl.BlockSpec((tile, deep), lambda i: (i, 0))] * len(rights)
    else:
        in_specs += [pl.BlockSpec((deep, tile), lambda i: (0, i))] * len(rights)
    operands = [*lefts, *rights]
    if packed is not None:
        in_specs.append(pl.BlockSpec(memory_space=pl.ANY))
        operands.append(packed)
    tokens = rows * len(lefts)
    return pl.pallas_call(
        functools.partial(grad_kernel, len(lefts), len(rights), turned),
        grid=(pl.cdiv(wide, tile),),
        in_specs=in_specs,
        out_specs=pl.BlockSpec((height, tile), lambda i: (0, first + i)),
        out_shape=jax.ShapeDtypeStruct((height, lanes), BFLOAT),
        scratch_shapes=[pltpu.VMEM((height, tokens), BFLOAT)],
        input_output_aliases={} if packed is None else {len(operands) - 1: 0},
        compiler_params=pltpu.CompilerParams(vmem_limit_bytes=40 * 2**20),
        cost_estimate=pl.CostEstimate(
            flops=4 * tokens * height * wide,
            bytes_accessed=2 * (tokens * height + tokens * wide + height * wide),
            transcendentals=0,
        ),
    )(*operands)


def flipped(index, bit):
    return index + (1 - 2 * lax.rem(lax.div(index, 2**bit), 2)) * 2**bit


def to_device(source, target, send, recv, where):
    return pltpu.make_async_remote_copy(
        src_ref=source,
        dst_ref=target,
        send_sem=send,
        recv_sem=recv,
        device_id=where,
        device_id_type=pl.DeviceIdType.MESH,
    )


def neighbours(place, split):
    return lax.rem(place + 1, split), lax.rem(place + split - 1, split)


def ring_kernel(split, start, places, *refs):
    raw_ref, left_refs, refs = refs[0], refs[1 : 1 + split], refs[1 + split :]
    text_ref, ckv_ref, packed_ref, sum_out, shift_out, grads_ref = refs[:6]
    weights_ref, turned, qkv_grad, text_grad, sent, got, load_sem, sems = refs[6:]
    loads = [
        pltpu.make_async_copy(packed_ref.at[:, start : start + weights_ref.shape[1]], weights_ref, load_sem.at[0]),
        pltpu.make_async_copy(
            qkv_grad, grads_ref.at[:, places[0] : places[0] + qkv_grad.shape[1]], load_sem.at[1]
        ),
        pltpu.make_async_copy(
            text_grad, grads_ref.at[:, places[1] : places[1] + text_grad.shape[1]], load_sem.at[2]
        ),
    ]
    loads[0].start()
    place = lax.axis_index("tensor")
    right, left = neighbours(place, split)
    barrier = pltpu.get_barrier_semaphore()
    for where in (left, right):
        pl.semaphore_signal(barrier, inc=1, device_id={"tensor": where}, device_id_type=pl.DeviceIdType.MESH)
    rows = sum_out.shape[0]

    def term(r):
        return dot(weights_ref[...], raw_ref[:, r * rows : (r + 1) * rows]).T

    def hop(step):
        return to_device(sent.at[step], got.at[step], sems.at[0, step], sems.at[1, step], {"tensor": right})

    def qkv_lanes(some):
        lanes = qkv_grad.shape[1] // 3
        for i in some:
            part = slice(i * lanes, (i + 1) * lanes)
            qkv_grad[:, part] = dot(turned[...], raw_ref[part, :], NT).astype(BFLOAT)

    def beside(step):
        if step == 1:
            for r in range(split):
                turned[:, r * rows : (r + 1) * rows] = left_refs[r][...].T
            qkv_lanes((0,))
        elif step == 2:
            qkv_lanes((1, 2))
            loads[1].start()
        elif step == 3:
            wide = ckv_ref.shape[1]
            text_grad[:, :wide] = dot(text_ref[...].T, ckv_ref[...]).astype(BFLOAT)
            text_grad[:, wide:] = jnp.zeros((text_grad.shape[0], text_grad.shape[1] - wide), BFLOAT)
            loads[2].start()

    loads[0].wait()
    part = term(1)
    total = jnp.sum(part, axis=0, keepdims=True)
    sent[0] = part.astype(BFLOAT)
    pl.semaphore_wait(barrier, 2)
    hop(0).start()
    for step in range(1, split):
        part = term((step + 1) % split)
        total = total + jnp.sum(part, axis=0, keepdims=True)
        beside(step)
        hop(step - 1).wait_recv()
        part = part + got[step - 1].astype(FLOAT)
        if step + 1 < split:
            sent[step] = part.astype(BFLOAT)
            hop(step).start()
        else:
            sum_out[...] = part
    shift_out[...] = jnp.broadcast_to(total, shift_out.shape)
    loads[1].wait()
    loads[2].wait()
    for step in range(split - 1):
        hop(step).wait_send()


def ring_sum(raw, lefts, text, ckv, packed, start, lanes, places, split):
    rows, width = raw.shape[1] // split, packed.shape[0]
    vmem = pl.BlockSpec(memory_space=pltpu.VMEM)
    anywhere = pl.BlockSpec(memory_space=pl.ANY)
    return pl.pallas_call(
        functools.partial(ring_kernel, split, start, places),
        in_specs=[vmem] * (3 + split) + [anywhere],
        out_specs=(vmem, vmem, anywhere),
        out_shape=(
            jax.ShapeDtypeStruct((rows, width), FLOAT),
            jax.ShapeDtypeStruct((8, width), FLOAT),
            jax.ShapeDtypeStruct((width, lanes), BFLOAT),
        ),
        scratch_shapes=[
            pltpu.VMEM((width, raw.shape[0]), BFLOAT),
            pltpu.VMEM((width, raw.shape[1]), BFLOAT),
            pltpu.VMEM((width, raw.shape[0]), BFLOAT),
            pltpu.VMEM((width, lanes - places[1]), BFLOAT),
            pltpu.VMEM((split - 1, rows, width), BFLOAT),
            pltpu.VMEM((split - 1, rows, width), BFLOAT),
            pltpu.SemaphoreType.DMA((3,)),
            pltpu.SemaphoreType.DMA((2, split - 1)),
        ],
        compiler_params=pltpu.CompilerParams(
            vmem_limit_bytes=48 * 2**20, collective_id=1, has_side_effects=True
        ),
        cost_estimate=pl.CostEstimate(flops=60_000_000_000, bytes_accessed=10_000_000, transcendentals=0),
    )(raw, *lefts, text, ckv, packed)


def skip_kernel(
    grad_ref, two_ref, one_ref, gain_ref, left_ref, packed_ref, out_ref, low_ref, rows_ref
):
    @pl.when(pl.program_id(0) == 0)
    def _():
        into, gain_grad, bias_grad = norm_rows_back(one_ref[...], gain_ref[...], grad_ref[...])
        grad_one = two_ref[...] + into
        low_ref[...] = grad_one.astype(BFLOAT)
        rows_ref[...] = jnp.concatenate(
            [gain_grad, bias_grad, jnp.sum(grad_one, axis=0, keepdims=True), jnp.zeros((5, grad_one.shape[1]), FLOAT)],
            axis=0,
        )

    out_ref[...] = dot(left_ref[...].T, low_ref[...]).astype(BFLOAT)


def skip_grads(packed, grad, two, one, gain, left):
    rows, width = one.shape
    fixed = pl.BlockSpec((rows, width), lambda i: (0, 0))
    return pl.pallas_call(
        skip_kernel,
        grid=(left.shape[1] // width,),
        in_specs=[fixed] * 3
        + [
            pl.BlockSpec((1, width), lambda i: (0, 0)),
            pl.BlockSpec((rows, width), lambda i: (0, i)),
            pl.BlockSpec(memory_space=pl.ANY),
        ],
        out_specs=(
            pl.BlockSpec((width, width), lambda i: (0, i)),
            pl.BlockSpec((rows, width), lambda i: (0, 0)),
            pl.BlockSpec((8, width), lambda i: (0, 0)),
        ),
        out_shape=(
            jax.ShapeDtypeStruct(packed.shape, BFLOAT),
            jax.ShapeDtypeStruct((rows, width), BFLOAT),
            jax.ShapeDtypeStruct((8, width), FLOAT),
        ),
        input_output_aliases={5: 0},
        compiler_params=pltpu.CompilerParams(vmem_limit_bytes=40 * 2**20),
        cost_estimate=pl.CostEstimate(flops=10_000_000_000, bytes_accessed=16_000_000, transcendentals=0),
    )(grad, two, one, gain, left, packed)


def side_kernel(shards, split, hops, text_start, *refs):
    low_ref, late_ref, shift_ref, table_ref, latent_ref, skip_ref, base_ref, hop_ref, summed_ref, ckv_ref = refs[:10]
    weights_ref, text_packed_ref, refs = refs[10], refs[11], refs[12:]
    out_refs, refs = refs[: hops + 1], refs[hops + 1 :]
    latent_out, skip_out, table_out, full_out, text_out, block_out = refs[:6]
    weights, text_weights, full_refs, text_refs, full_got, text_got, hop_sent, hop_got, table_sent, table_got = refs[6:16]
    load_sem, side_sems, hop_sems, table_sems = refs[16:]
    me, place = lax.axis_index("dp"), lax.axis_index("tensor")
    count = shards.bit_length() - 1
    width = latent_out.shape[1]
    part = width // shards
    right, _ = neighbours(place, split)

    loads = [
        pltpu.make_async_copy(weights_ref.at[:, half * width : (half + 1) * width], weights, load_sem.at[half])
        for half in range(2)
    ]
    text_stop = text_start + text_weights.shape[1]
    loads.append(pltpu.make_async_copy(text_packed_ref.at[:, text_start:text_stop], text_weights, load_sem.at[2]))
    loads[0].start()
    loads[2].start()
    barrier = pltpu.get_barrier_semaphore()
    for bit in range(count):
        pl.semaphore_signal(barrier, inc=1, device_id={"dp": flipped(me, bit)}, device_id_type=pl.DeviceIdType.MESH)
    for step in range(1, split):
        pl.semaphore_signal(
            barrier, inc=1, device_id={"tensor": lax.rem(place + step, split)}, device_id_type=pl.DeviceIdType.MESH
        )

    def side(step, i):
        return to_device(
            (full_refs, text_refs)[i].at[step],
            (full_got, text_got)[i].at[step - 1],
            side_sems.at[i, 0, step - 1],
            side_sems.at[i, 1, step - 1],
            {"tensor": lax.rem(place + split - step, split)},
        )

    def hop(step):
        return to_device(
            hop_sent.at[step], hop_got.at[step], hop_sems.at[0, step], hop_sems.at[1, step], {"tensor": right}
        )

    hop_sent[0] = (hop_ref[...].astype(FLOAT) + out_refs[1][...]).astype(BFLOAT)
    pl.semaphore_wait(barrier, count + split - 1)
    hop(0).start()
    low = low_ref[...]
    grads = []
    for half in range(2):
        loads[half].wait()
        grads.append(dot(low, weights[...], NT))
        if half == 0:
            loads[1].start()
    ordered = [grads[half][:, shard * part : (shard + 1) * part] for shard in range(shards) for half in range(2)]
    grads = [jnp.concatenate(ordered[:shards], axis=1), jnp.concatenate(ordered[shards:], axis=1)]
    values = [latent_ref[...].astype(FLOAT), skip_ref[...].astype(FLOAT)]

    def mean_of(one, two):
        return (jnp.sum(one, axis=-1, keepdims=True) + jnp.sum(two, axis=-1, keepdims=True)) * (0.5 / width)

    mean = mean_of(*values)
    centred = [item - mean for item in values]
    inverse = lax.rsqrt(mean_of(*[item * item for item in centred]) + EPSILON)
    normed = [item * inverse for item in centred]
    gain_rows = [jnp.sum(grads[i] * normed[i], axis=0, keepdims=True) for i in range(2)]
    bias_rows = [jnp.sum(grads[i], axis=0, keepdims=True) for i in range(2)]
    scaled = [grads[i] * table_ref[i : i + 1, :] for i in range(2)]
    mean = mean_of(*scaled)
    slope = mean_of(*[scaled[i] * normed[i] for i in range(2)])
    latent_out[...] = inverse * (scaled[0] - mean - normed[0] * slope)
    skip_out[...] = inverse * (scaled[1] - mean - normed[1] * slope)

    spare = table_out.shape[0] - 8
    table_sent[0] = jnp.concatenate(
        [
            *gain_rows,
            *bias_rows,
            late_ref[2:3, :],
            late_ref[0:2, :],
            shift_ref[0:1, :],
            jnp.zeros((spare, width), FLOAT),
        ],
        axis=0,
    )
    bits = split.bit_length() - 1
    shares = table_sent.shape[0]

    def share(step):
        where = {"tensor": flipped(place, step)} if step < bits else {"dp": flipped(me, step - bits)}
        return to_device(
            table_sent.at[step], table_got.at[step], table_sems.at[0, step], table_sems.at[1, step], where
        )

    def open_hop(step):
        hop(step - 1).wait_recv()
        hop_sent[step] = (hop_got[step - 1].astype(FLOAT) + out_refs[step + 1][...]).astype(BFLOAT)
        hop(step).start()

    def pass_on(step):
        share(step).wait_recv()
        total = table_sent[step] + table_got[step]
        if step + 1 == bits:
            at = lax.broadcasted_iota(jnp.int32, (8 + spare, 1), 0)
            total = jnp.where(at == 8 + me, total[7:8, :], total)
        if step + 1 < shares:
            table_sent[step + 1] = total
            share(step + 1).start()
        else:
            table_out[...] = total
    share(0).start()
    span = full_out.shape[1] // 3
    for r in range(split):
        full_refs[r] = jnp.concatenate(
            [summed_ref[:, k * width + r * span : k * width + (r + 1) * span] for k in range(3)], axis=1
        )
    for step in range(bits):
        pass_on(step)
    for step in range(1, split):
        side(step, 0).start()
    loads[2].wait()
    back = dot(ckv_ref[...], text_weights[:, : ckv_ref.shape[1]], NT).astype(BFLOAT)
    own_text = text_out.shape[0]
    for r in range(split):
        text_refs[lax.rem(place + split - r, split)] = back[r * own_text : (r + 1) * own_text]
    for step in range(1, split):
        side(step, 1).start()
    for step in range(1, hops):
        open_hop(step)
    for step in range(bits, shares):
        pass_on(step)
    for i, (terms, result) in enumerate(((full_refs, full_out), (text_refs, text_out))):
        if i == 1:
            hop(hops - 1).wait_recv()
            last = hop_got[hops - 1].astype(FLOAT) + out_refs[0][...]
            block_out[...] = (base_ref[...] + table_ref[2:3, :] + last).astype(BFLOAT)
        total = terms[0].astype(FLOAT)
        for step in range(1, split):
            side(step, i).wait_recv()
            total = total + (full_got, text_got)[i][step - 1].astype(FLOAT)
        result[...] = total
    for step in range(hops):
        hop(step).wait_send()
    for step in range(shares):
        share(step).wait_send()
    for step in range(1, split):
        for i in range(2):
            side(step, i).wait_send()


def side_sums(
    low, late, shift, table, latent, skip_in, base, hop, summed, ckv, weights, text_packed, text_start, out, shards, split
):
    rows, width = low.shape
    spare = pl.cdiv(shards, 8) * 8
    shares = shards.bit_length() - 1 + split.bit_length() - 1
    vmem = pl.BlockSpec(memory_space=pltpu.VMEM)
    wide = jax.ShapeDtypeStruct((rows, width), FLOAT)
    hops = len(out) - 1
    full, text = (summed.shape[0], summed.shape[1] // split), (ckv.shape[0] // split, width)
    return pl.pallas_call(
        functools.partial(side_kernel, shards, split, hops, text_start),
        in_specs=[vmem] * 10 + [pl.BlockSpec(memory_space=pl.ANY)] * 2 + [vmem] * len(out),
        out_specs=(vmem,) * 6,
        out_shape=(
            wide,
            wide,
            jax.ShapeDtypeStruct((8 + spare, width), FLOAT),
            jax.ShapeDtypeStruct(full, FLOAT),
            jax.ShapeDtypeStruct(text, FLOAT),
            jax.ShapeDtypeStruct((rows, width), BFLOAT),
        ),
        scratch_shapes=[
            pltpu.VMEM((width, width), BFLOAT),
            pltpu.VMEM((width, pl.cdiv(ckv.shape[1], LANES) * LANES), BFLOAT),
            pltpu.VMEM((split, *full), BFLOAT),
            pltpu.VMEM((split, *text), BFLOAT),
            pltpu.VMEM((split - 1, *full), BFLOAT),
            pltpu.VMEM((split - 1, *text), BFLOAT),
            pltpu.VMEM((hops, rows, width), BFLOAT),
            pltpu.VMEM((hops, rows, width), BFLOAT),
            pltpu.VMEM((shares, 8 + spare, width), FLOAT),
            pltpu.VMEM((shares, 8 + spare, width), FLOAT),
            pltpu.SemaphoreType.DMA((3,)),
            pltpu.SemaphoreType.DMA((2, 2, split - 1)),
            pltpu.SemaphoreType.DMA((2, hops)),
            pltpu.SemaphoreType.DMA((2, shares)),
        ],
        compiler_params=pltpu.CompilerParams(
            vmem_limit_bytes=56 * 2**20, collective_id=0, has_side_effects=True
        ),
        cost_estimate=pl.CostEstimate(flops=90_000_000_000, bytes_accessed=30_000_000, transcendentals=0),
    )(low, late, shift, table, latent, skip_in, base, hop, summed, ckv, weights, text_packed, *out)


def spread_kernel(split, starts, in_ref, skip_out, small_out, piece_sent, piece_got, pieces, whole, sems):
    place = lax.axis_index("tensor")
    part, width = skip_out.shape[0] // 2, skip_out.shape[1]
    wide = piece_sent.shape[2]
    barrier = pltpu.get_barrier_semaphore()
    for step in range(1, split):
        pl.semaphore_signal(
            barrier, inc=1, device_id={"tensor": lax.rem(place + step, split)}, device_id_type=pl.DeviceIdType.MESH
        )
    for i in range(split):
        piece_sent[i] = in_ref[:, starts[i] : starts[i] + wide]
    pl.semaphore_wait(barrier, split - 1)

    def scatter(step):
        where = lax.rem(place + step, split)
        return to_device(
            piece_sent.at[where], piece_got.at[step - 1], sems.at[0, step - 1], sems.at[1, step - 1], {"tensor": where}
        )

    def gather(step):
        return to_device(
            pieces.at[place], pieces.at[place], sems.at[2, step - 1], sems.at[3, step - 1],
            {"tensor": lax.rem(place + step, split)},
        )

    for step in range(1, split):
        scatter(step).start()
    total = piece_sent[place].astype(FLOAT)
    for step in range(1, split):
        scatter(step).wait_recv()
        total = total + piece_got[step - 1].astype(FLOAT)
    pieces[place] = total.astype(BFLOAT)
    for step in range(1, split):
        gather(step).start()
    for step in range(1, split):
        gather(step).wait_recv()
    for i in range(split):
        stop = starts[i + 1] if i + 1 < split else whole.shape[1]
        whole[:, starts[i] : stop] = pieces[i][:, : stop - starts[i]].astype(FLOAT)
    skip_out[:part] = whole[:, :width]
    skip_out[part:] = whole[:, width : 2 * width]
    small_out[...] = whole[:, 2 * width :]
    for step in range(1, split):
        scatter(step).wait_send()
        gather(step).wait_send()


def spread_sum(values, width, split):
    part, lanes = values.shape
    wide = pl.cdiv(lanes // LANES, split) * LANES
    starts = [min(i * wide, lanes - wide) for i in range(split)]
    vmem = pl.BlockSpec(memory_space=pltpu.VMEM)
    return pl.pallas_call(
        functools.partial(spread_kernel, split, starts),
        in_specs=[vmem],
        out_specs=(vmem,) * 2,
        out_shape=(
            jax.ShapeDtypeStruct((2 * part, width), FLOAT),
            jax.ShapeDtypeStruct((part, lanes - 2 * width), FLOAT),
        ),
        scratch_shapes=[
            pltpu.VMEM((split, part, wide), BFLOAT),
            pltpu.VMEM((split - 1, part, wide), BFLOAT),
            pltpu.VMEM((split, part, wide), BFLOAT),
            pltpu.VMEM((part, lanes), FLOAT),
            pltpu.SemaphoreType.DMA((4, split - 1)),
        ],
        compiler_params=pltpu.CompilerParams(
            vmem_limit_bytes=30 * 2**20, collective_id=2, has_side_effects=True
        ),
        cost_estimate=pl.CostEstimate(flops=40_000_000_000, bytes_accessed=4_000_000, transcendentals=0),
    )(values)


def text_forward_kernel(parts, start, text_ref, bias_ref, gain_ref, group_ref, packed_ref, raw_ref, *refs):
    low_refs, weights_ref, sems = refs[:parts], refs[parts], refs[parts + 1]
    span = gain_ref.shape[1]
    wide = 2 * span
    load = pltpu.make_async_copy(packed_ref.at[:, start : start + parts * wide], weights_ref, sems.at[0])
    load.start()
    load.wait()
    for r in range(parts):
        raw = dot(text_ref[...], weights_ref[:, r * wide : (r + 1) * wide]) + bias_ref[r : r + 1, :]
        if r == 0:
            raw_ref[...] = raw
        normed, _ = norm_heads(raw[:, :span], group_ref[...])
        low_refs[r][:, :span] = (normed * gain_ref[r : r + 1, :]).astype(BFLOAT)
        low_refs[r][:, span:] = raw[:, span:].astype(BFLOAT)


def text_forward(text, packed, start, bias, gain, group):
    parts, wide = bias.shape
    tokens, width = text.shape
    vmem = pl.BlockSpec(memory_space=pltpu.VMEM)
    return pl.pallas_call(
        functools.partial(text_forward_kernel, parts, start),
        in_specs=[vmem] * 4 + [pl.BlockSpec(memory_space=pl.ANY)],
        out_specs=(vmem,) * (1 + parts),
        out_shape=(
            jax.ShapeDtypeStruct((tokens, wide), FLOAT),
            *[jax.ShapeDtypeStruct((tokens, wide), BFLOAT) for _ in range(parts)],
        ),
        scratch_shapes=[pltpu.VMEM((width, parts * wide), BFLOAT), pltpu.SemaphoreType.DMA((1,))],
        compiler_params=pltpu.CompilerParams(vmem_limit_bytes=40 * 2**20),
        cost_estimate=pl.CostEstimate(flops=12_000_000_000, bytes_accessed=10_000_000, transcendentals=0),
    )(text, bias, gain, group, packed)


def text_kernel(parts, *refs):
    term_refs, (raw_ref, gain_ref, group_ref, low_ref, rows_ref) = refs[:parts], refs[parts:]
    span = gain_ref.shape[1]
    total = term_refs[0][...].astype(FLOAT)
    for ref in term_refs[1:]:
        total = total + ref[...].astype(FLOAT)
    group = group_ref[...]
    normed, inverse = norm_heads(raw_ref[:, :span], group)
    grad = total[:, :span]
    gain_grad = jnp.sum(grad * normed, axis=0, keepdims=True)
    grad = grad * gain_ref[...]
    grad = inverse * (grad - head_means(grad, group) - normed * head_means(grad * normed, group))
    low = jnp.concatenate([grad, total[:, span:]], axis=1).astype(BFLOAT)
    low_ref[...] = low
    zeros = jnp.zeros((1, span), FLOAT)
    rows_ref[...] = jnp.concatenate(
        [
            jnp.sum(low.astype(FLOAT), axis=0, keepdims=True),
            jnp.concatenate([gain_grad, zeros], axis=1),
            jnp.zeros((6, 2 * span), FLOAT),
        ],
        axis=0,
    )


def text_norm_back(terms, raw, gain, group):
    return pl.pallas_call(
        functools.partial(text_kernel, len(terms)),
        out_shape=(
            jax.ShapeDtypeStruct(terms[0].shape, BFLOAT),
            jax.ShapeDtypeStruct((8, terms[0].shape[1]), FLOAT),
        ),
        compiler_params=pltpu.CompilerParams(vmem_limit_bytes=30 * 2**20),
        cost_estimate=pl.CostEstimate(flops=5_000_000_000, bytes_accessed=4_000_000, transcendentals=0),
    )(*terms, raw, gain, group)


QUARTER = 24
DEEP = 4 * QUARTER


def expansion(heads):
    result = np.zeros((3 * heads * HD, 3 * heads * DEEP), np.float32)
    for part in range(3):
        for head in range(heads):
            for channel in range(HD):
                quarter = HD // 4
                place = channel if part == 2 else channel // quarter * QUARTER + channel % quarter
                result[(part * heads + head) * HD + channel, (part * heads + head) * DEEP + place] = 1.0
    return result


def real_rows():
    rows = lax.broadcasted_iota(jnp.int32, (DEEP, 1), 0)
    return (lax.rem(rows, QUARTER) < HD // 4).astype(FLOAT)


def norm_deep(values, mask):
    mean = jnp.sum(values, axis=0, keepdims=True) * (1.0 / HD)
    centred = (values - mean) * mask
    inverse = lax.rsqrt(jnp.sum(centred * centred, axis=0, keepdims=True) * (1.0 / HD) + EPSILON)
    return centred * inverse, inverse


def turn_deep(values, row_cos, row_sin, col_cos, col_sin):
    one, two, three, four = (values[i * QUARTER : (i + 1) * QUARTER] for i in range(4))
    return jnp.concatenate(
        [
            one * row_cos - two * row_sin,
            two * row_cos + one * row_sin,
            three * col_cos - four * col_sin,
            four * col_cos + three * col_sin,
        ],
        axis=0,
    )


def full_tile(values):
    return jnp.concatenate([values, jnp.zeros((LANES - DEEP, values.shape[1]), values.dtype)], axis=0)


def attend_forward_kernel(heads, parts, block, *refs):
    raw_refs, refs = refs[:parts], refs[parts:]
    turn_ref, gain_ref, refs = refs[0], refs[1], refs[2:]
    o_refs, (oturn_ref, qturn_ref, kturn_ref, k_ref, v_ref, lse_ref, vturn_ref) = refs[:parts], refs[parts:]
    rows = raw_refs[0].shape[1]
    length = parts * rows
    mask = real_rows()
    for r in range(parts):
        here = slice(r * rows, (r + 1) * rows)

        def prepare(head, carry):
            tables = [turn_ref[i, :, here] for i in range(4)]
            turned = []
            for part in range(2):
                at = pl.ds((part * heads + head) * DEEP, DEEP)
                normed, _ = norm_deep(raw_refs[r][at, :], mask)
                turned.append(full_tile(turn_deep(normed * gain_ref[at, :], *tables)))
            qturn_ref[head, :, here] = turned[0].astype(BFLOAT)
            kturn_ref[head, :, here] = turned[1].astype(BFLOAT)
            k_ref[head, here, :] = turned[1].T.astype(BFLOAT)
            values = full_tile(raw_refs[r][pl.ds((2 * heads + head) * DEEP, DEEP), :])
            vturn_ref[head, :, here] = values.astype(BFLOAT)
            v_ref[head, here, :] = values.T.astype(BFLOAT)
            return carry

        lax.fori_loop(0, heads, prepare, 0)
    for head in range(heads):
        for index in range(length // block):
            here = slice(index * block, (index + 1) * block)
            scores = dot(k_ref[head], qturn_ref[head, :, here])
            peak = jnp.max(scores, axis=0, keepdims=True)
            powers = jnp.exp2((scores - peak) * (SCALE * LOG2E))
            total = jnp.sum(powers, axis=0, keepdims=True)
            mixed = dot(vturn_ref[head], powers.astype(BFLOAT)) / total
            oturn_ref[head, :, here] = mixed.astype(BFLOAT)
            lse_ref[head, :, here] = peak * (SCALE * LOG2E) + jnp.log2(total)
    for r in range(parts):
        here = slice(r * rows, (r + 1) * rows)
        o_refs[r][...] = jnp.concatenate(
            [oturn_ref[head, :, here].astype(FLOAT).T[:, :HD] for head in range(heads)], axis=1
        ).astype(BFLOAT)


def attend_forward(raws, turns, gains, heads, block):
    rows = raws[0].shape[1]
    length = rows * len(raws)
    tall = jax.ShapeDtypeStruct((heads, LANES, length), BFLOAT)
    long = jax.ShapeDtypeStruct((heads, length, LANES), BFLOAT)
    return pl.pallas_call(
        functools.partial(attend_forward_kernel, heads, len(raws), block),
        out_shape=(
            *[jax.ShapeDtypeStruct((rows, heads * HD), BFLOAT) for _ in raws],
            tall,
            tall,
            tall,
            long,
            long,
            jax.ShapeDtypeStruct((heads, 1, length), FLOAT),
        ),
        scratch_shapes=[pltpu.VMEM((heads, LANES, length), BFLOAT)],
        compiler_params=pltpu.CompilerParams(vmem_limit_bytes=56 * 2**20),
        cost_estimate=pl.CostEstimate(flops=20_000_000_000, bytes_accessed=12_000_000, transcendentals=4_200_000),
    )(*raws, turns, gains)


def attend_backward_kernel(heads, parts, block, *refs):
    raw_refs, refs = refs[:parts], refs[parts:]
    turn_ref, gain_ref, oturn_ref, qturn_ref, kturn_ref, k_ref, v_ref, lse_ref = refs[:8]
    do_refs = refs[8 : 8 + parts]
    graw_ref, gain_out_ref, sums_ref, dturn_ref, dq_ref, dk_ref, dv_ref = refs[8 + parts :]
    rows = raw_refs[0].shape[1]
    length = parts * rows
    count = length // block
    mask = real_rows()
    for r in range(parts):
        here = slice(r * rows, (r + 1) * rows)
        values = do_refs[r][...].astype(FLOAT)
        for head in range(heads):
            wide = jnp.concatenate(
                [values[:, head * HD : (head + 1) * HD], jnp.zeros((rows, LANES - HD), FLOAT)], axis=1
            )
            dturn_ref[head, :, here] = wide.T.astype(BFLOAT)

    def attend(head, carry):
        for index in range(count):
            here = slice(index * block, (index + 1) * block)
            queries, grad = qturn_ref[head, :, here], dturn_ref[head, :, here]
            probs = jnp.exp2(dot(k_ref[head], queries) * (SCALE * LOG2E) - lse_ref[head, :, here])
            inner = jnp.sum(grad.astype(FLOAT) * oturn_ref[head, :, here].astype(FLOAT), axis=0, keepdims=True)
            grad_scores = (probs * (dot(v_ref[head], grad) - inner)).astype(BFLOAT)
            add_v = dot(grad, probs.astype(BFLOAT), NT)
            add_k = dot(queries, grad_scores, NT)
            dq_ref[head, :, here] = dot(kturn_ref[head], grad_scores)
            if index == 0:
                dv_ref[head] = add_v
                dk_ref[head] = add_k
            else:
                dv_ref[head] += add_v
                dk_ref[head] += add_k
        return carry

    lax.fori_loop(0, heads, attend, 0)
    gain_out_ref[...] = jnp.zeros_like(gain_out_ref)
    sums_ref[...] = jnp.zeros_like(sums_ref)

    def narrow(values):
        return sum(values[:, i * LANES : (i + 1) * LANES] for i in range(values.shape[1] // LANES))

    for r in range(parts):
        here = slice(r * rows, (r + 1) * rows)

        def finish(head, carry):
            row_cos, row_sin, col_cos, col_sin = (turn_ref[i, :, here] for i in range(4))
            for part, grad_ref in ((0, dq_ref), (1, dk_ref)):
                at = pl.ds((part * heads + head) * DEEP, DEEP)
                normed, inverse = norm_deep(raw_refs[r][at, :], mask)
                grad = turn_deep(grad_ref[head, :DEEP, here] * SCALE, row_cos, -row_sin, col_cos, -col_sin)
                gain_out_ref[at, :] += narrow(grad * normed)
                grad = grad * gain_ref[at, :]
                mean = jnp.sum(grad, axis=0, keepdims=True) * (1.0 / HD)
                slope = jnp.sum(grad * normed, axis=0, keepdims=True) * (1.0 / HD)
                low = ((inverse * (grad - mean - normed * slope)) * mask).astype(BFLOAT)
                graw_ref[at, here] = low
                sums_ref[at, :] += narrow(low.astype(FLOAT))
            at = pl.ds((2 * heads + head) * DEEP, DEEP)
            low = dv_ref[head, :DEEP, here].astype(BFLOAT)
            graw_ref[at, here] = low
            sums_ref[at, :] += narrow(low.astype(FLOAT))
            return carry

        lax.fori_loop(0, heads, finish, 0)


def attend_backward(raws, turns, gains, kept, grad_out, heads, block):
    length = raws[0].shape[1] * len(raws)
    return pl.pallas_call(
        functools.partial(attend_backward_kernel, heads, len(raws), block),
        out_shape=(
            jax.ShapeDtypeStruct((3 * heads * DEEP, length), BFLOAT),
            jax.ShapeDtypeStruct((2 * heads * DEEP, LANES), FLOAT),
            jax.ShapeDtypeStruct((3 * heads * DEEP, LANES), FLOAT),
        ),
        scratch_shapes=[
            pltpu.VMEM((heads, LANES, length), BFLOAT),
            pltpu.VMEM((heads, LANES, length), FLOAT),
            pltpu.VMEM((heads, LANES, length), FLOAT),
            pltpu.VMEM((heads, LANES, length), FLOAT),
        ],
        compiler_params=pltpu.CompilerParams(vmem_limit_bytes=56 * 2**20),
        cost_estimate=pl.CostEstimate(flops=28_000_000_000, bytes_accessed=16_000_000, transcendentals=4_200_000),
    )(*raws, turns, gains, *kept, *grad_out)


def norm_rows(values):
    count = values.shape[-1]
    mean = jnp.sum(values, axis=-1, keepdims=True) * (1.0 / count)
    centred = values - mean
    inverse = lax.rsqrt(jnp.sum(centred * centred, axis=-1, keepdims=True) * (1.0 / count) + EPSILON)
    return centred * inverse, inverse


def norm_rows_back(values, gain, grad):
    normed, inverse = norm_rows(values)
    count = values.shape[-1]
    gain_grad = jnp.sum(grad * normed, axis=0, keepdims=True)
    bias_grad = jnp.sum(grad, axis=0, keepdims=True)
    grad = grad * gain
    mean = jnp.sum(grad, axis=-1, keepdims=True) * (1.0 / count)
    slope = jnp.sum(grad * normed, axis=-1, keepdims=True) * (1.0 / count)
    return inverse * (grad - mean - normed * slope), gain_grad, bias_grad


def head_means(values, group):
    high = values.astype(BFLOAT)
    rest = (values - high.astype(FLOAT)).astype(BFLOAT)
    return (dot(high, group) + dot(rest, group)) * (1.0 / HD)


def norm_heads(values, group):
    centred = values - head_means(values, group)
    inverse = lax.rsqrt(head_means(centred * centred, group) + EPSILON)
    return centred * inverse, inverse


def head_masks(heads, span):
    lanes = lax.broadcasted_iota(jnp.int32, (1, span), 1)
    return [((lanes >= HD * head) & (lanes < HD * (head + 1))).astype(BFLOAT) for head in range(heads)]


def load_weights(weights_ref, kept_ref, sems):
    width = kept_ref.shape[-1]
    return [
        pltpu.make_async_copy(weights_ref.at[:, i * width : (i + 1) * width], kept_ref.at[i], sems.at[i])
        for i in range(3)
    ]


def middle_forward_kernel(
    heads, parts, *refs,
):
    mixed_refs, text_refs, refs = refs[:parts], refs[parts : 2 * parts], refs[2 * parts :]
    one_ref, table_ref, group_ref, weights_ref, two_ref, raw_ref, three_ref, mixed_ref, cross_ref = refs[:9]
    query_ref, cross_mixed_ref, mlp_ref, kept_ref, sems = refs[9:]
    span = heads * HD
    mixed_ref[...] = jnp.concatenate([ref[...] for ref in mixed_refs], axis=1)
    loads = load_weights(weights_ref, kept_ref, sems)
    for load in loads:
        load.start()
    row = lambda index: table_ref[index : index + 1, :]
    loads[0].wait()
    two = one_ref[...] + dot(mixed_ref[...], kept_ref[0], NT) + row(0)
    two_ref[...] = two
    cross = (norm_rows(two)[0] * row(1) + row(2)).astype(BFLOAT)
    cross_ref[...] = cross
    loads[1].wait()
    raw_ref[...] = dot(cross, kept_ref[1]) + row(3)
    group = group_ref[...]
    masks = head_masks(heads, span)
    pieces, mixes = [], []
    for r in range(parts):
        part = slice(r * span, (r + 1) * span)
        normed, _ = norm_heads(raw_ref[:, part], group)
        queries = (normed * table_ref[4:5, part]).astype(BFLOAT)
        pieces.append(queries)
        keys, values = text_refs[r][:, :span], text_refs[r][:, span:]
        mix = None
        for head in range(heads):
            scores = dot(queries * masks[head], keys, NT)
            peak = jnp.max(scores, axis=-1, keepdims=True)
            powers = jnp.exp2((scores - peak) * (SCALE * LOG2E))
            weights = (powers / jnp.sum(powers, axis=-1, keepdims=True)).astype(BFLOAT)
            term = dot(weights, values * masks[head])
            mix = term if mix is None else mix + term
        mixes.append(mix.astype(BFLOAT))
    query_ref[...] = jnp.concatenate(pieces, axis=1)
    cross_mixed_ref[...] = jnp.concatenate(mixes, axis=1)
    loads[2].wait()
    three = two_ref[...] + dot(cross_mixed_ref[...], kept_ref[2], NT) + row(5)
    three_ref[...] = three
    mlp_ref[...] = (norm_rows(three)[0] * row(6) + row(7)).astype(BFLOAT)


def middle_forward(mixed, one, table, text, group, weights, heads):
    rows, width = one.shape
    wide = jax.ShapeDtypeStruct((rows, width), FLOAT)
    low = jax.ShapeDtypeStruct((rows, width), BFLOAT)
    vmem = pl.BlockSpec(memory_space=pltpu.VMEM)
    return pl.pallas_call(
        functools.partial(middle_forward_kernel, heads, len(mixed)),
        in_specs=[vmem] * (2 * len(mixed) + 3) + [pl.BlockSpec(memory_space=pl.ANY)],
        out_shape=(wide, wide, wide, low, low, low, low, low),
        out_specs=(vmem,) * 8,
        scratch_shapes=[pltpu.VMEM((3, width, width), BFLOAT), pltpu.SemaphoreType.DMA((3,))],
        compiler_params=pltpu.CompilerParams(vmem_limit_bytes=56 * 2**20),
        cost_estimate=pl.CostEstimate(flops=26_000_000_000, bytes_accessed=24_000_000, transcendentals=1_300_000),
    )(*mixed, *text, one, table, group, weights)


def middle_backward_kernel(
    heads, parts, *refs,
):
    text_refs, refs = refs[:parts], refs[parts:]
    grad_ref, cot_ref, three_ref, two_ref, raw_ref, query_ref, table_ref, group_ref, weights_ref = refs[:9]
    three_low_ref, raw_low_ref, two_low_ref, grad_two_ref, rows_ref, refs = *refs[9:14], refs[14:]
    mixed_refs, text_grad_refs = refs[:parts], refs[parts : 2 * parts]
    kept_ref, grad_three_ref, mixed_ref, sems = refs[2 * parts :]
    span = heads * HD
    loads = load_weights(weights_ref, kept_ref, sems)
    for load in reversed(loads):
        load.start()
    row = lambda index: table_ref[index : index + 1, :]
    into, gain_grad, bias_grad = norm_rows_back(three_ref[...], row(6), grad_ref[...])
    rows_ref[0:1, :], rows_ref[1:2, :] = gain_grad, bias_grad
    grad_three = cot_ref[...].astype(FLOAT) + into
    grad_three_ref[...] = grad_three
    rows_ref[2:3, :] = jnp.sum(grad_three, axis=0, keepdims=True)
    three_low = grad_three.astype(BFLOAT)
    three_low_ref[...] = three_low
    loads[2].wait()
    mixed_ref[...] = dot(three_low, kept_ref[2]).astype(BFLOAT)
    group = group_ref[...]
    masks = head_masks(heads, span)
    pieces = []
    for r in range(parts):
        part = slice(r * span, (r + 1) * span)
        keys, values = text_refs[r][:, :span], text_refs[r][:, span:]
        queries, mixed = query_ref[:, part], mixed_ref[:, part]
        grad_q = grad_k = grad_v = None
        for head in range(heads):
            some, grad = queries * masks[head], mixed * masks[head]
            scores = dot(keys, some, NT)
            peak = jnp.max(scores, axis=0, keepdims=True)
            powers = jnp.exp2((scores - peak) * (SCALE * LOG2E))
            probs = powers / jnp.sum(powers, axis=0, keepdims=True)
            grad_probs = dot(values, grad, NT)
            inner = jnp.sum(probs * grad_probs, axis=0, keepdims=True)
            grad_scores = (probs * (grad_probs - inner)).astype(BFLOAT)
            add_q = dot(grad_scores, keys * masks[head], TN)
            add_k = dot(grad_scores, some)
            add_v = dot(probs.astype(BFLOAT), grad)
            if head == 0:
                grad_q, grad_k, grad_v = add_q, add_k, add_v
            else:
                grad_q, grad_k, grad_v = grad_q + add_q, grad_k + add_k, grad_v + add_v
        text_grad_refs[r][:, :span] = (grad_k * SCALE).astype(BFLOAT)
        text_grad_refs[r][:, span:] = grad_v.astype(BFLOAT)
        normed, inverse = norm_heads(raw_ref[:, part], group)
        grad_q = grad_q * SCALE
        rows_ref[7:8, part] = jnp.sum(grad_q * normed, axis=0, keepdims=True)
        grad_q = grad_q * table_ref[4:5, part]
        low = (
            inverse * (grad_q - head_means(grad_q, group) - normed * head_means(grad_q * normed, group))
        ).astype(BFLOAT)
        pieces.append(low)
    raw_low_ref[...] = jnp.concatenate(pieces, axis=1)
    rows_ref[6:7, :] = jnp.sum(raw_low_ref[...].astype(FLOAT), axis=0, keepdims=True)
    loads[1].wait()
    into, gain_grad, bias_grad = norm_rows_back(two_ref[...], row(1), dot(raw_low_ref[...], kept_ref[1], NT))
    rows_ref[3:4, :], rows_ref[4:5, :] = gain_grad, bias_grad
    grad_two = grad_three_ref[...] + into
    grad_two_ref[...] = grad_two
    rows_ref[5:6, :] = jnp.sum(grad_two, axis=0, keepdims=True)
    two_low = grad_two.astype(BFLOAT)
    two_low_ref[...] = two_low
    loads[0].wait()
    mixed = dot(two_low, kept_ref[0])
    for r in range(parts):
        mixed_refs[r][...] = mixed[:, r * span : (r + 1) * span].astype(BFLOAT)


def middle_backward(grad, cot, three, two, raw, queries, table, text, group, weights, heads):
    rows, width = three.shape
    low = jax.ShapeDtypeStruct((rows, width), BFLOAT)
    vmem = pl.BlockSpec(memory_space=pltpu.VMEM)
    return pl.pallas_call(
        functools.partial(middle_backward_kernel, heads, len(text)),
        in_specs=[vmem] * (8 + len(text)) + [pl.BlockSpec(memory_space=pl.ANY)],
        out_shape=(
            low,
            low,
            low,
            jax.ShapeDtypeStruct((rows, width), FLOAT),
            jax.ShapeDtypeStruct((8, width), FLOAT),
            *[jax.ShapeDtypeStruct((rows, heads * HD), BFLOAT) for _ in text],
            *[jax.ShapeDtypeStruct(item.shape, BFLOAT) for item in text],
        ),
        out_specs=(vmem,) * (5 + 2 * len(text)),
        scratch_shapes=[
            pltpu.VMEM((3, width, width), BFLOAT),
            pltpu.VMEM((rows, width), FLOAT),
            pltpu.VMEM((rows, width), BFLOAT),
            pltpu.SemaphoreType.DMA((3,)),
        ],
        compiler_params=pltpu.CompilerParams(vmem_limit_bytes=56 * 2**20),
        cost_estimate=pl.CostEstimate(flops=33_000_000_000, bytes_accessed=28_000_000, transcendentals=1_300_000),
    )(*text, grad, cot, three, two, raw, queries, table, group, weights)


def on_device(
    latent, skip_in, text_tokens, time_embed, t_index, grid_pos, skip_weight, mod_weight, vectors, up_bias,
    qkv_weight, proj_weight, query_weight, text_weight, cross_weight, up_weight, down_weight, out_grad,
):
    split = lax.axis_size("tensor")
    shards = lax.axis_size("dp")
    place = lax.axis_index("tensor")
    me = lax.axis_index("dp")
    own_rows, width = latent.shape
    own_text = text_tokens.shape[0]
    part = mod_weight.shape[0]
    heads = HEADS // split
    span = heads * HD
    hidden = up_weight.shape[1]
    rows_ahead = vectors.shape[0]

    def others(r):
        return lax.rem(place - r + split, split)

    condition = time_embed
    half = width // 2
    frequencies = jnp.exp(-math.log(10000.0) * jnp.arange(half, dtype=FLOAT) / half)
    angles = t_index.astype(FLOAT)[:, None] * frequencies[None, :]
    condition = time_embed + jnp.concatenate([jnp.cos(angles), jnp.sin(angles)], axis=-1)
    silu_low = silu(condition).astype(BFLOAT)
    small = jnp.concatenate([vectors.reshape(-1), up_bias, silu_low.reshape(-1)])
    small_all = small_gather(small)
    cut_one, cut_two = rows_ahead * part, rows_ahead * part + up_bias.shape[0]
    table = (
        small_all[:, :cut_one].reshape(shards, rows_ahead, part).transpose(1, 0, 2).reshape(rows_ahead, width)
    ).astype(FLOAT)
    bias_all = small_all[:, cut_one:cut_two].reshape(-1).astype(FLOAT)
    silu_all = small_all[:, cut_two:]

    expand = jnp.asarray(expansion(heads), BFLOAT)
    deep = heads * DEEP
    packed_one = jnp.concatenate(
        [
            skip_weight[:part],
            skip_weight[part:],
            dot(qkv_weight.reshape(part, 3 * span), expand).astype(BFLOAT),
        ],
        axis=1,
    )
    all_one = lax.all_gather(packed_one, "dp", axis=0, tiled=True)
    w_skip = all_one[:, : 2 * width]
    w_qkv = all_one[:, 2 * width : 2 * width + 3 * deep]

    own_full = jnp.stack([proj_weight.T, query_weight, cross_weight.T, text_weight[:, 0], text_weight[:, 1]])
    full_blocks, text_blocks = [own_full], [text_tokens]
    for _ in range(split - 1):
        both = lax.optimization_barrier((full_blocks[-1], text_blocks[-1]))
        full_blocks.append(rot(both[0], 1))
        text_blocks.append(rot(both[1], 1))
    packed_two = jnp.concatenate(
        [full_blocks[r][index] for index in range(3) for r in range(split)]
        + [full_blocks[r][index] for r in range(split) for index in (3, 4)],
        axis=1,
    )

    cot_blocks = [out_grad, rot(after(out_grad, all_one, full_blocks[-1], text_blocks[-1]), 1)]

    text_length = own_text * split
    text_full = jnp.zeros((text_length, width), BFLOAT)
    for r in range(split):
        text_full = lax.dynamic_update_slice_in_dim(text_full, text_blocks[r], others(r) * own_text, 0)

    def head_slice(index):
        return lax.dynamic_slice_in_dim(table[index], place * span, span, 0)

    def relative(index):
        return jnp.concatenate(
            [lax.dynamic_slice_in_dim(table[index], others(r) * span, span, 0) for r in range(split)]
        )

    def spread(values):
        return lax.dynamic_update_slice_in_dim(jnp.zeros((width,), FLOAT), values.reshape(-1), place * span, 0)

    def absolute(values):
        result = jnp.zeros((width,), FLOAT)
        for r in range(split):
            result = lax.dynamic_update_slice_in_dim(
                result, values.reshape(-1)[r * span : (r + 1) * span], others(r) * span, 0
            )
        return result

    def deepen(values):
        turned = jnp.pad(values[:2].reshape(2, heads, 4, HD // 4), ((0, 0), (0, 0), (0, 0), (0, QUARTER - HD // 4)))
        plain = jnp.pad(values[2].reshape(heads, HD), ((0, 0), (0, DEEP - HD)))
        return jnp.concatenate([turned.reshape(-1), plain.reshape(-1)])

    def undeepen(values):
        turned = values[: 2 * deep].reshape(2, heads, 4, QUARTER)[..., : HD // 4].reshape(2, span)
        if values.shape[0] == 2 * deep:
            return turned
        return jnp.concatenate([turned, values[2 * deep :].reshape(heads, DEEP)[:, :HD].reshape(1, span)])

    quarter = HD // 4
    rate = np.zeros((QUARTER, 1), np.float32)
    rate[:quarter, 0] = 10000.0 ** (-np.arange(quarter, dtype=np.float64) / quarter)
    grid_rel = jnp.concatenate(
        [lax.dynamic_slice_in_dim(grid_pos, others(r) * own_rows, own_rows, 1) for r in range(split)], axis=1
    ).astype(FLOAT)
    turn = grid_rel[:, None, :] * rate[None]
    turns = jnp.stack([jnp.cos(turn[0]), jnp.sin(turn[0]), jnp.cos(turn[1]), jnp.sin(turn[1])])

    silu_mine = lax.dynamic_slice_in_dim(silu_all, me * part, part, 1)
    shift_terms = dot(silu_mine, mod_weight)
    shift = jnp.sum(lax.all_to_all(shift_terms, "dp", 0, 0, tiled=True), axis=0, keepdims=True) + table[5]

    joined = jnp.concatenate([latent.astype(FLOAT), skip_in.astype(FLOAT)], axis=-1)
    joined_gain = jnp.concatenate([table[0], table[1]])
    joined_bias = jnp.concatenate([table[2], table[3]])
    normed_low = layer_norm(joined, joined_gain, joined_bias).astype(BFLOAT)
    normed_perm = normed_low.reshape(own_rows, shards, 2, part).transpose(0, 2, 1, 3).reshape(own_rows, 2 * width)
    packed_two = after(packed_two, normed_perm, shift, turns)
    all_two = lax.all_gather(packed_two, "dp", axis=0, tiled=True)
    packed_three = jnp.concatenate([up_weight, down_weight.T], axis=1)
    all_three = lax.all_gather(packed_three, "dp", axis=0, tiled=True)
    w_up, w_down_t = all_three[:, :hidden], all_three[:, hidden:]

    stream_one = (
        dot(normed_perm[:, :width], w_skip[:, :width]) + dot(normed_perm[:, width:], w_skip[:, width:]) + table[4]
    )
    attn_low = (layer_norm(stream_one, table[6], table[7]) + shift).astype(BFLOAT)
    attn_blocks = ring_gather(after(attn_low, cot_blocks[1]))
    qkv_bias = deepen(jnp.stack([head_slice(8), head_slice(9), head_slice(10)]))[:, None]
    raws = [dot(w_qkv, block, ((0,), (1,))) + qkv_bias for block in attn_blocks]
    zero_slice = jnp.zeros((span,), FLOAT)
    gains = deepen(jnp.stack([head_slice(12), head_slice(13), zero_slice]))[: 2 * deep, None]
    length = own_rows * split
    block = min(512, length)
    kept = attend_forward(raws, turns, gains, heads, block)
    mixed, kept = kept[:split], kept[split:]

    def blocks_of(values, rows):
        return [values[r * rows : (r + 1) * rows] for r in range(split)]

    lane_head = np.arange(span) // HD
    group = jnp.asarray((lane_head[:, None] == lane_head[None, :]).astype(np.float32), BFLOAT)
    text_bias = jnp.stack([relative(17).reshape(split, span), relative(18).reshape(split, span)], axis=1)
    text_raw, *text_rel = text_forward(
        text_full, all_two, 3 * width, text_bias.reshape(split, 2 * span), relative(21).reshape(split, span), group
    )
    mixed = exchange(mixed)
    cot_blocks[-1], mixed[-1], text_rel[0] = lax.optimization_barrier((cot_blocks[-1], mixed[-1], text_rel[0]))
    cot_blocks.append(rot(cot_blocks[-1], 1))
    middle_table = jnp.stack(
        [table[11], table[14], table[15], relative(16), relative(20), table[19], table[22], table[23]]
    )
    stream_two, cross_raw, stream_three, mixed_own, cross_low, cross_queries, cross_mixed, mlp_low = middle_forward(
        mixed, stream_one, middle_table, text_rel, group, all_two, heads
    )
    mlp_low, cot_blocks[-1] = lax.optimization_barrier((mlp_low, cot_blocks[-1]))
    while len(cot_blocks) < split:
        cot_blocks.append(rot(cot_blocks[-1], 1))
    mlp_blocks = ring_gather(mlp_low)
    hidden_bias = lax.dynamic_slice_in_dim(bias_all, place * hidden, hidden, 0)

    hidden_lows, pre_lows, out_parts, back_parts = [], [], [], []
    for r in range(split):
        hidden_pre = dot(mlp_blocks[r], w_up) + hidden_bias
        activated, pull = jax.vjp(gelu, hidden_pre)
        hidden_lows.append(activated.astype(BFLOAT))
        pre_lows.append(pull(dot(cot_blocks[r], w_down_t))[0].astype(BFLOAT))
        back_parts.append(dot(pre_lows[r], w_up, NT))
        out_parts.append(dot(hidden_lows[r], w_down_t, NT))
    grad_mlp_in = ring_scatter(back_parts)

    rows_grad = {}
    grad_bias = sum(jnp.sum(item, axis=0, dtype=FLOAT) for item in pre_lows)
    grads_one = pack_grad(None, mlp_blocks, pre_lows, 2 * hidden, 0, 512)
    grads_one = pack_grad(grads_one, cot_blocks, hidden_lows, 2 * hidden, hidden, 512)
    grads_one, grad_mlp_in, *out_parts = lax.optimization_barrier((grads_one, grad_mlp_in, *out_parts))
    out_hop = rot(out_parts[1].astype(BFLOAT), 1)
    summed_one = lax.psum_scatter(grads_one, "dp", scatter_dimension=0, tiled=True).astype(FLOAT)
    cot_here = out_grad.astype(FLOAT)
    rows_grad[24] = jnp.sum(cot_here, axis=0)
    three_low, cq_low, two_low, grad_two, middle_rows, *pieces = middle_backward(
        grad_mlp_in, out_grad, stream_three, stream_two, cross_raw, cross_queries, middle_table, text_rel, group,
        all_two, heads,
    )
    grad_mixed, text_terms = pieces[:split], pieces[split:]
    for index, number in enumerate((22, 23, 19, 14, 15, 11)):
        rows_grad[number] = middle_rows[index]
    rows_grad[16], rows_grad[20] = absolute(middle_rows[6]), absolute(middle_rows[7])
    out_hop, *grad_mixed = lax.optimization_barrier((out_hop, *grad_mixed))
    grad_mixed = exchange(grad_mixed)
    lanes_two = 3 * width
    grads_two = pack_grad(None, [two_low], [mixed_own], lanes_two, 0, width)
    grads_two = pack_grad(grads_two, [cross_low], [cq_low], lanes_two, width, width)
    grads_two = pack_grad(grads_two, [three_low], [cross_mixed], lanes_two, 2 * width, width)
    grads_two, *grad_mixed = lax.optimization_barrier((grads_two, *grad_mixed))
    summed_two = lax.psum_scatter(grads_two, "dp", scatter_dimension=0, tiled=True)
    text_terms[1:] = lax.optimization_barrier((*text_terms[1:], grad_mixed[-1]))[:-1]
    text_got = [rot(text_terms[r], split - r) for r in range(1, split)]
    grad_raw, gain_grads, raw_sums = attend_backward(
        raws, turns, gains, kept, grad_mixed, heads, block
    )
    grad_raw, summed_one = lax.optimization_barrier((grad_raw, summed_one))
    text_got[0], grad_raw = lax.optimization_barrier((text_got[0], grad_raw))
    ckv_low, text_rows = text_norm_back([text_terms[0], *text_got], text_raw, head_slice(21)[None], group)
    rows_grad[21] = spread(text_rows[1, :span])
    rows_grad[17], rows_grad[18] = spread(text_rows[0, :span]), spread(text_rows[0, span:])

    gain_grads = undeepen(jnp.sum(gain_grads, axis=1))
    raw_sums = undeepen(jnp.sum(raw_sums, axis=1))
    rows_grad[12], rows_grad[13] = spread(gain_grads[0]), spread(gain_grads[1])
    rows_grad[8], rows_grad[9], rows_grad[10] = spread(raw_sums[0]), spread(raw_sums[1]), spread(raw_sums[2])
    qkv_lanes = 3 * deep
    text_lanes = pl.cdiv(2 * span, LANES) * LANES
    shared = 2 * width + LANES
    qkv_start = pl.cdiv(shared, deep) * deep
    text_start = qkv_start + qkv_lanes
    lanes_three = text_start + text_lanes
    bias_part = up_bias.shape[0]
    bias_cols = pl.cdiv(bias_part, part)
    bias_spread = lax.dynamic_update_slice_in_dim(jnp.zeros(bias_all.shape, FLOAT), grad_bias, place * hidden, 0)
    zero_row = jnp.zeros((width,), FLOAT)
    table_grad = jnp.stack([rows_grad.get(index, zero_row) for index in range(rows_ahead)], axis=1)
    bias_grad = jnp.pad(bias_spread.reshape(shards, bias_part), ((0, 0), (0, bias_cols * part - bias_part)))
    bias_grad = bias_grad.reshape(shards, bias_cols, part).transpose(0, 2, 1).reshape(width, bias_cols)
    small_grads = jnp.concatenate([table_grad, bias_grad], axis=1).astype(BFLOAT)
    small_grads = jnp.pad(small_grads, ((0, 0), (0, qkv_start - 2 * width - small_grads.shape[1])))

    grad_attn_in, shift_part, grads_three = ring_sum(
        grad_raw, attn_blocks, text_full, ckv_low, all_one, 2 * width, lanes_three, (qkv_start, text_start), split
    )
    grads_three = lax.dynamic_update_slice(grads_three, small_grads, (0, 2 * width))
    grads_three, one_low, late_rows = skip_grads(
        grads_three, grad_attn_in, grad_two, stream_one, table[6:7], normed_perm
    )
    grads_three, summed_two, one_low = lax.optimization_barrier((grads_three, summed_two, one_low))
    summed_three = lax.psum_scatter(grads_three, "dp", scatter_dimension=0, tiled=True)
    latent_grad, skip_grad, late, full_sum, text_grad, block_out = side_sums(
        one_low, late_rows, shift_part, jnp.concatenate([table[:2], table[24:25]]), latent, skip_in, stream_three,
        out_hop, summed_two, ckv_low, all_one, all_two, 3 * width, [out_parts[0], *out_parts[2:]], shards, split,
    )
    shift_grads = late[8 : 8 + shards]
    late = lax.dynamic_slice_in_dim(late[:8], me * part, part, 1)
    silu_terms = lax.dot_general(
        shift_grads, mod_weight.astype(FLOAT), ((NT), ((), ())), precision=HIGHEST, preferred_element_type=FLOAT
    )
    summed_three = after(summed_three, silu_terms, full_sum, text_grad, summed_one)
    mod_grad = lax.dot_general(
        silu_mine.astype(FLOAT), shift_grads, ((TN), ((), ())), precision=HIGHEST, preferred_element_type=FLOAT
    )
    into_silu = lax.all_to_all(silu_terms, "dp", 0, 0, tiled=True).reshape(1, width)
    time_full = jax.vjp(silu, condition)[1](into_silu)[0]
    time_grad = lax.dynamic_slice_in_dim(time_full, place * (width // split), width // split, 1)

    qkv_part = summed_three[:, qkv_start:text_start]
    text_part = summed_three[:, text_start : text_start + 2 * span]
    skip_weight_grad, small_sum = spread_sum(summed_three[:, :shared], width, split)
    vectors_grad = jnp.concatenate([late[:5], late[7:8], late[5:7], small_sum[:, 8:rows_ahead].T])
    bias_grad = small_sum[:, rows_ahead : rows_ahead + bias_cols].T.reshape(-1)[:bias_part]
    qkv_sum = dot(qkv_part, expand, NT).reshape(part, 3, span)
    text_sum_grad = text_part.astype(FLOAT).reshape(part, 2, span)

    return (
        block_out,
        latent_grad,
        skip_grad,
        text_grad,
        time_grad,
        skip_weight_grad,
        mod_grad,
        vectors_grad,
        bias_grad,
        qkv_sum,
        full_sum[:, :span].T,
        full_sum[:, span : 2 * span],
        text_sum_grad,
        full_sum[:, 2 * span :].T,
        summed_one[:, :hidden],
        summed_one[:, hidden:].T,
    )


def solution(mesh):
    tokens = P(("dp", "tensor"), None)
    placed = (
        tokens,
        tokens,
        tokens,
        P("dp", None),
        P("dp"),
        P(None, "dp"),
        P("dp", None),
        P("dp", None),
        P(None, "dp"),
        P("dp"),
        P("dp", None, "tensor"),
        P("tensor", "dp"),
        P("dp", "tensor"),
        P("dp", None, "tensor"),
        P("tensor", "dp"),
        P("dp", "tensor"),
        P("tensor", "dp"),
        tokens,
    )
    return jax.shard_map(
        on_device,
        mesh=mesh,
        in_specs=placed,
        out_specs=(
            tokens,
            tokens,
            tokens,
            tokens,
            P("dp", "tensor"),
            P("dp", None),
            P("dp", None),
            P(None, "dp"),
            P("dp"),
            P("dp", None, "tensor"),
            P("tensor", "dp"),
            P("dp", "tensor"),
            P("dp", None, "tensor"),
            P("tensor", "dp"),
            P("dp", "tensor"),
            P("tensor", "dp"),
        ),
        check_vma=False,
    )
```

```python
import functools
import math

import jax
import jax.numpy as jnp
import numpy as np
from jax import lax
from jax.experimental import pallas as pl
from jax.experimental.pallas import tpu as pltpu
from jax.sharding import PartitionSpec as P

HEADS = 16
HD = 88
LANES = 128
EPSILON = 1e-06
HIGHEST = lax.Precision.HIGHEST
FLOAT = jnp.float32
BFLOAT = jnp.bfloat16
LOG2E = 1.4426950408889634
SCALE = 1.0 / math.sqrt(HD)


def layer_norm(values, norm_gain, norm_bias):
    centred = values - jnp.mean(values, axis=-1, keepdims=True)
    variance = jnp.mean(centred * centred, axis=-1, keepdims=True)
    return centred * lax.rsqrt(variance + EPSILON) * norm_gain + norm_bias


def head_norm(values, norm_gain):
    centred = values - jnp.mean(values, axis=-1, keepdims=True)
    variance = jnp.mean(centred * centred, axis=-1, keepdims=True)
    return centred * lax.rsqrt(variance + EPSILON) * norm_gain


def silu(values):
    return values / (1.0 + jnp.exp(-values))


def gelu(values):
    inner = math.sqrt(2.0 / math.pi) * (values + 0.044715 * values * values * values)
    return 0.5 * values * (1.0 + jnp.tanh(inner))


def dot(left, right, contract=((1,), (0,))):
    return lax.dot_general(left, right, (contract, ((), ())), preferred_element_type=FLOAT)


NT = ((1,), (1,))
TN = ((0,), (0,))


def rot(values, step):
    count = lax.axis_size("tensor")
    return lax.ppermute(values, "tensor", [(i, (i + step) % count) for i in range(count)])


def ring_gather(own):
    blocks = [own]
    for _ in range(lax.axis_size("tensor") - 1):
        blocks.append(rot(blocks[-1], 1))
    return blocks


def ring_scatter(parts):
    running = parts[1].astype(BFLOAT)
    for part in parts[2:]:
        running = (rot(running, 1).astype(FLOAT) + part.astype(FLOAT)).astype(BFLOAT)
    return rot(running, 1).astype(FLOAT) + parts[0].astype(FLOAT)


def direct_gather(own):
    return [own] + [rot(own, r) for r in range(1, lax.axis_size("tensor"))]


def direct_scatter(parts):
    count = len(parts)
    total = parts[0].astype(FLOAT)
    for r in range(1, count):
        total = total + rot(parts[r], count - r).astype(FLOAT)
    return total


def exchange(parts):
    count = len(parts)
    return [parts[0]] + [rot(parts[count - r], r) for r in range(1, count)]


def after(values, *earlier):
    return lax.optimization_barrier((values, *earlier))[0]


def small_gather(own):
    have = own[None]
    me = lax.axis_index("dp")
    count = lax.axis_size("dp")
    step = 1
    while step < count:
        other = lax.ppermute(have, "dp", [(i, i ^ step) for i in range(count)])
        upper = (me // step) % 2 == 1
        have = jnp.where(upper, jnp.concatenate([other, have]), jnp.concatenate([have, other]))
        step *= 2
    return have


def tensor_sum(values):
    total = values.astype(FLOAT)
    for step in range(1, lax.axis_size("tensor")):
        total = total + rot(values, step).astype(FLOAT)
    return total


def grad_kernel(lefts, rights, turned, *refs):
    left_refs, right_refs = refs[:lefts], refs[lefts : lefts + rights]
    out_ref, kept_ref = refs[-2], refs[-1]
    rows = left_refs[0].shape[0]

    @pl.when(pl.program_id(0) == 0)
    def _():
        for r in range(lefts):
            kept_ref[:, r * rows : (r + 1) * rows] = left_refs[r][...].T

    total = None
    for r in range(rights):
        span = lefts // rights * rows
        left = kept_ref[:, r * span : (r + 1) * span]
        term = dot(left, right_refs[r][...], NT if turned else ((1,), (0,)))
        total = term if total is None else total + term
    out_ref[...] = total.astype(BFLOAT)


def pack_grad(packed, lefts, rights, lanes, start, tile, turned=False):
    rows, height = lefts[0].shape
    deep = rights[0].shape[1 if turned else 0]
    wide = rights[0].shape[0 if turned else 1]
    first = start // tile
    in_specs = [pl.BlockSpec((rows, height), lambda i: (0, 0))] * len(lefts)
    if turned:
        in_specs += [pl.BlockSpec((tile, deep), lambda i: (i, 0))] * len(rights)
    else:
        in_specs += [pl.BlockSpec((deep, tile), lambda i: (0, i))] * len(rights)
    operands = [*lefts, *rights]
    if packed is not None:
        in_specs.append(pl.BlockSpec(memory_space=pl.ANY))
        operands.append(packed)
    tokens = rows * len(lefts)
    return pl.pallas_call(
        functools.partial(grad_kernel, len(lefts), len(rights), turned),
        grid=(pl.cdiv(wide, tile),),
        in_specs=in_specs,
        out_specs=pl.BlockSpec((height, tile), lambda i: (0, first + i)),
        out_shape=jax.ShapeDtypeStruct((height, lanes), BFLOAT),
        scratch_shapes=[pltpu.VMEM((height, tokens), BFLOAT)],
        input_output_aliases={} if packed is None else {len(operands) - 1: 0},
        compiler_params=pltpu.CompilerParams(vmem_limit_bytes=40 * 2**20),
        cost_estimate=pl.CostEstimate(
            flops=4 * tokens * height * wide,
            bytes_accessed=2 * (tokens * height + tokens * wide + height * wide),
            transcendentals=0,
        ),
    )(*operands)


def flipped(index, bit):
    return index + (1 - 2 * lax.rem(lax.div(index, 2**bit), 2)) * 2**bit


def to_device(source, target, send, recv, where):
    return pltpu.make_async_remote_copy(
        src_ref=source,
        dst_ref=target,
        send_sem=send,
        recv_sem=recv,
        device_id=where,
        device_id_type=pl.DeviceIdType.MESH,
    )


def neighbours(place, split):
    return lax.rem(place + 1, split), lax.rem(place + split - 1, split)


def ring_kernel(split, start, places, *refs):
    raw_ref, left_refs, refs = refs[0], refs[1 : 1 + split], refs[1 + split :]
    text_ref, ckv_ref, packed_ref, sum_out, shift_out, grads_ref = refs[:6]
    weights_ref, turned, qkv_grad, text_grad, sent, got, load_sem, sems = refs[6:]
    loads = [
        pltpu.make_async_copy(packed_ref.at[:, start : start + weights_ref.shape[1]], weights_ref, load_sem.at[0]),
        pltpu.make_async_copy(
            qkv_grad, grads_ref.at[:, places[0] : places[0] + qkv_grad.shape[1]], load_sem.at[1]
        ),
        pltpu.make_async_copy(
            text_grad, grads_ref.at[:, places[1] : places[1] + text_grad.shape[1]], load_sem.at[2]
        ),
    ]
    loads[0].start()
    place = lax.axis_index("tensor")
    right, left = neighbours(place, split)
    barrier = pltpu.get_barrier_semaphore()
    for where in (left, right):
        pl.semaphore_signal(barrier, inc=1, device_id={"tensor": where}, device_id_type=pl.DeviceIdType.MESH)
    rows = sum_out.shape[0]

    def term(r):
        return dot(weights_ref[...], raw_ref[:, r * rows : (r + 1) * rows]).T

    def hop(step):
        return to_device(sent.at[step], got.at[step], sems.at[0, step], sems.at[1, step], {"tensor": right})

    def qkv_lanes(some):
        lanes = qkv_grad.shape[1] // 3
        for i in some:
            part = slice(i * lanes, (i + 1) * lanes)
            qkv_grad[:, part] = dot(turned[...], raw_ref[part, :], NT).astype(BFLOAT)

    def beside(step):
        if step == 1:
            for r in range(split):
                turned[:, r * rows : (r + 1) * rows] = left_refs[r][...].T
            qkv_lanes((0,))
        elif step == 2:
            qkv_lanes((1, 2))
            loads[1].start()
        elif step == 3:
            wide = ckv_ref.shape[1]
            text_grad[:, :wide] = dot(text_ref[...].T, ckv_ref[...]).astype(BFLOAT)
            text_grad[:, wide:] = jnp.zeros((text_grad.shape[0], text_grad.shape[1] - wide), BFLOAT)
            loads[2].start()

    loads[0].wait()
    part = term(1)
    total = jnp.sum(part, axis=0, keepdims=True)
    sent[0] = part.astype(BFLOAT)
    pl.semaphore_wait(barrier, 2)
    hop(0).start()
    for step in range(1, split):
        part = term((step + 1) % split)
        total = total + jnp.sum(part, axis=0, keepdims=True)
        beside(step)
        hop(step - 1).wait_recv()
        part = part + got[step - 1].astype(FLOAT)
        if step + 1 < split:
            sent[step] = part.astype(BFLOAT)
            hop(step).start()
        else:
            sum_out[...] = part
    shift_out[...] = jnp.broadcast_to(total, shift_out.shape)
    loads[1].wait()
    loads[2].wait()
    for step in range(split - 1):
        hop(step).wait_send()


def ring_sum(raw, lefts, text, ckv, packed, start, lanes, places, split):
    rows, width = raw.shape[1] // split, packed.shape[0]
    vmem = pl.BlockSpec(memory_space=pltpu.VMEM)
    anywhere = pl.BlockSpec(memory_space=pl.ANY)
    return pl.pallas_call(
        functools.partial(ring_kernel, split, start, places),
        in_specs=[vmem] * (3 + split) + [anywhere],
        out_specs=(vmem, vmem, anywhere),
        out_shape=(
            jax.ShapeDtypeStruct((rows, width), FLOAT),
            jax.ShapeDtypeStruct((8, width), FLOAT),
            jax.ShapeDtypeStruct((width, lanes), BFLOAT),
        ),
        scratch_shapes=[
            pltpu.VMEM((width, raw.shape[0]), BFLOAT),
            pltpu.VMEM((width, raw.shape[1]), BFLOAT),
            pltpu.VMEM((width, raw.shape[0]), BFLOAT),
            pltpu.VMEM((width, lanes - places[1]), BFLOAT),
            pltpu.VMEM((split - 1, rows, width), BFLOAT),
            pltpu.VMEM((split - 1, rows, width), BFLOAT),
            pltpu.SemaphoreType.DMA((3,)),
            pltpu.SemaphoreType.DMA((2, split - 1)),
        ],
        compiler_params=pltpu.CompilerParams(
            vmem_limit_bytes=48 * 2**20, collective_id=1, has_side_effects=True
        ),
        cost_estimate=pl.CostEstimate(flops=60_000_000_000, bytes_accessed=10_000_000, transcendentals=0),
    )(raw, *lefts, text, ckv, packed)


def skip_kernel(
    grad_ref, two_ref, one_ref, gain_ref, left_ref, packed_ref, out_ref, low_ref, rows_ref
):
    @pl.when(pl.program_id(0) == 0)
    def _():
        into, gain_grad, bias_grad = norm_rows_back(one_ref[...], gain_ref[...], grad_ref[...])
        grad_one = two_ref[...] + into
        low_ref[...] = grad_one.astype(BFLOAT)
        rows_ref[...] = jnp.concatenate(
            [gain_grad, bias_grad, jnp.sum(grad_one, axis=0, keepdims=True), jnp.zeros((5, grad_one.shape[1]), FLOAT)],
            axis=0,
        )

    out_ref[...] = dot(left_ref[...].T, low_ref[...]).astype(BFLOAT)


def skip_grads(packed, grad, two, one, gain, left):
    rows, width = one.shape
    fixed = pl.BlockSpec((rows, width), lambda i: (0, 0))
    return pl.pallas_call(
        skip_kernel,
        grid=(left.shape[1] // width,),
        in_specs=[fixed] * 3
        + [
            pl.BlockSpec((1, width), lambda i: (0, 0)),
            pl.BlockSpec((rows, width), lambda i: (0, i)),
            pl.BlockSpec(memory_space=pl.ANY),
        ],
        out_specs=(
            pl.BlockSpec((width, width), lambda i: (0, i)),
            pl.BlockSpec((rows, width), lambda i: (0, 0)),
            pl.BlockSpec((8, width), lambda i: (0, 0)),
        ),
        out_shape=(
            jax.ShapeDtypeStruct(packed.shape, BFLOAT),
            jax.ShapeDtypeStruct((rows, width), BFLOAT),
            jax.ShapeDtypeStruct((8, width), FLOAT),
        ),
        input_output_aliases={5: 0},
        compiler_params=pltpu.CompilerParams(vmem_limit_bytes=40 * 2**20),
        cost_estimate=pl.CostEstimate(flops=10_000_000_000, bytes_accessed=16_000_000, transcendentals=0),
    )(grad, two, one, gain, left, packed)


def side_kernel(shards, split, hops, text_start, *refs):
    low_ref, late_ref, shift_ref, table_ref, latent_ref, skip_ref, base_ref, hop_ref, summed_ref, ckv_ref = refs[:10]
    weights_ref, text_packed_ref, refs = refs[10], refs[11], refs[12:]
    out_refs, refs = refs[: hops + 1], refs[hops + 1 :]
    latent_out, skip_out, table_out, full_out, text_out, block_out = refs[:6]
    weights, text_weights, full_refs, text_refs, full_got, text_got, hop_sent, hop_got, table_sent, table_got = refs[6:16]
    load_sem, side_sems, hop_sems, table_sems = refs[16:]
    me, place = lax.axis_index("dp"), lax.axis_index("tensor")
    count = shards.bit_length() - 1
    width = latent_out.shape[1]
    part = width // shards
    right, _ = neighbours(place, split)

    loads = [
        pltpu.make_async_copy(weights_ref.at[:, half * width : (half + 1) * width], weights, load_sem.at[half])
        for half in range(2)
    ]
    text_stop = text_start + text_weights.shape[1]
    loads.append(pltpu.make_async_copy(text_packed_ref.at[:, text_start:text_stop], text_weights, load_sem.at[2]))
    loads[0].start()
    loads[2].start()
    barrier = pltpu.get_barrier_semaphore()
    for bit in range(count):
        pl.semaphore_signal(barrier, inc=1, device_id={"dp": flipped(me, bit)}, device_id_type=pl.DeviceIdType.MESH)
    for step in range(1, split):
        pl.semaphore_signal(
            barrier, inc=1, device_id={"tensor": lax.rem(place + step, split)}, device_id_type=pl.DeviceIdType.MESH
        )

    def side(step, i):
        return to_device(
            (full_refs, text_refs)[i].at[step],
            (full_got, text_got)[i].at[step - 1],
            side_sems.at[i, 0, step - 1],
            side_sems.at[i, 1, step - 1],
            {"tensor": lax.rem(place + split - step, split)},
        )

    def hop(step):
        return to_device(
            hop_sent.at[step], hop_got.at[step], hop_sems.at[0, step], hop_sems.at[1, step], {"tensor": right}
        )

    hop_sent[0] = (hop_ref[...].astype(FLOAT) + out_refs[1][...]).astype(BFLOAT)
    pl.semaphore_wait(barrier, count + split - 1)
    hop(0).start()
    low = low_ref[...]
    grads = []
    for half in range(2):
        loads[half].wait()
        grads.append(dot(low, weights[...], NT))
        if half == 0:
            loads[1].start()
    ordered = [grads[half][:, shard * part : (shard + 1) * part] for shard in range(shards) for half in range(2)]
    grads = [jnp.concatenate(ordered[:shards], axis=1), jnp.concatenate(ordered[shards:], axis=1)]
    values = [latent_ref[...].astype(FLOAT), skip_ref[...].astype(FLOAT)]

    def mean_of(one, two):
        return (jnp.sum(one, axis=-1, keepdims=True) + jnp.sum(two, axis=-1, keepdims=True)) * (0.5 / width)

    mean = mean_of(*values)
    centred = [item - mean for item in values]
    inverse = lax.rsqrt(mean_of(*[item * item for item in centred]) + EPSILON)
    normed = [item * inverse for item in centred]
    gain_rows = [jnp.sum(grads[i] * normed[i], axis=0, keepdims=True) for i in range(2)]
    bias_rows = [jnp.sum(grads[i], axis=0, keepdims=True) for i in range(2)]
    scaled = [grads[i] * table_ref[i : i + 1, :] for i in range(2)]
    mean = mean_of(*scaled)
    slope = mean_of(*[scaled[i] * normed[i] for i in range(2)])
    latent_out[...] = inverse * (scaled[0] - mean - normed[0] * slope)
    skip_out[...] = inverse * (scaled[1] - mean - normed[1] * slope)

    spare = table_out.shape[0] - 8
    table_sent[0] = jnp.concatenate(
        [
            *gain_rows,
            *bias_rows,
            late_ref[2:3, :],
            late_ref[0:2, :],
            shift_ref[0:1, :],
            jnp.zeros((spare, width), FLOAT),
        ],
        axis=0,
    )
    bits = split.bit_length() - 1
    shares = table_sent.shape[0]

    def share(step):
        where = {"tensor": flipped(place, step)} if step < bits else {"dp": flipped(me, step - bits)}
        return to_device(
            table_sent.at[step], table_got.at[step], table_sems.at[0, step], table_sems.at[1, step], where
        )

    def open_hop(step):
        hop(step - 1).wait_recv()
        hop_sent[step] = (hop_got[step - 1].astype(FLOAT) + out_refs[step + 1][...]).astype(BFLOAT)
        hop(step).start()

    def pass_on(step):
        share(step).wait_recv()
        total = table_sent[step] + table_got[step]
        if step + 1 == bits:
            at = lax.broadcasted_iota(jnp.int32, (8 + spare, 1), 0)
            total = jnp.where(at == 8 + me, total[7:8, :], total)
        if step + 1 < shares:
            table_sent[step + 1] = total
            share(step + 1).start()
        else:
            table_out[...] = total
    share(0).start()
    span = full_out.shape[1] // 3
    for r in range(split):
        full_refs[r] = jnp.concatenate(
            [summed_ref[:, k * width + r * span : k * width + (r + 1) * span] for k in range(3)], axis=1
        )
    for step in range(bits):
        pass_on(step)
    for step in range(1, split):
        side(step, 0).start()
    loads[2].wait()
    back = dot(ckv_ref[...], text_weights[:, : ckv_ref.shape[1]], NT).astype(BFLOAT)
    own_text = text_out.shape[0]
    for r in range(split):
        text_refs[lax.rem(place + split - r, split)] = back[r * own_text : (r + 1) * own_text]
    for step in range(1, split):
        side(step, 1).start()
    for step in range(1, hops):
        open_hop(step)
    for step in range(bits, shares):
        pass_on(step)
    for i, (terms, result) in enumerate(((full_refs, full_out), (text_refs, text_out))):
        if i == 1:
            hop(hops - 1).wait_recv()
            last = hop_got[hops - 1].astype(FLOAT) + out_refs[0][...]
            block_out[...] = (base_ref[...] + table_ref[2:3, :] + last).astype(BFLOAT)
        total = terms[0].astype(FLOAT)
        for step in range(1, split):
            side(step, i).wait_recv()
            total = total + (full_got, text_got)[i][step - 1].astype(FLOAT)
        result[...] = total
    for step in range(hops):
        hop(step).wait_send()
    for step in range(shares):
        share(step).wait_send()
    for step in range(1, split):
        for i in range(2):
            side(step, i).wait_send()


def side_sums(
    low, late, shift, table, latent, skip_in, base, hop, summed, ckv, weights, text_packed, text_start, out, shards, split
):
    rows, width = low.shape
    spare = pl.cdiv(shards, 8) * 8
    shares = shards.bit_length() - 1 + split.bit_length() - 1
    vmem = pl.BlockSpec(memory_space=pltpu.VMEM)
    wide = jax.ShapeDtypeStruct((rows, width), FLOAT)
    hops = len(out) - 1
    full, text = (summed.shape[0], summed.shape[1] // split), (ckv.shape[0] // split, width)
    return pl.pallas_call(
        functools.partial(side_kernel, shards, split, hops, text_start),
        in_specs=[vmem] * 10 + [pl.BlockSpec(memory_space=pl.ANY)] * 2 + [vmem] * len(out),
        out_specs=(vmem,) * 6,
        out_shape=(
            wide,
            wide,
            jax.ShapeDtypeStruct((8 + spare, width), FLOAT),
            jax.ShapeDtypeStruct(full, FLOAT),
            jax.ShapeDtypeStruct(text, FLOAT),
            jax.ShapeDtypeStruct((rows, width), BFLOAT),
        ),
        scratch_shapes=[
            pltpu.VMEM((width, width), BFLOAT),
            pltpu.VMEM((width, pl.cdiv(ckv.shape[1], LANES) * LANES), BFLOAT),
            pltpu.VMEM((split, *full), BFLOAT),
            pltpu.VMEM((split, *text), BFLOAT),
            pltpu.VMEM((split - 1, *full), BFLOAT),
            pltpu.VMEM((split - 1, *text), BFLOAT),
            pltpu.VMEM((hops, rows, width), BFLOAT),
            pltpu.VMEM((hops, rows, width), BFLOAT),
            pltpu.VMEM((shares, 8 + spare, width), FLOAT),
            pltpu.VMEM((shares, 8 + spare, width), FLOAT),
            pltpu.SemaphoreType.DMA((3,)),
            pltpu.SemaphoreType.DMA((2, 2, split - 1)),
            pltpu.SemaphoreType.DMA((2, hops)),
            pltpu.SemaphoreType.DMA((2, shares)),
        ],
        compiler_params=pltpu.CompilerParams(
            vmem_limit_bytes=56 * 2**20, collective_id=0, has_side_effects=True
        ),
        cost_estimate=pl.CostEstimate(flops=90_000_000_000, bytes_accessed=30_000_000, transcendentals=0),
    )(low, late, shift, table, latent, skip_in, base, hop, summed, ckv, weights, text_packed, *out)


def spread_kernel(split, starts, in_ref, skip_out, small_out, piece_sent, piece_got, pieces, whole, sems):
    place = lax.axis_index("tensor")
    part, width = skip_out.shape[0] // 2, skip_out.shape[1]
    wide = piece_sent.shape[2]
    barrier = pltpu.get_barrier_semaphore()
    for step in range(1, split):
        pl.semaphore_signal(
            barrier, inc=1, device_id={"tensor": lax.rem(place + step, split)}, device_id_type=pl.DeviceIdType.MESH
        )
    for i in range(split):
        piece_sent[i] = in_ref[:, starts[i] : starts[i] + wide]
    pl.semaphore_wait(barrier, split - 1)

    def scatter(step):
        where = lax.rem(place + step, split)
        return to_device(
            piece_sent.at[where], piece_got.at[step - 1], sems.at[0, step - 1], sems.at[1, step - 1], {"tensor": where}
        )

    def gather(step):
        return to_device(
            pieces.at[place], pieces.at[place], sems.at[2, step - 1], sems.at[3, step - 1],
            {"tensor": lax.rem(place + step, split)},
        )

    for step in range(1, split):
        scatter(step).start()
    total = piece_sent[place].astype(FLOAT)
    for step in range(1, split):
        scatter(step).wait_recv()
        total = total + piece_got[step - 1].astype(FLOAT)
    pieces[place] = total.astype(BFLOAT)
    for step in range(1, split):
        gather(step).start()
    for step in range(1, split):
        gather(step).wait_recv()
    for i in range(split):
        stop = starts[i + 1] if i + 1 < split else whole.shape[1]
        whole[:, starts[i] : stop] = pieces[i][:, : stop - starts[i]].astype(FLOAT)
    skip_out[:part] = whole[:, :width]
    skip_out[part:] = whole[:, width : 2 * width]
    small_out[...] = whole[:, 2 * width :]
    for step in range(1, split):
        scatter(step).wait_send()
        gather(step).wait_send()


def spread_sum(values, width, split):
    part, lanes = values.shape
    wide = pl.cdiv(lanes // LANES, split) * LANES
    starts = [min(i * wide, lanes - wide) for i in range(split)]
    vmem = pl.BlockSpec(memory_space=pltpu.VMEM)
    return pl.pallas_call(
        functools.partial(spread_kernel, split, starts),
        in_specs=[vmem],
        out_specs=(vmem,) * 2,
        out_shape=(
            jax.ShapeDtypeStruct((2 * part, width), FLOAT),
            jax.ShapeDtypeStruct((part, lanes - 2 * width), FLOAT),
        ),
        scratch_shapes=[
            pltpu.VMEM((split, part, wide), BFLOAT),
            pltpu.VMEM((split - 1, part, wide), BFLOAT),
            pltpu.VMEM((split, part, wide), BFLOAT),
            pltpu.VMEM((part, lanes), FLOAT),
            pltpu.SemaphoreType.DMA((4, split - 1)),
        ],
        compiler_params=pltpu.CompilerParams(
            vmem_limit_bytes=30 * 2**20, collective_id=2, has_side_effects=True
        ),
        cost_estimate=pl.CostEstimate(flops=40_000_000_000, bytes_accessed=4_000_000, transcendentals=0),
    )(values)


def text_forward_kernel(parts, start, text_ref, bias_ref, gain_ref, group_ref, packed_ref, raw_ref, *refs):
    low_refs, weights_ref, sems = refs[:parts], refs[parts], refs[parts + 1]
    span = gain_ref.shape[1]
    wide = 2 * span
    load = pltpu.make_async_copy(packed_ref.at[:, start : start + parts * wide], weights_ref, sems.at[0])
    load.start()
    load.wait()
    for r in range(parts):
        raw = dot(text_ref[...], weights_ref[:, r * wide : (r + 1) * wide]) + bias_ref[r : r + 1, :]
        if r == 0:
            raw_ref[...] = raw
        normed, _ = norm_heads(raw[:, :span], group_ref[...])
        low_refs[r][:, :span] = (normed * gain_ref[r : r + 1, :]).astype(BFLOAT)
        low_refs[r][:, span:] = raw[:, span:].astype(BFLOAT)


def text_forward(text, packed, start, bias, gain, group):
    parts, wide = bias.shape
    tokens, width = text.shape
    vmem = pl.BlockSpec(memory_space=pltpu.VMEM)
    return pl.pallas_call(
        functools.partial(text_forward_kernel, parts, start),
        in_specs=[vmem] * 4 + [pl.BlockSpec(memory_space=pl.ANY)],
        out_specs=(vmem,) * (1 + parts),
        out_shape=(
            jax.ShapeDtypeStruct((tokens, wide), FLOAT),
            *[jax.ShapeDtypeStruct((tokens, wide), BFLOAT) for _ in range(parts)],
        ),
        scratch_shapes=[pltpu.VMEM((width, parts * wide), BFLOAT), pltpu.SemaphoreType.DMA((1,))],
        compiler_params=pltpu.CompilerParams(vmem_limit_bytes=40 * 2**20),
        cost_estimate=pl.CostEstimate(flops=12_000_000_000, bytes_accessed=10_000_000, transcendentals=0),
    )(text, bias, gain, group, packed)


def text_kernel(parts, *refs):
    term_refs, (raw_ref, gain_ref, group_ref, low_ref, rows_ref) = refs[:parts], refs[parts:]
    span = gain_ref.shape[1]
    total = term_refs[0][...].astype(FLOAT)
    for ref in term_refs[1:]:
        total = total + ref[...].astype(FLOAT)
    group = group_ref[...]
    normed, inverse = norm_heads(raw_ref[:, :span], group)
    grad = total[:, :span]
    gain_grad = jnp.sum(grad * normed, axis=0, keepdims=True)
    grad = grad * gain_ref[...]
    grad = inverse * (grad - head_means(grad, group) - normed * head_means(grad * normed, group))
    low = jnp.concatenate([grad, total[:, span:]], axis=1).astype(BFLOAT)
    low_ref[...] = low
    zeros = jnp.zeros((1, span), FLOAT)
    rows_ref[...] = jnp.concatenate(
        [
            jnp.sum(low.astype(FLOAT), axis=0, keepdims=True),
            jnp.concatenate([gain_grad, zeros], axis=1),
            jnp.zeros((6, 2 * span), FLOAT),
        ],
        axis=0,
    )


def text_norm_back(terms, raw, gain, group):
    return pl.pallas_call(
        functools.partial(text_kernel, len(terms)),
        out_shape=(
            jax.ShapeDtypeStruct(terms[0].shape, BFLOAT),
            jax.ShapeDtypeStruct((8, terms[0].shape[1]), FLOAT),
        ),
        compiler_params=pltpu.CompilerParams(vmem_limit_bytes=30 * 2**20),
        cost_estimate=pl.CostEstimate(flops=5_000_000_000, bytes_accessed=4_000_000, transcendentals=0),
    )(*terms, raw, gain, group)


QUARTER = 24
DEEP = 4 * QUARTER


def expansion(heads):
    result = np.zeros((3 * heads * HD, 3 * heads * DEEP), np.float32)
    for part in range(3):
        for head in range(heads):
            for channel in range(HD):
                quarter = HD // 4
                place = channel if part == 2 else channel // quarter * QUARTER + channel % quarter
                result[(part * heads + head) * HD + channel, (part * heads + head) * DEEP + place] = 1.0
    return result


def real_rows():
    rows = lax.broadcasted_iota(jnp.int32, (DEEP, 1), 0)
    return (lax.rem(rows, QUARTER) < HD // 4).astype(FLOAT)


def norm_deep(values, mask):
    mean = jnp.sum(values, axis=0, keepdims=True) * (1.0 / HD)
    centred = (values - mean) * mask
    inverse = lax.rsqrt(jnp.sum(centred * centred, axis=0, keepdims=True) * (1.0 / HD) + EPSILON)
    return centred * inverse, inverse


def turn_deep(values, row_cos, row_sin, col_cos, col_sin):
    one, two, three, four = (values[i * QUARTER : (i + 1) * QUARTER] for i in range(4))
    return jnp.concatenate(
        [
            one * row_cos - two * row_sin,
            two * row_cos + one * row_sin,
            three * col_cos - four * col_sin,
            four * col_cos + three * col_sin,
        ],
        axis=0,
    )


def full_tile(values):
    return jnp.concatenate([values, jnp.zeros((LANES - DEEP, values.shape[1]), values.dtype)], axis=0)


def attend_forward_kernel(heads, parts, block, *refs):
    raw_refs, refs = refs[:parts], refs[parts:]
    turn_ref, gain_ref, refs = refs[0], refs[1], refs[2:]
    o_refs, (oturn_ref, qturn_ref, kturn_ref, k_ref, v_ref, lse_ref, vturn_ref) = refs[:parts], refs[parts:]
    rows = raw_refs[0].shape[1]
    length = parts * rows
    mask = real_rows()
    for r in range(parts):
        here = slice(r * rows, (r + 1) * rows)

        def prepare(head, carry):
            tables = [turn_ref[i, :, here] for i in range(4)]
            turned = []
            for part in range(2):
                at = pl.ds((part * heads + head) * DEEP, DEEP)
                normed, _ = norm_deep(raw_refs[r][at, :], mask)
                turned.append(full_tile(turn_deep(normed * gain_ref[at, :], *tables)))
            qturn_ref[head, :, here] = turned[0].astype(BFLOAT)
            kturn_ref[head, :, here] = turned[1].astype(BFLOAT)
            k_ref[head, here, :] = turned[1].T.astype(BFLOAT)
            values = full_tile(raw_refs[r][pl.ds((2 * heads + head) * DEEP, DEEP), :])
            vturn_ref[head, :, here] = values.astype(BFLOAT)
            v_ref[head, here, :] = values.T.astype(BFLOAT)
            return carry

        lax.fori_loop(0, heads, prepare, 0)
    for head in range(heads):
        for index in range(length // block):
            here = slice(index * block, (index + 1) * block)
            scores = dot(k_ref[head], qturn_ref[head, :, here])
            peak = jnp.max(scores, axis=0, keepdims=True)
            powers = jnp.exp2((scores - peak) * (SCALE * LOG2E))
            total = jnp.sum(powers, axis=0, keepdims=True)
            mixed = dot(vturn_ref[head], powers.astype(BFLOAT)) / total
            oturn_ref[head, :, here] = mixed.astype(BFLOAT)
            lse_ref[head, :, here] = peak * (SCALE * LOG2E) + jnp.log2(total)
    for r in range(parts):
        here = slice(r * rows, (r + 1) * rows)
        o_refs[r][...] = jnp.concatenate(
            [oturn_ref[head, :, here].astype(FLOAT).T[:, :HD] for head in range(heads)], axis=1
        ).astype(BFLOAT)


def attend_forward(raws, turns, gains, heads, block):
    rows = raws[0].shape[1]
    length = rows * len(raws)
    tall = jax.ShapeDtypeStruct((heads, LANES, length), BFLOAT)
    long = jax.ShapeDtypeStruct((heads, length, LANES), BFLOAT)
    return pl.pallas_call(
        functools.partial(attend_forward_kernel, heads, len(raws), block),
        out_shape=(
            *[jax.ShapeDtypeStruct((rows, heads * HD), BFLOAT) for _ in raws],
            tall,
            tall,
            tall,
            long,
            long,
            jax.ShapeDtypeStruct((heads, 1, length), FLOAT),
        ),
        scratch_shapes=[pltpu.VMEM((heads, LANES, length), BFLOAT)],
        compiler_params=pltpu.CompilerParams(vmem_limit_bytes=56 * 2**20),
        cost_estimate=pl.CostEstimate(flops=20_000_000_000, bytes_accessed=12_000_000, transcendentals=4_200_000),
    )(*raws, turns, gains)


def attend_backward_kernel(heads, parts, block, *refs):
    raw_refs, refs = refs[:parts], refs[parts:]
    turn_ref, gain_ref, oturn_ref, qturn_ref, kturn_ref, k_ref, v_ref, lse_ref = refs[:8]
    do_refs = refs[8 : 8 + parts]
    graw_ref, gain_out_ref, sums_ref, dturn_ref, dq_ref, dk_ref, dv_ref = refs[8 + parts :]
    rows = raw_refs[0].shape[1]
    length = parts * rows
    count = length // block
    mask = real_rows()
    for r in range(parts):
        here = slice(r * rows, (r + 1) * rows)
        values = do_refs[r][...].astype(FLOAT)
        for head in range(heads):
            wide = jnp.concatenate(
                [values[:, head * HD : (head + 1) * HD], jnp.zeros((rows, LANES - HD), FLOAT)], axis=1
            )
            dturn_ref[head, :, here] = wide.T.astype(BFLOAT)

    def attend(head, carry):
        for index in range(count):
            here = slice(index * block, (index + 1) * block)
            queries, grad = qturn_ref[head, :, here], dturn_ref[head, :, here]
            probs = jnp.exp2(dot(k_ref[head], queries) * (SCALE * LOG2E) - lse_ref[head, :, here])
            inner = jnp.sum(grad.astype(FLOAT) * oturn_ref[head, :, here].astype(FLOAT), axis=0, keepdims=True)
            grad_scores = (probs * (dot(v_ref[head], grad) - inner)).astype(BFLOAT)
            add_v = dot(grad, probs.astype(BFLOAT), NT)
            add_k = dot(queries, grad_scores, NT)
            dq_ref[head, :, here] = dot(kturn_ref[head], grad_scores)
            if index == 0:
                dv_ref[head] = add_v
                dk_ref[head] = add_k
            else:
                dv_ref[head] += add_v
                dk_ref[head] += add_k
        return carry

    lax.fori_loop(0, heads, attend, 0)
    gain_out_ref[...] = jnp.zeros_like(gain_out_ref)
    sums_ref[...] = jnp.zeros_like(sums_ref)

    def narrow(values):
        return sum(values[:, i * LANES : (i + 1) * LANES] for i in range(values.shape[1] // LANES))

    for r in range(parts):
        here = slice(r * rows, (r + 1) * rows)

        def finish(head, carry):
            row_cos, row_sin, col_cos, col_sin = (turn_ref[i, :, here] for i in range(4))
            for part, grad_ref in ((0, dq_ref), (1, dk_ref)):
                at = pl.ds((part * heads + head) * DEEP, DEEP)
                normed, inverse = norm_deep(raw_refs[r][at, :], mask)
                grad = turn_deep(grad_ref[head, :DEEP, here] * SCALE, row_cos, -row_sin, col_cos, -col_sin)
                gain_out_ref[at, :] += narrow(grad * normed)
                grad = grad * gain_ref[at, :]
                mean = jnp.sum(grad, axis=0, keepdims=True) * (1.0 / HD)
                slope = jnp.sum(grad * normed, axis=0, keepdims=True) * (1.0 / HD)
                low = ((inverse * (grad - mean - normed * slope)) * mask).astype(BFLOAT)
                graw_ref[at, here] = low
                sums_ref[at, :] += narrow(low.astype(FLOAT))
            at = pl.ds((2 * heads + head) * DEEP, DEEP)
            low = dv_ref[head, :DEEP, here].astype(BFLOAT)
            graw_ref[at, here] = low
            sums_ref[at, :] += narrow(low.astype(FLOAT))
            return carry

        lax.fori_loop(0, heads, finish, 0)


def attend_backward(raws, turns, gains, kept, grad_out, heads, block):
    length = raws[0].shape[1] * len(raws)
    return pl.pallas_call(
        functools.partial(attend_backward_kernel, heads, len(raws), block),
        out_shape=(
            jax.ShapeDtypeStruct((3 * heads * DEEP, length), BFLOAT),
            jax.ShapeDtypeStruct((2 * heads * DEEP, LANES), FLOAT),
            jax.ShapeDtypeStruct((3 * heads * DEEP, LANES), FLOAT),
        ),
        scratch_shapes=[
            pltpu.VMEM((heads, LANES, length), BFLOAT),
            pltpu.VMEM((heads, LANES, length), FLOAT),
            pltpu.VMEM((heads, LANES, length), FLOAT),
            pltpu.VMEM((heads, LANES, length), FLOAT),
        ],
        compiler_params=pltpu.CompilerParams(vmem_limit_bytes=56 * 2**20),
        cost_estimate=pl.CostEstimate(flops=28_000_000_000, bytes_accessed=16_000_000, transcendentals=4_200_000),
    )(*raws, turns, gains, *kept, *grad_out)


def norm_rows(values):
    count = values.shape[-1]
    mean = jnp.sum(values, axis=-1, keepdims=True) * (1.0 / count)
    centred = values - mean
    inverse = lax.rsqrt(jnp.sum(centred * centred, axis=-1, keepdims=True) * (1.0 / count) + EPSILON)
    return centred * inverse, inverse


def norm_rows_back(values, gain, grad):
    normed, inverse = norm_rows(values)
    count = values.shape[-1]
    gain_grad = jnp.sum(grad * normed, axis=0, keepdims=True)
    bias_grad = jnp.sum(grad, axis=0, keepdims=True)
    grad = grad * gain
    mean = jnp.sum(grad, axis=-1, keepdims=True) * (1.0 / count)
    slope = jnp.sum(grad * normed, axis=-1, keepdims=True) * (1.0 / count)
    return inverse * (grad - mean - normed * slope), gain_grad, bias_grad


def head_means(values, group):
    high = values.astype(BFLOAT)
    rest = (values - high.astype(FLOAT)).astype(BFLOAT)
    return (dot(high, group) + dot(rest, group)) * (1.0 / HD)


def norm_heads(values, group):
    centred = values - head_means(values, group)
    inverse = lax.rsqrt(head_means(centred * centred, group) + EPSILON)
    return centred * inverse, inverse


def head_masks(heads, span):
    lanes = lax.broadcasted_iota(jnp.int32, (1, span), 1)
    return [((lanes >= HD * head) & (lanes < HD * (head + 1))).astype(BFLOAT) for head in range(heads)]


def load_weights(weights_ref, kept_ref, sems):
    width = kept_ref.shape[-1]
    return [
        pltpu.make_async_copy(weights_ref.at[:, i * width : (i + 1) * width], kept_ref.at[i], sems.at[i])
        for i in range(3)
    ]


def middle_forward_kernel(
    heads, parts, *refs,
):
    mixed_refs, text_refs, refs = refs[:parts], refs[parts : 2 * parts], refs[2 * parts :]
    one_ref, table_ref, group_ref, weights_ref, two_ref, raw_ref, three_ref, mixed_ref, cross_ref = refs[:9]
    query_ref, cross_mixed_ref, mlp_ref, kept_ref, sems = refs[9:]
    span = heads * HD
    mixed_ref[...] = jnp.concatenate([ref[...] for ref in mixed_refs], axis=1)
    loads = load_weights(weights_ref, kept_ref, sems)
    for load in loads:
        load.start()
    row = lambda index: table_ref[index : index + 1, :]
    loads[0].wait()
    two = one_ref[...] + dot(mixed_ref[...], kept_ref[0], NT) + row(0)
    two_ref[...] = two
    cross = (norm_rows(two)[0] * row(1) + row(2)).astype(BFLOAT)
    cross_ref[...] = cross
    loads[1].wait()
    raw_ref[...] = dot(cross, kept_ref[1]) + row(3)
    group = group_ref[...]
    masks = head_masks(heads, span)
    pieces, mixes = [], []
    for r in range(parts):
        part = slice(r * span, (r + 1) * span)
        normed, _ = norm_heads(raw_ref[:, part], group)
        queries = (normed * table_ref[4:5, part]).astype(BFLOAT)
        pieces.append(queries)
        keys, values = text_refs[r][:, :span], text_refs[r][:, span:]
        mix = None
        for head in range(heads):
            scores = dot(queries * masks[head], keys, NT)
            peak = jnp.max(scores, axis=-1, keepdims=True)
            powers = jnp.exp2((scores - peak) * (SCALE * LOG2E))
            weights = (powers / jnp.sum(powers, axis=-1, keepdims=True)).astype(BFLOAT)
            term = dot(weights, values * masks[head])
            mix = term if mix is None else mix + term
        mixes.append(mix.astype(BFLOAT))
    query_ref[...] = jnp.concatenate(pieces, axis=1)
    cross_mixed_ref[...] = jnp.concatenate(mixes, axis=1)
    loads[2].wait()
    three = two_ref[...] + dot(cross_mixed_ref[...], kept_ref[2], NT) + row(5)
    three_ref[...] = three
    mlp_ref[...] = (norm_rows(three)[0] * row(6) + row(7)).astype(BFLOAT)


def middle_forward(mixed, one, table, text, group, weights, heads):
    rows, width = one.shape
    wide = jax.ShapeDtypeStruct((rows, width), FLOAT)
    low = jax.ShapeDtypeStruct((rows, width), BFLOAT)
    vmem = pl.BlockSpec(memory_space=pltpu.VMEM)
    return pl.pallas_call(
        functools.partial(middle_forward_kernel, heads, len(mixed)),
        in_specs=[vmem] * (2 * len(mixed) + 3) + [pl.BlockSpec(memory_space=pl.ANY)],
        out_shape=(wide, wide, wide, low, low, low, low, low),
        out_specs=(vmem,) * 8,
        scratch_shapes=[pltpu.VMEM((3, width, width), BFLOAT), pltpu.SemaphoreType.DMA((3,))],
        compiler_params=pltpu.CompilerParams(vmem_limit_bytes=56 * 2**20),
        cost_estimate=pl.CostEstimate(flops=26_000_000_000, bytes_accessed=24_000_000, transcendentals=1_300_000),
    )(*mixed, *text, one, table, group, weights)


def middle_backward_kernel(
    heads, parts, *refs,
):
    text_refs, refs = refs[:parts], refs[parts:]
    grad_ref, cot_ref, three_ref, two_ref, raw_ref, query_ref, table_ref, group_ref, weights_ref = refs[:9]
    three_low_ref, raw_low_ref, two_low_ref, grad_two_ref, rows_ref, refs = *refs[9:14], refs[14:]
    mixed_refs, text_grad_refs = refs[:parts], refs[parts : 2 * parts]
    kept_ref, grad_three_ref, mixed_ref, sems = refs[2 * parts :]
    span = heads * HD
    loads = load_weights(weights_ref, kept_ref, sems)
    for load in reversed(loads):
        load.start()
    row = lambda index: table_ref[index : index + 1, :]
    into, gain_grad, bias_grad = norm_rows_back(three_ref[...], row(6), grad_ref[...])
    rows_ref[0:1, :], rows_ref[1:2, :] = gain_grad, bias_grad
    grad_three = cot_ref[...].astype(FLOAT) + into
    grad_three_ref[...] = grad_three
    rows_ref[2:3, :] = jnp.sum(grad_three, axis=0, keepdims=True)
    three_low = grad_three.astype(BFLOAT)
    three_low_ref[...] = three_low
    loads[2].wait()
    mixed_ref[...] = dot(three_low, kept_ref[2]).astype(BFLOAT)
    group = group_ref[...]
    masks = head_masks(heads, span)
    pieces = []
    for r in range(parts):
        part = slice(r * span, (r + 1) * span)
        keys, values = text_refs[r][:, :span], text_refs[r][:, span:]
        queries, mixed = query_ref[:, part], mixed_ref[:, part]
        grad_q = grad_k = grad_v = None
        for head in range(heads):
            some, grad = queries * masks[head], mixed * masks[head]
            scores = dot(keys, some, NT)
            peak = jnp.max(scores, axis=0, keepdims=True)
            powers = jnp.exp2((scores - peak) * (SCALE * LOG2E))
            probs = powers / jnp.sum(powers, axis=0, keepdims=True)
            grad_probs = dot(values, grad, NT)
            inner = jnp.sum(probs * grad_probs, axis=0, keepdims=True)
            grad_scores = (probs * (grad_probs - inner)).astype(BFLOAT)
            add_q = dot(grad_scores, keys * masks[head], TN)
            add_k = dot(grad_scores, some)
            add_v = dot(probs.astype(BFLOAT), grad)
            if head == 0:
                grad_q, grad_k, grad_v = add_q, add_k, add_v
            else:
                grad_q, grad_k, grad_v = grad_q + add_q, grad_k + add_k, grad_v + add_v
        text_grad_refs[r][:, :span] = (grad_k * SCALE).astype(BFLOAT)
        text_grad_refs[r][:, span:] = grad_v.astype(BFLOAT)
        normed, inverse = norm_heads(raw_ref[:, part], group)
        grad_q = grad_q * SCALE
        rows_ref[7:8, part] = jnp.sum(grad_q * normed, axis=0, keepdims=True)
        grad_q = grad_q * table_ref[4:5, part]
        low = (
            inverse * (grad_q - head_means(grad_q, group) - normed * head_means(grad_q * normed, group))
        ).astype(BFLOAT)
        pieces.append(low)
    raw_low_ref[...] = jnp.concatenate(pieces, axis=1)
    rows_ref[6:7, :] = jnp.sum(raw_low_ref[...].astype(FLOAT), axis=0, keepdims=True)
    loads[1].wait()
    into, gain_grad, bias_grad = norm_rows_back(two_ref[...], row(1), dot(raw_low_ref[...], kept_ref[1], NT))
    rows_ref[3:4, :], rows_ref[4:5, :] = gain_grad, bias_grad
    grad_two = grad_three_ref[...] + into
    grad_two_ref[...] = grad_two
    rows_ref[5:6, :] = jnp.sum(grad_two, axis=0, keepdims=True)
    two_low = grad_two.astype(BFLOAT)
    two_low_ref[...] = two_low
    loads[0].wait()
    mixed = dot(two_low, kept_ref[0])
    for r in range(parts):
        mixed_refs[r][...] = mixed[:, r * span : (r + 1) * span].astype(BFLOAT)


def middle_backward(grad, cot, three, two, raw, queries, table, text, group, weights, heads):
    rows, width = three.shape
    low = jax.ShapeDtypeStruct((rows, width), BFLOAT)
    vmem = pl.BlockSpec(memory_space=pltpu.VMEM)
    return pl.pallas_call(
        functools.partial(middle_backward_kernel, heads, len(text)),
        in_specs=[vmem] * (8 + len(text)) + [pl.BlockSpec(memory_space=pl.ANY)],
        out_shape=(
            low,
            low,
            low,
            jax.ShapeDtypeStruct((rows, width), FLOAT),
            jax.ShapeDtypeStruct((8, width), FLOAT),
            *[jax.ShapeDtypeStruct((rows, heads * HD), BFLOAT) for _ in text],
            *[jax.ShapeDtypeStruct(item.shape, BFLOAT) for item in text],
        ),
        out_specs=(vmem,) * (5 + 2 * len(text)),
        scratch_shapes=[
            pltpu.VMEM((3, width, width), BFLOAT),
            pltpu.VMEM((rows, width), FLOAT),
            pltpu.VMEM((rows, width), BFLOAT),
            pltpu.SemaphoreType.DMA((3,)),
        ],
        compiler_params=pltpu.CompilerParams(vmem_limit_bytes=56 * 2**20),
        cost_estimate=pl.CostEstimate(flops=33_000_000_000, bytes_accessed=28_000_000, transcendentals=1_300_000),
    )(*text, grad, cot, three, two, raw, queries, table, group, weights)


def on_device(
    latent, skip_in, text_tokens, time_embed, t_index, grid_pos, skip_weight, mod_weight, vectors, up_bias,
    qkv_weight, proj_weight, query_weight, text_weight, cross_weight, up_weight, down_weight, out_grad,
):
    split = lax.axis_size("tensor")
    shards = lax.axis_size("dp")
    place = lax.axis_index("tensor")
    me = lax.axis_index("dp")
    own_rows, width = latent.shape
    own_text = text_tokens.shape[0]
    part = mod_weight.shape[0]
    heads = HEADS // split
    span = heads * HD
    hidden = up_weight.shape[1]
    rows_ahead = vectors.shape[0]

    def others(r):
        return lax.rem(place - r + split, split)

    condition = time_embed
    half = width // 2
    frequencies = jnp.exp(-math.log(10000.0) * jnp.arange(half, dtype=FLOAT) / half)
    angles = t_index.astype(FLOAT)[:, None] * frequencies[None, :]
    condition = time_embed + jnp.concatenate([jnp.cos(angles), jnp.sin(angles)], axis=-1)
    silu_low = silu(condition).astype(BFLOAT)
    small = jnp.concatenate([vectors.reshape(-1), up_bias, silu_low.reshape(-1)])
    small_all = small_gather(small)
    cut_one, cut_two = rows_ahead * part, rows_ahead * part + up_bias.shape[0]
    table = (
        small_all[:, :cut_one].reshape(shards, rows_ahead, part).transpose(1, 0, 2).reshape(rows_ahead, width)
    ).astype(FLOAT)
    bias_all = small_all[:, cut_one:cut_two].reshape(-1).astype(FLOAT)
    silu_all = small_all[:, cut_two:]

    expand = jnp.asarray(expansion(heads), BFLOAT)
    deep = heads * DEEP
    packed_one = jnp.concatenate(
        [
            skip_weight[:part],
            skip_weight[part:],
            dot(qkv_weight.reshape(part, 3 * span), expand).astype(BFLOAT),
        ],
        axis=1,
    )
    all_one = lax.all_gather(packed_one, "dp", axis=0, tiled=True)
    w_skip = all_one[:, : 2 * width]
    w_qkv = all_one[:, 2 * width : 2 * width + 3 * deep]

    own_full = jnp.stack([proj_weight.T, query_weight, cross_weight.T, text_weight[:, 0], text_weight[:, 1]])
    full_blocks, text_blocks = [own_full], [text_tokens]
    for _ in range(split - 1):
        both = lax.optimization_barrier((full_blocks[-1], text_blocks[-1]))
        full_blocks.append(rot(both[0], 1))
        text_blocks.append(rot(both[1], 1))
    packed_two = jnp.concatenate(
        [full_blocks[r][index] for index in range(3) for r in range(split)]
        + [full_blocks[r][index] for r in range(split) for index in (3, 4)],
        axis=1,
    )


    text_length = own_text * split
    text_full = jnp.zeros((text_length, width), BFLOAT)
    for r in range(split):
        text_full = lax.dynamic_update_slice_in_dim(text_full, text_blocks[r], others(r) * own_text, 0)

    def head_slice(index):
        return lax.dynamic_slice_in_dim(table[index], place * span, span, 0)

    def relative(index):
        return jnp.concatenate(
            [lax.dynamic_slice_in_dim(table[index], others(r) * span, span, 0) for r in range(split)]
        )

    def spread(values):
        return lax.dynamic_update_slice_in_dim(jnp.zeros((width,), FLOAT), values.reshape(-1), place * span, 0)

    def absolute(values):
        result = jnp.zeros((width,), FLOAT)
        for r in range(split):
            result = lax.dynamic_update_slice_in_dim(
                result, values.reshape(-1)[r * span : (r + 1) * span], others(r) * span, 0
            )
        return result

    def deepen(values):
        turned = jnp.pad(values[:2].reshape(2, heads, 4, HD // 4), ((0, 0), (0, 0), (0, 0), (0, QUARTER - HD // 4)))
        plain = jnp.pad(values[2].reshape(heads, HD), ((0, 0), (0, DEEP - HD)))
        return jnp.concatenate([turned.reshape(-1), plain.reshape(-1)])

    def undeepen(values):
        turned = values[: 2 * deep].reshape(2, heads, 4, QUARTER)[..., : HD // 4].reshape(2, span)
        if values.shape[0] == 2 * deep:
            return turned
        return jnp.concatenate([turned, values[2 * deep :].reshape(heads, DEEP)[:, :HD].reshape(1, span)])

    quarter = HD // 4
    rate = np.zeros((QUARTER, 1), np.float32)
    rate[:quarter, 0] = 10000.0 ** (-np.arange(quarter, dtype=np.float64) / quarter)
    grid_rel = jnp.concatenate(
        [lax.dynamic_slice_in_dim(grid_pos, others(r) * own_rows, own_rows, 1) for r in range(split)], axis=1
    ).astype(FLOAT)
    turn = grid_rel[:, None, :] * rate[None]
    turns = jnp.stack([jnp.cos(turn[0]), jnp.sin(turn[0]), jnp.cos(turn[1]), jnp.sin(turn[1])])

    silu_mine = after(lax.dynamic_slice_in_dim(silu_all, me * part, part, 1), full_blocks[1])
    shift_terms = dot(silu_mine, mod_weight)
    shift = jnp.sum(lax.all_to_all(shift_terms, "dp", 0, 0, tiled=True), axis=0, keepdims=True) + table[5]

    joined = jnp.concatenate([latent.astype(FLOAT), skip_in.astype(FLOAT)], axis=-1)
    joined_gain = jnp.concatenate([table[0], table[1]])
    joined_bias = jnp.concatenate([table[2], table[3]])
    normed_low = layer_norm(joined, joined_gain, joined_bias).astype(BFLOAT)
    normed_perm = normed_low.reshape(own_rows, shards, 2, part).transpose(0, 2, 1, 3).reshape(own_rows, 2 * width)
    stream_one = (
        dot(normed_perm[:, :width], w_skip[:, :width]) + dot(normed_perm[:, width:], w_skip[:, width:]) + table[4]
    )
    packed_two = after(packed_two, normed_perm, shift, turns)
    all_two = lax.all_gather(packed_two, "dp", axis=0, tiled=True)
    packed_three = jnp.concatenate([up_weight, down_weight.T], axis=1)
    all_three = lax.all_gather(packed_three, "dp", axis=0, tiled=True)
    w_up, w_down_t = all_three[:, :hidden], all_three[:, hidden:]

    attn_low = (layer_norm(stream_one, table[6], table[7]) + shift).astype(BFLOAT)
    attn_blocks = ring_gather(attn_low)
    cot_blocks = [out_grad, rot(after(out_grad, attn_blocks[-1]), 1)]
    qkv_bias = deepen(jnp.stack([head_slice(8), head_slice(9), head_slice(10)]))[:, None]
    raws = [dot(w_qkv, block, ((0,), (1,))) + qkv_bias for block in attn_blocks]
    zero_slice = jnp.zeros((span,), FLOAT)
    gains = deepen(jnp.stack([head_slice(12), head_slice(13), zero_slice]))[: 2 * deep, None]
    length = own_rows * split
    block = min(512, length)
    kept = attend_forward(raws, turns, gains, heads, block)
    mixed, kept = kept[:split], kept[split:]
    *mixed, cot_blocks[1] = lax.optimization_barrier((*mixed, cot_blocks[1]))

    def blocks_of(values, rows):
        return [values[r * rows : (r + 1) * rows] for r in range(split)]

    lane_head = np.arange(span) // HD
    group = jnp.asarray((lane_head[:, None] == lane_head[None, :]).astype(np.float32), BFLOAT)
    text_bias = jnp.stack([relative(17).reshape(split, span), relative(18).reshape(split, span)], axis=1)
    text_raw, *text_rel = text_forward(
        text_full, all_two, 3 * width, text_bias.reshape(split, 2 * span), relative(21).reshape(split, span), group
    )
    mixed = exchange(mixed)
    cot_blocks[-1], mixed[-1], text_rel[0] = lax.optimization_barrier((cot_blocks[-1], mixed[-1], text_rel[0]))
    cot_blocks.append(rot(cot_blocks[-1], 1))
    middle_table = jnp.stack(
        [table[11], table[14], table[15], relative(16), relative(20), table[19], table[22], table[23]]
    )
    stream_two, cross_raw, stream_three, mixed_own, cross_low, cross_queries, cross_mixed, mlp_low = middle_forward(
        mixed, stream_one, middle_table, text_rel, group, all_two, heads
    )
    mlp_low, cot_blocks[-1] = lax.optimization_barrier((mlp_low, cot_blocks[-1]))
    while len(cot_blocks) < split:
        cot_blocks.append(rot(cot_blocks[-1], 1))
    mlp_blocks = ring_gather(mlp_low)
    hidden_bias = lax.dynamic_slice_in_dim(bias_all, place * hidden, hidden, 0)

    hidden_lows, pre_lows, out_parts, back_parts = [], [], [], []
    for r in range(split):
        hidden_pre = dot(mlp_blocks[r], w_up) + hidden_bias
        activated, pull = jax.vjp(gelu, hidden_pre)
        hidden_lows.append(activated.astype(BFLOAT))
        pre_lows.append(pull(dot(cot_blocks[r], w_down_t))[0].astype(BFLOAT))
        back_parts.append(dot(pre_lows[r], w_up, NT))
        out_parts.append(dot(hidden_lows[r], w_down_t, NT))
    grad_mlp_in = ring_scatter(back_parts)

    rows_grad = {}
    grad_bias = sum(jnp.sum(item, axis=0, dtype=FLOAT) for item in pre_lows)
    grads_one = pack_grad(None, mlp_blocks, pre_lows, 2 * hidden, 0, 512)
    grads_one = pack_grad(grads_one, cot_blocks, hidden_lows, 2 * hidden, hidden, 512)
    grads_one, grad_mlp_in, *out_parts = lax.optimization_barrier((grads_one, grad_mlp_in, *out_parts))
    out_hop = rot(out_parts[1].astype(BFLOAT), 1)
    summed_one = lax.psum_scatter(grads_one, "dp", scatter_dimension=0, tiled=True).astype(FLOAT)
    cot_here = out_grad.astype(FLOAT)
    rows_grad[24] = jnp.sum(cot_here, axis=0)
    three_low, cq_low, two_low, grad_two, middle_rows, *pieces = middle_backward(
        grad_mlp_in, out_grad, stream_three, stream_two, cross_raw, cross_queries, middle_table, text_rel, group,
        all_two, heads,
    )
    grad_mixed, text_terms = pieces[:split], pieces[split:]
    for index, number in enumerate((22, 23, 19, 14, 15, 11)):
        rows_grad[number] = middle_rows[index]
    rows_grad[16], rows_grad[20] = absolute(middle_rows[6]), absolute(middle_rows[7])
    out_hop, *grad_mixed = lax.optimization_barrier((out_hop, *grad_mixed))
    grad_mixed = exchange(grad_mixed)
    lanes_two = 3 * width
    grads_two = pack_grad(None, [two_low], [mixed_own], lanes_two, 0, width)
    grads_two = pack_grad(grads_two, [cross_low], [cq_low], lanes_two, width, width)
    grads_two = pack_grad(grads_two, [three_low], [cross_mixed], lanes_two, 2 * width, width)
    grads_two, *grad_mixed = lax.optimization_barrier((grads_two, *grad_mixed))
    summed_two = lax.psum_scatter(grads_two, "dp", scatter_dimension=0, tiled=True)
    text_terms[1:] = lax.optimization_barrier((*text_terms[1:], grad_mixed[-1]))[:-1]
    text_got = [rot(text_terms[r], split - r) for r in range(1, split)]
    grad_raw, gain_grads, raw_sums = attend_backward(
        raws, turns, gains, kept, grad_mixed, heads, block
    )
    grad_raw, summed_one = lax.optimization_barrier((grad_raw, summed_one))
    text_got[0], grad_raw = lax.optimization_barrier((text_got[0], grad_raw))
    ckv_low, text_rows = text_norm_back([text_terms[0], *text_got], text_raw, head_slice(21)[None], group)
    rows_grad[21] = spread(text_rows[1, :span])
    rows_grad[17], rows_grad[18] = spread(text_rows[0, :span]), spread(text_rows[0, span:])

    gain_grads = undeepen(jnp.sum(gain_grads, axis=1))
    raw_sums = undeepen(jnp.sum(raw_sums, axis=1))
    rows_grad[12], rows_grad[13] = spread(gain_grads[0]), spread(gain_grads[1])
    rows_grad[8], rows_grad[9], rows_grad[10] = spread(raw_sums[0]), spread(raw_sums[1]), spread(raw_sums[2])
    qkv_lanes = 3 * deep
    text_lanes = pl.cdiv(2 * span, LANES) * LANES
    shared = 2 * width + LANES
    qkv_start = pl.cdiv(shared, deep) * deep
    text_start = qkv_start + qkv_lanes
    lanes_three = text_start + text_lanes
    bias_part = up_bias.shape[0]
    bias_cols = pl.cdiv(bias_part, part)
    bias_spread = lax.dynamic_update_slice_in_dim(jnp.zeros(bias_all.shape, FLOAT), grad_bias, place * hidden, 0)
    zero_row = jnp.zeros((width,), FLOAT)
    table_grad = jnp.stack([rows_grad.get(index, zero_row) for index in range(rows_ahead)], axis=1)
    bias_grad = jnp.pad(bias_spread.reshape(shards, bias_part), ((0, 0), (0, bias_cols * part - bias_part)))
    bias_grad = bias_grad.reshape(shards, bias_cols, part).transpose(0, 2, 1).reshape(width, bias_cols)
    small_grads = jnp.concatenate([table_grad, bias_grad], axis=1).astype(BFLOAT)
    small_grads = jnp.pad(small_grads, ((0, 0), (0, qkv_start - 2 * width - small_grads.shape[1])))

    grad_attn_in, shift_part, grads_three = ring_sum(
        grad_raw, attn_blocks, text_full, ckv_low, all_one, 2 * width, lanes_three, (qkv_start, text_start), split
    )
    grads_three = lax.dynamic_update_slice(grads_three, small_grads, (0, 2 * width))
    grads_three, one_low, late_rows = skip_grads(
        grads_three, grad_attn_in, grad_two, stream_one, table[6:7], normed_perm
    )
    grads_three, summed_two, one_low = lax.optimization_barrier((grads_three, summed_two, one_low))
    summed_three = lax.psum_scatter(grads_three, "dp", scatter_dimension=0, tiled=True)
    latent_grad, skip_grad, late, full_sum, text_grad, block_out = side_sums(
        one_low, late_rows, shift_part, jnp.concatenate([table[:2], table[24:25]]), latent, skip_in, stream_three,
        out_hop, summed_two, ckv_low, all_one, all_two, 3 * width, [out_parts[0], *out_parts[2:]], shards, split,
    )
    shift_grads = late[8 : 8 + shards]
    late = lax.dynamic_slice_in_dim(late[:8], me * part, part, 1)
    silu_terms = lax.dot_general(
        shift_grads, mod_weight.astype(FLOAT), ((NT), ((), ())), precision=HIGHEST, preferred_element_type=FLOAT
    )
    summed_three = after(summed_three, silu_terms, full_sum, text_grad, summed_one)
    mod_grad = lax.dot_general(
        silu_mine.astype(FLOAT), shift_grads, ((TN), ((), ())), precision=HIGHEST, preferred_element_type=FLOAT
    )
    into_silu = lax.all_to_all(silu_terms, "dp", 0, 0, tiled=True).reshape(1, width)
    time_full = jax.vjp(silu, condition)[1](into_silu)[0]
    time_grad = lax.dynamic_slice_in_dim(time_full, place * (width // split), width // split, 1)

    qkv_part = summed_three[:, qkv_start:text_start]
    text_part = summed_three[:, text_start : text_start + 2 * span]
    skip_weight_grad, small_sum = spread_sum(summed_three[:, :shared], width, split)
    vectors_grad = jnp.concatenate([late[:5], late[7:8], late[5:7], small_sum[:, 8:rows_ahead].T])
    bias_grad = small_sum[:, rows_ahead : rows_ahead + bias_cols].T.reshape(-1)[:bias_part]
    qkv_sum = dot(qkv_part, expand, NT).reshape(part, 3, span)
    text_sum_grad = text_part.astype(FLOAT).reshape(part, 2, span)

    return (
        block_out,
        latent_grad,
        skip_grad,
        text_grad,
        time_grad,
        skip_weight_grad,
        mod_grad,
        vectors_grad,
        bias_grad,
        qkv_sum,
        full_sum[:, :span].T,
        full_sum[:, span : 2 * span],
        text_sum_grad,
        full_sum[:, 2 * span :].T,
        summed_one[:, :hidden],
        summed_one[:, hidden:].T,
    )


def solution(mesh):
    tokens = P(("dp", "tensor"), None)
    placed = (
        tokens,
        tokens,
        tokens,
        P("dp", None),
        P("dp"),
        P(None, "dp"),
        P("dp", None),
        P("dp", None),
        P(None, "dp"),
        P("dp"),
        P("dp", None, "tensor"),
        P("tensor", "dp"),
        P("dp", "tensor"),
        P("dp", None, "tensor"),
        P("tensor", "dp"),
        P("dp", "tensor"),
        P("tensor", "dp"),
        tokens,
    )
    return jax.shard_map(
        on_device,
        mesh=mesh,
        in_specs=placed,
        out_specs=(
            tokens,
            tokens,
            tokens,
            tokens,
            P("dp", "tensor"),
            P("dp", None),
            P("dp", None),
            P(None, "dp"),
            P("dp"),
            P("dp", None, "tensor"),
            P("tensor", "dp"),
            P("dp", "tensor"),
            P("dp", None, "tensor"),
            P("tensor", "dp"),
            P("dp", "tensor"),
            P("tensor", "dp"),
        ),
        check_vma=False,
    )
```

```python
import functools
import math

import jax
import jax.numpy as jnp
import numpy as np
from jax import lax
from jax.experimental import pallas as pl
from jax.experimental.pallas import tpu as pltpu
from jax.sharding import PartitionSpec as P

HEADS = 16
HD = 88
LANES = 128
EPSILON = 1e-06
HIGHEST = lax.Precision.HIGHEST
FLOAT = jnp.float32
BFLOAT = jnp.bfloat16
LOG2E = 1.4426950408889634
SCALE = 1.0 / math.sqrt(HD)


def layer_norm(values, norm_gain, norm_bias):
    centred = values - jnp.mean(values, axis=-1, keepdims=True)
    variance = jnp.mean(centred * centred, axis=-1, keepdims=True)
    return centred * lax.rsqrt(variance + EPSILON) * norm_gain + norm_bias


def head_norm(values, norm_gain):
    centred = values - jnp.mean(values, axis=-1, keepdims=True)
    variance = jnp.mean(centred * centred, axis=-1, keepdims=True)
    return centred * lax.rsqrt(variance + EPSILON) * norm_gain


def silu(values):
    return values / (1.0 + jnp.exp(-values))


def gelu(values):
    inner = math.sqrt(2.0 / math.pi) * (values + 0.044715 * values * values * values)
    return 0.5 * values * (1.0 + jnp.tanh(inner))


def dot(left, right, contract=((1,), (0,))):
    return lax.dot_general(left, right, (contract, ((), ())), preferred_element_type=FLOAT)


NT = ((1,), (1,))
TN = ((0,), (0,))


def rot(values, step):
    count = lax.axis_size("tensor")
    return lax.ppermute(values, "tensor", [(i, (i + step) % count) for i in range(count)])


def ring_gather(own):
    blocks = [own]
    for _ in range(lax.axis_size("tensor") - 1):
        blocks.append(rot(blocks[-1], 1))
    return blocks


def ring_scatter(parts):
    running = parts[1].astype(BFLOAT)
    for part in parts[2:]:
        running = (rot(running, 1).astype(FLOAT) + part.astype(FLOAT)).astype(BFLOAT)
    return rot(running, 1).astype(FLOAT) + parts[0].astype(FLOAT)


def direct_gather(own):
    return [own] + [rot(own, r) for r in range(1, lax.axis_size("tensor"))]


def direct_scatter(parts):
    count = len(parts)
    total = parts[0].astype(FLOAT)
    for r in range(1, count):
        total = total + rot(parts[r], count - r).astype(FLOAT)
    return total


def exchange(parts):
    count = len(parts)
    return [parts[0]] + [rot(parts[count - r], r) for r in range(1, count)]


def after(values, *earlier):
    return lax.optimization_barrier((values, *earlier))[0]


def small_gather(own):
    have = own[None]
    me = lax.axis_index("dp")
    count = lax.axis_size("dp")
    step = 1
    while step < count:
        other = lax.ppermute(have, "dp", [(i, i ^ step) for i in range(count)])
        upper = (me // step) % 2 == 1
        have = jnp.where(upper, jnp.concatenate([other, have]), jnp.concatenate([have, other]))
        step *= 2
    return have


def tensor_sum(values):
    total = values.astype(FLOAT)
    for step in range(1, lax.axis_size("tensor")):
        total = total + rot(values, step).astype(FLOAT)
    return total


def grad_kernel(lefts, rights, turned, *refs):
    left_refs, right_refs = refs[:lefts], refs[lefts : lefts + rights]
    out_ref, kept_ref = refs[-2], refs[-1]
    rows = left_refs[0].shape[0]

    @pl.when(pl.program_id(0) == 0)
    def _():
        for r in range(lefts):
            kept_ref[:, r * rows : (r + 1) * rows] = left_refs[r][...].T

    total = None
    for r in range(rights):
        span = lefts // rights * rows
        left = kept_ref[:, r * span : (r + 1) * span]
        term = dot(left, right_refs[r][...], NT if turned else ((1,), (0,)))
        total = term if total is None else total + term
    out_ref[...] = total.astype(BFLOAT)


def pack_grad(packed, lefts, rights, lanes, start, tile, turned=False):
    rows, height = lefts[0].shape
    deep = rights[0].shape[1 if turned else 0]
    wide = rights[0].shape[0 if turned else 1]
    first = start // tile
    in_specs = [pl.BlockSpec((rows, height), lambda i: (0, 0))] * len(lefts)
    if turned:
        in_specs += [pl.BlockSpec((tile, deep), lambda i: (i, 0))] * len(rights)
    else:
        in_specs += [pl.BlockSpec((deep, tile), lambda i: (0, i))] * len(rights)
    operands = [*lefts, *rights]
    if packed is not None:
        in_specs.append(pl.BlockSpec(memory_space=pl.ANY))
        operands.append(packed)
    tokens = rows * len(lefts)
    return pl.pallas_call(
        functools.partial(grad_kernel, len(lefts), len(rights), turned),
        grid=(pl.cdiv(wide, tile),),
        in_specs=in_specs,
        out_specs=pl.BlockSpec((height, tile), lambda i: (0, first + i)),
        out_shape=jax.ShapeDtypeStruct((height, lanes), BFLOAT),
        scratch_shapes=[pltpu.VMEM((height, tokens), BFLOAT)],
        input_output_aliases={} if packed is None else {len(operands) - 1: 0},
        compiler_params=pltpu.CompilerParams(vmem_limit_bytes=40 * 2**20),
        cost_estimate=pl.CostEstimate(
            flops=4 * tokens * height * wide,
            bytes_accessed=2 * (tokens * height + tokens * wide + height * wide),
            transcendentals=0,
        ),
    )(*operands)


def flipped(index, bit):
    return index + (1 - 2 * lax.rem(lax.div(index, 2**bit), 2)) * 2**bit


def to_device(source, target, send, recv, where):
    return pltpu.make_async_remote_copy(
        src_ref=source,
        dst_ref=target,
        send_sem=send,
        recv_sem=recv,
        device_id=where,
        device_id_type=pl.DeviceIdType.MESH,
    )


def neighbours(place, split):
    return lax.rem(place + 1, split), lax.rem(place + split - 1, split)


def ring_kernel(split, start, places, *refs):
    raw_ref, left_refs, refs = refs[0], refs[1 : 1 + split], refs[1 + split :]
    text_ref, ckv_ref, packed_ref, sum_out, shift_out, grads_ref = refs[:6]
    weights_ref, turned, qkv_grad, text_grad, sent, got, load_sem, sems = refs[6:]
    loads = [
        pltpu.make_async_copy(packed_ref.at[:, start : start + weights_ref.shape[1]], weights_ref, load_sem.at[0]),
        pltpu.make_async_copy(
            qkv_grad, grads_ref.at[:, places[0] : places[0] + qkv_grad.shape[1]], load_sem.at[1]
        ),
        pltpu.make_async_copy(
            text_grad, grads_ref.at[:, places[1] : places[1] + text_grad.shape[1]], load_sem.at[2]
        ),
    ]
    loads[0].start()
    place = lax.axis_index("tensor")
    right, left = neighbours(place, split)
    barrier = pltpu.get_barrier_semaphore()
    for where in (left, right):
        pl.semaphore_signal(barrier, inc=1, device_id={"tensor": where}, device_id_type=pl.DeviceIdType.MESH)
    rows = sum_out.shape[0]

    def term(r):
        return dot(weights_ref[...], raw_ref[:, r * rows : (r + 1) * rows]).T

    def hop(step):
        return to_device(sent.at[step], got.at[step], sems.at[0, step], sems.at[1, step], {"tensor": right})

    def qkv_lanes(some):
        lanes = qkv_grad.shape[1] // 3
        for i in some:
            part = slice(i * lanes, (i + 1) * lanes)
            qkv_grad[:, part] = dot(turned[...], raw_ref[part, :], NT).astype(BFLOAT)

    def beside(step):
        if step == 1:
            for r in range(split):
                turned[:, r * rows : (r + 1) * rows] = left_refs[r][...].T
            qkv_lanes((0,))
        elif step == 2:
            qkv_lanes((1, 2))
            loads[1].start()
        elif step == 3:
            wide = ckv_ref.shape[1]
            text_grad[:, :wide] = dot(text_ref[...].T, ckv_ref[...]).astype(BFLOAT)
            text_grad[:, wide:] = jnp.zeros((text_grad.shape[0], text_grad.shape[1] - wide), BFLOAT)
            loads[2].start()

    loads[0].wait()
    part = term(1)
    total = jnp.sum(part, axis=0, keepdims=True)
    sent[0] = part.astype(BFLOAT)
    pl.semaphore_wait(barrier, 2)
    hop(0).start()
    for step in range(1, split):
        part = term((step + 1) % split)
        total = total + jnp.sum(part, axis=0, keepdims=True)
        beside(step)
        hop(step - 1).wait_recv()
        part = part + got[step - 1].astype(FLOAT)
        if step + 1 < split:
            sent[step] = part.astype(BFLOAT)
            hop(step).start()
        else:
            sum_out[...] = part
    shift_out[...] = jnp.broadcast_to(total, shift_out.shape)
    loads[1].wait()
    loads[2].wait()
    for step in range(split - 1):
        hop(step).wait_send()


def ring_sum(raw, lefts, text, ckv, packed, start, lanes, places, split):
    rows, width = raw.shape[1] // split, packed.shape[0]
    vmem = pl.BlockSpec(memory_space=pltpu.VMEM)
    anywhere = pl.BlockSpec(memory_space=pl.ANY)
    return pl.pallas_call(
        functools.partial(ring_kernel, split, start, places),
        in_specs=[vmem] * (3 + split) + [anywhere],
        out_specs=(vmem, vmem, anywhere),
        out_shape=(
            jax.ShapeDtypeStruct((rows, width), FLOAT),
            jax.ShapeDtypeStruct((8, width), FLOAT),
            jax.ShapeDtypeStruct((width, lanes), BFLOAT),
        ),
        scratch_shapes=[
            pltpu.VMEM((width, raw.shape[0]), BFLOAT),
            pltpu.VMEM((width, raw.shape[1]), BFLOAT),
            pltpu.VMEM((width, raw.shape[0]), BFLOAT),
            pltpu.VMEM((width, lanes - places[1]), BFLOAT),
            pltpu.VMEM((split - 1, rows, width), BFLOAT),
            pltpu.VMEM((split - 1, rows, width), BFLOAT),
            pltpu.SemaphoreType.DMA((3,)),
            pltpu.SemaphoreType.DMA((2, split - 1)),
        ],
        compiler_params=pltpu.CompilerParams(
            vmem_limit_bytes=48 * 2**20, collective_id=1, has_side_effects=True
        ),
        cost_estimate=pl.CostEstimate(flops=60_000_000_000, bytes_accessed=10_000_000, transcendentals=0),
    )(raw, *lefts, text, ckv, packed)


def skip_kernel(
    grad_ref, two_ref, one_ref, gain_ref, left_ref, packed_ref, out_ref, low_ref, rows_ref
):
    @pl.when(pl.program_id(0) == 0)
    def _():
        into, gain_grad, bias_grad = norm_rows_back(one_ref[...], gain_ref[...], grad_ref[...])
        grad_one = two_ref[...] + into
        low_ref[...] = grad_one.astype(BFLOAT)
        rows_ref[...] = jnp.concatenate(
            [gain_grad, bias_grad, jnp.sum(grad_one, axis=0, keepdims=True), jnp.zeros((5, grad_one.shape[1]), FLOAT)],
            axis=0,
        )

    out_ref[...] = dot(left_ref[...].T, low_ref[...]).astype(BFLOAT)


def skip_grads(packed, grad, two, one, gain, left):
    rows, width = one.shape
    fixed = pl.BlockSpec((rows, width), lambda i: (0, 0))
    return pl.pallas_call(
        skip_kernel,
        grid=(left.shape[1] // width,),
        in_specs=[fixed] * 3
        + [
            pl.BlockSpec((1, width), lambda i: (0, 0)),
            pl.BlockSpec((rows, width), lambda i: (0, i)),
            pl.BlockSpec(memory_space=pl.ANY),
        ],
        out_specs=(
            pl.BlockSpec((width, width), lambda i: (0, i)),
            pl.BlockSpec((rows, width), lambda i: (0, 0)),
            pl.BlockSpec((8, width), lambda i: (0, 0)),
        ),
        out_shape=(
            jax.ShapeDtypeStruct(packed.shape, BFLOAT),
            jax.ShapeDtypeStruct((rows, width), BFLOAT),
            jax.ShapeDtypeStruct((8, width), FLOAT),
        ),
        input_output_aliases={5: 0},
        compiler_params=pltpu.CompilerParams(vmem_limit_bytes=40 * 2**20),
        cost_estimate=pl.CostEstimate(flops=10_000_000_000, bytes_accessed=16_000_000, transcendentals=0),
    )(grad, two, one, gain, left, packed)


def side_kernel(shards, split, hops, text_start, *refs):
    low_ref, late_ref, shift_ref, table_ref, latent_ref, skip_ref, base_ref, hop_ref, summed_ref, ckv_ref = refs[:10]
    weights_ref, text_packed_ref, refs = refs[10], refs[11], refs[12:]
    out_refs, refs = refs[: hops + 1], refs[hops + 1 :]
    latent_out, skip_out, table_out, full_out, text_out, block_out = refs[:6]
    weights, text_weights, full_refs, text_refs, full_got, text_got, hop_sent, hop_got, table_sent, table_got = refs[6:16]
    load_sem, side_sems, hop_sems, table_sems = refs[16:]
    me, place = lax.axis_index("dp"), lax.axis_index("tensor")
    count = shards.bit_length() - 1
    width = latent_out.shape[1]
    part = width // shards
    right, _ = neighbours(place, split)

    loads = [
        pltpu.make_async_copy(weights_ref.at[:, half * width : (half + 1) * width], weights, load_sem.at[half])
        for half in range(2)
    ]
    text_stop = text_start + text_weights.shape[1]
    loads.append(pltpu.make_async_copy(text_packed_ref.at[:, text_start:text_stop], text_weights, load_sem.at[2]))
    loads[0].start()
    loads[2].start()
    barrier = pltpu.get_barrier_semaphore()
    for bit in range(count):
        pl.semaphore_signal(barrier, inc=1, device_id={"dp": flipped(me, bit)}, device_id_type=pl.DeviceIdType.MESH)
    for step in range(1, split):
        pl.semaphore_signal(
            barrier, inc=1, device_id={"tensor": lax.rem(place + step, split)}, device_id_type=pl.DeviceIdType.MESH
        )

    def side(step, i):
        return to_device(
            (full_refs, text_refs)[i].at[step],
            (full_got, text_got)[i].at[step - 1],
            side_sems.at[i, 0, step - 1],
            side_sems.at[i, 1, step - 1],
            {"tensor": lax.rem(place + split - step, split)},
        )

    def hop(step):
        return to_device(
            hop_sent.at[step], hop_got.at[step], hop_sems.at[0, step], hop_sems.at[1, step], {"tensor": right}
        )

    hop_sent[0] = (hop_ref[...].astype(FLOAT) + out_refs[1][...]).astype(BFLOAT)
    pl.semaphore_wait(barrier, count + split - 1)
    hop(0).start()
    low = low_ref[...]
    grads = []
    for half in range(2):
        loads[half].wait()
        grads.append(dot(low, weights[...], NT))
        if half == 0:
            loads[1].start()
    ordered = [grads[half][:, shard * part : (shard + 1) * part] for shard in range(shards) for half in range(2)]
    grads = [jnp.concatenate(ordered[:shards], axis=1), jnp.concatenate(ordered[shards:], axis=1)]
    values = [latent_ref[...].astype(FLOAT), skip_ref[...].astype(FLOAT)]

    def mean_of(one, two):
        return (jnp.sum(one, axis=-1, keepdims=True) + jnp.sum(two, axis=-1, keepdims=True)) * (0.5 / width)

    mean = mean_of(*values)
    centred = [item - mean for item in values]
    inverse = lax.rsqrt(mean_of(*[item * item for item in centred]) + EPSILON)
    normed = [item * inverse for item in centred]
    gain_rows = [jnp.sum(grads[i] * normed[i], axis=0, keepdims=True) for i in range(2)]
    bias_rows = [jnp.sum(grads[i], axis=0, keepdims=True) for i in range(2)]
    scaled = [grads[i] * table_ref[i : i + 1, :] for i in range(2)]
    mean = mean_of(*scaled)
    slope = mean_of(*[scaled[i] * normed[i] for i in range(2)])
    latent_out[...] = inverse * (scaled[0] - mean - normed[0] * slope)
    skip_out[...] = inverse * (scaled[1] - mean - normed[1] * slope)

    spare = table_out.shape[0] - 8
    table_sent[0] = jnp.concatenate(
        [
            *gain_rows,
            *bias_rows,
            late_ref[2:3, :],
            late_ref[0:2, :],
            shift_ref[0:1, :],
            jnp.zeros((spare, width), FLOAT),
        ],
        axis=0,
    )
    bits = split.bit_length() - 1
    shares = table_sent.shape[0]

    def share(step):
        where = {"tensor": flipped(place, step)} if step < bits else {"dp": flipped(me, step - bits)}
        return to_device(
            table_sent.at[step], table_got.at[step], table_sems.at[0, step], table_sems.at[1, step], where
        )

    def open_hop(step):
        hop(step - 1).wait_recv()
        hop_sent[step] = (hop_got[step - 1].astype(FLOAT) + out_refs[step + 1][...]).astype(BFLOAT)
        hop(step).start()

    def pass_on(step):
        share(step).wait_recv()
        total = table_sent[step] + table_got[step]
        if step + 1 == bits:
            at = lax.broadcasted_iota(jnp.int32, (8 + spare, 1), 0)
            total = jnp.where(at == 8 + me, total[7:8, :], total)
        if step + 1 < shares:
            table_sent[step + 1] = total
            share(step + 1).start()
        else:
            table_out[...] = total
    share(0).start()
    span = full_out.shape[1] // 3
    for r in range(split):
        full_refs[r] = jnp.concatenate(
            [summed_ref[:, k * width + r * span : k * width + (r + 1) * span] for k in range(3)], axis=1
        )
    for step in range(bits):
        pass_on(step)
    for step in range(1, split):
        side(step, 0).start()
    loads[2].wait()
    back = dot(ckv_ref[...], text_weights[:, : ckv_ref.shape[1]], NT).astype(BFLOAT)
    own_text = text_out.shape[0]
    for r in range(split):
        text_refs[lax.rem(place + split - r, split)] = back[r * own_text : (r + 1) * own_text]
    for step in range(1, split):
        side(step, 1).start()
    for step in range(1, hops):
        open_hop(step)
    for step in range(bits, shares):
        pass_on(step)
    for i, (terms, result) in enumerate(((full_refs, full_out), (text_refs, text_out))):
        if i == 1:
            hop(hops - 1).wait_recv()
            last = hop_got[hops - 1].astype(FLOAT) + out_refs[0][...]
            block_out[...] = (base_ref[...] + table_ref[2:3, :] + last).astype(BFLOAT)
        total = terms[0].astype(FLOAT)
        for step in range(1, split):
            side(step, i).wait_recv()
            total = total + (full_got, text_got)[i][step - 1].astype(FLOAT)
        result[...] = total
    for step in range(hops):
        hop(step).wait_send()
    for step in range(shares):
        share(step).wait_send()
    for step in range(1, split):
        for i in range(2):
            side(step, i).wait_send()


def side_sums(
    low, late, shift, table, latent, skip_in, base, hop, summed, ckv, weights, text_packed, text_start, out, shards, split
):
    rows, width = low.shape
    spare = pl.cdiv(shards, 8) * 8
    shares = shards.bit_length() - 1 + split.bit_length() - 1
    vmem = pl.BlockSpec(memory_space=pltpu.VMEM)
    wide = jax.ShapeDtypeStruct((rows, width), FLOAT)
    hops = len(out) - 1
    full, text = (summed.shape[0], summed.shape[1] // split), (ckv.shape[0] // split, width)
    return pl.pallas_call(
        functools.partial(side_kernel, shards, split, hops, text_start),
        in_specs=[vmem] * 10 + [pl.BlockSpec(memory_space=pl.ANY)] * 2 + [vmem] * len(out),
        out_specs=(vmem,) * 6,
        out_shape=(
            wide,
            wide,
            jax.ShapeDtypeStruct((8 + spare, width), FLOAT),
            jax.ShapeDtypeStruct(full, FLOAT),
            jax.ShapeDtypeStruct(text, FLOAT),
            jax.ShapeDtypeStruct((rows, width), BFLOAT),
        ),
        scratch_shapes=[
            pltpu.VMEM((width, width), BFLOAT),
            pltpu.VMEM((width, pl.cdiv(ckv.shape[1], LANES) * LANES), BFLOAT),
            pltpu.VMEM((split, *full), BFLOAT),
            pltpu.VMEM((split, *text), BFLOAT),
            pltpu.VMEM((split - 1, *full), BFLOAT),
            pltpu.VMEM((split - 1, *text), BFLOAT),
            pltpu.VMEM((hops, rows, width), BFLOAT),
            pltpu.VMEM((hops, rows, width), BFLOAT),
            pltpu.VMEM((shares, 8 + spare, width), FLOAT),
            pltpu.VMEM((shares, 8 + spare, width), FLOAT),
            pltpu.SemaphoreType.DMA((3,)),
            pltpu.SemaphoreType.DMA((2, 2, split - 1)),
            pltpu.SemaphoreType.DMA((2, hops)),
            pltpu.SemaphoreType.DMA((2, shares)),
        ],
        compiler_params=pltpu.CompilerParams(
            vmem_limit_bytes=56 * 2**20, collective_id=0, has_side_effects=True
        ),
        cost_estimate=pl.CostEstimate(flops=90_000_000_000, bytes_accessed=30_000_000, transcendentals=0),
    )(low, late, shift, table, latent, skip_in, base, hop, summed, ckv, weights, text_packed, *out)


def spread_kernel(split, starts, in_ref, skip_out, small_out, piece_sent, piece_got, pieces, whole, sems):
    place = lax.axis_index("tensor")
    part, width = skip_out.shape[0] // 2, skip_out.shape[1]
    wide = piece_sent.shape[2]
    barrier = pltpu.get_barrier_semaphore()
    for step in range(1, split):
        pl.semaphore_signal(
            barrier, inc=1, device_id={"tensor": lax.rem(place + step, split)}, device_id_type=pl.DeviceIdType.MESH
        )
    for i in range(split):
        piece_sent[i] = in_ref[:, starts[i] : starts[i] + wide]
    pl.semaphore_wait(barrier, split - 1)

    def scatter(step):
        where = lax.rem(place + step, split)
        return to_device(
            piece_sent.at[where], piece_got.at[step - 1], sems.at[0, step - 1], sems.at[1, step - 1], {"tensor": where}
        )

    def gather(step):
        return to_device(
            pieces.at[place], pieces.at[place], sems.at[2, step - 1], sems.at[3, step - 1],
            {"tensor": lax.rem(place + step, split)},
        )

    for step in range(1, split):
        scatter(step).start()
    total = piece_sent[place].astype(FLOAT)
    for step in range(1, split):
        scatter(step).wait_recv()
        total = total + piece_got[step - 1].astype(FLOAT)
    pieces[place] = total.astype(BFLOAT)
    for step in range(1, split):
        gather(step).start()
    for step in range(1, split):
        gather(step).wait_recv()
    for i in range(split):
        stop = starts[i + 1] if i + 1 < split else whole.shape[1]
        whole[:, starts[i] : stop] = pieces[i][:, : stop - starts[i]].astype(FLOAT)
    skip_out[:part] = whole[:, :width]
    skip_out[part:] = whole[:, width : 2 * width]
    small_out[...] = whole[:, 2 * width :]
    for step in range(1, split):
        scatter(step).wait_send()
        gather(step).wait_send()


def spread_sum(values, width, split):
    part, lanes = values.shape
    wide = pl.cdiv(lanes // LANES, split) * LANES
    starts = [min(i * wide, lanes - wide) for i in range(split)]
    vmem = pl.BlockSpec(memory_space=pltpu.VMEM)
    return pl.pallas_call(
        functools.partial(spread_kernel, split, starts),
        in_specs=[vmem],
        out_specs=(vmem,) * 2,
        out_shape=(
            jax.ShapeDtypeStruct((2 * part, width), FLOAT),
            jax.ShapeDtypeStruct((part, lanes - 2 * width), FLOAT),
        ),
        scratch_shapes=[
            pltpu.VMEM((split, part, wide), BFLOAT),
            pltpu.VMEM((split - 1, part, wide), BFLOAT),
            pltpu.VMEM((split, part, wide), BFLOAT),
            pltpu.VMEM((part, lanes), FLOAT),
            pltpu.SemaphoreType.DMA((4, split - 1)),
        ],
        compiler_params=pltpu.CompilerParams(
            vmem_limit_bytes=30 * 2**20, collective_id=2, has_side_effects=True
        ),
        cost_estimate=pl.CostEstimate(flops=40_000_000_000, bytes_accessed=4_000_000, transcendentals=0),
    )(values)


def text_forward_kernel(parts, start, text_ref, bias_ref, gain_ref, group_ref, packed_ref, raw_ref, *refs):
    low_refs, weights_ref, sems = refs[:parts], refs[parts], refs[parts + 1]
    span = gain_ref.shape[1]
    wide = 2 * span
    load = pltpu.make_async_copy(packed_ref.at[:, start : start + parts * wide], weights_ref, sems.at[0])
    load.start()
    load.wait()
    for r in range(parts):
        raw = dot(text_ref[...], weights_ref[:, r * wide : (r + 1) * wide]) + bias_ref[r : r + 1, :]
        if r == 0:
            raw_ref[...] = raw
        normed, _ = norm_heads(raw[:, :span], group_ref[...])
        low_refs[r][:, :span] = (normed * gain_ref[r : r + 1, :]).astype(BFLOAT)
        low_refs[r][:, span:] = raw[:, span:].astype(BFLOAT)


def text_forward(text, packed, start, bias, gain, group):
    parts, wide = bias.shape
    tokens, width = text.shape
    vmem = pl.BlockSpec(memory_space=pltpu.VMEM)
    return pl.pallas_call(
        functools.partial(text_forward_kernel, parts, start),
        in_specs=[vmem] * 4 + [pl.BlockSpec(memory_space=pl.ANY)],
        out_specs=(vmem,) * (1 + parts),
        out_shape=(
            jax.ShapeDtypeStruct((tokens, wide), FLOAT),
            *[jax.ShapeDtypeStruct((tokens, wide), BFLOAT) for _ in range(parts)],
        ),
        scratch_shapes=[pltpu.VMEM((width, parts * wide), BFLOAT), pltpu.SemaphoreType.DMA((1,))],
        compiler_params=pltpu.CompilerParams(vmem_limit_bytes=40 * 2**20),
        cost_estimate=pl.CostEstimate(flops=12_000_000_000, bytes_accessed=10_000_000, transcendentals=0),
    )(text, bias, gain, group, packed)


def text_kernel(parts, *refs):
    term_refs, (raw_ref, gain_ref, group_ref, low_ref, rows_ref) = refs[:parts], refs[parts:]
    span = gain_ref.shape[1]
    total = term_refs[0][...].astype(FLOAT)
    for ref in term_refs[1:]:
        total = total + ref[...].astype(FLOAT)
    group = group_ref[...]
    normed, inverse = norm_heads(raw_ref[:, :span], group)
    grad = total[:, :span]
    gain_grad = jnp.sum(grad * normed, axis=0, keepdims=True)
    grad = grad * gain_ref[...]
    grad = inverse * (grad - head_means(grad, group) - normed * head_means(grad * normed, group))
    low = jnp.concatenate([grad, total[:, span:]], axis=1).astype(BFLOAT)
    low_ref[...] = low
    zeros = jnp.zeros((1, span), FLOAT)
    rows_ref[...] = jnp.concatenate(
        [
            jnp.sum(low.astype(FLOAT), axis=0, keepdims=True),
            jnp.concatenate([gain_grad, zeros], axis=1),
            jnp.zeros((6, 2 * span), FLOAT),
        ],
        axis=0,
    )


def text_norm_back(terms, raw, gain, group):
    return pl.pallas_call(
        functools.partial(text_kernel, len(terms)),
        out_shape=(
            jax.ShapeDtypeStruct(terms[0].shape, BFLOAT),
            jax.ShapeDtypeStruct((8, terms[0].shape[1]), FLOAT),
        ),
        compiler_params=pltpu.CompilerParams(vmem_limit_bytes=30 * 2**20),
        cost_estimate=pl.CostEstimate(flops=5_000_000_000, bytes_accessed=4_000_000, transcendentals=0),
    )(*terms, raw, gain, group)


QUARTER = 24
DEEP = 4 * QUARTER


def expansion(heads):
    result = np.zeros((3 * heads * HD, 3 * heads * DEEP), np.float32)
    for part in range(3):
        for head in range(heads):
            for channel in range(HD):
                quarter = HD // 4
                place = channel if part == 2 else channel // quarter * QUARTER + channel % quarter
                result[(part * heads + head) * HD + channel, (part * heads + head) * DEEP + place] = 1.0
    return result


def real_rows():
    rows = lax.broadcasted_iota(jnp.int32, (DEEP, 1), 0)
    return (lax.rem(rows, QUARTER) < HD // 4).astype(FLOAT)


def norm_deep(values, mask):
    mean = jnp.sum(values, axis=0, keepdims=True) * (1.0 / HD)
    centred = (values - mean) * mask
    inverse = lax.rsqrt(jnp.sum(centred * centred, axis=0, keepdims=True) * (1.0 / HD) + EPSILON)
    return centred * inverse, inverse


def turn_deep(values, row_cos, row_sin, col_cos, col_sin):
    one, two, three, four = (values[i * QUARTER : (i + 1) * QUARTER] for i in range(4))
    return jnp.concatenate(
        [
            one * row_cos - two * row_sin,
            two * row_cos + one * row_sin,
            three * col_cos - four * col_sin,
            four * col_cos + three * col_sin,
        ],
        axis=0,
    )


def full_tile(values):
    return jnp.concatenate([values, jnp.zeros((LANES - DEEP, values.shape[1]), values.dtype)], axis=0)


def attend_forward_kernel(heads, parts, block, *refs):
    raw_refs, refs = refs[:parts], refs[parts:]
    turn_ref, gain_ref, refs = refs[0], refs[1], refs[2:]
    o_refs, (oturn_ref, qturn_ref, kturn_ref, k_ref, v_ref, lse_ref, vturn_ref) = refs[:parts], refs[parts:]
    rows = raw_refs[0].shape[1]
    length = parts * rows
    mask = real_rows()
    for r in range(parts):
        here = slice(r * rows, (r + 1) * rows)

        def prepare(head, carry):
            tables = [turn_ref[i, :, here] for i in range(4)]
            turned = []
            for part in range(2):
                at = pl.ds((part * heads + head) * DEEP, DEEP)
                normed, _ = norm_deep(raw_refs[r][at, :], mask)
                turned.append(full_tile(turn_deep(normed * gain_ref[at, :], *tables)))
            qturn_ref[head, :, here] = turned[0].astype(BFLOAT)
            kturn_ref[head, :, here] = turned[1].astype(BFLOAT)
            k_ref[head, here, :] = turned[1].T.astype(BFLOAT)
            values = full_tile(raw_refs[r][pl.ds((2 * heads + head) * DEEP, DEEP), :])
            vturn_ref[head, :, here] = values.astype(BFLOAT)
            v_ref[head, here, :] = values.T.astype(BFLOAT)
            return carry

        lax.fori_loop(0, heads, prepare, 0)
    for head in range(heads):
        for index in range(length // block):
            here = slice(index * block, (index + 1) * block)
            scores = dot(k_ref[head], qturn_ref[head, :, here])
            peak = jnp.max(scores, axis=0, keepdims=True)
            powers = jnp.exp2((scores - peak) * (SCALE * LOG2E))
            total = jnp.sum(powers, axis=0, keepdims=True)
            mixed = dot(vturn_ref[head], powers.astype(BFLOAT)) / total
            oturn_ref[head, :, here] = mixed.astype(BFLOAT)
            lse_ref[head, :, here] = peak * (SCALE * LOG2E) + jnp.log2(total)
    for r in range(parts):
        here = slice(r * rows, (r + 1) * rows)
        o_refs[r][...] = jnp.concatenate(
            [oturn_ref[head, :, here].astype(FLOAT).T[:, :HD] for head in range(heads)], axis=1
        ).astype(BFLOAT)


def attend_forward(raws, turns, gains, heads, block):
    rows = raws[0].shape[1]
    length = rows * len(raws)
    tall = jax.ShapeDtypeStruct((heads, LANES, length), BFLOAT)
    long = jax.ShapeDtypeStruct((heads, length, LANES), BFLOAT)
    return pl.pallas_call(
        functools.partial(attend_forward_kernel, heads, len(raws), block),
        out_shape=(
            *[jax.ShapeDtypeStruct((rows, heads * HD), BFLOAT) for _ in raws],
            tall,
            tall,
            tall,
            long,
            long,
            jax.ShapeDtypeStruct((heads, 1, length), FLOAT),
        ),
        scratch_shapes=[pltpu.VMEM((heads, LANES, length), BFLOAT)],
        compiler_params=pltpu.CompilerParams(vmem_limit_bytes=56 * 2**20),
        cost_estimate=pl.CostEstimate(flops=20_000_000_000, bytes_accessed=12_000_000, transcendentals=4_200_000),
    )(*raws, turns, gains)


def attend_backward_kernel(heads, parts, block, *refs):
    raw_refs, refs = refs[:parts], refs[parts:]
    turn_ref, gain_ref, oturn_ref, qturn_ref, kturn_ref, k_ref, v_ref, lse_ref = refs[:8]
    do_refs = refs[8 : 8 + parts]
    graw_ref, gain_out_ref, sums_ref, dturn_ref, dq_ref, dk_ref, dv_ref = refs[8 + parts :]
    rows = raw_refs[0].shape[1]
    length = parts * rows
    count = length // block
    mask = real_rows()
    for r in range(parts):
        here = slice(r * rows, (r + 1) * rows)
        values = do_refs[r][...].astype(FLOAT)
        for head in range(heads):
            wide = jnp.concatenate(
                [values[:, head * HD : (head + 1) * HD], jnp.zeros((rows, LANES - HD), FLOAT)], axis=1
            )
            dturn_ref[head, :, here] = wide.T.astype(BFLOAT)

    def attend(head, carry):
        for index in range(count):
            here = slice(index * block, (index + 1) * block)
            queries, grad = qturn_ref[head, :, here], dturn_ref[head, :, here]
            probs = jnp.exp2(dot(k_ref[head], queries) * (SCALE * LOG2E) - lse_ref[head, :, here])
            inner = jnp.sum(grad.astype(FLOAT) * oturn_ref[head, :, here].astype(FLOAT), axis=0, keepdims=True)
            grad_scores = (probs * (dot(v_ref[head], grad) - inner)).astype(BFLOAT)
            add_v = dot(grad, probs.astype(BFLOAT), NT)
            add_k = dot(queries, grad_scores, NT)
            dq_ref[head, :, here] = dot(kturn_ref[head], grad_scores)
            if index == 0:
                dv_ref[head] = add_v
                dk_ref[head] = add_k
            else:
                dv_ref[head] += add_v
                dk_ref[head] += add_k
        return carry

    lax.fori_loop(0, heads, attend, 0)
    gain_out_ref[...] = jnp.zeros_like(gain_out_ref)
    sums_ref[...] = jnp.zeros_like(sums_ref)

    def narrow(values):
        return sum(values[:, i * LANES : (i + 1) * LANES] for i in range(values.shape[1] // LANES))

    for r in range(parts):
        here = slice(r * rows, (r + 1) * rows)

        def finish(head, carry):
            row_cos, row_sin, col_cos, col_sin = (turn_ref[i, :, here] for i in range(4))
            for part, grad_ref in ((0, dq_ref), (1, dk_ref)):
                at = pl.ds((part * heads + head) * DEEP, DEEP)
                normed, inverse = norm_deep(raw_refs[r][at, :], mask)
                grad = turn_deep(grad_ref[head, :DEEP, here] * SCALE, row_cos, -row_sin, col_cos, -col_sin)
                gain_out_ref[at, :] += narrow(grad * normed)
                grad = grad * gain_ref[at, :]
                mean = jnp.sum(grad, axis=0, keepdims=True) * (1.0 / HD)
                slope = jnp.sum(grad * normed, axis=0, keepdims=True) * (1.0 / HD)
                low = ((inverse * (grad - mean - normed * slope)) * mask).astype(BFLOAT)
                graw_ref[at, here] = low
                sums_ref[at, :] += narrow(low.astype(FLOAT))
            at = pl.ds((2 * heads + head) * DEEP, DEEP)
            low = dv_ref[head, :DEEP, here].astype(BFLOAT)
            graw_ref[at, here] = low
            sums_ref[at, :] += narrow(low.astype(FLOAT))
            return carry

        lax.fori_loop(0, heads, finish, 0)


def attend_backward(raws, turns, gains, kept, grad_out, heads, block):
    length = raws[0].shape[1] * len(raws)
    return pl.pallas_call(
        functools.partial(attend_backward_kernel, heads, len(raws), block),
        out_shape=(
            jax.ShapeDtypeStruct((3 * heads * DEEP, length), BFLOAT),
            jax.ShapeDtypeStruct((2 * heads * DEEP, LANES), FLOAT),
            jax.ShapeDtypeStruct((3 * heads * DEEP, LANES), FLOAT),
        ),
        scratch_shapes=[
            pltpu.VMEM((heads, LANES, length), BFLOAT),
            pltpu.VMEM((heads, LANES, length), FLOAT),
            pltpu.VMEM((heads, LANES, length), FLOAT),
            pltpu.VMEM((heads, LANES, length), FLOAT),
        ],
        compiler_params=pltpu.CompilerParams(vmem_limit_bytes=56 * 2**20),
        cost_estimate=pl.CostEstimate(flops=28_000_000_000, bytes_accessed=16_000_000, transcendentals=4_200_000),
    )(*raws, turns, gains, *kept, *grad_out)


def norm_rows(values):
    count = values.shape[-1]
    mean = jnp.sum(values, axis=-1, keepdims=True) * (1.0 / count)
    centred = values - mean
    inverse = lax.rsqrt(jnp.sum(centred * centred, axis=-1, keepdims=True) * (1.0 / count) + EPSILON)
    return centred * inverse, inverse


def norm_rows_back(values, gain, grad):
    normed, inverse = norm_rows(values)
    count = values.shape[-1]
    gain_grad = jnp.sum(grad * normed, axis=0, keepdims=True)
    bias_grad = jnp.sum(grad, axis=0, keepdims=True)
    grad = grad * gain
    mean = jnp.sum(grad, axis=-1, keepdims=True) * (1.0 / count)
    slope = jnp.sum(grad * normed, axis=-1, keepdims=True) * (1.0 / count)
    return inverse * (grad - mean - normed * slope), gain_grad, bias_grad


def head_means(values, group):
    high = values.astype(BFLOAT)
    rest = (values - high.astype(FLOAT)).astype(BFLOAT)
    return (dot(high, group) + dot(rest, group)) * (1.0 / HD)


def norm_heads(values, group):
    centred = values - head_means(values, group)
    inverse = lax.rsqrt(head_means(centred * centred, group) + EPSILON)
    return centred * inverse, inverse


def head_masks(heads, span):
    lanes = lax.broadcasted_iota(jnp.int32, (1, span), 1)
    return [((lanes >= HD * head) & (lanes < HD * (head + 1))).astype(BFLOAT) for head in range(heads)]


def load_weights(weights_ref, kept_ref, sems):
    width = kept_ref.shape[-1]
    return [
        pltpu.make_async_copy(weights_ref.at[:, i * width : (i + 1) * width], kept_ref.at[i], sems.at[i])
        for i in range(3)
    ]


def middle_forward_kernel(
    heads, parts, *refs,
):
    mixed_refs, text_refs, refs = refs[:parts], refs[parts : 2 * parts], refs[2 * parts :]
    one_ref, table_ref, group_ref, weights_ref, two_ref, raw_ref, three_ref, mixed_ref, cross_ref = refs[:9]
    query_ref, cross_mixed_ref, mlp_ref, kept_ref, sems = refs[9:]
    span = heads * HD
    mixed_ref[...] = jnp.concatenate([ref[...] for ref in mixed_refs], axis=1)
    loads = load_weights(weights_ref, kept_ref, sems)
    for load in loads:
        load.start()
    row = lambda index: table_ref[index : index + 1, :]
    loads[0].wait()
    two = one_ref[...] + dot(mixed_ref[...], kept_ref[0], NT) + row(0)
    two_ref[...] = two
    cross = (norm_rows(two)[0] * row(1) + row(2)).astype(BFLOAT)
    cross_ref[...] = cross
    loads[1].wait()
    raw_ref[...] = dot(cross, kept_ref[1]) + row(3)
    group = group_ref[...]
    masks = head_masks(heads, span)
    pieces, mixes = [], []
    for r in range(parts):
        part = slice(r * span, (r + 1) * span)
        normed, _ = norm_heads(raw_ref[:, part], group)
        queries = (normed * table_ref[4:5, part]).astype(BFLOAT)
        pieces.append(queries)
        keys, values = text_refs[r][:, :span], text_refs[r][:, span:]
        mix = None
        for head in range(heads):
            scores = dot(queries * masks[head], keys, NT)
            peak = jnp.max(scores, axis=-1, keepdims=True)
            powers = jnp.exp2((scores - peak) * (SCALE * LOG2E))
            weights = (powers / jnp.sum(powers, axis=-1, keepdims=True)).astype(BFLOAT)
            term = dot(weights, values * masks[head])
            mix = term if mix is None else mix + term
        mixes.append(mix.astype(BFLOAT))
    query_ref[...] = jnp.concatenate(pieces, axis=1)
    cross_mixed_ref[...] = jnp.concatenate(mixes, axis=1)
    loads[2].wait()
    three = two_ref[...] + dot(cross_mixed_ref[...], kept_ref[2], NT) + row(5)
    three_ref[...] = three
    mlp_ref[...] = (norm_rows(three)[0] * row(6) + row(7)).astype(BFLOAT)


def middle_forward(mixed, one, table, text, group, weights, heads):
    rows, width = one.shape
    wide = jax.ShapeDtypeStruct((rows, width), FLOAT)
    low = jax.ShapeDtypeStruct((rows, width), BFLOAT)
    vmem = pl.BlockSpec(memory_space=pltpu.VMEM)
    return pl.pallas_call(
        functools.partial(middle_forward_kernel, heads, len(mixed)),
        in_specs=[vmem] * (2 * len(mixed) + 3) + [pl.BlockSpec(memory_space=pl.ANY)],
        out_shape=(wide, wide, wide, low, low, low, low, low),
        out_specs=(vmem,) * 8,
        scratch_shapes=[pltpu.VMEM((3, width, width), BFLOAT), pltpu.SemaphoreType.DMA((3,))],
        compiler_params=pltpu.CompilerParams(vmem_limit_bytes=56 * 2**20),
        cost_estimate=pl.CostEstimate(flops=26_000_000_000, bytes_accessed=24_000_000, transcendentals=1_300_000),
    )(*mixed, *text, one, table, group, weights)


def middle_backward_kernel(
    heads, parts, *refs,
):
    text_refs, refs = refs[:parts], refs[parts:]
    grad_ref, cot_ref, three_ref, two_ref, raw_ref, query_ref, table_ref, group_ref, weights_ref = refs[:9]
    three_low_ref, raw_low_ref, two_low_ref, grad_two_ref, rows_ref, refs = *refs[9:14], refs[14:]
    mixed_refs, text_grad_refs = refs[:parts], refs[parts : 2 * parts]
    kept_ref, grad_three_ref, mixed_ref, sems = refs[2 * parts :]
    span = heads * HD
    loads = load_weights(weights_ref, kept_ref, sems)
    for load in reversed(loads):
        load.start()
    row = lambda index: table_ref[index : index + 1, :]
    into, gain_grad, bias_grad = norm_rows_back(three_ref[...], row(6), grad_ref[...])
    rows_ref[0:1, :], rows_ref[1:2, :] = gain_grad, bias_grad
    grad_three = cot_ref[...].astype(FLOAT) + into
    grad_three_ref[...] = grad_three
    rows_ref[2:3, :] = jnp.sum(grad_three, axis=0, keepdims=True)
    three_low = grad_three.astype(BFLOAT)
    three_low_ref[...] = three_low
    loads[2].wait()
    mixed_ref[...] = dot(three_low, kept_ref[2]).astype(BFLOAT)
    group = group_ref[...]
    masks = head_masks(heads, span)
    pieces = []
    for r in range(parts):
        part = slice(r * span, (r + 1) * span)
        keys, values = text_refs[r][:, :span], text_refs[r][:, span:]
        queries, mixed = query_ref[:, part], mixed_ref[:, part]
        grad_q = grad_k = grad_v = None
        for head in range(heads):
            some, grad = queries * masks[head], mixed * masks[head]
            scores = dot(keys, some, NT)
            peak = jnp.max(scores, axis=0, keepdims=True)
            powers = jnp.exp2((scores - peak) * (SCALE * LOG2E))
            probs = powers / jnp.sum(powers, axis=0, keepdims=True)
            grad_probs = dot(values, grad, NT)
            inner = jnp.sum(probs * grad_probs, axis=0, keepdims=True)
            grad_scores = (probs * (grad_probs - inner)).astype(BFLOAT)
            add_q = dot(grad_scores, keys * masks[head], TN)
            add_k = dot(grad_scores, some)
            add_v = dot(probs.astype(BFLOAT), grad)
            if head == 0:
                grad_q, grad_k, grad_v = add_q, add_k, add_v
            else:
                grad_q, grad_k, grad_v = grad_q + add_q, grad_k + add_k, grad_v + add_v
        text_grad_refs[r][:, :span] = (grad_k * SCALE).astype(BFLOAT)
        text_grad_refs[r][:, span:] = grad_v.astype(BFLOAT)
        normed, inverse = norm_heads(raw_ref[:, part], group)
        grad_q = grad_q * SCALE
        rows_ref[7:8, part] = jnp.sum(grad_q * normed, axis=0, keepdims=True)
        grad_q = grad_q * table_ref[4:5, part]
        low = (
            inverse * (grad_q - head_means(grad_q, group) - normed * head_means(grad_q * normed, group))
        ).astype(BFLOAT)
        pieces.append(low)
    raw_low_ref[...] = jnp.concatenate(pieces, axis=1)
    rows_ref[6:7, :] = jnp.sum(raw_low_ref[...].astype(FLOAT), axis=0, keepdims=True)
    loads[1].wait()
    into, gain_grad, bias_grad = norm_rows_back(two_ref[...], row(1), dot(raw_low_ref[...], kept_ref[1], NT))
    rows_ref[3:4, :], rows_ref[4:5, :] = gain_grad, bias_grad
    grad_two = grad_three_ref[...] + into
    grad_two_ref[...] = grad_two
    rows_ref[5:6, :] = jnp.sum(grad_two, axis=0, keepdims=True)
    two_low = grad_two.astype(BFLOAT)
    two_low_ref[...] = two_low
    loads[0].wait()
    mixed = dot(two_low, kept_ref[0])
    for r in range(parts):
        mixed_refs[r][...] = mixed[:, r * span : (r + 1) * span].astype(BFLOAT)


def middle_backward(grad, cot, three, two, raw, queries, table, text, group, weights, heads):
    rows, width = three.shape
    low = jax.ShapeDtypeStruct((rows, width), BFLOAT)
    vmem = pl.BlockSpec(memory_space=pltpu.VMEM)
    return pl.pallas_call(
        functools.partial(middle_backward_kernel, heads, len(text)),
        in_specs=[vmem] * (8 + len(text)) + [pl.BlockSpec(memory_space=pl.ANY)],
        out_shape=(
            low,
            low,
            low,
            jax.ShapeDtypeStruct((rows, width), FLOAT),
            jax.ShapeDtypeStruct((8, width), FLOAT),
            *[jax.ShapeDtypeStruct((rows, heads * HD), BFLOAT) for _ in text],
            *[jax.ShapeDtypeStruct(item.shape, BFLOAT) for item in text],
        ),
        out_specs=(vmem,) * (5 + 2 * len(text)),
        scratch_shapes=[
            pltpu.VMEM((3, width, width), BFLOAT),
            pltpu.VMEM((rows, width), FLOAT),
            pltpu.VMEM((rows, width), BFLOAT),
            pltpu.SemaphoreType.DMA((3,)),
        ],
        compiler_params=pltpu.CompilerParams(vmem_limit_bytes=56 * 2**20),
        cost_estimate=pl.CostEstimate(flops=33_000_000_000, bytes_accessed=28_000_000, transcendentals=1_300_000),
    )(*text, grad, cot, three, two, raw, queries, table, group, weights)


def on_device(
    latent, skip_in, text_tokens, time_embed, t_index, grid_pos, skip_weight, mod_weight, vectors, up_bias,
    qkv_weight, proj_weight, query_weight, text_weight, cross_weight, up_weight, down_weight, out_grad,
):
    split = lax.axis_size("tensor")
    shards = lax.axis_size("dp")
    place = lax.axis_index("tensor")
    me = lax.axis_index("dp")
    own_rows, width = latent.shape
    own_text = text_tokens.shape[0]
    part = mod_weight.shape[0]
    heads = HEADS // split
    span = heads * HD
    hidden = up_weight.shape[1]
    rows_ahead = vectors.shape[0]

    def others(r):
        return lax.rem(place - r + split, split)

    condition = time_embed
    half = width // 2
    frequencies = jnp.exp(-math.log(10000.0) * jnp.arange(half, dtype=FLOAT) / half)
    angles = t_index.astype(FLOAT)[:, None] * frequencies[None, :]
    condition = time_embed + jnp.concatenate([jnp.cos(angles), jnp.sin(angles)], axis=-1)
    silu_low = silu(condition).astype(BFLOAT)
    small = jnp.concatenate([vectors.reshape(-1), up_bias, silu_low.reshape(-1)])
    small_all = small_gather(small)
    cut_one, cut_two = rows_ahead * part, rows_ahead * part + up_bias.shape[0]
    table = (
        small_all[:, :cut_one].reshape(shards, rows_ahead, part).transpose(1, 0, 2).reshape(rows_ahead, width)
    ).astype(FLOAT)
    bias_all = small_all[:, cut_one:cut_two].reshape(-1).astype(FLOAT)
    silu_all = small_all[:, cut_two:]

    expand = jnp.asarray(expansion(heads), BFLOAT)
    deep = heads * DEEP
    packed_one = jnp.concatenate(
        [
            skip_weight[:part],
            skip_weight[part:],
            dot(qkv_weight.reshape(part, 3 * span), expand).astype(BFLOAT),
        ],
        axis=1,
    )
    all_one = lax.all_gather(packed_one, "dp", axis=0, tiled=True)
    w_skip = all_one[:, : 2 * width]
    w_qkv = all_one[:, 2 * width : 2 * width + 3 * deep]

    own_full = jnp.stack([proj_weight.T, query_weight, cross_weight.T, text_weight[:, 0], text_weight[:, 1]])
    full_blocks, text_blocks = [own_full], [text_tokens]
    for _ in range(split - 1):
        both = lax.optimization_barrier((full_blocks[-1], text_blocks[-1]))
        full_blocks.append(rot(both[0], 1))
        text_blocks.append(rot(both[1], 1))
    packed_two = jnp.concatenate(
        [full_blocks[r][index] for index in range(3) for r in range(split)]
        + [full_blocks[r][index] for r in range(split) for index in (3, 4)],
        axis=1,
    )


    text_length = own_text * split
    text_full = jnp.zeros((text_length, width), BFLOAT)
    for r in range(split):
        text_full = lax.dynamic_update_slice_in_dim(text_full, text_blocks[r], others(r) * own_text, 0)

    def head_slice(index):
        return lax.dynamic_slice_in_dim(table[index], place * span, span, 0)

    def relative(index):
        return jnp.concatenate(
            [lax.dynamic_slice_in_dim(table[index], others(r) * span, span, 0) for r in range(split)]
        )

    def spread(values):
        return lax.dynamic_update_slice_in_dim(jnp.zeros((width,), FLOAT), values.reshape(-1), place * span, 0)

    def absolute(values):
        result = jnp.zeros((width,), FLOAT)
        for r in range(split):
            result = lax.dynamic_update_slice_in_dim(
                result, values.reshape(-1)[r * span : (r + 1) * span], others(r) * span, 0
            )
        return result

    def deepen(values):
        turned = jnp.pad(values[:2].reshape(2, heads, 4, HD // 4), ((0, 0), (0, 0), (0, 0), (0, QUARTER - HD // 4)))
        plain = jnp.pad(values[2].reshape(heads, HD), ((0, 0), (0, DEEP - HD)))
        return jnp.concatenate([turned.reshape(-1), plain.reshape(-1)])

    def undeepen(values):
        turned = values[: 2 * deep].reshape(2, heads, 4, QUARTER)[..., : HD // 4].reshape(2, span)
        if values.shape[0] == 2 * deep:
            return turned
        return jnp.concatenate([turned, values[2 * deep :].reshape(heads, DEEP)[:, :HD].reshape(1, span)])

    quarter = HD // 4
    rate = np.zeros((QUARTER, 1), np.float32)
    rate[:quarter, 0] = 10000.0 ** (-np.arange(quarter, dtype=np.float64) / quarter)
    grid_rel = jnp.concatenate(
        [lax.dynamic_slice_in_dim(grid_pos, others(r) * own_rows, own_rows, 1) for r in range(split)], axis=1
    ).astype(FLOAT)
    turn = grid_rel[:, None, :] * rate[None]
    turns = jnp.stack([jnp.cos(turn[0]), jnp.sin(turn[0]), jnp.cos(turn[1]), jnp.sin(turn[1])])

    silu_mine = after(lax.dynamic_slice_in_dim(silu_all, me * part, part, 1), full_blocks[1])
    shift_terms = dot(silu_mine, mod_weight)
    shift = jnp.sum(lax.all_to_all(shift_terms, "dp", 0, 0, tiled=True), axis=0, keepdims=True) + table[5]

    joined = jnp.concatenate([latent.astype(FLOAT), skip_in.astype(FLOAT)], axis=-1)
    joined_gain = jnp.concatenate([table[0], table[1]])
    joined_bias = jnp.concatenate([table[2], table[3]])
    normed_low = layer_norm(joined, joined_gain, joined_bias).astype(BFLOAT)
    normed_perm = normed_low.reshape(own_rows, shards, 2, part).transpose(0, 2, 1, 3).reshape(own_rows, 2 * width)
    stream_one = (
        dot(normed_perm[:, :width], w_skip[:, :width]) + dot(normed_perm[:, width:], w_skip[:, width:]) + table[4]
    )
    packed_two = after(packed_two, normed_perm, shift, turns)
    all_two = lax.all_gather(packed_two, "dp", axis=0, tiled=True)
    packed_three = jnp.concatenate([up_weight, down_weight.T], axis=1)
    all_three = lax.all_gather(packed_three, "dp", axis=0, tiled=True)
    w_up, w_down_t = all_three[:, :hidden], all_three[:, hidden:]

    attn_low = (layer_norm(stream_one, table[6], table[7]) + shift).astype(BFLOAT)
    attn_blocks = ring_gather(attn_low)
    cot_blocks = [out_grad, rot(after(out_grad, attn_blocks[-1]), 1)]
    qkv_bias = deepen(jnp.stack([head_slice(8), head_slice(9), head_slice(10)]))[:, None]
    raws = [dot(w_qkv, block, ((0,), (1,))) + qkv_bias for block in attn_blocks]
    zero_slice = jnp.zeros((span,), FLOAT)
    gains = deepen(jnp.stack([head_slice(12), head_slice(13), zero_slice]))[: 2 * deep, None]
    length = own_rows * split
    block = min(512, length)
    kept = attend_forward(raws, turns, gains, heads, block)
    mixed, kept = kept[:split], kept[split:]
    *mixed, cot_blocks[1] = lax.optimization_barrier((*mixed, cot_blocks[1]))

    def blocks_of(values, rows):
        return [values[r * rows : (r + 1) * rows] for r in range(split)]

    lane_head = np.arange(span) // HD
    group = jnp.asarray((lane_head[:, None] == lane_head[None, :]).astype(np.float32), BFLOAT)
    text_bias = jnp.stack([relative(17).reshape(split, span), relative(18).reshape(split, span)], axis=1)
    text_raw, *text_rel = text_forward(
        text_full, all_two, 3 * width, text_bias.reshape(split, 2 * span), relative(21).reshape(split, span), group
    )
    mixed = exchange(mixed)
    cot_blocks[-1], mixed[-1], text_rel[0] = lax.optimization_barrier((cot_blocks[-1], mixed[-1], text_rel[0]))
    cot_blocks.append(rot(cot_blocks[-1], 1))
    middle_table = jnp.stack(
        [table[11], table[14], table[15], relative(16), relative(20), table[19], table[22], table[23]]
    )
    stream_two, cross_raw, stream_three, mixed_own, cross_low, cross_queries, cross_mixed, mlp_low = middle_forward(
        mixed, stream_one, middle_table, text_rel, group, all_two, heads
    )
    mlp_low, cot_blocks[-1] = lax.optimization_barrier((mlp_low, cot_blocks[-1]))
    while len(cot_blocks) < split:
        cot_blocks.append(rot(cot_blocks[-1], 1))
    mlp_blocks = ring_gather(mlp_low)
    w_up, w_down_t, mlp_blocks[1] = lax.optimization_barrier((w_up, w_down_t, mlp_blocks[1]))
    hidden_bias = lax.dynamic_slice_in_dim(bias_all, place * hidden, hidden, 0)

    hidden_lows, pre_lows, out_parts, back_parts = [], [], [], []
    for r in range(split):
        hidden_pre = dot(mlp_blocks[r], w_up) + hidden_bias
        activated, pull = jax.vjp(gelu, hidden_pre)
        hidden_lows.append(activated.astype(BFLOAT))
        pre_lows.append(pull(dot(cot_blocks[r], w_down_t))[0].astype(BFLOAT))
        back_parts.append(dot(pre_lows[r], w_up, NT))
        out_parts.append(dot(hidden_lows[r], w_down_t, NT))
    grad_mlp_in = ring_scatter(back_parts)

    rows_grad = {}
    grad_bias = sum(jnp.sum(item, axis=0, dtype=FLOAT) for item in pre_lows)
    grads_one = pack_grad(None, mlp_blocks, pre_lows, 2 * hidden, 0, 512)
    grads_one = pack_grad(grads_one, cot_blocks, hidden_lows, 2 * hidden, hidden, 512)
    grads_one, grad_mlp_in, *out_parts = lax.optimization_barrier((grads_one, grad_mlp_in, *out_parts))
    out_hop = rot(out_parts[1].astype(BFLOAT), 1)
    summed_one = lax.psum_scatter(grads_one, "dp", scatter_dimension=0, tiled=True).astype(FLOAT)
    cot_here = out_grad.astype(FLOAT)
    rows_grad[24] = jnp.sum(cot_here, axis=0)
    three_low, cq_low, two_low, grad_two, middle_rows, *pieces = middle_backward(
        grad_mlp_in, out_grad, stream_three, stream_two, cross_raw, cross_queries, middle_table, text_rel, group,
        all_two, heads,
    )
    grad_mixed, text_terms = pieces[:split], pieces[split:]
    for index, number in enumerate((22, 23, 19, 14, 15, 11)):
        rows_grad[number] = middle_rows[index]
    rows_grad[16], rows_grad[20] = absolute(middle_rows[6]), absolute(middle_rows[7])
    out_hop, *grad_mixed = lax.optimization_barrier((out_hop, *grad_mixed))
    grad_mixed = exchange(grad_mixed)
    lanes_two = 3 * width
    grads_two = pack_grad(None, [two_low], [mixed_own], lanes_two, 0, width)
    grads_two = pack_grad(grads_two, [cross_low], [cq_low], lanes_two, width, width)
    grads_two = pack_grad(grads_two, [three_low], [cross_mixed], lanes_two, 2 * width, width)
    grads_two, *grad_mixed = lax.optimization_barrier((grads_two, *grad_mixed))
    summed_two = lax.psum_scatter(grads_two, "dp", scatter_dimension=0, tiled=True)
    text_terms[1:] = lax.optimization_barrier((*text_terms[1:], grad_mixed[-1]))[:-1]
    text_got = [rot(text_terms[r], split - r) for r in range(1, split)]
    grad_raw, gain_grads, raw_sums = attend_backward(
        raws, turns, gains, kept, grad_mixed, heads, block
    )
    grad_raw, summed_one = lax.optimization_barrier((grad_raw, summed_one))
    text_got[0], grad_raw = lax.optimization_barrier((text_got[0], grad_raw))
    ckv_low, text_rows = text_norm_back([text_terms[0], *text_got], text_raw, head_slice(21)[None], group)
    rows_grad[21] = spread(text_rows[1, :span])
    rows_grad[17], rows_grad[18] = spread(text_rows[0, :span]), spread(text_rows[0, span:])

    gain_grads = undeepen(jnp.sum(gain_grads, axis=1))
    raw_sums = undeepen(jnp.sum(raw_sums, axis=1))
    rows_grad[12], rows_grad[13] = spread(gain_grads[0]), spread(gain_grads[1])
    rows_grad[8], rows_grad[9], rows_grad[10] = spread(raw_sums[0]), spread(raw_sums[1]), spread(raw_sums[2])
    qkv_lanes = 3 * deep
    text_lanes = pl.cdiv(2 * span, LANES) * LANES
    shared = 2 * width + LANES
    qkv_start = pl.cdiv(shared, deep) * deep
    text_start = qkv_start + qkv_lanes
    lanes_three = text_start + text_lanes
    bias_part = up_bias.shape[0]
    bias_cols = pl.cdiv(bias_part, part)
    bias_spread = lax.dynamic_update_slice_in_dim(jnp.zeros(bias_all.shape, FLOAT), grad_bias, place * hidden, 0)
    zero_row = jnp.zeros((width,), FLOAT)
    table_grad = jnp.stack([rows_grad.get(index, zero_row) for index in range(rows_ahead)], axis=1)
    bias_grad = jnp.pad(bias_spread.reshape(shards, bias_part), ((0, 0), (0, bias_cols * part - bias_part)))
    bias_grad = bias_grad.reshape(shards, bias_cols, part).transpose(0, 2, 1).reshape(width, bias_cols)
    small_grads = jnp.concatenate([table_grad, bias_grad], axis=1).astype(BFLOAT)
    small_grads = jnp.pad(small_grads, ((0, 0), (0, qkv_start - 2 * width - small_grads.shape[1])))

    grad_attn_in, shift_part, grads_three = ring_sum(
        grad_raw, attn_blocks, text_full, ckv_low, all_one, 2 * width, lanes_three, (qkv_start, text_start), split
    )
    grads_three = lax.dynamic_update_slice(grads_three, small_grads, (0, 2 * width))
    grads_three, one_low, late_rows = skip_grads(
        grads_three, grad_attn_in, grad_two, stream_one, table[6:7], normed_perm
    )
    grads_three, summed_two, one_low = lax.optimization_barrier((grads_three, summed_two, one_low))
    summed_three = lax.psum_scatter(grads_three, "dp", scatter_dimension=0, tiled=True)
    latent_grad, skip_grad, late, full_sum, text_grad, block_out = side_sums(
        one_low, late_rows, shift_part, jnp.concatenate([table[:2], table[24:25]]), latent, skip_in, stream_three,
        out_hop, summed_two, ckv_low, all_one, all_two, 3 * width, [out_parts[0], *out_parts[2:]], shards, split,
    )
    shift_grads = late[8 : 8 + shards]
    late = lax.dynamic_slice_in_dim(late[:8], me * part, part, 1)
    silu_terms = lax.dot_general(
        shift_grads, mod_weight.astype(FLOAT), ((NT), ((), ())), precision=HIGHEST, preferred_element_type=FLOAT
    )
    summed_three = after(summed_three, silu_terms, full_sum, text_grad, summed_one)
    mod_grad = lax.dot_general(
        silu_mine.astype(FLOAT), shift_grads, ((TN), ((), ())), precision=HIGHEST, preferred_element_type=FLOAT
    )
    into_silu = lax.all_to_all(silu_terms, "dp", 0, 0, tiled=True).reshape(1, width)
    time_full = jax.vjp(silu, condition)[1](into_silu)[0]
    time_grad = lax.dynamic_slice_in_dim(time_full, place * (width // split), width // split, 1)

    qkv_part = summed_three[:, qkv_start:text_start]
    text_part = summed_three[:, text_start : text_start + 2 * span]
    skip_weight_grad, small_sum = spread_sum(summed_three[:, :shared], width, split)
    vectors_grad = jnp.concatenate([late[:5], late[7:8], late[5:7], small_sum[:, 8:rows_ahead].T])
    bias_grad = small_sum[:, rows_ahead : rows_ahead + bias_cols].T.reshape(-1)[:bias_part]
    qkv_sum = dot(qkv_part, expand, NT).reshape(part, 3, span)
    text_sum_grad = text_part.astype(FLOAT).reshape(part, 2, span)

    return (
        block_out,
        latent_grad,
        skip_grad,
        text_grad,
        time_grad,
        skip_weight_grad,
        mod_grad,
        vectors_grad,
        bias_grad,
        qkv_sum,
        full_sum[:, :span].T,
        full_sum[:, span : 2 * span],
        text_sum_grad,
        full_sum[:, 2 * span :].T,
        summed_one[:, :hidden],
        summed_one[:, hidden:].T,
    )


def solution(mesh):
    tokens = P(("dp", "tensor"), None)
    placed = (
        tokens,
        tokens,
        tokens,
        P("dp", None),
        P("dp"),
        P(None, "dp"),
        P("dp", None),
        P("dp", None),
        P(None, "dp"),
        P("dp"),
        P("dp", None, "tensor"),
        P("tensor", "dp"),
        P("dp", "tensor"),
        P("dp", None, "tensor"),
        P("tensor", "dp"),
        P("dp", "tensor"),
        P("tensor", "dp"),
        tokens,
    )
    return jax.shard_map(
        on_device,
        mesh=mesh,
        in_specs=placed,
        out_specs=(
            tokens,
            tokens,
            tokens,
            tokens,
            P("dp", "tensor"),
            P("dp", None),
            P("dp", None),
            P(None, "dp"),
            P("dp"),
            P("dp", None, "tensor"),
            P("tensor", "dp"),
            P("dp", "tensor"),
            P("dp", None, "tensor"),
            P("tensor", "dp"),
            P("dp", "tensor"),
            P("tensor", "dp"),
        ),
        check_vma=False,
    )
```

```python
import functools
import math

import jax
import jax.numpy as jnp
import numpy as np
from jax import lax
from jax.experimental import pallas as pl
from jax.experimental.pallas import tpu as pltpu
from jax.sharding import PartitionSpec as P

HEADS = 16
HD = 88
LANES = 128
EPSILON = 1e-06
HIGHEST = lax.Precision.HIGHEST
FLOAT = jnp.float32
BFLOAT = jnp.bfloat16
LOG2E = 1.4426950408889634
SCALE = 1.0 / math.sqrt(HD)


def layer_norm(values, norm_gain, norm_bias):
    centred = values - jnp.mean(values, axis=-1, keepdims=True)
    variance = jnp.mean(centred * centred, axis=-1, keepdims=True)
    return centred * lax.rsqrt(variance + EPSILON) * norm_gain + norm_bias


def head_norm(values, norm_gain):
    centred = values - jnp.mean(values, axis=-1, keepdims=True)
    variance = jnp.mean(centred * centred, axis=-1, keepdims=True)
    return centred * lax.rsqrt(variance + EPSILON) * norm_gain


def silu(values):
    return values / (1.0 + jnp.exp(-values))


def gelu(values):
    inner = math.sqrt(2.0 / math.pi) * (values + 0.044715 * values * values * values)
    return 0.5 * values * (1.0 + jnp.tanh(inner))


def dot(left, right, contract=((1,), (0,))):
    return lax.dot_general(left, right, (contract, ((), ())), preferred_element_type=FLOAT)


NT = ((1,), (1,))
TN = ((0,), (0,))


def rot(values, step):
    count = lax.axis_size("tensor")
    return lax.ppermute(values, "tensor", [(i, (i + step) % count) for i in range(count)])


def ring_gather(own):
    blocks = [own]
    for _ in range(lax.axis_size("tensor") - 1):
        blocks.append(rot(blocks[-1], 1))
    return blocks


def ring_scatter(parts):
    running = parts[1].astype(BFLOAT)
    for part in parts[2:]:
        running = (rot(running, 1).astype(FLOAT) + part.astype(FLOAT)).astype(BFLOAT)
    return rot(running, 1).astype(FLOAT) + parts[0].astype(FLOAT)


def direct_gather(own):
    return [own] + [rot(own, r) for r in range(1, lax.axis_size("tensor"))]


def direct_scatter(parts):
    count = len(parts)
    total = parts[0].astype(FLOAT)
    for r in range(1, count):
        total = total + rot(parts[r], count - r).astype(FLOAT)
    return total


def exchange(parts):
    count = len(parts)
    return [parts[0]] + [rot(parts[count - r], r) for r in range(1, count)]


def after(values, *earlier):
    return lax.optimization_barrier((values, *earlier))[0]


def small_gather(own):
    have = own[None]
    me = lax.axis_index("dp")
    count = lax.axis_size("dp")
    step = 1
    while step < count:
        other = lax.ppermute(have, "dp", [(i, i ^ step) for i in range(count)])
        upper = (me // step) % 2 == 1
        have = jnp.where(upper, jnp.concatenate([other, have]), jnp.concatenate([have, other]))
        step *= 2
    return have


def tensor_sum(values):
    total = values.astype(FLOAT)
    for step in range(1, lax.axis_size("tensor")):
        total = total + rot(values, step).astype(FLOAT)
    return total


def grad_kernel(lefts, rights, turned, *refs):
    left_refs, right_refs = refs[:lefts], refs[lefts : lefts + rights]
    out_ref, kept_ref = refs[-2], refs[-1]
    rows = left_refs[0].shape[0]

    @pl.when(pl.program_id(0) == 0)
    def _():
        for r in range(lefts):
            kept_ref[:, r * rows : (r + 1) * rows] = left_refs[r][...].T

    total = None
    for r in range(rights):
        span = lefts // rights * rows
        left = kept_ref[:, r * span : (r + 1) * span]
        term = dot(left, right_refs[r][...], NT if turned else ((1,), (0,)))
        total = term if total is None else total + term
    out_ref[...] = total.astype(BFLOAT)


def pack_grad(packed, lefts, rights, lanes, start, tile, turned=False):
    rows, height = lefts[0].shape
    deep = rights[0].shape[1 if turned else 0]
    wide = rights[0].shape[0 if turned else 1]
    first = start // tile
    in_specs = [pl.BlockSpec((rows, height), lambda i: (0, 0))] * len(lefts)
    if turned:
        in_specs += [pl.BlockSpec((tile, deep), lambda i: (i, 0))] * len(rights)
    else:
        in_specs += [pl.BlockSpec((deep, tile), lambda i: (0, i))] * len(rights)
    operands = [*lefts, *rights]
    if packed is not None:
        in_specs.append(pl.BlockSpec(memory_space=pl.ANY))
        operands.append(packed)
    tokens = rows * len(lefts)
    return pl.pallas_call(
        functools.partial(grad_kernel, len(lefts), len(rights), turned),
        grid=(pl.cdiv(wide, tile),),
        in_specs=in_specs,
        out_specs=pl.BlockSpec((height, tile), lambda i: (0, first + i)),
        out_shape=jax.ShapeDtypeStruct((height, lanes), BFLOAT),
        scratch_shapes=[pltpu.VMEM((height, tokens), BFLOAT)],
        input_output_aliases={} if packed is None else {len(operands) - 1: 0},
        compiler_params=pltpu.CompilerParams(vmem_limit_bytes=40 * 2**20),
        cost_estimate=pl.CostEstimate(
            flops=4 * tokens * height * wide,
            bytes_accessed=2 * (tokens * height + tokens * wide + height * wide),
            transcendentals=0,
        ),
    )(*operands)


def flipped(index, bit):
    return index + (1 - 2 * lax.rem(lax.div(index, 2**bit), 2)) * 2**bit


def to_device(source, target, send, recv, where):
    return pltpu.make_async_remote_copy(
        src_ref=source,
        dst_ref=target,
        send_sem=send,
        recv_sem=recv,
        device_id=where,
        device_id_type=pl.DeviceIdType.MESH,
    )


def neighbours(place, split):
    return lax.rem(place + 1, split), lax.rem(place + split - 1, split)


def ring_kernel(split, start, places, *refs):
    raw_ref, left_refs, refs = refs[0], refs[1 : 1 + split], refs[1 + split :]
    text_ref, ckv_ref, packed_ref, sum_out, shift_out, grads_ref = refs[:6]
    weights_ref, turned, qkv_grad, text_grad, sent, got, load_sem, sems = refs[6:]
    loads = [
        pltpu.make_async_copy(packed_ref.at[:, start : start + weights_ref.shape[1]], weights_ref, load_sem.at[0]),
        pltpu.make_async_copy(
            qkv_grad, grads_ref.at[:, places[0] : places[0] + qkv_grad.shape[1]], load_sem.at[1]
        ),
        pltpu.make_async_copy(
            text_grad, grads_ref.at[:, places[1] : places[1] + text_grad.shape[1]], load_sem.at[2]
        ),
    ]
    loads[0].start()
    place = lax.axis_index("tensor")
    right, left = neighbours(place, split)
    barrier = pltpu.get_barrier_semaphore()
    for where in (left, right):
        pl.semaphore_signal(barrier, inc=1, device_id={"tensor": where}, device_id_type=pl.DeviceIdType.MESH)
    rows = sum_out.shape[0]

    def term(r):
        return dot(weights_ref[...], raw_ref[:, r * rows : (r + 1) * rows]).T

    def hop(step):
        return to_device(sent.at[step], got.at[step], sems.at[0, step], sems.at[1, step], {"tensor": right})

    def qkv_lanes(some):
        lanes = qkv_grad.shape[1] // 3
        for i in some:
            part = slice(i * lanes, (i + 1) * lanes)
            qkv_grad[:, part] = dot(turned[...], raw_ref[part, :], NT).astype(BFLOAT)

    def beside(step):
        if step == 1:
            for r in range(split):
                turned[:, r * rows : (r + 1) * rows] = left_refs[r][...].T
            qkv_lanes((0,))
        elif step == 2:
            qkv_lanes((1, 2))
            loads[1].start()
        elif step == 3:
            wide = ckv_ref.shape[1]
            text_grad[:, :wide] = dot(text_ref[...].T, ckv_ref[...]).astype(BFLOAT)
            text_grad[:, wide:] = jnp.zeros((text_grad.shape[0], text_grad.shape[1] - wide), BFLOAT)
            loads[2].start()

    loads[0].wait()
    part = term(1)
    total = jnp.sum(part, axis=0, keepdims=True)
    sent[0] = part.astype(BFLOAT)
    pl.semaphore_wait(barrier, 2)
    hop(0).start()
    for step in range(1, split):
        part = term((step + 1) % split)
        total = total + jnp.sum(part, axis=0, keepdims=True)
        beside(step)
        hop(step - 1).wait_recv()
        part = part + got[step - 1].astype(FLOAT)
        if step + 1 < split:
            sent[step] = part.astype(BFLOAT)
            hop(step).start()
        else:
            sum_out[...] = part
    shift_out[...] = jnp.broadcast_to(total, shift_out.shape)
    loads[1].wait()
    loads[2].wait()
    for step in range(split - 1):
        hop(step).wait_send()


def ring_sum(raw, lefts, text, ckv, packed, start, lanes, places, split):
    rows, width = raw.shape[1] // split, packed.shape[0]
    vmem = pl.BlockSpec(memory_space=pltpu.VMEM)
    anywhere = pl.BlockSpec(memory_space=pl.ANY)
    return pl.pallas_call(
        functools.partial(ring_kernel, split, start, places),
        in_specs=[vmem] * (3 + split) + [anywhere],
        out_specs=(vmem, vmem, anywhere),
        out_shape=(
            jax.ShapeDtypeStruct((rows, width), FLOAT),
            jax.ShapeDtypeStruct((8, width), FLOAT),
            jax.ShapeDtypeStruct((width, lanes), BFLOAT),
        ),
        scratch_shapes=[
            pltpu.VMEM((width, raw.shape[0]), BFLOAT),
            pltpu.VMEM((width, raw.shape[1]), BFLOAT),
            pltpu.VMEM((width, raw.shape[0]), BFLOAT),
            pltpu.VMEM((width, lanes - places[1]), BFLOAT),
            pltpu.VMEM((split - 1, rows, width), BFLOAT),
            pltpu.VMEM((split - 1, rows, width), BFLOAT),
            pltpu.SemaphoreType.DMA((3,)),
            pltpu.SemaphoreType.DMA((2, split - 1)),
        ],
        compiler_params=pltpu.CompilerParams(
            vmem_limit_bytes=48 * 2**20, collective_id=1, has_side_effects=True
        ),
        cost_estimate=pl.CostEstimate(flops=60_000_000_000, bytes_accessed=10_000_000, transcendentals=0),
    )(raw, *lefts, text, ckv, packed)


def skip_kernel(
    grad_ref, two_ref, one_ref, gain_ref, left_ref, packed_ref, out_ref, low_ref, rows_ref
):
    @pl.when(pl.program_id(0) == 0)
    def _():
        into, gain_grad, bias_grad = norm_rows_back(one_ref[...], gain_ref[...], grad_ref[...])
        grad_one = two_ref[...] + into
        low_ref[...] = grad_one.astype(BFLOAT)
        rows_ref[...] = jnp.concatenate(
            [gain_grad, bias_grad, jnp.sum(grad_one, axis=0, keepdims=True), jnp.zeros((5, grad_one.shape[1]), FLOAT)],
            axis=0,
        )

    out_ref[...] = dot(left_ref[...].T, low_ref[...]).astype(BFLOAT)


def skip_grads(packed, grad, two, one, gain, left):
    rows, width = one.shape
    fixed = pl.BlockSpec((rows, width), lambda i: (0, 0))
    return pl.pallas_call(
        skip_kernel,
        grid=(left.shape[1] // width,),
        in_specs=[fixed] * 3
        + [
            pl.BlockSpec((1, width), lambda i: (0, 0)),
            pl.BlockSpec((rows, width), lambda i: (0, i)),
            pl.BlockSpec(memory_space=pl.ANY),
        ],
        out_specs=(
            pl.BlockSpec((width, width), lambda i: (0, i)),
            pl.BlockSpec((rows, width), lambda i: (0, 0)),
            pl.BlockSpec((8, width), lambda i: (0, 0)),
        ),
        out_shape=(
            jax.ShapeDtypeStruct(packed.shape, BFLOAT),
            jax.ShapeDtypeStruct((rows, width), BFLOAT),
            jax.ShapeDtypeStruct((8, width), FLOAT),
        ),
        input_output_aliases={5: 0},
        compiler_params=pltpu.CompilerParams(vmem_limit_bytes=40 * 2**20),
        cost_estimate=pl.CostEstimate(flops=10_000_000_000, bytes_accessed=16_000_000, transcendentals=0),
    )(grad, two, one, gain, left, packed)


def side_kernel(shards, split, hops, text_start, *refs):
    low_ref, late_ref, shift_ref, table_ref, latent_ref, skip_ref, base_ref, hop_ref, summed_ref, ckv_ref = refs[:10]
    weights_ref, text_packed_ref, refs = refs[10], refs[11], refs[12:]
    out_refs, refs = refs[: hops + 1], refs[hops + 1 :]
    latent_out, skip_out, table_out, full_out, text_out, block_out = refs[:6]
    weights, text_weights, full_refs, text_refs, full_got, text_got, hop_sent, hop_got, table_sent, table_got = refs[6:16]
    load_sem, side_sems, hop_sems, table_sems = refs[16:]
    me, place = lax.axis_index("dp"), lax.axis_index("tensor")
    count = shards.bit_length() - 1
    width = latent_out.shape[1]
    part = width // shards
    right, _ = neighbours(place, split)

    loads = [
        pltpu.make_async_copy(weights_ref.at[:, half * width : (half + 1) * width], weights, load_sem.at[half])
        for half in range(2)
    ]
    text_stop = text_start + text_weights.shape[1]
    loads.append(pltpu.make_async_copy(text_packed_ref.at[:, text_start:text_stop], text_weights, load_sem.at[2]))
    loads[0].start()
    loads[2].start()
    barrier = pltpu.get_barrier_semaphore()
    for bit in range(count):
        pl.semaphore_signal(barrier, inc=1, device_id={"dp": flipped(me, bit)}, device_id_type=pl.DeviceIdType.MESH)
    for step in range(1, split):
        pl.semaphore_signal(
            barrier, inc=1, device_id={"tensor": lax.rem(place + step, split)}, device_id_type=pl.DeviceIdType.MESH
        )

    def side(step, i):
        return to_device(
            (full_refs, text_refs)[i].at[step],
            (full_got, text_got)[i].at[step - 1],
            side_sems.at[i, 0, step - 1],
            side_sems.at[i, 1, step - 1],
            {"tensor": lax.rem(place + split - step, split)},
        )

    def hop(step):
        return to_device(
            hop_sent.at[step], hop_got.at[step], hop_sems.at[0, step], hop_sems.at[1, step], {"tensor": right}
        )

    hop_sent[0] = (hop_ref[...].astype(FLOAT) + out_refs[1][...]).astype(BFLOAT)
    pl.semaphore_wait(barrier, count + split - 1)
    hop(0).start()
    low = low_ref[...]
    grads = []
    for half in range(2):
        loads[half].wait()
        grads.append(dot(low, weights[...], NT))
        if half == 0:
            loads[1].start()
    ordered = [grads[half][:, shard * part : (shard + 1) * part] for shard in range(shards) for half in range(2)]
    grads = [jnp.concatenate(ordered[:shards], axis=1), jnp.concatenate(ordered[shards:], axis=1)]
    values = [latent_ref[...].astype(FLOAT), skip_ref[...].astype(FLOAT)]

    def mean_of(one, two):
        return (jnp.sum(one, axis=-1, keepdims=True) + jnp.sum(two, axis=-1, keepdims=True)) * (0.5 / width)

    mean = mean_of(*values)
    centred = [item - mean for item in values]
    inverse = lax.rsqrt(mean_of(*[item * item for item in centred]) + EPSILON)
    normed = [item * inverse for item in centred]
    gain_rows = [jnp.sum(grads[i] * normed[i], axis=0, keepdims=True) for i in range(2)]
    bias_rows = [jnp.sum(grads[i], axis=0, keepdims=True) for i in range(2)]
    scaled = [grads[i] * table_ref[i : i + 1, :] for i in range(2)]
    mean = mean_of(*scaled)
    slope = mean_of(*[scaled[i] * normed[i] for i in range(2)])
    latent_out[...] = inverse * (scaled[0] - mean - normed[0] * slope)
    skip_out[...] = inverse * (scaled[1] - mean - normed[1] * slope)

    spare = table_out.shape[0] - 8
    table_sent[0] = jnp.concatenate(
        [
            *gain_rows,
            *bias_rows,
            late_ref[2:3, :],
            late_ref[0:2, :],
            shift_ref[0:1, :],
            jnp.zeros((spare, width), FLOAT),
        ],
        axis=0,
    )
    bits = split.bit_length() - 1
    shares = table_sent.shape[0]

    def share(step):
        where = {"tensor": flipped(place, step)} if step < bits else {"dp": flipped(me, step - bits)}
        return to_device(
            table_sent.at[step], table_got.at[step], table_sems.at[0, step], table_sems.at[1, step], where
        )

    def open_hop(step):
        hop(step - 1).wait_recv()
        hop_sent[step] = (hop_got[step - 1].astype(FLOAT) + out_refs[step + 1][...]).astype(BFLOAT)
        hop(step).start()

    def pass_on(step):
        share(step).wait_recv()
        total = table_sent[step] + table_got[step]
        if step + 1 == bits:
            at = lax.broadcasted_iota(jnp.int32, (8 + spare, 1), 0)
            total = jnp.where(at == 8 + me, total[7:8, :], total)
        if step + 1 < shares:
            table_sent[step + 1] = total
            share(step + 1).start()
        else:
            table_out[...] = total
    share(0).start()
    span = full_out.shape[1] // 3
    for r in range(split):
        full_refs[r] = jnp.concatenate(
            [summed_ref[:, k * width + r * span : k * width + (r + 1) * span] for k in range(3)], axis=1
        )
    for step in range(bits):
        pass_on(step)
    for step in range(1, split):
        side(step, 0).start()
    loads[2].wait()
    back = dot(ckv_ref[...], text_weights[:, : ckv_ref.shape[1]], NT).astype(BFLOAT)
    own_text = text_out.shape[0]
    for r in range(split):
        text_refs[lax.rem(place + split - r, split)] = back[r * own_text : (r + 1) * own_text]
    for step in range(1, split):
        side(step, 1).start()
    for step in range(1, hops):
        open_hop(step)
    for step in range(bits, shares):
        pass_on(step)
    for i, (terms, result) in enumerate(((full_refs, full_out), (text_refs, text_out))):
        if i == 1:
            hop(hops - 1).wait_recv()
            last = hop_got[hops - 1].astype(FLOAT) + out_refs[0][...]
            block_out[...] = (base_ref[...] + table_ref[2:3, :] + last).astype(BFLOAT)
        total = terms[0].astype(FLOAT)
        for step in range(1, split):
            side(step, i).wait_recv()
            total = total + (full_got, text_got)[i][step - 1].astype(FLOAT)
        result[...] = total
    for step in range(hops):
        hop(step).wait_send()
    for step in range(shares):
        share(step).wait_send()
    for step in range(1, split):
        for i in range(2):
            side(step, i).wait_send()


def side_sums(
    low, late, shift, table, latent, skip_in, base, hop, summed, ckv, weights, text_packed, text_start, out, shards, split
):
    rows, width = low.shape
    spare = pl.cdiv(shards, 8) * 8
    shares = shards.bit_length() - 1 + split.bit_length() - 1
    vmem = pl.BlockSpec(memory_space=pltpu.VMEM)
    wide = jax.ShapeDtypeStruct((rows, width), FLOAT)
    hops = len(out) - 1
    full, text = (summed.shape[0], summed.shape[1] // split), (ckv.shape[0] // split, width)
    return pl.pallas_call(
        functools.partial(side_kernel, shards, split, hops, text_start),
        in_specs=[vmem] * 10 + [pl.BlockSpec(memory_space=pl.ANY)] * 2 + [vmem] * len(out),
        out_specs=(vmem,) * 6,
        out_shape=(
            wide,
            wide,
            jax.ShapeDtypeStruct((8 + spare, width), FLOAT),
            jax.ShapeDtypeStruct(full, FLOAT),
            jax.ShapeDtypeStruct(text, FLOAT),
            jax.ShapeDtypeStruct((rows, width), BFLOAT),
        ),
        scratch_shapes=[
            pltpu.VMEM((width, width), BFLOAT),
            pltpu.VMEM((width, pl.cdiv(ckv.shape[1], LANES) * LANES), BFLOAT),
            pltpu.VMEM((split, *full), BFLOAT),
            pltpu.VMEM((split, *text), BFLOAT),
            pltpu.VMEM((split - 1, *full), BFLOAT),
            pltpu.VMEM((split - 1, *text), BFLOAT),
            pltpu.VMEM((hops, rows, width), BFLOAT),
            pltpu.VMEM((hops, rows, width), BFLOAT),
            pltpu.VMEM((shares, 8 + spare, width), FLOAT),
            pltpu.VMEM((shares, 8 + spare, width), FLOAT),
            pltpu.SemaphoreType.DMA((3,)),
            pltpu.SemaphoreType.DMA((2, 2, split - 1)),
            pltpu.SemaphoreType.DMA((2, hops)),
            pltpu.SemaphoreType.DMA((2, shares)),
        ],
        compiler_params=pltpu.CompilerParams(
            vmem_limit_bytes=56 * 2**20, collective_id=0, has_side_effects=True
        ),
        cost_estimate=pl.CostEstimate(flops=90_000_000_000, bytes_accessed=30_000_000, transcendentals=0),
    )(low, late, shift, table, latent, skip_in, base, hop, summed, ckv, weights, text_packed, *out)


def spread_kernel(split, starts, in_ref, skip_out, small_out, piece_sent, piece_got, pieces, whole, sems):
    place = lax.axis_index("tensor")
    part, width = skip_out.shape[0] // 2, skip_out.shape[1]
    wide = piece_sent.shape[2]
    barrier = pltpu.get_barrier_semaphore()
    for step in range(1, split):
        pl.semaphore_signal(
            barrier, inc=1, device_id={"tensor": lax.rem(place + step, split)}, device_id_type=pl.DeviceIdType.MESH
        )
    for i in range(split):
        piece_sent[i] = in_ref[:, starts[i] : starts[i] + wide]
    pl.semaphore_wait(barrier, split - 1)

    def scatter(step):
        where = lax.rem(place + step, split)
        return to_device(
            piece_sent.at[where], piece_got.at[step - 1], sems.at[0, step - 1], sems.at[1, step - 1], {"tensor": where}
        )

    def gather(step):
        return to_device(
            pieces.at[place], pieces.at[place], sems.at[2, step - 1], sems.at[3, step - 1],
            {"tensor": lax.rem(place + step, split)},
        )

    for step in range(1, split):
        scatter(step).start()
    total = piece_sent[place].astype(FLOAT)
    for step in range(1, split):
        scatter(step).wait_recv()
        total = total + piece_got[step - 1].astype(FLOAT)
    pieces[place] = total.astype(BFLOAT)
    for step in range(1, split):
        gather(step).start()
    for step in range(1, split):
        gather(step).wait_recv()
    for i in range(split):
        stop = starts[i + 1] if i + 1 < split else whole.shape[1]
        whole[:, starts[i] : stop] = pieces[i][:, : stop - starts[i]].astype(FLOAT)
    skip_out[:part] = whole[:, :width]
    skip_out[part:] = whole[:, width : 2 * width]
    small_out[...] = whole[:, 2 * width :]
    for step in range(1, split):
        scatter(step).wait_send()
        gather(step).wait_send()


def spread_sum(values, width, split):
    part, lanes = values.shape
    wide = pl.cdiv(lanes // LANES, split) * LANES
    starts = [min(i * wide, lanes - wide) for i in range(split)]
    vmem = pl.BlockSpec(memory_space=pltpu.VMEM)
    return pl.pallas_call(
        functools.partial(spread_kernel, split, starts),
        in_specs=[vmem],
        out_specs=(vmem,) * 2,
        out_shape=(
            jax.ShapeDtypeStruct((2 * part, width), FLOAT),
            jax.ShapeDtypeStruct((part, lanes - 2 * width), FLOAT),
        ),
        scratch_shapes=[
            pltpu.VMEM((split, part, wide), BFLOAT),
            pltpu.VMEM((split - 1, part, wide), BFLOAT),
            pltpu.VMEM((split, part, wide), BFLOAT),
            pltpu.VMEM((part, lanes), FLOAT),
            pltpu.SemaphoreType.DMA((4, split - 1)),
        ],
        compiler_params=pltpu.CompilerParams(
            vmem_limit_bytes=30 * 2**20, collective_id=2, has_side_effects=True
        ),
        cost_estimate=pl.CostEstimate(flops=40_000_000_000, bytes_accessed=4_000_000, transcendentals=0),
    )(values)


def text_forward_kernel(parts, start, text_ref, bias_ref, gain_ref, group_ref, packed_ref, raw_ref, *refs):
    low_refs, weights_ref, sems = refs[:parts], refs[parts], refs[parts + 1]
    span = gain_ref.shape[1]
    wide = 2 * span
    load = pltpu.make_async_copy(packed_ref.at[:, start : start + parts * wide], weights_ref, sems.at[0])
    load.start()
    load.wait()
    for r in range(parts):
        raw = dot(text_ref[...], weights_ref[:, r * wide : (r + 1) * wide]) + bias_ref[r : r + 1, :]
        if r == 0:
            raw_ref[...] = raw
        normed, _ = norm_heads(raw[:, :span], group_ref[...])
        low_refs[r][:, :span] = (normed * gain_ref[r : r + 1, :]).astype(BFLOAT)
        low_refs[r][:, span:] = raw[:, span:].astype(BFLOAT)


def text_forward(text, packed, start, bias, gain, group):
    parts, wide = bias.shape
    tokens, width = text.shape
    vmem = pl.BlockSpec(memory_space=pltpu.VMEM)
    return pl.pallas_call(
        functools.partial(text_forward_kernel, parts, start),
        in_specs=[vmem] * 4 + [pl.BlockSpec(memory_space=pl.ANY)],
        out_specs=(vmem,) * (1 + parts),
        out_shape=(
            jax.ShapeDtypeStruct((tokens, wide), FLOAT),
            *[jax.ShapeDtypeStruct((tokens, wide), BFLOAT) for _ in range(parts)],
        ),
        scratch_shapes=[pltpu.VMEM((width, parts * wide), BFLOAT), pltpu.SemaphoreType.DMA((1,))],
        compiler_params=pltpu.CompilerParams(vmem_limit_bytes=40 * 2**20),
        cost_estimate=pl.CostEstimate(flops=12_000_000_000, bytes_accessed=10_000_000, transcendentals=0),
    )(text, bias, gain, group, packed)


def text_kernel(parts, *refs):
    term_refs, (raw_ref, gain_ref, group_ref, low_ref, rows_ref) = refs[:parts], refs[parts:]
    span = gain_ref.shape[1]
    total = term_refs[0][...].astype(FLOAT)
    for ref in term_refs[1:]:
        total = total + ref[...].astype(FLOAT)
    group = group_ref[...]
    normed, inverse = norm_heads(raw_ref[:, :span], group)
    grad = total[:, :span]
    gain_grad = jnp.sum(grad * normed, axis=0, keepdims=True)
    grad = grad * gain_ref[...]
    grad = inverse * (grad - head_means(grad, group) - normed * head_means(grad * normed, group))
    low = jnp.concatenate([grad, total[:, span:]], axis=1).astype(BFLOAT)
    low_ref[...] = low
    zeros = jnp.zeros((1, span), FLOAT)
    rows_ref[...] = jnp.concatenate(
        [
            jnp.sum(low.astype(FLOAT), axis=0, keepdims=True),
            jnp.concatenate([gain_grad, zeros], axis=1),
            jnp.zeros((6, 2 * span), FLOAT),
        ],
        axis=0,
    )


def text_norm_back(terms, raw, gain, group):
    return pl.pallas_call(
        functools.partial(text_kernel, len(terms)),
        out_shape=(
            jax.ShapeDtypeStruct(terms[0].shape, BFLOAT),
            jax.ShapeDtypeStruct((8, terms[0].shape[1]), FLOAT),
        ),
        compiler_params=pltpu.CompilerParams(vmem_limit_bytes=30 * 2**20),
        cost_estimate=pl.CostEstimate(flops=5_000_000_000, bytes_accessed=4_000_000, transcendentals=0),
    )(*terms, raw, gain, group)


QUARTER = 24
DEEP = 4 * QUARTER


def expansion(heads):
    result = np.zeros((3 * heads * HD, 3 * heads * DEEP), np.float32)
    for part in range(3):
        for head in range(heads):
            for channel in range(HD):
                quarter = HD // 4
                place = channel if part == 2 else channel // quarter * QUARTER + channel % quarter
                result[(part * heads + head) * HD + channel, (part * heads + head) * DEEP + place] = 1.0
    return result


def real_rows():
    rows = lax.broadcasted_iota(jnp.int32, (DEEP, 1), 0)
    return (lax.rem(rows, QUARTER) < HD // 4).astype(FLOAT)


def norm_deep(values, mask):
    mean = jnp.sum(values, axis=0, keepdims=True) * (1.0 / HD)
    centred = (values - mean) * mask
    inverse = lax.rsqrt(jnp.sum(centred * centred, axis=0, keepdims=True) * (1.0 / HD) + EPSILON)
    return centred * inverse, inverse


def turn_deep(values, row_cos, row_sin, col_cos, col_sin):
    one, two, three, four = (values[i * QUARTER : (i + 1) * QUARTER] for i in range(4))
    return jnp.concatenate(
        [
            one * row_cos - two * row_sin,
            two * row_cos + one * row_sin,
            three * col_cos - four * col_sin,
            four * col_cos + three * col_sin,
        ],
        axis=0,
    )


def full_tile(values):
    return jnp.concatenate([values, jnp.zeros((LANES - DEEP, values.shape[1]), values.dtype)], axis=0)


def attend_forward_kernel(heads, parts, block, *refs):
    raw_refs, refs = refs[:parts], refs[parts:]
    turn_ref, gain_ref, refs = refs[0], refs[1], refs[2:]
    o_refs, (oturn_ref, qturn_ref, kturn_ref, k_ref, v_ref, lse_ref, vturn_ref) = refs[:parts], refs[parts:]
    rows = raw_refs[0].shape[1]
    length = parts * rows
    mask = real_rows()
    for r in range(parts):
        here = slice(r * rows, (r + 1) * rows)

        def prepare(head, carry):
            tables = [turn_ref[i, :, here] for i in range(4)]
            turned = []
            for part in range(2):
                at = pl.ds((part * heads + head) * DEEP, DEEP)
                normed, _ = norm_deep(raw_refs[r][at, :], mask)
                turned.append(full_tile(turn_deep(normed * gain_ref[at, :], *tables)))
            qturn_ref[head, :, here] = turned[0].astype(BFLOAT)
            kturn_ref[head, :, here] = turned[1].astype(BFLOAT)
            k_ref[head, here, :] = turned[1].T.astype(BFLOAT)
            values = full_tile(raw_refs[r][pl.ds((2 * heads + head) * DEEP, DEEP), :])
            vturn_ref[head, :, here] = values.astype(BFLOAT)
            v_ref[head, here, :] = values.T.astype(BFLOAT)
            return carry

        lax.fori_loop(0, heads, prepare, 0)
    for head in range(heads):
        for index in range(length // block):
            here = slice(index * block, (index + 1) * block)
            scores = dot(k_ref[head], qturn_ref[head, :, here])
            peak = jnp.max(scores, axis=0, keepdims=True)
            powers = jnp.exp2((scores - peak) * (SCALE * LOG2E))
            total = jnp.sum(powers, axis=0, keepdims=True)
            mixed = dot(vturn_ref[head], powers.astype(BFLOAT)) / total
            oturn_ref[head, :, here] = mixed.astype(BFLOAT)
            lse_ref[head, :, here] = peak * (SCALE * LOG2E) + jnp.log2(total)
    for r in range(parts):
        here = slice(r * rows, (r + 1) * rows)
        o_refs[r][...] = jnp.concatenate(
            [oturn_ref[head, :, here].astype(FLOAT).T[:, :HD] for head in range(heads)], axis=1
        ).astype(BFLOAT)


def attend_forward(raws, turns, gains, heads, block):
    rows = raws[0].shape[1]
    length = rows * len(raws)
    tall = jax.ShapeDtypeStruct((heads, LANES, length), BFLOAT)
    long = jax.ShapeDtypeStruct((heads, length, LANES), BFLOAT)
    return pl.pallas_call(
        functools.partial(attend_forward_kernel, heads, len(raws), block),
        out_shape=(
            *[jax.ShapeDtypeStruct((rows, heads * HD), BFLOAT) for _ in raws],
            tall,
            tall,
            tall,
            long,
            long,
            jax.ShapeDtypeStruct((heads, 1, length), FLOAT),
        ),
        scratch_shapes=[pltpu.VMEM((heads, LANES, length), BFLOAT)],
        compiler_params=pltpu.CompilerParams(vmem_limit_bytes=56 * 2**20),
        cost_estimate=pl.CostEstimate(flops=20_000_000_000, bytes_accessed=12_000_000, transcendentals=4_200_000),
    )(*raws, turns, gains)


def attend_backward_kernel(heads, parts, block, *refs):
    raw_refs, refs = refs[:parts], refs[parts:]
    turn_ref, gain_ref, oturn_ref, qturn_ref, kturn_ref, k_ref, v_ref, lse_ref = refs[:8]
    do_refs = refs[8 : 8 + parts]
    graw_ref, gain_out_ref, sums_ref, dturn_ref, dq_ref, dk_ref, dv_ref = refs[8 + parts :]
    rows = raw_refs[0].shape[1]
    length = parts * rows
    count = length // block
    mask = real_rows()
    for r in range(parts):
        here = slice(r * rows, (r + 1) * rows)
        values = do_refs[r][...].astype(FLOAT)
        for head in range(heads):
            wide = jnp.concatenate(
                [values[:, head * HD : (head + 1) * HD], jnp.zeros((rows, LANES - HD), FLOAT)], axis=1
            )
            dturn_ref[head, :, here] = wide.T.astype(BFLOAT)

    def attend(head, carry):
        for index in range(count):
            here = slice(index * block, (index + 1) * block)
            queries, grad = qturn_ref[head, :, here], dturn_ref[head, :, here]
            probs = jnp.exp2(dot(k_ref[head], queries) * (SCALE * LOG2E) - lse_ref[head, :, here])
            inner = jnp.sum(grad.astype(FLOAT) * oturn_ref[head, :, here].astype(FLOAT), axis=0, keepdims=True)
            grad_scores = (probs * (dot(v_ref[head], grad) - inner)).astype(BFLOAT)
            add_v = dot(grad, probs.astype(BFLOAT), NT)
            add_k = dot(queries, grad_scores, NT)
            dq_ref[head, :, here] = dot(kturn_ref[head], grad_scores)
            if index == 0:
                dv_ref[head] = add_v
                dk_ref[head] = add_k
            else:
                dv_ref[head] += add_v
                dk_ref[head] += add_k
        return carry

    lax.fori_loop(0, heads, attend, 0)
    gain_out_ref[...] = jnp.zeros_like(gain_out_ref)
    sums_ref[...] = jnp.zeros_like(sums_ref)

    def narrow(values):
        return sum(values[:, i * LANES : (i + 1) * LANES] for i in range(values.shape[1] // LANES))

    for r in range(parts):
        here = slice(r * rows, (r + 1) * rows)

        def finish(head, carry):
            row_cos, row_sin, col_cos, col_sin = (turn_ref[i, :, here] for i in range(4))
            for part, grad_ref in ((0, dq_ref), (1, dk_ref)):
                at = pl.ds((part * heads + head) * DEEP, DEEP)
                normed, inverse = norm_deep(raw_refs[r][at, :], mask)
                grad = turn_deep(grad_ref[head, :DEEP, here] * SCALE, row_cos, -row_sin, col_cos, -col_sin)
                gain_out_ref[at, :] += narrow(grad * normed)
                grad = grad * gain_ref[at, :]
                mean = jnp.sum(grad, axis=0, keepdims=True) * (1.0 / HD)
                slope = jnp.sum(grad * normed, axis=0, keepdims=True) * (1.0 / HD)
                low = ((inverse * (grad - mean - normed * slope)) * mask).astype(BFLOAT)
                graw_ref[at, here] = low
                sums_ref[at, :] += narrow(low.astype(FLOAT))
            at = pl.ds((2 * heads + head) * DEEP, DEEP)
            low = dv_ref[head, :DEEP, here].astype(BFLOAT)
            graw_ref[at, here] = low
            sums_ref[at, :] += narrow(low.astype(FLOAT))
            return carry

        lax.fori_loop(0, heads, finish, 0)


def attend_backward(raws, turns, gains, kept, grad_out, heads, block):
    length = raws[0].shape[1] * len(raws)
    return pl.pallas_call(
        functools.partial(attend_backward_kernel, heads, len(raws), block),
        out_shape=(
            jax.ShapeDtypeStruct((3 * heads * DEEP, length), BFLOAT),
            jax.ShapeDtypeStruct((2 * heads * DEEP, LANES), FLOAT),
            jax.ShapeDtypeStruct((3 * heads * DEEP, LANES), FLOAT),
        ),
        scratch_shapes=[
            pltpu.VMEM((heads, LANES, length), BFLOAT),
            pltpu.VMEM((heads, LANES, length), FLOAT),
            pltpu.VMEM((heads, LANES, length), FLOAT),
            pltpu.VMEM((heads, LANES, length), FLOAT),
        ],
        compiler_params=pltpu.CompilerParams(vmem_limit_bytes=56 * 2**20),
        cost_estimate=pl.CostEstimate(flops=28_000_000_000, bytes_accessed=16_000_000, transcendentals=4_200_000),
    )(*raws, turns, gains, *kept, *grad_out)


def norm_rows(values):
    count = values.shape[-1]
    mean = jnp.sum(values, axis=-1, keepdims=True) * (1.0 / count)
    centred = values - mean
    inverse = lax.rsqrt(jnp.sum(centred * centred, axis=-1, keepdims=True) * (1.0 / count) + EPSILON)
    return centred * inverse, inverse


def norm_rows_back(values, gain, grad):
    normed, inverse = norm_rows(values)
    count = values.shape[-1]
    gain_grad = jnp.sum(grad * normed, axis=0, keepdims=True)
    bias_grad = jnp.sum(grad, axis=0, keepdims=True)
    grad = grad * gain
    mean = jnp.sum(grad, axis=-1, keepdims=True) * (1.0 / count)
    slope = jnp.sum(grad * normed, axis=-1, keepdims=True) * (1.0 / count)
    return inverse * (grad - mean - normed * slope), gain_grad, bias_grad


def head_means(values, group):
    high = values.astype(BFLOAT)
    rest = (values - high.astype(FLOAT)).astype(BFLOAT)
    return (dot(high, group) + dot(rest, group)) * (1.0 / HD)


def norm_heads(values, group):
    centred = values - head_means(values, group)
    inverse = lax.rsqrt(head_means(centred * centred, group) + EPSILON)
    return centred * inverse, inverse


def head_masks(heads, span):
    lanes = lax.broadcasted_iota(jnp.int32, (1, span), 1)
    return [((lanes >= HD * head) & (lanes < HD * (head + 1))).astype(BFLOAT) for head in range(heads)]


def load_weights(weights_ref, kept_ref, sems):
    width = kept_ref.shape[-1]
    return [
        pltpu.make_async_copy(weights_ref.at[:, i * width : (i + 1) * width], kept_ref.at[i], sems.at[i])
        for i in range(3)
    ]


def middle_forward_kernel(
    heads, parts, *refs,
):
    mixed_refs, text_refs, refs = refs[:parts], refs[parts : 2 * parts], refs[2 * parts :]
    one_ref, table_ref, group_ref, weights_ref, two_ref, raw_ref, three_ref, mixed_ref, cross_ref = refs[:9]
    query_ref, cross_mixed_ref, mlp_ref, kept_ref, sems = refs[9:]
    span = heads * HD
    mixed_ref[...] = jnp.concatenate([ref[...] for ref in mixed_refs], axis=1)
    loads = load_weights(weights_ref, kept_ref, sems)
    for load in loads:
        load.start()
    row = lambda index: table_ref[index : index + 1, :]
    loads[0].wait()
    two = one_ref[...] + dot(mixed_ref[...], kept_ref[0], NT) + row(0)
    two_ref[...] = two
    cross = (norm_rows(two)[0] * row(1) + row(2)).astype(BFLOAT)
    cross_ref[...] = cross
    loads[1].wait()
    raw_ref[...] = dot(cross, kept_ref[1]) + row(3)
    group = group_ref[...]
    masks = head_masks(heads, span)
    pieces, mixes = [], []
    for r in range(parts):
        part = slice(r * span, (r + 1) * span)
        normed, _ = norm_heads(raw_ref[:, part], group)
        queries = (normed * table_ref[4:5, part]).astype(BFLOAT)
        pieces.append(queries)
        keys, values = text_refs[r][:, :span], text_refs[r][:, span:]
        mix = None
        for head in range(heads):
            scores = dot(queries * masks[head], keys, NT)
            peak = jnp.max(scores, axis=-1, keepdims=True)
            powers = jnp.exp2((scores - peak) * (SCALE * LOG2E))
            weights = (powers / jnp.sum(powers, axis=-1, keepdims=True)).astype(BFLOAT)
            term = dot(weights, values * masks[head])
            mix = term if mix is None else mix + term
        mixes.append(mix.astype(BFLOAT))
    query_ref[...] = jnp.concatenate(pieces, axis=1)
    cross_mixed_ref[...] = jnp.concatenate(mixes, axis=1)
    loads[2].wait()
    three = two_ref[...] + dot(cross_mixed_ref[...], kept_ref[2], NT) + row(5)
    three_ref[...] = three
    mlp_ref[...] = (norm_rows(three)[0] * row(6) + row(7)).astype(BFLOAT)


def middle_forward(mixed, one, table, text, group, weights, heads):
    rows, width = one.shape
    wide = jax.ShapeDtypeStruct((rows, width), FLOAT)
    low = jax.ShapeDtypeStruct((rows, width), BFLOAT)
    vmem = pl.BlockSpec(memory_space=pltpu.VMEM)
    return pl.pallas_call(
        functools.partial(middle_forward_kernel, heads, len(mixed)),
        in_specs=[vmem] * (2 * len(mixed) + 3) + [pl.BlockSpec(memory_space=pl.ANY)],
        out_shape=(wide, wide, wide, low, low, low, low, low),
        out_specs=(vmem,) * 8,
        scratch_shapes=[pltpu.VMEM((3, width, width), BFLOAT), pltpu.SemaphoreType.DMA((3,))],
        compiler_params=pltpu.CompilerParams(vmem_limit_bytes=56 * 2**20),
        cost_estimate=pl.CostEstimate(flops=26_000_000_000, bytes_accessed=24_000_000, transcendentals=1_300_000),
    )(*mixed, *text, one, table, group, weights)


def middle_backward_kernel(
    heads, parts, *refs,
):
    text_refs, refs = refs[:parts], refs[parts:]
    grad_ref, cot_ref, three_ref, two_ref, raw_ref, query_ref, table_ref, group_ref, weights_ref = refs[:9]
    three_low_ref, raw_low_ref, two_low_ref, grad_two_ref, rows_ref, refs = *refs[9:14], refs[14:]
    mixed_refs, text_grad_refs = refs[:parts], refs[parts : 2 * parts]
    kept_ref, grad_three_ref, mixed_ref, sems = refs[2 * parts :]
    span = heads * HD
    loads = load_weights(weights_ref, kept_ref, sems)
    for load in reversed(loads):
        load.start()
    row = lambda index: table_ref[index : index + 1, :]
    into, gain_grad, bias_grad = norm_rows_back(three_ref[...], row(6), grad_ref[...])
    rows_ref[0:1, :], rows_ref[1:2, :] = gain_grad, bias_grad
    grad_three = cot_ref[...].astype(FLOAT) + into
    grad_three_ref[...] = grad_three
    rows_ref[2:3, :] = jnp.sum(grad_three, axis=0, keepdims=True)
    three_low = grad_three.astype(BFLOAT)
    three_low_ref[...] = three_low
    loads[2].wait()
    mixed_ref[...] = dot(three_low, kept_ref[2]).astype(BFLOAT)
    group = group_ref[...]
    masks = head_masks(heads, span)
    pieces = []
    for r in range(parts):
        part = slice(r * span, (r + 1) * span)
        keys, values = text_refs[r][:, :span], text_refs[r][:, span:]
        queries, mixed = query_ref[:, part], mixed_ref[:, part]
        grad_q = grad_k = grad_v = None
        for head in range(heads):
            some, grad = queries * masks[head], mixed * masks[head]
            scores = dot(keys, some, NT)
            peak = jnp.max(scores, axis=0, keepdims=True)
            powers = jnp.exp2((scores - peak) * (SCALE * LOG2E))
            probs = powers / jnp.sum(powers, axis=0, keepdims=True)
            grad_probs = dot(values, grad, NT)
            inner = jnp.sum(probs * grad_probs, axis=0, keepdims=True)
            grad_scores = (probs * (grad_probs - inner)).astype(BFLOAT)
            add_q = dot(grad_scores, keys * masks[head], TN)
            add_k = dot(grad_scores, some)
            add_v = dot(probs.astype(BFLOAT), grad)
            if head == 0:
                grad_q, grad_k, grad_v = add_q, add_k, add_v
            else:
                grad_q, grad_k, grad_v = grad_q + add_q, grad_k + add_k, grad_v + add_v
        text_grad_refs[r][:, :span] = (grad_k * SCALE).astype(BFLOAT)
        text_grad_refs[r][:, span:] = grad_v.astype(BFLOAT)
        normed, inverse = norm_heads(raw_ref[:, part], group)
        grad_q = grad_q * SCALE
        rows_ref[7:8, part] = jnp.sum(grad_q * normed, axis=0, keepdims=True)
        grad_q = grad_q * table_ref[4:5, part]
        low = (
            inverse * (grad_q - head_means(grad_q, group) - normed * head_means(grad_q * normed, group))
        ).astype(BFLOAT)
        pieces.append(low)
    raw_low_ref[...] = jnp.concatenate(pieces, axis=1)
    rows_ref[6:7, :] = jnp.sum(raw_low_ref[...].astype(FLOAT), axis=0, keepdims=True)
    loads[1].wait()
    into, gain_grad, bias_grad = norm_rows_back(two_ref[...], row(1), dot(raw_low_ref[...], kept_ref[1], NT))
    rows_ref[3:4, :], rows_ref[4:5, :] = gain_grad, bias_grad
    grad_two = grad_three_ref[...] + into
    grad_two_ref[...] = grad_two
    rows_ref[5:6, :] = jnp.sum(grad_two, axis=0, keepdims=True)
    two_low = grad_two.astype(BFLOAT)
    two_low_ref[...] = two_low
    loads[0].wait()
    mixed = dot(two_low, kept_ref[0])
    for r in range(parts):
        mixed_refs[r][...] = mixed[:, r * span : (r + 1) * span].astype(BFLOAT)


def middle_backward(grad, cot, three, two, raw, queries, table, text, group, weights, heads):
    rows, width = three.shape
    low = jax.ShapeDtypeStruct((rows, width), BFLOAT)
    vmem = pl.BlockSpec(memory_space=pltpu.VMEM)
    return pl.pallas_call(
        functools.partial(middle_backward_kernel, heads, len(text)),
        in_specs=[vmem] * (8 + len(text)) + [pl.BlockSpec(memory_space=pl.ANY)],
        out_shape=(
            low,
            low,
            low,
            jax.ShapeDtypeStruct((rows, width), FLOAT),
            jax.ShapeDtypeStruct((8, width), FLOAT),
            *[jax.ShapeDtypeStruct((rows, heads * HD), BFLOAT) for _ in text],
            *[jax.ShapeDtypeStruct(item.shape, BFLOAT) for item in text],
        ),
        out_specs=(vmem,) * (5 + 2 * len(text)),
        scratch_shapes=[
            pltpu.VMEM((3, width, width), BFLOAT),
            pltpu.VMEM((rows, width), FLOAT),
            pltpu.VMEM((rows, width), BFLOAT),
            pltpu.SemaphoreType.DMA((3,)),
        ],
        compiler_params=pltpu.CompilerParams(vmem_limit_bytes=56 * 2**20),
        cost_estimate=pl.CostEstimate(flops=33_000_000_000, bytes_accessed=28_000_000, transcendentals=1_300_000),
    )(*text, grad, cot, three, two, raw, queries, table, group, weights)


def on_device(
    latent, skip_in, text_tokens, time_embed, t_index, grid_pos, skip_weight, mod_weight, vectors, up_bias,
    qkv_weight, proj_weight, query_weight, text_weight, cross_weight, up_weight, down_weight, out_grad,
):
    split = lax.axis_size("tensor")
    shards = lax.axis_size("dp")
    place = lax.axis_index("tensor")
    me = lax.axis_index("dp")
    own_rows, width = latent.shape
    own_text = text_tokens.shape[0]
    part = mod_weight.shape[0]
    heads = HEADS // split
    span = heads * HD
    hidden = up_weight.shape[1]
    rows_ahead = vectors.shape[0]

    def others(r):
        return lax.rem(place - r + split, split)

    condition = time_embed
    half = width // 2
    frequencies = jnp.exp(-math.log(10000.0) * jnp.arange(half, dtype=FLOAT) / half)
    angles = t_index.astype(FLOAT)[:, None] * frequencies[None, :]
    condition = time_embed + jnp.concatenate([jnp.cos(angles), jnp.sin(angles)], axis=-1)
    silu_low = silu(condition).astype(BFLOAT)
    small = jnp.concatenate([vectors.reshape(-1), up_bias, silu_low.reshape(-1)])
    small_all = small_gather(small)
    cut_one, cut_two = rows_ahead * part, rows_ahead * part + up_bias.shape[0]
    table = (
        small_all[:, :cut_one].reshape(shards, rows_ahead, part).transpose(1, 0, 2).reshape(rows_ahead, width)
    ).astype(FLOAT)
    bias_all = small_all[:, cut_one:cut_two].reshape(-1).astype(FLOAT)
    silu_all = small_all[:, cut_two:]

    expand = jnp.asarray(expansion(heads), BFLOAT)
    deep = heads * DEEP
    packed_one = jnp.concatenate(
        [
            skip_weight[:part],
            skip_weight[part:],
            dot(qkv_weight.reshape(part, 3 * span), expand).astype(BFLOAT),
        ],
        axis=1,
    )
    all_one = lax.all_gather(packed_one, "dp", axis=0, tiled=True)
    w_skip = all_one[:, : 2 * width]
    w_qkv = all_one[:, 2 * width : 2 * width + 3 * deep]

    own_full = jnp.stack([proj_weight.T, query_weight, cross_weight.T, text_weight[:, 0], text_weight[:, 1]])
    full_blocks, text_blocks = [own_full], [text_tokens]
    for _ in range(split - 1):
        both = lax.optimization_barrier((full_blocks[-1], text_blocks[-1]))
        full_blocks.append(rot(both[0], 1))
        text_blocks.append(rot(both[1], 1))
    packed_two = jnp.concatenate(
        [full_blocks[r][index] for index in range(3) for r in range(split)]
        + [full_blocks[r][index] for r in range(split) for index in (3, 4)],
        axis=1,
    )

    cot_blocks = [out_grad, rot(after(out_grad, all_one, full_blocks[-1], text_blocks[-1]), 1)]

    text_length = own_text * split
    text_full = jnp.zeros((text_length, width), BFLOAT)
    for r in range(split):
        text_full = lax.dynamic_update_slice_in_dim(text_full, text_blocks[r], others(r) * own_text, 0)

    def head_slice(index):
        return lax.dynamic_slice_in_dim(table[index], place * span, span, 0)

    def relative(index):
        return jnp.concatenate(
            [lax.dynamic_slice_in_dim(table[index], others(r) * span, span, 0) for r in range(split)]
        )

    def spread(values):
        return lax.dynamic_update_slice_in_dim(jnp.zeros((width,), FLOAT), values.reshape(-1), place * span, 0)

    def absolute(values):
        result = jnp.zeros((width,), FLOAT)
        for r in range(split):
            result = lax.dynamic_update_slice_in_dim(
                result, values.reshape(-1)[r * span : (r + 1) * span], others(r) * span, 0
            )
        return result

    def deepen(values):
        turned = jnp.pad(values[:2].reshape(2, heads, 4, HD // 4), ((0, 0), (0, 0), (0, 0), (0, QUARTER - HD // 4)))
        plain = jnp.pad(values[2].reshape(heads, HD), ((0, 0), (0, DEEP - HD)))
        return jnp.concatenate([turned.reshape(-1), plain.reshape(-1)])

    def undeepen(values):
        turned = values[: 2 * deep].reshape(2, heads, 4, QUARTER)[..., : HD // 4].reshape(2, span)
        if values.shape[0] == 2 * deep:
            return turned
        return jnp.concatenate([turned, values[2 * deep :].reshape(heads, DEEP)[:, :HD].reshape(1, span)])

    quarter = HD // 4
    rate = np.zeros((QUARTER, 1), np.float32)
    rate[:quarter, 0] = 10000.0 ** (-np.arange(quarter, dtype=np.float64) / quarter)
    grid_rel = jnp.concatenate(
        [lax.dynamic_slice_in_dim(grid_pos, others(r) * own_rows, own_rows, 1) for r in range(split)], axis=1
    ).astype(FLOAT)
    turn = grid_rel[:, None, :] * rate[None]
    turns = jnp.stack([jnp.cos(turn[0]), jnp.sin(turn[0]), jnp.cos(turn[1]), jnp.sin(turn[1])])

    silu_mine = lax.dynamic_slice_in_dim(silu_all, me * part, part, 1)
    shift_terms = dot(silu_mine, mod_weight)
    shift = jnp.sum(lax.all_to_all(shift_terms, "dp", 0, 0, tiled=True), axis=0, keepdims=True) + table[5]

    joined = jnp.concatenate([latent.astype(FLOAT), skip_in.astype(FLOAT)], axis=-1)
    joined_gain = jnp.concatenate([table[0], table[1]])
    joined_bias = jnp.concatenate([table[2], table[3]])
    normed_low = layer_norm(joined, joined_gain, joined_bias).astype(BFLOAT)
    normed_perm = normed_low.reshape(own_rows, shards, 2, part).transpose(0, 2, 1, 3).reshape(own_rows, 2 * width)
    packed_two = after(packed_two, normed_perm, shift, turns)
    all_two = lax.all_gather(packed_two, "dp", axis=0, tiled=True)
    packed_three = jnp.concatenate([up_weight, down_weight.T], axis=1)
    all_three = lax.all_gather(packed_three, "dp", axis=0, tiled=True)
    w_up, w_down_t = all_three[:, :hidden], all_three[:, hidden:]

    stream_one = (
        dot(normed_perm[:, :width], w_skip[:, :width]) + dot(normed_perm[:, width:], w_skip[:, width:]) + table[4]
    )
    attn_low = (layer_norm(stream_one, table[6], table[7]) + shift).astype(BFLOAT)
    attn_blocks = ring_gather(after(attn_low, cot_blocks[1]))
    qkv_bias = deepen(jnp.stack([head_slice(8), head_slice(9), head_slice(10)]))[:, None]
    raws = [dot(w_qkv, block, ((0,), (1,))) + qkv_bias for block in attn_blocks]
    zero_slice = jnp.zeros((span,), FLOAT)
    gains = deepen(jnp.stack([head_slice(12), head_slice(13), zero_slice]))[: 2 * deep, None]
    length = own_rows * split
    block = min(512, length)
    kept = attend_forward(raws, turns, gains, heads, block)
    mixed, kept = kept[:split], kept[split:]

    def blocks_of(values, rows):
        return [values[r * rows : (r + 1) * rows] for r in range(split)]

    lane_head = np.arange(span) // HD
    group = jnp.asarray((lane_head[:, None] == lane_head[None, :]).astype(np.float32), BFLOAT)
    text_bias = jnp.stack([relative(17).reshape(split, span), relative(18).reshape(split, span)], axis=1)
    text_raw, *text_rel = text_forward(
        text_full, all_two, 3 * width, text_bias.reshape(split, 2 * span), relative(21).reshape(split, span), group
    )
    mixed = exchange(mixed)
    cot_blocks[-1], mixed[-1], text_rel[0] = lax.optimization_barrier((cot_blocks[-1], mixed[-1], text_rel[0]))
    cot_blocks.append(rot(cot_blocks[-1], 1))
    middle_table = jnp.stack(
        [table[11], table[14], table[15], relative(16), relative(20), table[19], table[22], table[23]]
    )
    stream_two, cross_raw, stream_three, mixed_own, cross_low, cross_queries, cross_mixed, mlp_low = middle_forward(
        mixed, stream_one, middle_table, text_rel, group, all_two, heads
    )
    mlp_low, cot_blocks[-1] = lax.optimization_barrier((mlp_low, cot_blocks[-1]))
    while len(cot_blocks) < split:
        cot_blocks.append(rot(cot_blocks[-1], 1))
    mlp_blocks = ring_gather(mlp_low)
    hidden_bias = lax.dynamic_slice_in_dim(bias_all, place * hidden, hidden, 0)

    hidden_lows, pre_lows, out_parts, back_parts = [], [], [], []
    for r in range(split):
        hidden_pre = dot(mlp_blocks[r], w_up) + hidden_bias
        activated, pull = jax.vjp(gelu, hidden_pre)
        hidden_lows.append(activated.astype(BFLOAT))
        pre_lows.append(pull(dot(cot_blocks[r], w_down_t))[0].astype(BFLOAT))
        back_parts.append(dot(pre_lows[r], w_up, NT))
        out_parts.append(dot(hidden_lows[r], w_down_t, NT))
    grad_mlp_in = ring_scatter(back_parts)

    rows_grad = {}
    grad_bias = sum(jnp.sum(item, axis=0, dtype=FLOAT) for item in pre_lows)
    grads_one = pack_grad(None, mlp_blocks, pre_lows, 2 * hidden, 0, 512)
    grads_one = pack_grad(grads_one, cot_blocks, hidden_lows, 2 * hidden, hidden, 512)
    grads_one, grad_mlp_in, out_parts[1] = lax.optimization_barrier((grads_one, grad_mlp_in, out_parts[1]))
    out_hop = rot(out_parts[1].astype(BFLOAT), 1)
    summed_one = lax.psum_scatter(grads_one, "dp", scatter_dimension=0, tiled=True).astype(FLOAT)
    cot_here = out_grad.astype(FLOAT)
    rows_grad[24] = jnp.sum(cot_here, axis=0)
    three_low, cq_low, two_low, grad_two, middle_rows, *pieces = middle_backward(
        grad_mlp_in, out_grad, stream_three, stream_two, cross_raw, cross_queries, middle_table, text_rel, group,
        all_two, heads,
    )
    grad_mixed, text_terms = pieces[:split], pieces[split:]
    for index, number in enumerate((22, 23, 19, 14, 15, 11)):
        rows_grad[number] = middle_rows[index]
    rows_grad[16], rows_grad[20] = absolute(middle_rows[6]), absolute(middle_rows[7])
    out_hop, *grad_mixed = lax.optimization_barrier((out_hop, *grad_mixed))
    grad_mixed = exchange(grad_mixed)
    lanes_two = 3 * width
    grads_two = pack_grad(None, [two_low], [mixed_own], lanes_two, 0, width)
    grads_two = pack_grad(grads_two, [cross_low], [cq_low], lanes_two, width, width)
    grads_two = pack_grad(grads_two, [three_low], [cross_mixed], lanes_two, 2 * width, width)
    grads_two, *grad_mixed = lax.optimization_barrier((grads_two, *grad_mixed))
    summed_two = lax.psum_scatter(grads_two, "dp", scatter_dimension=0, tiled=True)
    text_terms[1:] = lax.optimization_barrier((*text_terms[1:], grad_mixed[-1]))[:-1]
    text_got = [rot(text_terms[r], split - r) for r in range(1, split)]
    grad_raw, gain_grads, raw_sums = attend_backward(
        raws, turns, gains, kept, grad_mixed, heads, block
    )
    grad_raw, summed_one = lax.optimization_barrier((grad_raw, summed_one))
    text_got[0], grad_raw = lax.optimization_barrier((text_got[0], grad_raw))
    ckv_low, text_rows = text_norm_back([text_terms[0], *text_got], text_raw, head_slice(21)[None], group)
    rows_grad[21] = spread(text_rows[1, :span])
    rows_grad[17], rows_grad[18] = spread(text_rows[0, :span]), spread(text_rows[0, span:])

    gain_grads = undeepen(jnp.sum(gain_grads, axis=1))
    raw_sums = undeepen(jnp.sum(raw_sums, axis=1))
    rows_grad[12], rows_grad[13] = spread(gain_grads[0]), spread(gain_grads[1])
    rows_grad[8], rows_grad[9], rows_grad[10] = spread(raw_sums[0]), spread(raw_sums[1]), spread(raw_sums[2])
    qkv_lanes = 3 * deep
    text_lanes = pl.cdiv(2 * span, LANES) * LANES
    shared = 2 * width + LANES
    qkv_start = pl.cdiv(shared, deep) * deep
    text_start = qkv_start + qkv_lanes
    lanes_three = text_start + text_lanes
    bias_part = up_bias.shape[0]
    bias_cols = pl.cdiv(bias_part, part)
    bias_spread = lax.dynamic_update_slice_in_dim(jnp.zeros(bias_all.shape, FLOAT), grad_bias, place * hidden, 0)
    zero_row = jnp.zeros((width,), FLOAT)
    table_grad = jnp.stack([rows_grad.get(index, zero_row) for index in range(rows_ahead)], axis=1)
    bias_grad = jnp.pad(bias_spread.reshape(shards, bias_part), ((0, 0), (0, bias_cols * part - bias_part)))
    bias_grad = bias_grad.reshape(shards, bias_cols, part).transpose(0, 2, 1).reshape(width, bias_cols)
    small_grads = jnp.concatenate([table_grad, bias_grad], axis=1).astype(BFLOAT)
    small_grads = jnp.pad(small_grads, ((0, 0), (0, qkv_start - 2 * width - small_grads.shape[1])))

    grad_attn_in, shift_part, grads_three = ring_sum(
        grad_raw, attn_blocks, text_full, ckv_low, all_one, 2 * width, lanes_three, (qkv_start, text_start), split
    )
    grads_three = lax.dynamic_update_slice(grads_three, small_grads, (0, 2 * width))
    grads_three, one_low, late_rows = skip_grads(
        grads_three, grad_attn_in, grad_two, stream_one, table[6:7], normed_perm
    )
    grads_three, summed_two, one_low = lax.optimization_barrier((grads_three, summed_two, one_low))
    summed_three = lax.psum_scatter(grads_three, "dp", scatter_dimension=0, tiled=True)
    latent_grad, skip_grad, late, full_sum, text_grad, block_out = side_sums(
        one_low, late_rows, shift_part, jnp.concatenate([table[:2], table[24:25]]), latent, skip_in, stream_three,
        out_hop, summed_two, ckv_low, all_one, all_two, 3 * width, [out_parts[0], *out_parts[2:]], shards, split,
    )
    shift_grads = late[8 : 8 + shards]
    late = lax.dynamic_slice_in_dim(late[:8], me * part, part, 1)
    silu_terms = lax.dot_general(
        shift_grads, mod_weight.astype(FLOAT), ((NT), ((), ())), precision=HIGHEST, preferred_element_type=FLOAT
    )
    summed_three = after(summed_three, silu_terms, full_sum, text_grad, summed_one)
    mod_grad = lax.dot_general(
        silu_mine.astype(FLOAT), shift_grads, ((TN), ((), ())), precision=HIGHEST, preferred_element_type=FLOAT
    )
    into_silu = lax.all_to_all(silu_terms, "dp", 0, 0, tiled=True).reshape(1, width)
    time_full = jax.vjp(silu, condition)[1](into_silu)[0]
    time_grad = lax.dynamic_slice_in_dim(time_full, place * (width // split), width // split, 1)

    qkv_part = summed_three[:, qkv_start:text_start]
    text_part = summed_three[:, text_start : text_start + 2 * span]
    skip_weight_grad, small_sum = spread_sum(summed_three[:, :shared], width, split)
    vectors_grad = jnp.concatenate([late[:5], late[7:8], late[5:7], small_sum[:, 8:rows_ahead].T])
    bias_grad = small_sum[:, rows_ahead : rows_ahead + bias_cols].T.reshape(-1)[:bias_part]
    qkv_sum = dot(qkv_part, expand, NT).reshape(part, 3, span)
    text_sum_grad = text_part.astype(FLOAT).reshape(part, 2, span)

    return (
        block_out,
        latent_grad,
        skip_grad,
        text_grad,
        time_grad,
        skip_weight_grad,
        mod_grad,
        vectors_grad,
        bias_grad,
        qkv_sum,
        full_sum[:, :span].T,
        full_sum[:, span : 2 * span],
        text_sum_grad,
        full_sum[:, 2 * span :].T,
        summed_one[:, :hidden],
        summed_one[:, hidden:].T,
    )


def solution(mesh):
    tokens = P(("dp", "tensor"), None)
    placed = (
        tokens,
        tokens,
        tokens,
        P("dp", None),
        P("dp"),
        P(None, "dp"),
        P("dp", None),
        P("dp", None),
        P(None, "dp"),
        P("dp"),
        P("dp", None, "tensor"),
        P("tensor", "dp"),
        P("dp", "tensor"),
        P("dp", None, "tensor"),
        P("tensor", "dp"),
        P("dp", "tensor"),
        P("tensor", "dp"),
        tokens,
    )
    return jax.shard_map(
        on_device,
        mesh=mesh,
        in_specs=placed,
        out_specs=(
            tokens,
            tokens,
            tokens,
            tokens,
            P("dp", "tensor"),
            P("dp", None),
            P("dp", None),
            P(None, "dp"),
            P("dp"),
            P("dp", None, "tensor"),
            P("tensor", "dp"),
            P("dp", "tensor"),
            P("dp", None, "tensor"),
            P("tensor", "dp"),
            P("dp", "tensor"),
            P("tensor", "dp"),
        ),
        check_vma=False,
    )
```
